32 devices in a mesh: dom: 16 (over z, y, core), feat: 2 (over x).
Axes of the slice: x: 2, y: 2, z: 4, core: 2. Of those that a mesh axis runs over, the one named last changes fastest.
Arguments:
- node_features: bfloat16 [16384, 128], P('dom'), may hold values from -6 to 6
- weight: bfloat16 [128, 256], P(None, 'feat'), may hold values from -0.5 to 0.5
- bias: float32 [256], P('feat'), may hold values from -3 to 3
- tile_values: bfloat16 [1536, 128, 128], P('dom')
- tile_src: int32 [1536], P('dom'), may hold values from 0 to 7
- tile_dst: int32 [1536], P('dom'), may hold values from 0 to 31, as said below
- tile_counts: int32 [16], P('dom'), may hold values from 4 to 96
- out_grad: bfloat16 [16384, 256], P('dom', 'feat'), may hold values from -6 to 6
Outputs:
- output: bfloat16 [16384, 256], P('dom', 'feat')
- weight_grad: float32 [128, 256], P(None, 'feat')
- bias_grad: float32 [256], P('feat')
- input_grad: bfloat16 [16384, 128], P('dom', 'feat')
The draws below stay inside these ranges and needn't reach their ends.
Inputs may be any that keep to these rules, and one draw needn't show every extreme that they name: The partition offset tile_dst[k] // 8 of slot k of a partition equals k mod 4.
All inputs are finite; a program needn't handle non-finite values.
Results may differ from the reference program's by a relative error of at most 0.0075.
Values may be sent and summed in bfloat16 or wider, within the bound.
No kernel may reach another device: no remote copies, remote signals or barrier semaphores. Data moves between devices by JAX's collectives and lax.ppermute only.
A program may use at most 64 MiB of HBM per device.

```python
import math
import jax
import jax.numpy as jnp
from jax import lax

F_IN = 128
HID = 256
BLOCK = 128
REACH = 4
NODE_DEV = 1024
CAP = 96
NB = 8
NODES = 16384
TILES = 1536
N_DOM = 16


def draw_tile_values(key, part):
    key = jax.random.fold_in(key, 11)
    mask_key, value_key = jax.random.split(key)
    present = (jax.random.randint(mask_key, (TILES, BLOCK, BLOCK), 0, 4) == 0).astype(jnp.float32)
    factor = 2.0 / math.sqrt(BLOCK * max(CAP // (NODE_DEV // BLOCK), 1))
    entries = jax.random.uniform(value_key, (TILES, BLOCK, BLOCK), jnp.float32, 0.5, 1.5)
    return (present * entries * factor).astype(jnp.bfloat16)


def draw_tile_dst(key, part):
    key = jax.random.fold_in(key, 12)
    blocks_dev = NODE_DEV // BLOCK
    within = jax.random.randint(key, (TILES,), 0, blocks_dev)
    slot_number = jnp.arange(TILES, dtype=jnp.int32) % CAP
    return (slot_number % REACH * blocks_dev + within).astype(jnp.int32)


def draw_tile_counts(key, part):
    key = jax.random.fold_in(key, 13)
    base_key, full_key, pick_key = jax.random.split(key, 3)
    lowest = max(REACH, CAP // 5)
    highest = max(lowest + 1, CAP // 2) + 1
    counts = jax.random.randint(base_key, (N_DOM,), lowest, highest)
    full = jax.random.randint(full_key, (N_DOM,), 0, 8) == 0
    chosen = jax.random.randint(pick_key, (), 0, N_DOM)
    full = full | (jnp.arange(N_DOM, dtype=jnp.int32) == chosen)
    return jnp.where(full, CAP, counts).astype(jnp.int32)


def with_ends(array, own_key, low, high):
    longest = array.shape.index(max(array.shape))
    spots = []
    for shift in (0, 1):
        where = [jax.random.randint(jax.random.fold_in(own_key, axis), (), 0, length) for axis, length in enumerate(array.shape)]
        where[longest] = (where[longest] + shift) % array.shape[longest]
        spots.append(tuple(where))
    return array.at[spots[0]].set(low).at[spots[1]].set(high)


def block_levels(own_key, extent, cuts, low, top_value):
    def one(position, shards_of):
        steps = jax.random.uniform(jax.random.fold_in(jax.random.fold_in(own_key, 6), position), (shards_of,), jnp.float32, low / len(cuts), top_value / len(cuts))
        return jnp.repeat(jnp.exp(steps), extent[position] // shards_of).reshape((-1,) + (1,) * (len(extent) - position - 1))

    level = one(*cuts[0])
    for cut in cuts[1:]:
        level = level * one(*cut)
    return level


def centred(stream_key, shape, width, bound, cuts=(), kind=jnp.bfloat16):
    values = width * jax.random.normal(stream_key, shape, jnp.float32)
    if cuts:
        values = values * block_levels(stream_key, shape, cuts, -0.22, 0.18)
    return jnp.clip(values, -bound, bound).astype(kind)


def setup_inputs(seed: int = 0) -> dict:
    arg_keys = jax.random.split(jax.random.key(seed), 9)
    node_features = centred(arg_keys[0], (NODES, F_IN), 1.0, 6.0, ((0, 16),))
    weight = centred(arg_keys[1], (F_IN, HID), F_IN ** -0.5, 0.5, ((1, 2),))
    bias = centred(arg_keys[2], (HID,), 0.5, 3.0, ((0, 2),), jnp.float32)
    tile_values = draw_tile_values(jax.random.fold_in(arg_keys[8], 71), 0)
    tile_src = with_ends(jax.random.randint(arg_keys[4], (TILES,), 0, NB), jax.random.fold_in(arg_keys[4], 1), 0, NB - 1).astype(jnp.int32)
    tile_dst = draw_tile_dst(jax.random.fold_in(arg_keys[8], 71), 0)
    tile_counts = draw_tile_counts(jax.random.fold_in(arg_keys[8], 71), 0)
    out_grad = centred(arg_keys[7], (NODES, HID), 1.0, 6.0, ((0, 16), (1, 2)))
    return dict(node_features=node_features, weight=weight, bias=bias, tile_values=tile_values, tile_src=tile_src, tile_dst=tile_dst, tile_counts=tile_counts, out_grad=out_grad)


def reference(node_features, weight, bias, tile_values, tile_src, tile_dst, tile_counts, out_grad):
    blocks_dev = NODE_DEV // BLOCK
    all_blocks = blocks_dev * N_DOM
    projected = jnp.dot(node_features, weight, preferred_element_type=jnp.float32).astype(jnp.bfloat16)
    proj_blocks = projected.reshape(all_blocks, BLOCK, HID)
    values_dev = tile_values.reshape(N_DOM, CAP, BLOCK, BLOCK)
    src_dev = tile_src.reshape(N_DOM, CAP)
    dst_dev = tile_dst.reshape(N_DOM, CAP)
    owners = jnp.arange(N_DOM, dtype=jnp.int32)
    slots = jnp.arange(CAP, dtype=jnp.int32)

    def indices(owner, sources, targets, used):
        src_global = (owner * blocks_dev + sources).astype(jnp.int32)
        dst_global = (((owner + targets // blocks_dev) % N_DOM) * blocks_dev + targets % blocks_dev).astype(jnp.int32)
        live_slots = (slots < used).astype(jnp.float32)
        return src_global, dst_global, live_slots

    def forward_step(running, items):
        owner, tiles, sources, targets, used = items
        src_global, dst_global, live_slots = indices(owner, sources, targets, used)
        terms = jnp.einsum("kij,kjf->kif", tiles.astype(jnp.float32), proj_blocks[src_global].astype(jnp.float32))
        return running.at[dst_global].add(terms * live_slots[:, None, None]), None

    start = jnp.zeros((all_blocks, BLOCK, HID), jnp.float32)
    aggregated, _ = lax.scan(forward_step, start, (owners, values_dev, src_dev, dst_dev, tile_counts))
    pre = aggregated.reshape(NODE_DEV * N_DOM, HID) + bias[None, :]
    output = jax.nn.silu(pre).astype(jnp.bfloat16)
    sigmoid_pre = jax.nn.sigmoid(pre)
    grad_pre = (out_grad.astype(jnp.float32) * sigmoid_pre * (1.0 + pre * (1.0 - sigmoid_pre))).astype(jnp.bfloat16)
    grad_blocks = grad_pre.reshape(all_blocks, BLOCK, HID)

    def backward_step(running, items):
        owner, tiles, sources, targets, used = items
        src_global, dst_global, live_slots = indices(owner, sources, targets, used)
        terms = jnp.einsum("kji,kjf->kif", tiles.astype(jnp.float32), grad_blocks[dst_global].astype(jnp.float32))
        return running.at[src_global].add(terms * live_slots[:, None, None]), None

    upstream, _ = lax.scan(backward_step, start, (owners, values_dev, src_dev, dst_dev, tile_counts))
    upstream = upstream.reshape(NODE_DEV * N_DOM, HID).astype(jnp.bfloat16)
    weight_grad = jnp.dot(node_features.T, upstream, preferred_element_type=jnp.float32)
    bias_grad = jnp.sum(grad_pre.astype(jnp.float32), axis=0)
    input_grad = jnp.dot(upstream, weight.T, preferred_element_type=jnp.float32).astype(jnp.bfloat16)
    return output, weight_grad, bias_grad, input_grad
```

```python
import functools

import jax
import jax.numpy as jnp
from jax import lax
from jax.experimental import pallas as pl
from jax.experimental.pallas import tpu as pltpu
from jax.sharding import PartitionSpec as P

BLOCK = 128
REACH = 4
UNROLL = 2
F32 = jnp.float32
BF16 = jnp.bfloat16
VMEM = pl.BlockSpec(memory_space=pltpu.VMEM)
SMEM = pl.BlockSpec(memory_space=pltpu.SMEM)


def call(kernel, out_shape, n_smem, n_vmem, scratch, flops):
    return pl.pallas_call(
        kernel,
        out_shape=out_shape,
        in_specs=[SMEM] * n_smem + [VMEM] * n_vmem,
        out_specs=[VMEM] * len(out_shape),
        scratch_shapes=scratch,
        compiler_params=pltpu.CompilerParams(vmem_limit_bytes=24 * 1024 * 1024),
        cost_estimate=pl.CostEstimate(flops=flops, bytes_accessed=2**20, transcendentals=0),
    )


def slot_loop(count, capacity, body):
    step = REACH * UNROLL if capacity % (REACH * UNROLL) == 0 else REACH

    def group(g, carry):
        for u in range(step):
            k = g * step + u
            body(k, u % REACH, k < count)
        return carry

    lax.fori_loop(0, (count + step - 1) // step, group, 0)


def forward_kernel(count_ref, src_ref, dst_ref, x_ref, tiles_ref, p0, p1, p2, p3, xt, *acc):
    blocks, width, _ = xt.shape
    capacity = tiles_ref.shape[0]
    first = pl.multiple_of(lax.axis_index("feat") * width, width)
    for b in range(blocks):
        xt[b] = x_ref[b * BLOCK : (b + 1) * BLOCK, :].T[: , :] if width == x_ref.shape[1] else (
            columns(x_ref, b, first, width)
        )
    for a in acc:
        a[...] = jnp.zeros_like(a)

    def body(k, o, live):
        d = jnp.where(live, dst_ref[k] - o * blocks, blocks)
        acc[o][d] += lax.dot_general(
            xt[src_ref[k]], tiles_ref[k], (((1,), (1,)), ((), ())), preferred_element_type=F32
        )

    slot_loop(count_ref[0], capacity, body)
    for out, a in zip((p0, p1, p2, p3), acc):
        out[...] = a[:blocks].astype(out.dtype)


def columns(x_ref, b, first, width):
    whole = x_ref[b * BLOCK : (b + 1) * BLOCK, :].astype(F32).T
    picked = whole[:width]
    for q in range(1, whole.shape[0] // width):
        picked = jnp.where(first == q * width, whole[q * width : (q + 1) * width], picked)
    return picked.astype(BF16)


def sum_kernel(n, *refs):
    total = refs[0][...].astype(F32)
    for r in refs[1:n]:
        total = total + r[...].astype(F32)
    refs[n][...] = total.astype(refs[n].dtype)


def middle_kernel(parts, bias_ref, w_ref, og_ref, *refs):
    h_refs, (out_ref, wg_ref), g_refs, (ht, grads) = (
        refs[:parts],
        refs[parts : parts + 2],
        refs[parts + 2 : parts + 2 + parts],
        refs[2 * parts + 2 :],
    )
    blocks, width, _ = h_refs[0].shape
    f_in = w_ref.shape[0]
    me = lax.axis_index("feat")
    for q in range(parts):
        row = pl.multiple_of(lax.rem(me + q, parts) * width, width)
        for b in range(blocks):
            ht[pl.ds(row, width), b * BLOCK : (b + 1) * BLOCK] = h_refs[q][b]
    ht[f_in:, :] = jnp.ones((ht.shape[0] - f_in, ht.shape[1]), BF16)
    for b in range(blocks):
        rows = slice(b * BLOCK, (b + 1) * BLOCK)
        pre = lax.dot_general(
            ht[:f_in, rows], w_ref[...], (((0,), (0,)), ((), ())), preferred_element_type=F32
        ) + bias_ref[...]
        s = jax.nn.sigmoid(pre)
        out_ref[rows, :] = (pre * s).astype(BF16)
        grad = (og_ref[rows, :].astype(F32) * s * (1.0 + pre * (1.0 - s))).astype(BF16)
        grads[rows, :] = grad
        for q in range(parts):
            row = pl.multiple_of(lax.rem(me + q, parts) * width, width)
            g_refs[q][b] = lax.dot_general(
                w_ref[pl.ds(row, width), :], grad, (((1,), (1,)), ((), ())), preferred_element_type=F32
            ).astype(g_refs[q].dtype)
    wg_ref[...] = jnp.dot(ht[...], grads[...], preferred_element_type=F32)


def backward_kernel(count_ref, src_ref, dst_ref, tiles_ref, g0, g1, g2, g3, out_ref, *acc):
    blocks = g0.shape[0]
    gs = (g0, g1, g2, g3)
    for a in acc:
        a[...] = jnp.zeros_like(a)

    def body(k, o, live):
        s = jnp.where(live, src_ref[k], blocks)
        acc[o][s] += jnp.dot(gs[o][dst_ref[k] - o * blocks], tiles_ref[k], preferred_element_type=F32)

    slot_loop(count_ref[0], tiles_ref.shape[0], body)
    for b in range(blocks):
        total = acc[0][b] + acc[1][b] + acc[2][b] + acc[3][b]
        out_ref[:, b * BLOCK : (b + 1) * BLOCK] = total.astype(BF16)


def passed_along(block, axis, distance):
    n = lax.axis_size(axis)
    return lax.ppermute(block, axis, [(i, (i + distance) % n) for i in range(n)])


def radices(n):
    out = []
    while n > 1:
        r = 4 if n % 4 == 0 else 2 if n % 2 == 0 else n
        out.append(r)
        n //= r
    return out


def sum_over(part, axis):
    n = lax.axis_size(axis)
    stride = 1
    for r in radices(n):
        def moved(i, step):
            digit = i // stride % r
            return i + ((digit + step) % r - digit) * stride

        received = [lax.ppermute(part, axis, [(i, moved(i, s)) for i in range(n)]) for s in range(1, r)]
        for other in received:
            part = part + other
        stride *= r
    return part


def shards(node_features, weight, bias, tile_values, tile_src, tile_dst, tile_counts, out_grad):
    nodes, f_in = node_features.shape
    hid = weight.shape[1]
    blocks = nodes // BLOCK
    parts = lax.axis_size("feat")
    width = f_in // parts
    capacity = tile_values.shape[0]
    piece = (blocks, width, BLOCK)
    bf_piece = jax.ShapeDtypeStruct(piece, BF16)
    f32_piece = jax.ShapeDtypeStruct(piece, F32)
    accs = [pltpu.VMEM((blocks + 1, width, BLOCK), F32)] * REACH
    tile_flops = 2 * capacity * BLOCK * BLOCK * width

    own, *partials = call(
        forward_kernel, [f32_piece] + [bf_piece] * (REACH - 1), 3, 2, [pltpu.VMEM(piece, BF16)] + accs, tile_flops
    )(tile_counts, tile_src, tile_dst, node_features, tile_values)
    received = [passed_along(p, "dom", o + 1) for o, p in enumerate(partials)]
    (h,) = call(functools.partial(sum_kernel, REACH), [bf_piece], 0, REACH, [], 0)(own, *received)
    hs = [h] + [passed_along(h, "feat", -q) for q in range(1, parts)]
    output, wg, g_own, *g_others = call(
        functools.partial(middle_kernel, parts),
        [
            jax.ShapeDtypeStruct((nodes, hid), BF16),
            jax.ShapeDtypeStruct((f_in + 16, hid), F32),
            f32_piece,
        ]
        + [bf_piece] * (parts - 1),
        0,
        3 + parts,
        [pltpu.VMEM((f_in + 16, nodes), BF16), pltpu.VMEM((nodes, hid), BF16)],
        6 * nodes * f_in * hid,
    )(bias.reshape(1, hid), weight, out_grad, *hs)
    g_received = [passed_along(g, "feat", q + 1) for q, g in enumerate(g_others)]
    (g,) = call(functools.partial(sum_kernel, parts), [bf_piece], 0, parts, [], 0)(g_own, *g_received)
    gs = [g] + [passed_along(g, "dom", -o) for o in range(1, REACH)]
    (input_grad,) = call(
        backward_kernel, [jax.ShapeDtypeStruct((width, nodes), BF16)], 3, 1 + REACH, accs, tile_flops
    )(tile_counts, tile_src, tile_dst, tile_values, *gs)
    wg = sum_over(wg[: f_in + 8], "dom")
    return output, wg[:f_in], wg[f_in], input_grad.T


def solution(mesh):
    return jax.shard_map(
        shards,
        mesh=mesh,
        in_specs=(
            P("dom", None),
            P(None, "feat"),
            P("feat"),
            P("dom", None, None),
            P("dom"),
            P("dom"),
            P("dom"),
            P("dom", "feat"),
        ),
        out_specs=(P("dom", "feat"), P(None, "feat"), P("feat"), P("dom", "feat")),
        check_vma=False,
    )
```

```python
import functools

import jax
import jax.numpy as jnp
from jax import lax
from jax.experimental import pallas as pl
from jax.experimental.pallas import tpu as pltpu
from jax.sharding import PartitionSpec as P

BLOCK = 128
REACH = 4
F32 = jnp.float32
BF16 = jnp.bfloat16
VMEM = pl.BlockSpec(memory_space=pltpu.VMEM)
SMEM = pl.BlockSpec(memory_space=pltpu.SMEM)
HBM = pl.BlockSpec(memory_space=pltpu.HBM)


def call(kernel, out_shape, in_specs, scratch=(), flops=0):
    return pl.pallas_call(
        kernel,
        out_shape=out_shape,
        in_specs=in_specs,
        out_specs=[VMEM] * len(out_shape),
        scratch_shapes=list(scratch),
        compiler_params=pltpu.CompilerParams(vmem_limit_bytes=24 * 1024 * 1024),
        cost_estimate=pl.CostEstimate(flops=flops, bytes_accessed=2**20, transcendentals=0),
    )


def groups_at_once(groups):
    return next(m for m in (4, 3, 2, 1) if groups % m == 0)


def in_hbm(a):
    return pltpu.with_memory_space_constraint(a, pltpu.HBM)


def own_core():
    return lax.rem(lax.axis_index("dom"), 2)


def slot_loop(count, groups, offsets, body, arrive=None):
    m = groups_at_once(groups)

    def chunk(i, carry):
        if arrive is not None:
            arrive(i)

        @pl.when(i * (m * REACH) < count)
        def _():
            for u in range(m):
                for o in offsets:
                    j = i * m + u
                    body(j, o, j * REACH + o < count)

        return carry

    lax.fori_loop(0, groups // m, chunk, 0)


def push(xt, tiles_ref, src_ref, dst_ref, j, o, live, acc):
    blocks = xt.shape[0]
    k = j * REACH + o
    d = jnp.where(live, dst_ref[k] - o * blocks, blocks)
    acc[d] += lax.dot_general(
        xt[src_ref[k]], tiles_ref[j, o], (((1,), (1,)), ((), ())), preferred_element_type=F32
    )


def forward_far_kernel(
    count, src_hbm, dst_hbm, x_hbm, tiles_hbm, tiles, xt, direct, swap, x, src, dst, acc1, acc3, small, large
):
    blocks, width, _ = xt.shape
    groups = tiles.shape[0]
    m = groups_at_once(groups)
    copies = [
        pltpu.make_async_copy(a, b, small.at[i])
        for i, (a, b) in enumerate(((x_hbm, x), (src_hbm, src), (dst_hbm, dst)))
    ]

    def chunk(i):
        part = pl.ds(i * m, m)
        return pltpu.make_async_copy(tiles_hbm.at[part], tiles.at[part], large.at[i])

    for c in copies:
        c.start()
    for i in range(groups // m):
        chunk(i).start()
    for a in (acc1, acc3):
        a[...] = jnp.zeros_like(a)
    row = lax.broadcasted_iota(jnp.int32, (width, x.shape[1]), 0)
    column = lax.broadcasted_iota(jnp.int32, (width, x.shape[1]), 1)
    pick = (column == row + lax.axis_index("feat") * width).astype(BF16)
    for c in copies:
        c.wait()
    for b in range(blocks):
        xt[b] = lax.dot_general(
            pick, x[b * BLOCK : (b + 1) * BLOCK, :], (((1,), (1,)), ((), ())), preferred_element_type=F32
        ).astype(BF16)

    def body(j, o, live):
        push(xt, tiles, src, dst, j, o, live, acc1 if o == 1 else acc3)

    slot_loop(count[0], groups, (1, 3), body, lambda i: chunk(i).wait())
    first = own_core() == 0

    @pl.when(first)
    def _():
        direct[...] = acc1[:blocks].astype(BF16)
        swap[...] = acc3[:blocks].astype(BF16)

    @pl.when(jnp.logical_not(first))
    def _():
        direct[...] = acc3[:blocks].astype(BF16)
        swap[...] = acc1[:blocks].astype(BF16)


def forward_near_kernel(count, src, dst, xt, tiles, acc0, acc2):
    for a in (acc0, acc2):
        a[...] = jnp.zeros_like(a)

    def body(j, o, live):
        push(xt, tiles, src, dst, j, o, live, acc2 if o == 2 else acc0)

    slot_loop(count[0], tiles.shape[0], (2, 0), body)


def sum_kernel(n, *refs):
    out = refs[n]
    blocks = out.shape[0]
    total = refs[0][:blocks].astype(F32)
    for r in refs[1:n]:
        total = total + r[:blocks].astype(F32)
    out[...] = total.astype(out.dtype)


def middle_kernel(parts, bias_ref, w_ref, og_ref, *refs):
    h_refs, (out_ref, ht, grads), g_refs = refs[:parts], refs[parts : parts + 3], refs[parts + 3 :]
    blocks, width, _ = h_refs[0].shape
    f_in = w_ref.shape[0]
    me = lax.axis_index("feat")
    for q in range(parts):
        row = pl.multiple_of(lax.rem(me + q, parts) * width, width)
        for b in range(blocks):
            ht[pl.ds(row, width), b * BLOCK : (b + 1) * BLOCK] = h_refs[q][b]
    ht[f_in:, :] = jnp.ones((ht.shape[0] - f_in, ht.shape[1]), BF16)
    for b in range(blocks):
        rows = slice(b * BLOCK, (b + 1) * BLOCK)
        pre = lax.dot_general(
            ht[:f_in, rows], w_ref[...], (((0,), (0,)), ((), ())), preferred_element_type=F32
        ) + bias_ref[...]
        s = jax.nn.sigmoid(pre)
        out_ref[rows, :] = (pre * s).astype(BF16)
        grad = (og_ref[rows, :].astype(F32) * s * (1.0 + pre * (1.0 - s))).astype(BF16)
        grads[rows, :] = grad
        for q in range(parts):
            row = pl.multiple_of(lax.rem(me + q, parts) * width, width)
            g_refs[q][b] = lax.dot_general(
                w_ref[pl.ds(row, width), :], grad, (((1,), (1,)), ((), ())), preferred_element_type=F32
            ).astype(g_refs[q].dtype)


def weight_grad_kernel(ht, grads, out):
    full = jnp.dot(ht[...], grads[...], preferred_element_type=F32)
    out[...] = full[: out.shape[0]]


def pull(g, tiles, src, dst, j, o, live, acc):
    blocks = g.shape[0]
    k = j * REACH + o
    s = jnp.where(live, src[k], blocks)
    acc[s] += jnp.dot(g[dst[k] - o * blocks], tiles[j, o], preferred_element_type=F32)


def backward_own_kernel(count, src, dst, tiles, g0, acc):
    acc[...] = jnp.zeros_like(acc)
    slot_loop(
        count[0], tiles.shape[0], (0,), lambda j, o, live: pull(g0, tiles, src, dst, j, o, live, acc)
    )


def backward_near_kernel(count, src, dst, tiles, g2, gd, acc2, accd):
    acc2[...] = jnp.zeros_like(acc2)
    accd[...] = jnp.zeros_like(accd)
    far = 1 + 2 * own_core()

    def body(j, o, live):
        if o == 2:
            pull(g2, tiles, src, dst, j, o, live, acc2)
        else:
            pull(gd, tiles, src, dst, j, far, j * REACH + far < count[0], accd)

    slot_loop(count[0], tiles.shape[0], (2, 1), body)


def backward_last_kernel(count, src, dst, tiles, g, acc0, acc2, accd, out, acc):
    blocks = g.shape[0]
    acc[...] = jnp.zeros_like(acc)
    far = 3 - 2 * own_core()
    slot_loop(
        count[0],
        tiles.shape[0],
        (0,),
        lambda j, o, live: pull(g, tiles, src, dst, j, far, j * REACH + far < count[0], acc),
    )
    for b in range(blocks):
        total = acc[b] + acc0[b] + acc2[b] + accd[b]
        out[:, b * BLOCK : (b + 1) * BLOCK] = total.astype(BF16)


def moved(block, axis, target):
    n = lax.axis_size(axis)
    return lax.ppermute(block, axis, [(i, target(i) % n) for i in range(n)])


def radices(n):
    out = []
    while n > 1:
        r = 2 if n % 2 == 0 else n
        out.append(r)
        n //= r
    return out


def sum_step(part, axis, stride, r):
    def target(step, i):
        digit = i // stride % r
        return i + ((digit + step) % r - digit) * stride

    received = [moved(part, axis, functools.partial(target, s)) for s in range(1, r)]
    for other in received:
        part = part + other
    return part


def shards(node_features, weight, bias, tile_values, tile_src, tile_dst, tile_counts, out_grad):
    nodes, f_in = node_features.shape
    hid = weight.shape[1]
    blocks = nodes // BLOCK
    parts = lax.axis_size("feat")
    width = f_in // parts
    capacity = tile_values.shape[0]
    groups = capacity // REACH
    piece = jax.ShapeDtypeStruct((blocks, width, BLOCK), BF16)
    wide = jax.ShapeDtypeStruct((blocks, width, BLOCK), F32)
    totals = jax.ShapeDtypeStruct((blocks + 1, width, BLOCK), F32)
    acc = pltpu.VMEM(totals.shape, F32)
    tiles = jax.ShapeDtypeStruct((groups, REACH, BLOCK, BLOCK), BF16)
    m = groups_at_once(groups)
    flops = 2 * capacity * BLOCK * BLOCK * width // REACH
    index = (tile_counts, tile_src, tile_dst)

    def swapped(i):
        return i ^ 1

    tiles, xt, direct, swap = call(
        forward_far_kernel,
        [tiles, piece, piece, piece],
        [SMEM] + [HBM] * 4,
        [
            pltpu.VMEM(node_features.shape, BF16),
            pltpu.SMEM((capacity,), jnp.int32),
            pltpu.SMEM((capacity,), jnp.int32),
            acc,
            acc,
            pltpu.SemaphoreType.DMA((3,)),
            pltpu.SemaphoreType.DMA((groups // m,)),
        ],
        2 * flops,
    )(tile_counts, *(in_hbm(a) for a in (tile_src, tile_dst, node_features, tile_values.reshape(tiles.shape))))
    swap = moved(swap, "dom", swapped)
    direct = moved(direct, "dom", lambda i: i + 1 + 2 * (i % 2))
    acc0, acc2 = call(forward_near_kernel, [totals, totals], [SMEM] * 3 + [VMEM] * 2, (), 2 * flops)(
        *index, xt, tiles
    )
    (chip,) = call(functools.partial(sum_kernel, 2), [piece], [VMEM] * 2)(acc2, swap)
    chip = moved(chip, "dom", lambda i: i + 2)
    (h,) = call(functools.partial(sum_kernel, 3), [piece], [VMEM] * 3)(acc0, direct, chip)
    hs = [h] + [moved(h, "feat", lambda i, q=q: i - q) for q in range(1, parts)]
    output, ht, grads, g_own, *g_others = call(
        functools.partial(middle_kernel, parts),
        [
            jax.ShapeDtypeStruct((nodes, hid), BF16),
            jax.ShapeDtypeStruct((f_in + 16, nodes), BF16),
            jax.ShapeDtypeStruct((nodes, hid), BF16),
            wide,
        ]
        + [piece] * (parts - 1),
        [VMEM] * (3 + parts),
        (),
        4 * nodes * f_in * hid,
    )(bias.reshape(1, hid), weight, out_grad, *hs)
    g_received = [moved(g, "feat", lambda i, q=q + 1: i + q) for q, g in enumerate(g_others)]
    (wg,) = call(
        weight_grad_kernel,
        [jax.ShapeDtypeStruct((f_in + 8, hid), F32)],
        [VMEM] * 2,
        (),
        2 * nodes * f_in * hid,
    )(ht, grads)
    (g,) = call(functools.partial(sum_kernel, parts), [piece], [VMEM] * parts)(g_own, *g_received)
    stride, *steps = radices(lax.axis_size("dom"))
    wg = sum_step(wg, "dom", 1, stride)
    g, wg = lax.optimization_barrier((g, wg))
    g_chip = moved(g, "dom", lambda i: i - 2)
    g_direct = moved(g, "dom", lambda i: i - 3 + 2 * (i % 2))
    (back0,) = call(backward_own_kernel, [totals], [SMEM] * 3 + [VMEM] * 2, (), flops)(*index, tiles, g)
    g_swap = moved(g_chip, "dom", swapped)
    back2, backd = call(backward_near_kernel, [totals, totals], [SMEM] * 3 + [VMEM] * 3, (), 2 * flops)(
        *index, tiles, g_chip, g_direct
    )
    (input_grad,) = call(
        backward_last_kernel,
        [jax.ShapeDtypeStruct((width, nodes), BF16)],
        [SMEM] * 3 + [VMEM] * 5,
        [acc],
        flops,
    )(*index, tiles, g_swap, back0, back2, backd)
    for r in steps:
        wg = sum_step(wg, "dom", stride, r)
        stride *= r
    return output, wg[:f_in], wg[f_in], input_grad.T


def solution(mesh):
    return jax.shard_map(
        shards,
        mesh=mesh,
        in_specs=(
            P("dom", None),
            P(None, "feat"),
            P("feat"),
            P("dom", None, None),
            P("dom"),
            P("dom"),
            P("dom"),
            P("dom", "feat"),
        ),
        out_specs=(P("dom", "feat"), P(None, "feat"), P("feat"), P("dom", "feat")),
        check_vma=False,
    )
```

```python
import functools

import jax
import jax.numpy as jnp
from jax import lax
from jax.experimental import pallas as pl
from jax.experimental.pallas import tpu as pltpu
from jax.sharding import PartitionSpec as P

BLOCK = 128
REACH = 4
F32 = jnp.float32
BF16 = jnp.bfloat16
VMEM = pl.BlockSpec(memory_space=pltpu.VMEM)
SMEM = pl.BlockSpec(memory_space=pltpu.SMEM)
HBM = pl.BlockSpec(memory_space=pltpu.HBM)


def call(kernel, out_shape, in_specs, out_specs, scratch=(), flops=0):
    return pl.pallas_call(
        kernel,
        out_shape=out_shape,
        in_specs=in_specs,
        out_specs=out_specs,
        scratch_shapes=list(scratch),
        compiler_params=pltpu.CompilerParams(vmem_limit_bytes=24 * 1024 * 1024),
        cost_estimate=pl.CostEstimate(flops=flops, bytes_accessed=2**20, transcendentals=0),
    )


def groups_at_once(groups):
    return next(m for m in (4, 3, 2, 1) if groups % m == 0)


def in_hbm(a):
    return pltpu.with_memory_space_constraint(a, pltpu.HBM)


def own_core():
    return lax.rem(lax.axis_index("dom"), 2)


def slot_loop(count, groups, offsets, body, arrive=None):
    m = groups_at_once(groups)

    def chunk(i, carry):
        if arrive is not None:
            arrive(i)

        @pl.when(i * (m * REACH) < count)
        def _():
            for u in range(m):
                for o in offsets:
                    j = i * m + u
                    body(j, o, j * REACH + o < count)

        return carry

    lax.fori_loop(0, groups // m, chunk, 0)


def push(xt, tiles_ref, src_ref, dst_ref, acc, j, o, live):
    blocks = xt.shape[0]
    k = j * REACH + o
    d = jnp.where(live, dst_ref[k] - o * blocks, blocks)
    acc[d] += lax.dot_general(
        xt[src_ref[k]], tiles_ref[j, o], (((1,), (1,)), ((), ())), preferred_element_type=F32
    )


def forward_swap_kernel(
    count, src_hbm, dst_hbm, x_hbm, tiles_hbm, tiles, xt, swap, src, dst, x, acc, small, large
):
    blocks, width, _ = xt.shape
    groups = tiles.shape[0]
    m = groups_at_once(groups)
    copies = [
        pltpu.make_async_copy(a, b, small.at[i])
        for i, (a, b) in enumerate(((x_hbm, x), (src_hbm, src), (dst_hbm, dst)))
    ]

    def chunk(i):
        part = pl.ds(i * m, m)
        return pltpu.make_async_copy(tiles_hbm.at[part], tiles.at[part], large.at[i])

    for c in copies:
        c.start()
    for i in range(groups // m):
        chunk(i).start()
    acc[...] = jnp.zeros_like(acc)
    row = lax.broadcasted_iota(jnp.int32, (width, x.shape[1]), 0)
    column = lax.broadcasted_iota(jnp.int32, (width, x.shape[1]), 1)
    pick = (column == row + lax.axis_index("feat") * width).astype(BF16)
    for c in copies:
        c.wait()
    for b in range(blocks):
        xt[b] = lax.dot_general(
            pick, x[b * BLOCK : (b + 1) * BLOCK, :], (((1,), (1,)), ((), ())), preferred_element_type=F32
        ).astype(BF16)
    o = 3 - 2 * own_core()
    slot_loop(
        count[0], groups, (o,), functools.partial(push, xt, tiles, src, dst, acc), lambda i: chunk(i).wait()
    )
    swap[...] = acc[:blocks].astype(BF16)


def forward_send_kernel(count, src, dst, xt, tiles, acc2, direct, acc):
    acc2[...] = jnp.zeros_like(acc2)
    acc[...] = jnp.zeros_like(acc)
    far = 1 + 2 * own_core()

    def body(j, o, live):
        push(xt, tiles, src, dst, acc2 if isinstance(o, int) else acc, j, o, live)

    slot_loop(count[0], tiles.shape[0], (2, far), body)
    direct[...] = acc[: direct.shape[0]].astype(BF16)


def forward_own_kernel(count, src, dst, xt, tiles, acc):
    acc[...] = jnp.zeros_like(acc)
    slot_loop(count[0], tiles.shape[0], (0,), functools.partial(push, xt, tiles, src, dst, acc))


def sum_kernel(n, *refs):
    out = refs[n]
    blocks = out.shape[0]
    total = refs[0][:blocks].astype(F32)
    for r in refs[1:n]:
        total = total + r[:blocks].astype(F32)
    out[...] = total.astype(out.dtype)


def middle_kernel(parts, bias_ref, w_ref, og_ref, *refs):
    h_refs, (out_ref, ht, grads), g_refs = refs[:parts], refs[parts : parts + 3], refs[parts + 3 :]
    blocks, width, _ = h_refs[0].shape
    f_in = w_ref.shape[0]
    me = lax.axis_index("feat")
    for q in range(parts):
        row = pl.multiple_of(lax.rem(me + q, parts) * width, width)
        for b in range(blocks):
            ht[pl.ds(row, width), b * BLOCK : (b + 1) * BLOCK] = h_refs[q][b]
    ht[f_in:, :] = jnp.ones((ht.shape[0] - f_in, ht.shape[1]), BF16)
    for b in range(blocks):
        rows = slice(b * BLOCK, (b + 1) * BLOCK)
        pre = lax.dot_general(
            ht[:f_in, rows], w_ref[...], (((0,), (0,)), ((), ())), preferred_element_type=F32
        ) + bias_ref[...]
        s = jax.nn.sigmoid(pre)
        out_ref[rows, :] = (pre * s).astype(BF16)
        grad = (og_ref[rows, :].astype(F32) * s * (1.0 + pre * (1.0 - s))).astype(BF16)
        grads[rows, :] = grad
        for q in range(parts):
            row = pl.multiple_of(lax.rem(me + q, parts) * width, width)
            g_refs[q][b] = lax.dot_general(
                w_ref[pl.ds(row, width), :], grad, (((1,), (1,)), ((), ())), preferred_element_type=F32
            ).astype(g_refs[q].dtype)


def weight_grad_kernel(ht, grads, act, out, wg, sem):
    copy = pltpu.make_async_copy(act, out, sem)
    copy.start()
    full = jnp.dot(ht[...], grads[...], preferred_element_type=F32)
    wg[...] = full[: wg.shape[0]]
    copy.wait()


def pull(g, tiles, src, dst, acc, j, o, live):
    blocks = g.shape[0]
    k = j * REACH + o
    s = jnp.where(live, src[k], blocks)
    acc[s] += jnp.dot(g[dst[k] - o * blocks], tiles[j, o], preferred_element_type=F32)


def backward_own_kernel(count, src, dst, tiles, g0, acc):
    acc[...] = jnp.zeros_like(acc)
    slot_loop(count[0], tiles.shape[0], (0,), functools.partial(pull, g0, tiles, src, dst, acc))


def backward_near_kernel(count, src, dst, tiles, g2, gd, acc2, accd):
    acc2[...] = jnp.zeros_like(acc2)
    accd[...] = jnp.zeros_like(accd)
    far = 1 + 2 * own_core()

    def body(j, o, live):
        if isinstance(o, int):
            pull(g2, tiles, src, dst, acc2, j, o, live)
        else:
            pull(gd, tiles, src, dst, accd, j, o, live)

    slot_loop(count[0], tiles.shape[0], (2, far), body)


def backward_last_kernel(count, src, dst, tiles, g, acc0, acc2, accd, *refs):
    parts, (out, wg, bias, acc) = refs[:-4], refs[-4:]
    blocks = g.shape[0]
    acc[...] = jnp.zeros_like(acc)
    far = 3 - 2 * own_core()
    slot_loop(count[0], tiles.shape[0], (far,), functools.partial(pull, g, tiles, src, dst, acc))
    for b in range(blocks):
        total = acc[b] + acc0[b] + acc2[b] + accd[b]
        out[:, b * BLOCK : (b + 1) * BLOCK] = total.astype(BF16)
    whole = paired_sum([r[...] for r in parts])
    f_in = wg.shape[0]
    wg[...] = whole[:f_in]
    bias[...] = whole[f_in : f_in + 1]


def paired_sum(parts):
    if len(parts) == 4:
        return (parts[0] + parts[2]) + (parts[1] + parts[3])
    return functools.reduce(lambda a, b: a + b, parts)


def paired_sum_kernel(*refs):
    refs[-1][...] = paired_sum([r[...] for r in refs[:-1]])


def moved(block, axis, target):
    n = lax.axis_size(axis)
    return lax.ppermute(block, axis, [(i, target(i) % n) for i in range(n)])


def radices(n):
    out = []
    while n > 1:
        r = 4 if n % 4 == 0 else 2 if n % 2 == 0 else n
        out.append(r)
        n //= r
    return out


def exchanged(part, axis, stride, r):
    def target(step, i):
        digit = i // stride % r
        return i + ((digit + step) % r - digit) * stride

    return [part] + [moved(part, axis, functools.partial(target, s)) for s in range(1, r)]


def shards(node_features, weight, bias, tile_values, tile_src, tile_dst, tile_counts, out_grad):
    nodes, f_in = node_features.shape
    hid = weight.shape[1]
    blocks = nodes // BLOCK
    parts = lax.axis_size("feat")
    width = f_in // parts
    capacity = tile_values.shape[0]
    groups = capacity // REACH
    piece = jax.ShapeDtypeStruct((blocks, width, BLOCK), BF16)
    wide = jax.ShapeDtypeStruct((blocks, width, BLOCK), F32)
    totals = jax.ShapeDtypeStruct((blocks + 1, width, BLOCK), F32)
    acc = pltpu.VMEM(totals.shape, F32)
    tiles = jax.ShapeDtypeStruct((groups, REACH, BLOCK, BLOCK), BF16)
    slots = jax.ShapeDtypeStruct((capacity,), jnp.int32)
    rows = jax.ShapeDtypeStruct((nodes, hid), BF16)
    gradient = jax.ShapeDtypeStruct((f_in + 8, hid), F32)
    m = groups_at_once(groups)
    flops = 2 * capacity * BLOCK * BLOCK * width // REACH

    def swapped(i):
        return i ^ 1

    tiles, xt, swap, src, dst = call(
        forward_swap_kernel,
        [tiles, piece, piece, slots, slots],
        [SMEM] + [HBM] * 4,
        [VMEM] * 3 + [SMEM] * 2,
        [
            pltpu.VMEM(node_features.shape, BF16),
            acc,
            pltpu.SemaphoreType.DMA((3,)),
            pltpu.SemaphoreType.DMA((groups // m,)),
        ],
        flops,
    )(tile_counts, *(in_hbm(a) for a in (tile_src, tile_dst, node_features, tile_values.reshape(tiles.shape))))
    index = (tile_counts, src, dst)
    swap = moved(swap, "dom", swapped)
    acc2, direct = call(
        forward_send_kernel, [totals, piece], [SMEM] * 3 + [VMEM] * 2, [VMEM] * 2, [acc], 2 * flops
    )(*index, xt, tiles)
    (chip,) = call(functools.partial(sum_kernel, 2), [piece], [VMEM] * 2, [VMEM])(acc2, swap)
    chip = moved(chip, "dom", lambda i: i + 2)
    direct = moved(direct, "dom", lambda i: i + 1 + 2 * (i % 2))
    (acc0,) = call(forward_own_kernel, [totals], [SMEM] * 3 + [VMEM] * 2, [VMEM], (), flops)(*index, xt, tiles)
    (h,) = call(functools.partial(sum_kernel, 3), [piece], [VMEM] * 3, [VMEM])(acc0, direct, chip)
    hs = [h] + [moved(h, "feat", lambda i, q=q: i - q) for q in range(1, parts)]
    act, ht, grads, g_own, *g_others = call(
        functools.partial(middle_kernel, parts),
        [rows, jax.ShapeDtypeStruct((f_in + 16, nodes), BF16), rows, wide] + [piece] * (parts - 1),
        [VMEM] * (3 + parts),
        [VMEM] * (3 + parts),
        (),
        4 * nodes * f_in * hid,
    )(bias.reshape(1, hid), weight, out_grad, *hs)
    g_received = [moved(g, "feat", lambda i, q=q + 1: i + q) for q, g in enumerate(g_others)]
    output, wg = call(
        weight_grad_kernel,
        [rows, gradient],
        [VMEM] * 3,
        [HBM, VMEM],
        [pltpu.SemaphoreType.DMA],
        2 * nodes * f_in * hid,
    )(ht, grads, act)
    g_own, wg = lax.optimization_barrier((g_own, wg))
    (g,) = call(functools.partial(sum_kernel, parts), [piece], [VMEM] * parts, [VMEM])(g_own, *g_received)
    g_chip = moved(g, "dom", lambda i: i - 2)
    g_direct = moved(g, "dom", lambda i: i - 3 + 2 * (i % 2))
    wgs, stride = [wg], 1
    for r in radices(lax.axis_size("dom")):
        if len(wgs) > 1:
            (wg,) = call(paired_sum_kernel, [gradient], [VMEM] * len(wgs), [VMEM])(*wgs)
        wgs = exchanged(wg, "dom", stride, r)
        stride *= r
    (back0,) = call(backward_own_kernel, [totals], [SMEM] * 3 + [VMEM] * 2, [VMEM], (), flops)(*index, tiles, g)
    g_swap = moved(g_chip, "dom", swapped)
    back2, backd = call(
        backward_near_kernel, [totals, totals], [SMEM] * 3 + [VMEM] * 3, [VMEM] * 2, (), 2 * flops
    )(*index, tiles, g_chip, g_direct)
    input_grad, weight_grad, bias_grad = call(
        backward_last_kernel,
        [
            jax.ShapeDtypeStruct((width, nodes), BF16),
            jax.ShapeDtypeStruct((f_in, hid), F32),
            jax.ShapeDtypeStruct((1, hid), F32),
        ],
        [SMEM] * 3 + [VMEM] * (5 + len(wgs)),
        [VMEM] * 3,
        [acc],
        flops,
    )(*index, tiles, g_swap, back0, back2, backd, *wgs)
    return output, weight_grad, bias_grad.reshape(hid), input_grad.T


def solution(mesh):
    return jax.shard_map(
        shards,
        mesh=mesh,
        in_specs=(
            P("dom", None),
            P(None, "feat"),
            P("feat"),
            P("dom", None, None),
            P("dom"),
            P("dom"),
            P("dom"),
            P("dom", "feat"),
        ),
        out_specs=(P("dom", "feat"), P(None, "feat"), P("feat"), P("dom", "feat")),
        check_vma=False,
    )
```

```python
import functools

import jax
import jax.numpy as jnp
from jax import lax
from jax.experimental import pallas as pl
from jax.experimental.pallas import tpu as pltpu
from jax.sharding import PartitionSpec as P

BLOCK = 128
REACH = 4
F32 = jnp.float32
BF16 = jnp.bfloat16
VMEM = pl.BlockSpec(memory_space=pltpu.VMEM)
SMEM = pl.BlockSpec(memory_space=pltpu.SMEM)
HBM = pl.BlockSpec(memory_space=pltpu.HBM)


def call(kernel, out_shape, in_specs, out_specs, scratch=(), flops=0):
    return pl.pallas_call(
        kernel,
        out_shape=out_shape,
        in_specs=in_specs,
        out_specs=out_specs,
        scratch_shapes=list(scratch),
        compiler_params=pltpu.CompilerParams(vmem_limit_bytes=24 * 1024 * 1024),
        cost_estimate=pl.CostEstimate(flops=flops, bytes_accessed=2**20, transcendentals=0),
    )


def groups_at_once(groups):
    return next(m for m in (4, 3, 2, 1) if groups % m == 0)


def in_hbm(a):
    return pltpu.with_memory_space_constraint(a, pltpu.HBM)


def own_core():
    return lax.rem(lax.axis_index("dom"), 2)


def slot_loop(count, groups, offsets, body, arrive=None):
    m = groups_at_once(groups)

    def chunk(i, carry):
        if arrive is not None:
            arrive(i)

        @pl.when(i * (m * REACH) < count)
        def _():
            for u in range(m):
                for o in offsets:
                    j = i * m + u
                    body(j, o, j * REACH + o < count)

        return carry

    lax.fori_loop(0, groups // m, chunk, 0)


def push(xt, tiles_ref, src_ref, dst_ref, acc, j, o, live):
    blocks = xt.shape[0]
    k = j * REACH + o
    d = jnp.where(live, dst_ref[k] - o * blocks, blocks)
    acc[d] += lax.dot_general(
        xt[src_ref[k]], tiles_ref[j, o], (((1,), (1,)), ((), ())), preferred_element_type=F32
    )


def forward_swap_kernel(
    count, src_hbm, dst_hbm, x_hbm, tiles_hbm, tiles, xt, swap, src, dst, x, acc, small, large
):
    blocks, width, _ = xt.shape
    groups = tiles.shape[0]
    m = groups_at_once(groups)
    copies = [
        pltpu.make_async_copy(a, b, small.at[i])
        for i, (a, b) in enumerate(((x_hbm, x), (src_hbm, src), (dst_hbm, dst)))
    ]

    def chunk(i):
        part = pl.ds(i * m, m)
        return pltpu.make_async_copy(tiles_hbm.at[part], tiles.at[part], large.at[i])

    for c in copies:
        c.start()
    for i in range(groups // m):
        chunk(i).start()
    acc[...] = jnp.zeros_like(acc)
    row = lax.broadcasted_iota(jnp.int32, (width, x.shape[1]), 0)
    column = lax.broadcasted_iota(jnp.int32, (width, x.shape[1]), 1)
    pick = (column == row + lax.axis_index("feat") * width).astype(BF16)
    for c in copies:
        c.wait()
    for b in range(blocks):
        xt[b] = lax.dot_general(
            pick, x[b * BLOCK : (b + 1) * BLOCK, :], (((1,), (1,)), ((), ())), preferred_element_type=F32
        ).astype(BF16)
    o = 3 - 2 * own_core()
    slot_loop(
        count[0], groups, (o,), functools.partial(push, xt, tiles, src, dst, acc), lambda i: chunk(i).wait()
    )
    swap[...] = acc[:blocks].astype(BF16)


def forward_send_kernel(count, src, dst, xt, tiles, acc2, direct, acc):
    acc2[...] = jnp.zeros_like(acc2)
    acc[...] = jnp.zeros_like(acc)
    far = 1 + 2 * own_core()

    def body(j, o, live):
        push(xt, tiles, src, dst, acc2 if isinstance(o, int) else acc, j, o, live)

    slot_loop(count[0], tiles.shape[0], (2, far), body)
    direct[...] = acc[: direct.shape[0]].astype(BF16)


def forward_own_kernel(count, src, dst, xt, tiles, acc):
    acc[...] = jnp.zeros_like(acc)
    slot_loop(count[0], tiles.shape[0], (0,), functools.partial(push, xt, tiles, src, dst, acc))


def sum_kernel(n, *refs):
    out = refs[n]
    blocks = out.shape[0]
    total = refs[0][:blocks].astype(F32)
    for r in refs[1:n]:
        total = total + r[:blocks].astype(F32)
    out[...] = total.astype(out.dtype)


def middle_kernel(parts, bias_ref, w_ref, og_ref, *refs):
    h_refs, (out_ref, ht, grads), g_refs = refs[:parts], refs[parts : parts + 3], refs[parts + 3 :]
    blocks, width, _ = h_refs[0].shape
    f_in = w_ref.shape[0]
    me = lax.axis_index("feat")
    for q in range(parts):
        row = pl.multiple_of(lax.rem(me + q, parts) * width, width)
        for b in range(blocks):
            ht[pl.ds(row, width), b * BLOCK : (b + 1) * BLOCK] = h_refs[q][b]
    ht[f_in:, :] = jnp.ones((ht.shape[0] - f_in, ht.shape[1]), BF16)
    for b in range(blocks):
        rows = slice(b * BLOCK, (b + 1) * BLOCK)
        pre = lax.dot_general(
            ht[:f_in, rows], w_ref[...], (((0,), (0,)), ((), ())), preferred_element_type=F32
        ) + bias_ref[...]
        s = jax.nn.sigmoid(pre)
        out_ref[rows, :] = (pre * s).astype(BF16)
        grad = (og_ref[rows, :].astype(F32) * s * (1.0 + pre * (1.0 - s))).astype(BF16)
        grads[rows, :] = grad
        for q in range(parts):
            row = pl.multiple_of(lax.rem(me + q, parts) * width, width)
            g_refs[q][b] = lax.dot_general(
                w_ref[pl.ds(row, width), :], grad, (((1,), (1,)), ((), ())), preferred_element_type=F32
            ).astype(g_refs[q].dtype)


def weight_grad_kernel(ht, grads, act, out, wg, sem):
    copy = pltpu.make_async_copy(act, out, sem)
    copy.start()
    full = jnp.dot(ht[...], grads[...], preferred_element_type=F32)
    wg[...] = full[: wg.shape[0]]
    copy.wait()


def pull(g, tiles, src, dst, acc, j, o, live):
    blocks = g.shape[0]
    k = j * REACH + o
    s = jnp.where(live, src[k], blocks)
    acc[s] += jnp.dot(g[dst[k] - o * blocks], tiles[j, o], preferred_element_type=F32)


def backward_own_kernel(count, src, dst, tiles, g0, acc):
    acc[...] = jnp.zeros_like(acc)
    slot_loop(count[0], tiles.shape[0], (0,), functools.partial(pull, g0, tiles, src, dst, acc))


def backward_near_kernel(count, src, dst, tiles, g2, gd, acc2, accd):
    acc2[...] = jnp.zeros_like(acc2)
    accd[...] = jnp.zeros_like(accd)
    far = 1 + 2 * own_core()

    def body(j, o, live):
        if isinstance(o, int):
            pull(g2, tiles, src, dst, acc2, j, o, live)
        else:
            pull(gd, tiles, src, dst, accd, j, o, live)

    slot_loop(count[0], tiles.shape[0], (2, far), body)


def backward_last_kernel(count, src, dst, tiles, g, acc0, acc2, accd, *refs):
    parts, (out, wg, bias, acc) = refs[:-4], refs[-4:]
    blocks = g.shape[0]
    acc[...] = jnp.zeros_like(acc)
    far = 3 - 2 * own_core()
    slot_loop(count[0], tiles.shape[0], (far,), functools.partial(pull, g, tiles, src, dst, acc))
    for b in range(blocks):
        total = acc[b] + acc0[b] + acc2[b] + accd[b]
        out[:, b * BLOCK : (b + 1) * BLOCK] = total.astype(BF16)
    whole = paired_sum([r[...] for r in parts])
    f_in = wg.shape[0]
    wg[...] = whole[:f_in]
    bias[...] = whole[f_in : f_in + 1]


def paired_sum(parts):
    if len(parts) == 4:
        return (parts[0] + parts[2]) + (parts[1] + parts[3])
    return functools.reduce(lambda a, b: a + b, parts)


def piece_sum_kernel(pieces, out):
    total = functools.reduce(lambda a, b: a + b, [pieces[i] for i in range(pieces.shape[0])])
    for i in range(pieces.shape[0]):
        out[i] = total


def paired_sum_kernel(*refs):
    refs[-1][...] = paired_sum([r[...] for r in refs[:-1]])


def moved(block, axis, target):
    n = lax.axis_size(axis)
    return lax.ppermute(block, axis, [(i, target(i) % n) for i in range(n)])


def radices(n):
    out = []
    while n > 1:
        r = 4 if n % 4 == 0 else 2 if n % 2 == 0 else n
        out.append(r)
        n //= r
    return out


def exchanged(part, axis, stride, r):
    def target(step, i):
        digit = i // stride % r
        return i + ((digit + step) % r - digit) * stride

    return [part] + [moved(part, axis, functools.partial(target, s)) for s in range(1, r)]


def shards(node_features, weight, bias, tile_values, tile_src, tile_dst, tile_counts, out_grad):
    nodes, f_in = node_features.shape
    hid = weight.shape[1]
    blocks = nodes // BLOCK
    parts = lax.axis_size("feat")
    width = f_in // parts
    capacity = tile_values.shape[0]
    groups = capacity // REACH
    piece = jax.ShapeDtypeStruct((blocks, width, BLOCK), BF16)
    wide = jax.ShapeDtypeStruct((blocks, width, BLOCK), F32)
    totals = jax.ShapeDtypeStruct((blocks + 1, width, BLOCK), F32)
    acc = pltpu.VMEM(totals.shape, F32)
    tiles = jax.ShapeDtypeStruct((groups, REACH, BLOCK, BLOCK), BF16)
    slots = jax.ShapeDtypeStruct((capacity,), jnp.int32)
    rows = jax.ShapeDtypeStruct((nodes, hid), BF16)
    gradient = jax.ShapeDtypeStruct((f_in + 128, hid), F32)
    m = groups_at_once(groups)
    flops = 2 * capacity * BLOCK * BLOCK * width // REACH

    def swapped(i):
        return i ^ 1

    tiles, xt, swap, src, dst = call(
        forward_swap_kernel,
        [tiles, piece, piece, slots, slots],
        [SMEM] + [HBM] * 4,
        [VMEM] * 3 + [SMEM] * 2,
        [
            pltpu.VMEM(node_features.shape, BF16),
            acc,
            pltpu.SemaphoreType.DMA((3,)),
            pltpu.SemaphoreType.DMA((groups // m,)),
        ],
        flops,
    )(tile_counts, *(in_hbm(a) for a in (tile_src, tile_dst, node_features, tile_values.reshape(tiles.shape))))
    index = (tile_counts, src, dst)
    swap = moved(swap, "dom", swapped)
    acc2, direct = call(
        forward_send_kernel, [totals, piece], [SMEM] * 3 + [VMEM] * 2, [VMEM] * 2, [acc], 2 * flops
    )(*index, xt, tiles)
    (chip,) = call(functools.partial(sum_kernel, 2), [piece], [VMEM] * 2, [VMEM])(acc2, swap)
    chip = moved(chip, "dom", lambda i: i + 2)
    direct = moved(direct, "dom", lambda i: i + 1 + 2 * (i % 2))
    (acc0,) = call(forward_own_kernel, [totals], [SMEM] * 3 + [VMEM] * 2, [VMEM], (), flops)(*index, xt, tiles)
    (h,) = call(functools.partial(sum_kernel, 3), [piece], [VMEM] * 3, [VMEM])(acc0, direct, chip)
    hs = [h] + [moved(h, "feat", lambda i, q=q: i - q) for q in range(1, parts)]
    act, ht, grads, g_own, *g_others = call(
        functools.partial(middle_kernel, parts),
        [rows, jax.ShapeDtypeStruct((f_in + 128, nodes), BF16), rows, wide] + [piece] * (parts - 1),
        [VMEM] * (3 + parts),
        [VMEM] * (3 + parts),
        (),
        4 * nodes * f_in * hid,
    )(bias.reshape(1, hid), weight, out_grad, *hs)
    g_received = [moved(g, "feat", lambda i, q=q + 1: i + q) for q, g in enumerate(g_others)]
    output, wg = call(
        weight_grad_kernel,
        [rows, gradient],
        [VMEM] * 3,
        [HBM, VMEM],
        [pltpu.SemaphoreType.DMA],
        2 * nodes * f_in * hid,
    )(ht, grads, act)
    g_own, wg = lax.optimization_barrier((g_own, wg))
    (g,) = call(functools.partial(sum_kernel, parts), [piece], [VMEM] * parts, [VMEM])(g_own, *g_received)
    g_chip = moved(g, "dom", lambda i: i - 2)
    g_direct = moved(g, "dom", lambda i: i - 3 + 2 * (i % 2))
    n = lax.axis_size("dom")
    pieces = lax.all_to_all(wg.reshape(n, -1, hid), "dom", 0, 0)
    (wg,) = call(piece_sum_kernel, [jax.ShapeDtypeStruct(pieces.shape, F32)], [VMEM], [VMEM])(pieces)
    wg = lax.all_to_all(wg, "dom", 0, 0).reshape(gradient.shape)
    wgs = [wg]
    (back0,) = call(backward_own_kernel, [totals], [SMEM] * 3 + [VMEM] * 2, [VMEM], (), flops)(*index, tiles, g)
    g_swap = moved(g_chip, "dom", swapped)
    back2, backd = call(
        backward_near_kernel, [totals, totals], [SMEM] * 3 + [VMEM] * 3, [VMEM] * 2, (), 2 * flops
    )(*index, tiles, g_chip, g_direct)
    input_grad, weight_grad, bias_grad = call(
        backward_last_kernel,
        [
            jax.ShapeDtypeStruct((width, nodes), BF16),
            jax.ShapeDtypeStruct((f_in, hid), F32),
            jax.ShapeDtypeStruct((1, hid), F32),
        ],
        [SMEM] * 3 + [VMEM] * (5 + len(wgs)),
        [VMEM] * 3,
        [acc],
        flops,
    )(*index, tiles, g_swap, back0, back2, backd, *wgs)
    return output, weight_grad, bias_grad.reshape(hid), input_grad.T


def solution(mesh):
    return jax.shard_map(
        shards,
        mesh=mesh,
        in_specs=(
            P("dom", None),
            P(None, "feat"),
            P("feat"),
            P("dom", None, None),
            P("dom"),
            P("dom"),
            P("dom"),
            P("dom", "feat"),
        ),
        out_specs=(P("dom", "feat"), P(None, "feat"), P("feat"), P("dom", "feat")),
        check_vma=False,
    )
```

```python
import functools

import jax
import jax.numpy as jnp
from jax import lax
from jax.experimental import pallas as pl
from jax.experimental.pallas import tpu as pltpu
from jax.sharding import PartitionSpec as P

BLOCK = 128
REACH = 4
F32 = jnp.float32
BF16 = jnp.bfloat16
VMEM = pl.BlockSpec(memory_space=pltpu.VMEM)
SMEM = pl.BlockSpec(memory_space=pltpu.SMEM)
HBM = pl.BlockSpec(memory_space=pltpu.HBM)


def call(kernel, out_shape, in_specs, out_specs, scratch=(), flops=0):
    return pl.pallas_call(
        kernel,
        out_shape=out_shape,
        in_specs=in_specs,
        out_specs=out_specs,
        scratch_shapes=list(scratch),
        compiler_params=pltpu.CompilerParams(vmem_limit_bytes=24 * 1024 * 1024),
        cost_estimate=pl.CostEstimate(flops=flops, bytes_accessed=2**20, transcendentals=0),
    )


def groups_at_once(groups):
    return next(m for m in (4, 3, 2, 1) if groups % m == 0)


def in_hbm(a):
    return pltpu.with_memory_space_constraint(a, pltpu.HBM)


def own_core():
    return lax.rem(lax.axis_index("dom"), 2)


def slot_loop(count, groups, offsets, body, arrive=None):
    m = groups_at_once(groups)

    def chunk(i, carry):
        if arrive is not None:
            arrive(i)

        @pl.when(i * (m * REACH) < count)
        def _():
            for u in range(m):
                for o in offsets:
                    j = i * m + u
                    body(j, o, j * REACH + o < count)

        return carry

    lax.fori_loop(0, groups // m, chunk, 0)


def push(xt, tiles_ref, src_ref, dst_ref, acc, j, o, live):
    blocks = xt.shape[0]
    k = j * REACH + o
    d = jnp.where(live, dst_ref[k] - o * blocks, blocks)
    acc[d] += lax.dot_general(
        xt[src_ref[k]], tiles_ref[j, o], (((1,), (1,)), ((), ())), preferred_element_type=F32
    )


def forward_swap_kernel(
    count, src_hbm, dst_hbm, x_hbm, tiles_hbm, tiles, xt, swap, src, dst, x, acc, small, large
):
    blocks, width, _ = xt.shape
    groups = tiles.shape[0]
    m = groups_at_once(groups)
    copies = [
        pltpu.make_async_copy(a, b, small.at[i])
        for i, (a, b) in enumerate(((x_hbm, x), (src_hbm, src), (dst_hbm, dst)))
    ]

    def chunk(i):
        part = pl.ds(i * m, m)
        return pltpu.make_async_copy(tiles_hbm.at[part], tiles.at[part], large.at[i])

    for c in copies:
        c.start()
    for i in range(groups // m):
        chunk(i).start()
    acc[...] = jnp.zeros_like(acc)
    row = lax.broadcasted_iota(jnp.int32, (width, x.shape[1]), 0)
    column = lax.broadcasted_iota(jnp.int32, (width, x.shape[1]), 1)
    pick = (column == row + lax.axis_index("feat") * width).astype(BF16)
    for c in copies:
        c.wait()
    for b in range(blocks):
        xt[b] = lax.dot_general(
            pick, x[b * BLOCK : (b + 1) * BLOCK, :], (((1,), (1,)), ((), ())), preferred_element_type=F32
        ).astype(BF16)
    o = 3 - 2 * own_core()
    slot_loop(
        count[0], groups, (o,), functools.partial(push, xt, tiles, src, dst, acc), lambda i: chunk(i).wait()
    )
    swap[...] = acc[:blocks].astype(BF16)


def forward_send_kernel(count, src, dst, xt, tiles, acc2, direct, acc):
    acc2[...] = jnp.zeros_like(acc2)
    acc[...] = jnp.zeros_like(acc)
    far = 1 + 2 * own_core()

    def body(j, o, live):
        push(xt, tiles, src, dst, acc2 if isinstance(o, int) else acc, j, o, live)

    slot_loop(count[0], tiles.shape[0], (2, far), body)
    direct[...] = acc[: direct.shape[0]].astype(BF16)


def forward_own_kernel(count, src, dst, xt, tiles, acc):
    acc[...] = jnp.zeros_like(acc)
    slot_loop(count[0], tiles.shape[0], (0,), functools.partial(push, xt, tiles, src, dst, acc))


def sum_kernel(n, *refs):
    out = refs[n]
    blocks = out.shape[0]
    total = refs[0][:blocks].astype(F32)
    for r in refs[1:n]:
        total = total + r[:blocks].astype(F32)
    out[...] = total.astype(out.dtype)


def middle_kernel(parts, bias_ref, w_ref, og_ref, *refs):
    h_refs, (out_ref, ht, grads), g_refs = refs[:parts], refs[parts : parts + 3], refs[parts + 3 :]
    blocks, width, _ = h_refs[0].shape
    f_in = w_ref.shape[0]
    me = lax.axis_index("feat")
    for q in range(parts):
        row = pl.multiple_of(lax.rem(me + q, parts) * width, width)
        for b in range(blocks):
            ht[pl.ds(row, width), b * BLOCK : (b + 1) * BLOCK] = h_refs[q][b]
    ht[f_in:, :] = jnp.ones((ht.shape[0] - f_in, ht.shape[1]), BF16)
    for b in range(blocks):
        rows = slice(b * BLOCK, (b + 1) * BLOCK)
        pre = lax.dot_general(
            ht[:f_in, rows], w_ref[...], (((0,), (0,)), ((), ())), preferred_element_type=F32
        ) + bias_ref[...]
        s = jax.nn.sigmoid(pre)
        out_ref[rows, :] = (pre * s).astype(BF16)
        grad = (og_ref[rows, :].astype(F32) * s * (1.0 + pre * (1.0 - s))).astype(BF16)
        grads[rows, :] = grad
        for q in range(parts):
            row = pl.multiple_of(lax.rem(me + q, parts) * width, width)
            g_refs[q][b] = lax.dot_general(
                w_ref[pl.ds(row, width), :], grad, (((1,), (1,)), ((), ())), preferred_element_type=F32
            ).astype(g_refs[q].dtype)


def weight_grad_kernel(ht, grads, act, out, wg, sem):
    copy = pltpu.make_async_copy(act, out, sem)
    copy.start()
    full = jnp.dot(ht[...], grads[...], preferred_element_type=F32)
    wg[...] = full[: wg.shape[0]]
    copy.wait()


def pull(g, tiles, src, dst, acc, j, o, live):
    blocks = g.shape[0]
    k = j * REACH + o
    s = jnp.where(live, src[k], blocks)
    acc[s] += jnp.dot(g[dst[k] - o * blocks], tiles[j, o], preferred_element_type=F32)


def backward_own_kernel(count, src, dst, tiles, g0, acc):
    acc[...] = jnp.zeros_like(acc)
    slot_loop(count[0], tiles.shape[0], (0,), functools.partial(pull, g0, tiles, src, dst, acc))


def backward_near_kernel(count, src, dst, tiles, g2, gd, acc2, accd):
    acc2[...] = jnp.zeros_like(acc2)
    accd[...] = jnp.zeros_like(accd)
    far = 1 + 2 * own_core()

    def body(j, o, live):
        if isinstance(o, int):
            pull(g2, tiles, src, dst, acc2, j, o, live)
        else:
            pull(gd, tiles, src, dst, accd, j, o, live)

    slot_loop(count[0], tiles.shape[0], (2, far), body)


def backward_last_kernel(count, src, dst, tiles, g, acc0, acc2, accd, *refs):
    parts, (out, wg, bias, acc) = refs[:-4], refs[-4:]
    blocks = g.shape[0]
    acc[...] = jnp.zeros_like(acc)
    far = 3 - 2 * own_core()
    slot_loop(count[0], tiles.shape[0], (far,), functools.partial(pull, g, tiles, src, dst, acc))
    for b in range(blocks):
        total = acc[b] + acc0[b] + acc2[b] + accd[b]
        out[:, b * BLOCK : (b + 1) * BLOCK] = total.astype(BF16)
    whole = paired_sum([r[...] for r in parts])
    f_in = wg.shape[0]
    wg[...] = whole[:f_in]
    bias[...] = whole[f_in : f_in + 1]


def paired_sum(parts):
    parts = [p.astype(F32) for p in parts]
    while len(parts) > 1:
        parts = [parts[i] + parts[i + 1] for i in range(0, len(parts), 2)]
    return parts[0]


def paired_sum_kernel(*refs):
    refs[-1][...] = paired_sum([r[...] for r in refs[:-1]]).astype(refs[-1].dtype)


def moved(block, axis, target):
    n = lax.axis_size(axis)
    return lax.ppermute(block, axis, [(i, target(i) % n) for i in range(n)])


def radices(n):
    out = []
    while n > 1:
        r = 4 if n % 4 == 0 else 2
        out.append(r)
        n //= r
    return out


def exchanged(part, axis, stride, r):
    return [part] + [moved(part, axis, lambda i, s=s: i ^ (s * stride)) for s in range(1, r)]


def shards(node_features, weight, bias, tile_values, tile_src, tile_dst, tile_counts, out_grad):
    nodes, f_in = node_features.shape
    hid = weight.shape[1]
    blocks = nodes // BLOCK
    parts = lax.axis_size("feat")
    width = f_in // parts
    capacity = tile_values.shape[0]
    groups = capacity // REACH
    piece = jax.ShapeDtypeStruct((blocks, width, BLOCK), BF16)
    wide = jax.ShapeDtypeStruct((blocks, width, BLOCK), F32)
    totals = jax.ShapeDtypeStruct((blocks + 1, width, BLOCK), F32)
    acc = pltpu.VMEM(totals.shape, F32)
    tiles = jax.ShapeDtypeStruct((groups, REACH, BLOCK, BLOCK), BF16)
    slots = jax.ShapeDtypeStruct((capacity,), jnp.int32)
    rows = jax.ShapeDtypeStruct((nodes, hid), BF16)
    gradient = jax.ShapeDtypeStruct((f_in + 8, hid), F32)
    m = groups_at_once(groups)
    flops = 2 * capacity * BLOCK * BLOCK * width // REACH

    def swapped(i):
        return i ^ 1

    tiles, xt, swap, src, dst = call(
        forward_swap_kernel,
        [tiles, piece, piece, slots, slots],
        [SMEM] + [HBM] * 4,
        [VMEM] * 3 + [SMEM] * 2,
        [
            pltpu.VMEM(node_features.shape, BF16),
            acc,
            pltpu.SemaphoreType.DMA((3,)),
            pltpu.SemaphoreType.DMA((groups // m,)),
        ],
        flops,
    )(tile_counts, *(in_hbm(a) for a in (tile_src, tile_dst, node_features, tile_values.reshape(tiles.shape))))
    index = (tile_counts, src, dst)
    swap = moved(swap, "dom", swapped)
    acc2, direct = call(
        forward_send_kernel, [totals, piece], [SMEM] * 3 + [VMEM] * 2, [VMEM] * 2, [acc], 2 * flops
    )(*index, xt, tiles)
    (chip,) = call(functools.partial(sum_kernel, 2), [piece], [VMEM] * 2, [VMEM])(acc2, swap)
    chip = moved(chip, "dom", lambda i: i + 2)
    direct = moved(direct, "dom", lambda i: i + 1 + 2 * (i % 2))
    (acc0,) = call(forward_own_kernel, [totals], [SMEM] * 3 + [VMEM] * 2, [VMEM], (), flops)(*index, xt, tiles)
    (h,) = call(functools.partial(sum_kernel, 3), [piece], [VMEM] * 3, [VMEM])(acc0, direct, chip)
    hs = [h] + [moved(h, "feat", lambda i, q=q: i - q) for q in range(1, parts)]
    act, ht, grads, g_own, *g_others = call(
        functools.partial(middle_kernel, parts),
        [rows, jax.ShapeDtypeStruct((f_in + 16, nodes), BF16), rows, wide] + [piece] * (parts - 1),
        [VMEM] * (3 + parts),
        [VMEM] * (3 + parts),
        (),
        4 * nodes * f_in * hid,
    )(bias.reshape(1, hid), weight, out_grad, *hs)
    g_received = [moved(g, "feat", lambda i, q=q + 1: i + q) for q, g in enumerate(g_others)]
    output, wg = call(
        weight_grad_kernel,
        [rows, gradient],
        [VMEM] * 3,
        [HBM, VMEM],
        [pltpu.SemaphoreType.DMA],
        2 * nodes * f_in * hid,
    )(ht, grads, act)
    r, *more = radices(lax.axis_size("dom"))
    wgs = exchanged(wg, "dom", 1, r)
    g_own, *wgs = lax.optimization_barrier((g_own, *wgs))
    (g,) = call(functools.partial(sum_kernel, parts), [piece], [VMEM] * parts, [VMEM])(g_own, *g_received)
    g_chip = moved(g, "dom", lambda i: i - 2)
    g_direct = moved(g, "dom", lambda i: i - 3 + 2 * (i % 2))
    stride = r
    for r in more:
        (wg,) = call(
            paired_sum_kernel, [jax.ShapeDtypeStruct(gradient.shape, BF16)], [VMEM] * len(wgs), [VMEM]
        )(*wgs)
        wgs = exchanged(wg, "dom", stride, r)
        stride *= r
    g, wgs[0] = lax.optimization_barrier((g, wgs[0]))
    (back0,) = call(backward_own_kernel, [totals], [SMEM] * 3 + [VMEM] * 2, [VMEM], (), flops)(*index, tiles, g)
    g_chip, back0, *wgs = lax.optimization_barrier((g_chip, back0, *wgs))
    g_swap = moved(g_chip, "dom", swapped)
    back2, backd = call(
        backward_near_kernel, [totals, totals], [SMEM] * 3 + [VMEM] * 3, [VMEM] * 2, (), 2 * flops
    )(*index, tiles, g_chip, g_direct)
    input_grad, weight_grad, bias_grad = call(
        backward_last_kernel,
        [
            jax.ShapeDtypeStruct((width, nodes), BF16),
            jax.ShapeDtypeStruct((f_in, hid), F32),
            jax.ShapeDtypeStruct((1, hid), F32),
        ],
        [SMEM] * 3 + [VMEM] * (5 + len(wgs)),
        [VMEM] * 3,
        [acc],
        flops,
    )(*index, tiles, g_swap, back0, back2, backd, *wgs)
    return output, weight_grad, bias_grad.reshape(hid), input_grad.T


def solution(mesh):
    return jax.shard_map(
        shards,
        mesh=mesh,
        in_specs=(
            P("dom", None),
            P(None, "feat"),
            P("feat"),
            P("dom", None, None),
            P("dom"),
            P("dom"),
            P("dom"),
            P("dom", "feat"),
        ),
        out_specs=(P("dom", "feat"), P(None, "feat"), P("feat"), P("dom", "feat")),
        check_vma=False,
    )
```

```python
import functools

import jax
import jax.numpy as jnp
from jax import lax
from jax.experimental import pallas as pl
from jax.experimental.pallas import tpu as pltpu
from jax.sharding import PartitionSpec as P

BLOCK = 128
REACH = 4
F32 = jnp.float32
BF16 = jnp.bfloat16
VMEM = pl.BlockSpec(memory_space=pltpu.VMEM)
SMEM = pl.BlockSpec(memory_space=pltpu.SMEM)
HBM = pl.BlockSpec(memory_space=pltpu.HBM)


def call(kernel, out_shape, in_specs, out_specs, scratch=(), flops=0):
    return pl.pallas_call(
        kernel,
        out_shape=out_shape,
        in_specs=in_specs,
        out_specs=out_specs,
        scratch_shapes=list(scratch),
        compiler_params=pltpu.CompilerParams(vmem_limit_bytes=24 * 1024 * 1024),
        cost_estimate=pl.CostEstimate(flops=flops, bytes_accessed=2**20, transcendentals=0),
    )


def groups_at_once(groups):
    return next(m for m in (4, 3, 2, 1) if groups % m == 0)


def in_hbm(a):
    return pltpu.with_memory_space_constraint(a, pltpu.HBM)


def own_core():
    return lax.rem(lax.axis_index("dom"), 2)


def slot_loop(count, groups, offsets, body, arrive=None):
    m = groups_at_once(groups)

    def chunk(i, carry):
        if arrive is not None:
            arrive(i)

        @pl.when(i * (m * REACH) < count)
        def _():
            for u in range(m):
                for o in offsets:
                    j = i * m + u
                    body(j, o, j * REACH + o < count)

        return carry

    lax.fori_loop(0, groups // m, chunk, 0)


def push(xt, tiles_ref, src_ref, dst_ref, acc, j, o, live):
    blocks = xt.shape[0]
    k = j * REACH + o
    d = jnp.where(live, dst_ref[k] - o * blocks, blocks)
    acc[d] += lax.dot_general(
        xt[src_ref[k]], tiles_ref[j, o], (((1,), (1,)), ((), ())), preferred_element_type=F32
    )


def forward_swap_kernel(
    count, src_hbm, dst_hbm, x_hbm, tiles_hbm, tiles, xt, swap, src, dst, x, acc, small, large
):
    blocks, width, _ = xt.shape
    groups = tiles.shape[0]
    m = groups_at_once(groups)
    copies = [
        pltpu.make_async_copy(a, b, small.at[i])
        for i, (a, b) in enumerate(((x_hbm, x), (src_hbm, src), (dst_hbm, dst)))
    ]

    def chunk(i):
        part = pl.ds(i * m, m)
        return pltpu.make_async_copy(tiles_hbm.at[part], tiles.at[part], large.at[i])

    for c in copies:
        c.start()
    for i in range(groups // m):
        chunk(i).start()
    acc[...] = jnp.zeros_like(acc)
    row = lax.broadcasted_iota(jnp.int32, (width, x.shape[1]), 0)
    column = lax.broadcasted_iota(jnp.int32, (width, x.shape[1]), 1)
    pick = (column == row + lax.axis_index("feat") * width).astype(BF16)
    for c in copies:
        c.wait()
    for b in range(blocks):
        xt[b] = lax.dot_general(
            pick, x[b * BLOCK : (b + 1) * BLOCK, :], (((1,), (1,)), ((), ())), preferred_element_type=F32
        ).astype(BF16)
    o = 3 - 2 * own_core()
    slot_loop(
        count[0], groups, (o,), functools.partial(push, xt, tiles, src, dst, acc), lambda i: chunk(i).wait()
    )
    swap[...] = acc[:blocks].astype(BF16)


def forward_send_kernel(count, src, dst, xt, tiles, acc2, direct, acc):
    acc2[...] = jnp.zeros_like(acc2)
    acc[...] = jnp.zeros_like(acc)
    far = 1 + 2 * own_core()

    def body(j, o, live):
        push(xt, tiles, src, dst, acc2 if isinstance(o, int) else acc, j, o, live)

    slot_loop(count[0], tiles.shape[0], (2, far), body)
    direct[...] = acc[: direct.shape[0]].astype(BF16)


def forward_own_kernel(count, src, dst, xt, tiles, acc):
    acc[...] = jnp.zeros_like(acc)
    slot_loop(count[0], tiles.shape[0], (0,), functools.partial(push, xt, tiles, src, dst, acc))


def sum_kernel(n, first, *refs):
    for out in refs[n:]:
        blocks = out.shape[0]
        total = None
        for r in refs[:n]:
            part = r[...] if r.shape[0] == blocks else r[first : first + blocks]
            total = part.astype(F32) if total is None else total + part.astype(F32)
        out[...] = total.astype(out.dtype)
        first += blocks


def join_kernel(parts, *refs):
    out = refs[-1]
    halves = [refs[i : i + parts] for i in range(0, len(refs) - 1, parts)]
    first = 0
    for half in halves:
        blocks = half[0].shape[0]
        total = half[0][...].astype(F32)
        for r in half[1:]:
            total = total + r[...].astype(F32)
        out[first : first + blocks] = total.astype(out.dtype)
        first += blocks


def middle_kernel(parts, first, bias_ref, w_ref, og_ref, *refs):
    h_refs, (act, ht, grads), g_refs = refs[:parts], refs[parts : parts + 3], refs[parts + 3 :]
    blocks, width, _ = h_refs[0].shape
    f_in = w_ref.shape[0]
    me = lax.axis_index("feat")
    for q in range(parts):
        row = pl.multiple_of(lax.rem(me + q, parts) * width, width)
        for b in range(blocks):
            ht[pl.ds(row, width), b * BLOCK : (b + 1) * BLOCK] = h_refs[q][b]
    ht[f_in:, :] = jnp.ones((ht.shape[0] - f_in, ht.shape[1]), BF16)
    for b in range(blocks):
        rows = slice(b * BLOCK, (b + 1) * BLOCK)
        pre = lax.dot_general(
            ht[:f_in, rows], w_ref[...], (((0,), (0,)), ((), ())), preferred_element_type=F32
        ) + bias_ref[...]
        s = jax.nn.sigmoid(pre)
        act[rows, :] = (pre * s).astype(BF16)
        og = og_ref[(first + b) * BLOCK : (first + b + 1) * BLOCK, :].astype(F32)
        grad = (og * s * (1.0 + pre * (1.0 - s))).astype(BF16)
        grads[rows, :] = grad
        for q in range(parts):
            row = pl.multiple_of(lax.rem(me + q, parts) * width, width)
            g_refs[q][b] = lax.dot_general(
                w_ref[pl.ds(row, width), :], grad, (((1,), (1,)), ((), ())), preferred_element_type=F32
            ).astype(g_refs[q].dtype)


def weight_grad_kernel(n, *refs):
    hts, grads, acts, (out, wg, sems) = refs[:n], refs[n : 2 * n], refs[2 * n : 3 * n], refs[3 * n :]
    copies, first = [], 0
    for i, act in enumerate(acts):
        rows = act.shape[0]
        copies.append(pltpu.make_async_copy(act, out.at[pl.ds(first, rows)], sems.at[i]))
        copies[-1].start()
        first += rows
    full = sum(jnp.dot(h[...], g[...], preferred_element_type=F32) for h, g in zip(hts, grads))
    wg[...] = full[: wg.shape[0]].astype(wg.dtype)
    for c in copies:
        c.wait()


def pull(g, tiles, src, dst, acc, j, o, live):
    blocks = g.shape[0]
    k = j * REACH + o
    s = jnp.where(live, src[k], blocks)
    acc[s] += jnp.dot(g[dst[k] - o * blocks], tiles[j, o], preferred_element_type=F32)


def backward_own_kernel(count, src, dst, tiles, g0, acc):
    acc[...] = jnp.zeros_like(acc)
    slot_loop(count[0], tiles.shape[0], (0,), functools.partial(pull, g0, tiles, src, dst, acc))


def backward_near_kernel(count, src, dst, tiles, g2, gd, acc2, accd):
    acc2[...] = jnp.zeros_like(acc2)
    accd[...] = jnp.zeros_like(accd)
    far = 1 + 2 * own_core()

    def body(j, o, live):
        if isinstance(o, int):
            pull(g2, tiles, src, dst, acc2, j, o, live)
        else:
            pull(gd, tiles, src, dst, accd, j, o, live)

    slot_loop(count[0], tiles.shape[0], (2, far), body)


def backward_last_kernel(count, src, dst, tiles, g, acc0, acc2, accd, *refs):
    parts, (out, wg, bias, acc) = refs[:-4], refs[-4:]
    blocks = g.shape[0]
    acc[...] = jnp.zeros_like(acc)
    far = 3 - 2 * own_core()
    slot_loop(count[0], tiles.shape[0], (far,), functools.partial(pull, g, tiles, src, dst, acc))
    for b in range(blocks):
        total = acc[b] + acc0[b] + acc2[b] + accd[b]
        out[:, b * BLOCK : (b + 1) * BLOCK] = total.astype(BF16)
    whole = paired_sum([r[...] for r in parts])
    f_in = wg.shape[0]
    wg[...] = whole[:f_in]
    bias[...] = whole[f_in : f_in + 1]


def paired_sum(parts):
    parts = [p.astype(F32) for p in parts]
    while len(parts) > 1:
        parts = [parts[i] + parts[i + 1] for i in range(0, len(parts), 2)]
    return parts[0]


def paired_sum_kernel(*refs):
    refs[-1][...] = paired_sum([r[...] for r in refs[:-1]]).astype(refs[-1].dtype)


def moved(block, axis, target):
    n = lax.axis_size(axis)
    return lax.ppermute(block, axis, [(i, target(i) % n) for i in range(n)])


def radices(n):
    out = []
    while n > 1:
        r = 4 if n % 4 == 0 else 2
        out.append(r)
        n //= r
    return out


def exchanged(part, axis, stride, r):
    return [part] + [moved(part, axis, lambda i, s=s: i ^ (s * stride)) for s in range(1, r)]


def shards(node_features, weight, bias, tile_values, tile_src, tile_dst, tile_counts, out_grad):
    nodes, f_in = node_features.shape
    hid = weight.shape[1]
    blocks = nodes // BLOCK
    parts = lax.axis_size("feat")
    width = f_in // parts
    capacity = tile_values.shape[0]
    groups = capacity // REACH
    piece = jax.ShapeDtypeStruct((blocks, width, BLOCK), BF16)
    totals = jax.ShapeDtypeStruct((blocks + 1, width, BLOCK), F32)
    acc = pltpu.VMEM(totals.shape, F32)
    tiles = jax.ShapeDtypeStruct((groups, REACH, BLOCK, BLOCK), BF16)
    slots = jax.ShapeDtypeStruct((capacity,), jnp.int32)
    rows = jax.ShapeDtypeStruct((nodes, hid), BF16)
    gradient = jax.ShapeDtypeStruct((f_in + 16, hid), BF16)
    m = groups_at_once(groups)
    flops = 2 * capacity * BLOCK * BLOCK * width // REACH

    def swapped(i):
        return i ^ 1

    tiles, xt, swap, src, dst = call(
        forward_swap_kernel,
        [tiles, piece, piece, slots, slots],
        [SMEM] + [HBM] * 4,
        [VMEM] * 3 + [SMEM] * 2,
        [
            pltpu.VMEM(node_features.shape, BF16),
            acc,
            pltpu.SemaphoreType.DMA((3,)),
            pltpu.SemaphoreType.DMA((groups // m,)),
        ],
        flops,
    )(tile_counts, *(in_hbm(a) for a in (tile_src, tile_dst, node_features, tile_values.reshape(tiles.shape))))
    index = (tile_counts, src, dst)
    swap = moved(swap, "dom", swapped)
    acc2, direct = call(
        forward_send_kernel, [totals, piece], [SMEM] * 3 + [VMEM] * 2, [VMEM] * 2, [acc], 2 * flops
    )(*index, xt, tiles)
    cut = 2 if blocks % 2 == 0 else 1
    starts = range(0, blocks, blocks // cut)
    half = jax.ShapeDtypeStruct((blocks // cut, width, BLOCK), BF16)
    half_wide = jax.ShapeDtypeStruct(half.shape, F32)
    half_rows = jax.ShapeDtypeStruct((nodes // cut, hid), BF16)
    half_columns = jax.ShapeDtypeStruct((f_in + 16, nodes // cut), BF16)
    chip = call(functools.partial(sum_kernel, 2, 0), [half] * cut, [VMEM] * 2, [VMEM] * cut)(acc2, swap)
    chip = [moved(c, "dom", lambda i: i + 2) for c in chip]
    direct = moved(direct, "dom", lambda i: i + 1 + 2 * (i % 2))
    (acc0,) = call(forward_own_kernel, [totals], [SMEM] * 3 + [VMEM] * 2, [VMEM], (), flops)(*index, xt, tiles)
    h_lists = []
    for first, c in zip(starts, chip):
        (h,) = call(functools.partial(sum_kernel, 3, first), [half], [VMEM] * 3, [VMEM])(acc0, direct, c)
        h_lists.append([h] + [moved(h, "feat", lambda i, q=q: i - q) for q in range(1, parts)])
    acts, hts, grads, g_list = [], [], [], []
    for first, hs in zip(starts, h_lists):
        act, ht, grad, g_own, *g_others = call(
            functools.partial(middle_kernel, parts, first),
            [half_rows, half_columns, half_rows, half_wide] + [half] * (parts - 1),
            [VMEM] * (3 + parts),
            [VMEM] * (3 + parts),
            (),
            4 * nodes * f_in * hid // cut,
        )(bias.reshape(1, hid), weight, out_grad, *hs)
        acts.append(act)
        hts.append(ht)
        grads.append(grad)
        g_list += [g_own] + [moved(g, "feat", lambda i, q=q + 1: i + q) for q, g in enumerate(g_others)]
    output, wg = call(
        functools.partial(weight_grad_kernel, cut),
        [rows, gradient],
        [VMEM] * (3 * cut),
        [HBM, VMEM],
        [pltpu.SemaphoreType.DMA((cut,))],
        2 * nodes * f_in * hid,
    )(*hts, *grads, *acts)
    r, *more = radices(lax.axis_size("dom"))
    wgs = exchanged(wg, "dom", 1, r)
    g_list[0], wgs[1] = lax.optimization_barrier((g_list[0], wgs[1]))
    (g,) = call(functools.partial(join_kernel, parts), [piece], [VMEM] * len(g_list), [VMEM])(*g_list)
    g_chip = moved(g, "dom", lambda i: i - 2)
    g_direct = moved(g, "dom", lambda i: i - 3 + 2 * (i % 2))
    (back0,) = call(backward_own_kernel, [totals], [SMEM] * 3 + [VMEM] * 2, [VMEM], (), flops)(*index, tiles, g)
    stride = r
    for r in more:
        back0, *wgs = lax.optimization_barrier((back0, *wgs))
        (wg,) = call(paired_sum_kernel, [gradient], [VMEM] * len(wgs), [VMEM])(*wgs)
        wgs = exchanged(wg, "dom", stride, r)
        stride *= r
    g_chip, g_direct, *wgs = lax.optimization_barrier((g_chip, g_direct, *wgs))
    g_swap = moved(g_chip, "dom", swapped)
    back2, backd = call(
        backward_near_kernel, [totals, totals], [SMEM] * 3 + [VMEM] * 3, [VMEM] * 2, (), 2 * flops
    )(*index, tiles, g_chip, g_direct)
    input_grad, weight_grad, bias_grad = call(
        backward_last_kernel,
        [
            jax.ShapeDtypeStruct((width, nodes), BF16),
            jax.ShapeDtypeStruct((f_in, hid), F32),
            jax.ShapeDtypeStruct((1, hid), F32),
        ],
        [SMEM] * 3 + [VMEM] * (5 + len(wgs)),
        [VMEM] * 3,
        [acc],
        flops,
    )(*index, tiles, g_swap, back0, back2, backd, *wgs)
    return output, weight_grad, bias_grad.reshape(hid), input_grad.T


def solution(mesh):
    return jax.shard_map(
        shards,
        mesh=mesh,
        in_specs=(
            P("dom", None),
            P(None, "feat"),
            P("feat"),
            P("dom", None, None),
            P("dom"),
            P("dom"),
            P("dom"),
            P("dom", "feat"),
        ),
        out_specs=(P("dom", "feat"), P(None, "feat"), P("feat"), P("dom", "feat")),
        check_vma=False,
    )
```

```python
import functools

import jax
import jax.numpy as jnp
from jax import lax
from jax.experimental import pallas as pl
from jax.experimental.pallas import tpu as pltpu
from jax.sharding import PartitionSpec as P

BLOCK = 128
REACH = 4
F32 = jnp.float32
BF16 = jnp.bfloat16
VMEM = pl.BlockSpec(memory_space=pltpu.VMEM)
SMEM = pl.BlockSpec(memory_space=pltpu.SMEM)
HBM = pl.BlockSpec(memory_space=pltpu.HBM)


def call(kernel, out_shape, in_specs, out_specs, scratch=(), flops=0):
    return pl.pallas_call(
        kernel,
        out_shape=out_shape,
        in_specs=in_specs,
        out_specs=out_specs,
        scratch_shapes=list(scratch),
        compiler_params=pltpu.CompilerParams(vmem_limit_bytes=24 * 1024 * 1024),
        cost_estimate=pl.CostEstimate(flops=flops, bytes_accessed=2**20, transcendentals=0),
    )


def groups_at_once(groups):
    return next(m for m in (4, 3, 2, 1) if groups % m == 0)


def in_hbm(a):
    return pltpu.with_memory_space_constraint(a, pltpu.HBM)


def own_core():
    return lax.rem(lax.axis_index("dom"), 2)


def slot_loop(count, groups, offsets, body, arrive=None):
    m = groups_at_once(groups)

    def chunk(i, carry):
        if arrive is not None:
            arrive(i)

        @pl.when(i * (m * REACH) < count)
        def _():
            for u in range(m):
                for o in offsets:
                    j = i * m + u
                    body(j, o, j * REACH + o < count)

        return carry

    lax.fori_loop(0, groups // m, chunk, 0)


def push(xt, tiles_ref, src_ref, dst_ref, acc, j, o, live):
    blocks = xt.shape[0]
    k = j * REACH + o
    d = jnp.where(live, dst_ref[k] - o * blocks, blocks)
    acc[d] += lax.dot_general(
        xt[src_ref[k]], tiles_ref[j, o], (((1,), (1,)), ((), ())), preferred_element_type=F32
    )


def forward_swap_kernel(
    count, src_hbm, dst_hbm, x_hbm, tiles_hbm, tiles, xt, swap, src, dst, x, acc, small, large
):
    blocks, width, _ = xt.shape
    groups = tiles.shape[0]
    m = groups_at_once(groups)
    copies = [
        pltpu.make_async_copy(a, b, small.at[i])
        for i, (a, b) in enumerate(((x_hbm, x), (src_hbm, src), (dst_hbm, dst)))
    ]

    def chunk(i):
        part = pl.ds(i * m, m)
        return pltpu.make_async_copy(tiles_hbm.at[part], tiles.at[part], large.at[i])

    for c in copies:
        c.start()
    for i in range(groups // m):
        chunk(i).start()
    acc[...] = jnp.zeros_like(acc)
    row = lax.broadcasted_iota(jnp.int32, (width, x.shape[1]), 0)
    column = lax.broadcasted_iota(jnp.int32, (width, x.shape[1]), 1)
    pick = (column == row + lax.axis_index("feat") * width).astype(BF16)
    for c in copies:
        c.wait()
    for b in range(blocks):
        xt[b] = lax.dot_general(
            pick, x[b * BLOCK : (b + 1) * BLOCK, :], (((1,), (1,)), ((), ())), preferred_element_type=F32
        ).astype(BF16)
    o = 3 - 2 * own_core()
    slot_loop(
        count[0], groups, (o,), functools.partial(push, xt, tiles, src, dst, acc), lambda i: chunk(i).wait()
    )
    swap[...] = acc[:blocks].astype(BF16)


def forward_send_kernel(count, src, dst, xt, tiles, acc2, direct, acc):
    acc2[...] = jnp.zeros_like(acc2)
    acc[...] = jnp.zeros_like(acc)
    far = 1 + 2 * own_core()

    def body(j, o, live):
        push(xt, tiles, src, dst, acc2 if isinstance(o, int) else acc, j, o, live)

    slot_loop(count[0], tiles.shape[0], (2, far), body)
    direct[...] = acc[: direct.shape[0]].astype(BF16)


def forward_own_kernel(count, src, dst, xt, tiles, acc):
    acc[...] = jnp.zeros_like(acc)
    slot_loop(count[0], tiles.shape[0], (0,), functools.partial(push, xt, tiles, src, dst, acc))


def sum_kernel(n, first, *refs):
    for out in refs[n:]:
        blocks = out.shape[0]
        total = None
        for r in refs[:n]:
            part = r[...] if r.shape[0] == blocks else r[first : first + blocks]
            total = part.astype(F32) if total is None else total + part.astype(F32)
        out[...] = total.astype(out.dtype)
        first += blocks


def join_kernel(parts, *refs):
    out = refs[-1]
    halves = [refs[i : i + parts] for i in range(0, len(refs) - 1, parts)]
    first = 0
    for half in halves:
        blocks = half[0].shape[0]
        total = half[0][...].astype(F32)
        for r in half[1:]:
            total = total + r[...].astype(F32)
        out[first : first + blocks] = total.astype(out.dtype)
        first += blocks


def middle_kernel(parts, first, bias_ref, w_ref, og_ref, *refs):
    h_refs, (act, ht, grads), g_refs = refs[:parts], refs[parts : parts + 3], refs[parts + 3 :]
    blocks, width, _ = h_refs[0].shape
    f_in = w_ref.shape[0]
    me = lax.axis_index("feat")
    for q in range(parts):
        row = pl.multiple_of(lax.rem(me + q, parts) * width, width)
        for b in range(blocks):
            ht[pl.ds(row, width), b * BLOCK : (b + 1) * BLOCK] = h_refs[q][b]
    ht[f_in:, :] = jnp.ones((ht.shape[0] - f_in, ht.shape[1]), BF16)
    for b in range(blocks):
        rows = slice(b * BLOCK, (b + 1) * BLOCK)
        pre = lax.dot_general(
            ht[:f_in, rows], w_ref[...], (((0,), (0,)), ((), ())), preferred_element_type=F32
        ) + bias_ref[...]
        s = jax.nn.sigmoid(pre)
        act[rows, :] = (pre * s).astype(BF16)
        og = og_ref[(first + b) * BLOCK : (first + b + 1) * BLOCK, :].astype(F32)
        grad = (og * s * (1.0 + pre * (1.0 - s))).astype(BF16)
        grads[rows, :] = grad
        for q in range(parts):
            row = pl.multiple_of(lax.rem(me + q, parts) * width, width)
            g_refs[q][b] = lax.dot_general(
                w_ref[pl.ds(row, width), :], grad, (((1,), (1,)), ((), ())), preferred_element_type=F32
            ).astype(g_refs[q].dtype)


def weight_grad_kernel(n, *refs):
    hts, grads, acts, (out, mine, other, sems) = refs[:n], refs[n : 2 * n], refs[2 * n : 3 * n], refs[3 * n :]
    copies, first = [], 0
    for i, act in enumerate(acts):
        rows = act.shape[0]
        copies.append(pltpu.make_async_copy(act, out.at[pl.ds(first, rows)], sems.at[i]))
        copies[-1].start()
        first += rows
    full = sum(jnp.dot(h[...], g[...], preferred_element_type=F32) for h, g in zip(hts, grads))
    full = full.astype(BF16)
    rows = mine.shape[0]
    low, high = full[:rows], full[rows:]
    first = own_core() == 0
    mine[...] = jnp.where(first, low, high)
    other[...] = jnp.where(first, high, low)
    for c in copies:
        c.wait()


def swap_payload_kernel(g, *refs):
    parts, out = refs[:-1], refs[-1]
    blocks, width, _ = g.shape
    for b in range(blocks):
        out[b * width : (b + 1) * width, :] = g[b]
    total = paired_sum([r[...] for r in parts]).astype(BF16)
    rows, hid = total.shape
    if hid < out.shape[1]:
        out[blocks * width :, :] = jnp.zeros((rows, out.shape[1]), BF16)
    out[blocks * width :, :hid] = total


def pull(g, tiles, src, dst, acc, j, o, live):
    blocks = g.shape[0]
    k = j * REACH + o
    s = jnp.where(live, src[k], blocks)
    acc[s] += jnp.dot(g[dst[k] - o * blocks], tiles[j, o], preferred_element_type=F32)


def backward_own_kernel(count, src, dst, tiles, g0, acc):
    acc[...] = jnp.zeros_like(acc)
    slot_loop(count[0], tiles.shape[0], (0,), functools.partial(pull, g0, tiles, src, dst, acc))


def backward_near_kernel(count, src, dst, tiles, g2, gd, acc2, accd):
    acc2[...] = jnp.zeros_like(acc2)
    accd[...] = jnp.zeros_like(accd)
    far = 1 + 2 * own_core()

    def body(j, o, live):
        if isinstance(o, int):
            pull(g2, tiles, src, dst, acc2, j, o, live)
        else:
            pull(gd, tiles, src, dst, accd, j, o, live)

    slot_loop(count[0], tiles.shape[0], (2, far), body)


def backward_last_kernel(count, src, dst, tiles, sent, got, acc0, acc2, accd, out, wg, bias, acc):
    blocks, width = acc.shape[0] - 1, acc.shape[1]
    f_in, hid = wg.shape
    acc[...] = jnp.zeros_like(acc)
    core = own_core()
    far = 3 - 2 * core

    def body(j, o, live):
        k = j * REACH + o
        s = jnp.where(live, src[k], blocks)
        d = pl.multiple_of((dst[k] - o * blocks) * width, width)
        acc[s] += jnp.dot(got[pl.ds(d, width), :], tiles[j, o], preferred_element_type=F32)

    slot_loop(count[0], tiles.shape[0], (far,), body)
    for b in range(blocks):
        total = acc[b] + acc0[b] + acc2[b] + accd[b]
        out[:, b * BLOCK : (b + 1) * BLOCK] = total.astype(BF16)
    a, b = (r[blocks * width :, :hid].astype(F32) for r in (sent, got))
    low, high = jnp.where(core == 0, a, b), jnp.where(core == 0, b, a)
    rows = low.shape[0]
    wg[:rows, :] = low
    wg[rows:, :] = high[: f_in - rows]
    bias[...] = high[f_in - rows : f_in - rows + 1]


def paired_sum(parts):
    parts = [p.astype(F32) for p in parts]
    while len(parts) > 1:
        parts = [parts[i] + parts[i + 1] for i in range(0, len(parts), 2)]
    return parts[0]


def paired_sum_kernel(*refs):
    refs[-1][...] = paired_sum([r[...] for r in refs[:-1]]).astype(refs[-1].dtype)


def moved(block, axis, target):
    n = lax.axis_size(axis)
    return lax.ppermute(block, axis, [(i, target(i) % n) for i in range(n)])


def radices(n):
    out = []
    while n > 1:
        r = 4 if n % 4 == 0 else 2
        out.append(r)
        n //= r
    return out


def exchanged(part, axis, stride, r):
    return [part] + [moved(part, axis, lambda i, s=s: i ^ (s * stride)) for s in range(1, r)]


def shards(node_features, weight, bias, tile_values, tile_src, tile_dst, tile_counts, out_grad):
    nodes, f_in = node_features.shape
    hid = weight.shape[1]
    blocks = nodes // BLOCK
    parts = lax.axis_size("feat")
    width = f_in // parts
    capacity = tile_values.shape[0]
    groups = capacity // REACH
    piece = jax.ShapeDtypeStruct((blocks, width, BLOCK), BF16)
    totals = jax.ShapeDtypeStruct((blocks + 1, width, BLOCK), F32)
    acc = pltpu.VMEM(totals.shape, F32)
    tiles = jax.ShapeDtypeStruct((groups, REACH, BLOCK, BLOCK), BF16)
    slots = jax.ShapeDtypeStruct((capacity,), jnp.int32)
    rows = jax.ShapeDtypeStruct((nodes, hid), BF16)
    gradient = jax.ShapeDtypeStruct(((f_in + 32) // 2, hid), BF16)
    m = groups_at_once(groups)
    flops = 2 * capacity * BLOCK * BLOCK * width // REACH

    def swapped(i):
        return i ^ 1

    tiles, xt, swap, src, dst = call(
        forward_swap_kernel,
        [tiles, piece, piece, slots, slots],
        [SMEM] + [HBM] * 4,
        [VMEM] * 3 + [SMEM] * 2,
        [
            pltpu.VMEM(node_features.shape, BF16),
            acc,
            pltpu.SemaphoreType.DMA((3,)),
            pltpu.SemaphoreType.DMA((groups // m,)),
        ],
        flops,
    )(tile_counts, *(in_hbm(a) for a in (tile_src, tile_dst, node_features, tile_values.reshape(tiles.shape))))
    index = (tile_counts, src, dst)
    swap = moved(swap, "dom", swapped)
    acc2, direct = call(
        forward_send_kernel, [totals, piece], [SMEM] * 3 + [VMEM] * 2, [VMEM] * 2, [acc], 2 * flops
    )(*index, xt, tiles)
    cut = 2 if blocks % 2 == 0 else 1
    starts = range(0, blocks, blocks // cut)
    half = jax.ShapeDtypeStruct((blocks // cut, width, BLOCK), BF16)
    half_wide = jax.ShapeDtypeStruct(half.shape, F32)
    half_rows = jax.ShapeDtypeStruct((nodes // cut, hid), BF16)
    half_columns = jax.ShapeDtypeStruct((f_in + 32, nodes // cut), BF16)
    chip = call(functools.partial(sum_kernel, 2, 0), [half] * cut, [VMEM] * 2, [VMEM] * cut)(acc2, swap)
    chip = [moved(c, "dom", lambda i: i + 2) for c in chip]
    direct = moved(direct, "dom", lambda i: i + 1 + 2 * (i % 2))
    (acc0,) = call(forward_own_kernel, [totals], [SMEM] * 3 + [VMEM] * 2, [VMEM], (), flops)(*index, xt, tiles)
    h_lists = []
    for first, c in zip(starts, chip):
        (h,) = call(functools.partial(sum_kernel, 3, first), [half], [VMEM] * 3, [VMEM])(acc0, direct, c)
        h_lists.append([h] + [moved(h, "feat", lambda i, q=q: i - q) for q in range(1, parts)])
    acts, hts, grads, g_list = [], [], [], []
    for first, hs in zip(starts, h_lists):
        act, ht, grad, g_own, *g_others = call(
            functools.partial(middle_kernel, parts, first),
            [half_rows, half_columns, half_rows, half_wide] + [half] * (parts - 1),
            [VMEM] * (3 + parts),
            [VMEM] * (3 + parts),
            (),
            4 * nodes * f_in * hid // cut,
        )(bias.reshape(1, hid), weight, out_grad, *hs)
        acts.append(act)
        hts.append(ht)
        grads.append(grad)
        g_list += [g_own] + [moved(g, "feat", lambda i, q=q + 1: i + q) for q, g in enumerate(g_others)]
    output, wg, wg_other = call(
        functools.partial(weight_grad_kernel, cut),
        [rows, gradient, gradient],
        [VMEM] * (3 * cut),
        [HBM, VMEM, VMEM],
        [pltpu.SemaphoreType.DMA((cut,))],
        2 * nodes * f_in * hid,
    )(*hts, *grads, *acts)
    r, *more = radices(lax.axis_size("dom"))
    wgs = [wg] + [moved(wg_other if s % 2 else wg, "dom", lambda i, s=s: i ^ s) for s in range(1, r)]
    g_list[0], *wgs = lax.optimization_barrier((g_list[0], *wgs))
    (g,) = call(functools.partial(join_kernel, parts), [piece], [VMEM] * len(g_list), [VMEM])(*g_list)
    g_chip = moved(g, "dom", lambda i: i - 2)
    g_direct = moved(g, "dom", lambda i: i - 3 + 2 * (i % 2))
    (back0,) = call(backward_own_kernel, [totals], [SMEM] * 3 + [VMEM] * 2, [VMEM], (), flops)(*index, tiles, g)
    stride = r
    for r in more:
        (wg,) = call(paired_sum_kernel, [gradient], [VMEM] * len(wgs), [VMEM])(*wgs)
        wgs = exchanged(wg, "dom", stride, r)
        stride *= r
    back0, g_chip, g_direct, *wgs = lax.optimization_barrier((back0, g_chip, g_direct, *wgs))
    payload = jax.ShapeDtypeStruct((blocks * width + gradient.shape[0], BLOCK), BF16)
    (sent,) = call(swap_payload_kernel, [payload], [VMEM] * (1 + len(wgs)), [VMEM])(g_chip, *wgs)
    got = moved(sent, "dom", swapped)
    back2, backd = call(
        backward_near_kernel, [totals, totals], [SMEM] * 3 + [VMEM] * 3, [VMEM] * 2, (), 2 * flops
    )(*index, tiles, g_chip, g_direct)
    input_grad, weight_grad, bias_grad = call(
        backward_last_kernel,
        [
            jax.ShapeDtypeStruct((width, nodes), BF16),
            jax.ShapeDtypeStruct((f_in, hid), F32),
            jax.ShapeDtypeStruct((1, hid), F32),
        ],
        [SMEM] * 3 + [VMEM] * 6,
        [VMEM] * 3,
        [acc],
        flops,
    )(*index, tiles, sent, got, back0, back2, backd)
    return output, weight_grad, bias_grad.reshape(hid), input_grad.T


def solution(mesh):
    return jax.shard_map(
        shards,
        mesh=mesh,
        in_specs=(
            P("dom", None),
            P(None, "feat"),
            P("feat"),
            P("dom", None, None),
            P("dom"),
            P("dom"),
            P("dom"),
            P("dom", "feat"),
        ),
        out_specs=(P("dom", "feat"), P(None, "feat"), P("feat"), P("dom", "feat")),
        check_vma=False,
    )
```

```python
import functools
import math

import jax
import jax.numpy as jnp
from jax import lax
from jax.experimental import pallas as pl
from jax.experimental.pallas import tpu as pltpu
from jax.sharding import PartitionSpec as P

BLOCK = 128
REACH = 4
F32 = jnp.float32
BF16 = jnp.bfloat16
VMEM = pl.BlockSpec(memory_space=pltpu.VMEM)
SMEM = pl.BlockSpec(memory_space=pltpu.SMEM)
HBM = pl.BlockSpec(memory_space=pltpu.HBM)


def call(kernel, out_shape, in_specs, out_specs, scratch=(), flops=0):
    return pl.pallas_call(
        kernel,
        out_shape=out_shape,
        in_specs=in_specs,
        out_specs=out_specs,
        scratch_shapes=list(scratch),
        compiler_params=pltpu.CompilerParams(vmem_limit_bytes=24 * 1024 * 1024),
        cost_estimate=pl.CostEstimate(flops=flops, bytes_accessed=2**20, transcendentals=0),
    )


def groups_at_once(groups):
    return next(m for m in (4, 3, 2, 1) if groups % m == 0)


def in_hbm(a):
    return pltpu.with_memory_space_constraint(a, pltpu.HBM)


def own_core():
    return lax.rem(lax.axis_index("dom"), 2)


def slot_loop(count, groups, offsets, body):
    m = groups_at_once(groups)

    def chunk(i, carry):
        @pl.when(i * (m * REACH) < count)
        def _():
            for u in range(m):
                for o in offsets:
                    j = i * m + u
                    body(j, o, j * REACH + o < count)

        return carry

    lax.fori_loop(0, groups // m, chunk, 0)


def push(xt, tiles_ref, src_ref, dst_ref, acc, j, o, live):
    blocks = xt.shape[0]
    k = j * REACH + o
    d = jnp.where(live, dst_ref[k] - o * blocks, blocks)
    acc[d] += lax.dot_general(
        xt[src_ref[k]], tiles_ref[j, o], (((1,), (1,)), ((), ())), preferred_element_type=F32
    )


def forward_swap_kernel(
    count, src_hbm, dst_hbm, x_hbm, tiles_hbm, tiles, xt, swap, src, dst, x, acc, small, large
):
    blocks, width, _ = xt.shape
    groups = tiles.shape[0]
    copies = [
        pltpu.make_async_copy(a, b, small.at[i])
        for i, (a, b) in enumerate(((x_hbm, x), (src_hbm, src), (dst_hbm, dst)))
    ]

    o = 3 - 2 * own_core()
    loads = [
        pltpu.make_async_copy(tiles_hbm.at[:, p], tiles.at[:, p], large.at[i])
        for i, p in enumerate((o, 2, 4 - o, 0))
    ]
    for c in copies + loads:
        c.start()
    acc[...] = jnp.zeros_like(acc)
    row = lax.broadcasted_iota(jnp.int32, (width, x.shape[1]), 0)
    column = lax.broadcasted_iota(jnp.int32, (width, x.shape[1]), 1)
    pick = (column == row + lax.axis_index("feat") * width).astype(BF16)
    for c in copies:
        c.wait()
    for b in range(blocks):
        xt[b] = lax.dot_general(
            pick, x[b * BLOCK : (b + 1) * BLOCK, :], (((1,), (1,)), ((), ())), preferred_element_type=F32
        ).astype(BF16)
    loads[0].wait()
    slot_loop(count[0], groups, (o,), functools.partial(push, xt, tiles, src, dst, acc))
    swap[...] = acc[:blocks].astype(BF16)
    for c in loads[1:]:
        c.wait()


def forward_send_kernel(count, src, dst, xt, tiles, acc2, direct, acc):
    acc2[...] = jnp.zeros_like(acc2)
    acc[...] = jnp.zeros_like(acc)
    far = 1 + 2 * own_core()

    def body(j, o, live):
        push(xt, tiles, src, dst, acc2 if isinstance(o, int) else acc, j, o, live)

    slot_loop(count[0], tiles.shape[0], (2, far), body)
    direct[...] = acc[: direct.shape[0]].astype(BF16)


def forward_own_kernel(count, src, dst, xt, tiles, acc):
    acc[...] = jnp.zeros_like(acc)
    slot_loop(count[0], tiles.shape[0], (0,), functools.partial(push, xt, tiles, src, dst, acc))


def sum_kernel(n, first, *refs):
    for out in refs[n:]:
        blocks = out.shape[0]
        total = None
        for r in refs[:n]:
            part = r[...] if r.shape[0] == blocks else r[first : first + blocks]
            total = part.astype(F32) if total is None else total + part.astype(F32)
        out[...] = total.astype(out.dtype)
        first += blocks


def join_kernel(parts, *refs):
    out = refs[-1]
    halves = [refs[i : i + parts] for i in range(0, len(refs) - 1, parts)]
    first = 0
    for half in halves:
        blocks = half[0].shape[0]
        total = half[0][...].astype(F32)
        for r in half[1:]:
            total = total + r[...].astype(F32)
        out[first : first + blocks] = total.astype(out.dtype)
        first += blocks


def middle_kernel(parts, first, bias_ref, w_ref, og_ref, *refs):
    h_refs, (act, ht, grads), g_refs = refs[:parts], refs[parts : parts + 3], refs[parts + 3 :]
    blocks, width, _ = h_refs[0].shape
    f_in = w_ref.shape[0]
    me = lax.axis_index("feat")
    for q in range(parts):
        row = pl.multiple_of(lax.rem(me + q, parts) * width, width)
        for b in range(blocks):
            ht[pl.ds(row, width), b * BLOCK : (b + 1) * BLOCK] = h_refs[q][b]
    ht[f_in:, :] = jnp.ones((ht.shape[0] - f_in, ht.shape[1]), BF16)
    for b in range(blocks):
        rows = slice(b * BLOCK, (b + 1) * BLOCK)
        pre = lax.dot_general(
            ht[:f_in, rows], w_ref[...], (((0,), (0,)), ((), ())), preferred_element_type=F32
        ) + bias_ref[...]
        s = jax.nn.sigmoid(pre)
        act[rows, :] = (pre * s).astype(BF16)
        og = og_ref[(first + b) * BLOCK : (first + b + 1) * BLOCK, :].astype(F32)
        grad = (og * s * (1.0 + pre * (1.0 - s))).astype(BF16)
        grads[rows, :] = grad
        for q in range(parts):
            row = pl.multiple_of(lax.rem(me + q, parts) * width, width)
            g_refs[q][b] = lax.dot_general(
                w_ref[pl.ds(row, width), :], grad, (((1,), (1,)), ((), ())), preferred_element_type=F32
            ).astype(g_refs[q].dtype)


def weight_grad_kernel(n, *refs):
    hts, grads, (mine, other) = refs[:n], refs[n : 2 * n], refs[2 * n :]
    full = sum(jnp.dot(h[...], g[...], preferred_element_type=F32) for h, g in zip(hts, grads))
    full = full.astype(BF16)
    rows = mine.shape[0]
    low, high = full[:rows], full[rows:]
    first = own_core() == 0
    mine[...] = jnp.where(first, low, high)
    other[...] = jnp.where(first, high, low)


def swap_payload_kernel(g, *refs):
    parts, out = refs[:-1], refs[-1]
    blocks, width, _ = g.shape
    for b in range(blocks):
        out[b * width : (b + 1) * width, :] = g[b]
    total = paired_sum([r[...] for r in parts]).astype(BF16)
    rows, hid = total.shape
    if hid < out.shape[1]:
        out[blocks * width :, :] = jnp.zeros((rows, out.shape[1]), BF16)
    out[blocks * width :, :hid] = total


def pull(g, tiles, src, dst, acc, j, o, live):
    blocks = g.shape[0]
    k = j * REACH + o
    s = jnp.where(live, src[k], blocks)
    acc[s] += jnp.dot(g[dst[k] - o * blocks], tiles[j, o], preferred_element_type=F32)


def backward_own_kernel(count, src, dst, tiles, g0, *refs):
    acts, (acc, out, sems) = refs[:-3], refs[-3:]
    copies, first = [], 0
    for i, act in enumerate(acts):
        rows = act.shape[0]
        copies.append(pltpu.make_async_copy(act, out.at[pl.ds(first, rows)], sems.at[i]))
        copies[-1].start()
        first += rows
    acc[...] = jnp.zeros_like(acc)
    slot_loop(count[0], tiles.shape[0], (0,), functools.partial(pull, g0, tiles, src, dst, acc))
    for c in copies:
        c.wait()


def backward_near_kernel(count, src, dst, tiles, g2, gd, acc2, accd):
    acc2[...] = jnp.zeros_like(acc2)
    accd[...] = jnp.zeros_like(accd)
    far = 1 + 2 * own_core()

    def body(j, o, live):
        if isinstance(o, int):
            pull(g2, tiles, src, dst, acc2, j, o, live)
        else:
            pull(gd, tiles, src, dst, accd, j, o, live)

    slot_loop(count[0], tiles.shape[0], (2, far), body)


def backward_last_kernel(count, src, dst, tiles, sent, got, acc0, acc2, accd, out, wg, bias, acc):
    blocks, width = acc.shape[0] - 1, acc.shape[1]
    f_in, hid = wg.shape
    acc[...] = jnp.zeros_like(acc)
    core = own_core()
    far = 3 - 2 * core

    def body(j, o, live):
        k = j * REACH + o
        s = jnp.where(live, src[k], blocks)
        d = pl.multiple_of((dst[k] - o * blocks) * width, width)
        acc[s] += jnp.dot(got[pl.ds(d, width), :], tiles[j, o], preferred_element_type=F32)

    slot_loop(count[0], tiles.shape[0], (far,), body)
    for b in range(blocks):
        total = acc[b] + acc0[b] + acc2[b] + accd[b]
        out[:, b * BLOCK : (b + 1) * BLOCK] = total.astype(BF16)
    a, b = (r[blocks * width :, :hid].astype(F32) for r in (sent, got))
    low, high = jnp.where(core == 0, a, b), jnp.where(core == 0, b, a)
    rows = low.shape[0]
    wg[:rows, :] = low
    wg[rows:, :] = high[: f_in - rows]
    bias[...] = high[f_in - rows : f_in - rows + 1]


def paired_sum(parts):
    parts = [p.astype(F32) for p in parts]
    while len(parts) > 1:
        parts = [parts[i] + parts[i + 1] for i in range(0, len(parts), 2)]
    return parts[0]


def paired_sum_kernel(*refs):
    refs[-1][...] = paired_sum([r[...] for r in refs[:-1]]).astype(refs[-1].dtype)


def moved(block, axis, target):
    n = lax.axis_size(axis)
    return lax.ppermute(block, axis, [(i, target(i) % n) for i in range(n)])


def radices(n):
    out = [4]
    while math.prod(out) < n:
        out.append(2)
    return out


def exchanged(part, axis, stride, r):
    return [part] + [moved(part, axis, lambda i, s=s: i ^ (s * stride)) for s in range(1, r)]


def shards(node_features, weight, bias, tile_values, tile_src, tile_dst, tile_counts, out_grad):
    nodes, f_in = node_features.shape
    hid = weight.shape[1]
    blocks = nodes // BLOCK
    parts = lax.axis_size("feat")
    width = f_in // parts
    capacity = tile_values.shape[0]
    groups = capacity // REACH
    piece = jax.ShapeDtypeStruct((blocks, width, BLOCK), BF16)
    totals = jax.ShapeDtypeStruct((blocks + 1, width, BLOCK), F32)
    acc = pltpu.VMEM(totals.shape, F32)
    tiles = jax.ShapeDtypeStruct((groups, REACH, BLOCK, BLOCK), BF16)
    slots = jax.ShapeDtypeStruct((capacity,), jnp.int32)
    rows = jax.ShapeDtypeStruct((nodes, hid), BF16)
    gradient = jax.ShapeDtypeStruct(((f_in + 32) // 2, hid), BF16)
    flops = 2 * capacity * BLOCK * BLOCK * width // REACH

    def swapped(i):
        return i ^ 1

    tiles, xt, swap, src, dst = call(
        forward_swap_kernel,
        [tiles, piece, piece, slots, slots],
        [SMEM] + [HBM] * 4,
        [VMEM] * 3 + [SMEM] * 2,
        [
            pltpu.VMEM(node_features.shape, BF16),
            acc,
            pltpu.SemaphoreType.DMA((3,)),
            pltpu.SemaphoreType.DMA((REACH,)),
        ],
        flops,
    )(tile_counts, *(in_hbm(a) for a in (tile_src, tile_dst, node_features, tile_values.reshape(tiles.shape))))
    index = (tile_counts, src, dst)
    swap = moved(swap, "dom", swapped)
    acc2, direct = call(
        forward_send_kernel, [totals, piece], [SMEM] * 3 + [VMEM] * 2, [VMEM] * 2, [acc], 2 * flops
    )(*index, xt, tiles)
    cut = 2 if blocks % 2 == 0 else 1
    starts = range(0, blocks, blocks // cut)
    half = jax.ShapeDtypeStruct((blocks // cut, width, BLOCK), BF16)
    half_wide = jax.ShapeDtypeStruct(half.shape, F32)
    half_rows = jax.ShapeDtypeStruct((nodes // cut, hid), BF16)
    half_columns = jax.ShapeDtypeStruct((f_in + 32, nodes // cut), BF16)
    chip = call(functools.partial(sum_kernel, 2, 0), [half] * cut, [VMEM] * 2, [VMEM] * cut)(acc2, swap)
    chip = [moved(c, "dom", lambda i: i + 2) for c in chip]
    direct = moved(direct, "dom", lambda i: i + 1 + 2 * (i % 2))
    (acc0,) = call(forward_own_kernel, [totals], [SMEM] * 3 + [VMEM] * 2, [VMEM], (), flops)(*index, xt, tiles)
    h_lists = []
    for first, c in zip(starts, chip):
        (h,) = call(functools.partial(sum_kernel, 3, first), [half], [VMEM] * 3, [VMEM])(acc0, direct, c)
        h_lists.append([h] + [moved(h, "feat", lambda i, q=q: i - q) for q in range(1, parts)])
    acts, hts, grads, g_list = [], [], [], []
    for first, hs in zip(starts, h_lists):
        act, ht, grad, g_own, *g_others = call(
            functools.partial(middle_kernel, parts, first),
            [half_rows, half_columns, half_rows, half_wide] + [half] * (parts - 1),
            [VMEM] * (3 + parts),
            [VMEM] * (3 + parts),
            (),
            4 * nodes * f_in * hid // cut,
        )(bias.reshape(1, hid), weight, out_grad, *hs)
        acts.append(act)
        hts.append(ht)
        grads.append(grad)
        g_list += [g_own] + [moved(g, "feat", lambda i, q=q + 1: i + q) for q, g in enumerate(g_others)]
    wg, wg_other = call(
        functools.partial(weight_grad_kernel, cut),
        [gradient, gradient],
        [VMEM] * (2 * cut),
        [VMEM, VMEM],
        (),
        2 * nodes * f_in * hid,
    )(*hts, *grads)
    r, *more = radices(lax.axis_size("dom"))
    wgs = [wg] + [moved(wg_other if s % 2 else wg, "dom", lambda i, s=s: i ^ s) for s in range(1, r)]
    g_list[0], *wgs = lax.optimization_barrier((g_list[0], *wgs))
    (g,) = call(functools.partial(join_kernel, parts), [piece], [VMEM] * len(g_list), [VMEM])(*g_list)
    g_chip = moved(g, "dom", lambda i: i - 2)
    g_direct = moved(g, "dom", lambda i: i - 3 + 2 * (i % 2))
    stride = r
    for i, r in enumerate(more):
        if i == 1:
            back0, *wgs = lax.optimization_barrier((back0, *wgs))
        (wg,) = call(paired_sum_kernel, [gradient], [VMEM] * len(wgs), [VMEM])(*wgs)
        wgs = exchanged(wg, "dom", stride, r)
        stride *= r
        if i == 0:
            back0, output = call(
                backward_own_kernel,
                [totals, rows],
                [SMEM] * 3 + [VMEM] * (2 + cut),
                [VMEM, HBM],
                [pltpu.SemaphoreType.DMA((cut,))],
                flops,
            )(*index, tiles, g, *acts)
    back0, g_chip, g_direct, *wgs = lax.optimization_barrier((back0, g_chip, g_direct, *wgs))
    payload = jax.ShapeDtypeStruct((blocks * width + gradient.shape[0], BLOCK), BF16)
    (sent,) = call(swap_payload_kernel, [payload], [VMEM] * (1 + len(wgs)), [VMEM])(g_chip, *wgs)
    got = moved(sent, "dom", swapped)
    back2, backd = call(
        backward_near_kernel, [totals, totals], [SMEM] * 3 + [VMEM] * 3, [VMEM] * 2, (), 2 * flops
    )(*index, tiles, g_chip, g_direct)
    input_grad, weight_grad, bias_grad = call(
        backward_last_kernel,
        [
            jax.ShapeDtypeStruct((width, nodes), BF16),
            jax.ShapeDtypeStruct((f_in, hid), F32),
            jax.ShapeDtypeStruct((1, hid), F32),
        ],
        [SMEM] * 3 + [VMEM] * 6,
        [VMEM] * 3,
        [acc],
        flops,
    )(*index, tiles, sent, got, back0, back2, backd)
    return output, weight_grad, bias_grad.reshape(hid), input_grad.T


def solution(mesh):
    return jax.shard_map(
        shards,
        mesh=mesh,
        in_specs=(
            P("dom", None),
            P(None, "feat"),
            P("feat"),
            P("dom", None, None),
            P("dom"),
            P("dom"),
            P("dom"),
            P("dom", "feat"),
        ),
        out_specs=(P("dom", "feat"), P(None, "feat"), P("feat"), P("dom", "feat")),
        check_vma=False,
    )
```

```python
import functools

import jax
import jax.numpy as jnp
from jax import lax
from jax.experimental import pallas as pl
from jax.experimental.pallas import tpu as pltpu
from jax.sharding import PartitionSpec as P

BLOCK = 128
REACH = 4
SUM_FLOPS = 10**9
SRC_UNIT = 2**16
F32 = jnp.float32
BF16 = jnp.bfloat16
VMEM = pl.BlockSpec(memory_space=pltpu.VMEM)
SMEM = pl.BlockSpec(memory_space=pltpu.SMEM)
HBM = pl.BlockSpec(memory_space=pltpu.HBM)


def call(kernel, out_shape, in_specs, out_specs, scratch=(), flops=0):
    return pl.pallas_call(
        kernel,
        out_shape=out_shape,
        in_specs=in_specs,
        out_specs=out_specs,
        scratch_shapes=list(scratch),
        compiler_params=pltpu.CompilerParams(vmem_limit_bytes=24 * 1024 * 1024),
        cost_estimate=pl.CostEstimate(flops=flops, bytes_accessed=2**20, transcendentals=0),
    )


def groups_at_once(groups):
    return next(m for m in (4, 3, 2, 1) if groups % m == 0)


def in_hbm(a):
    return pltpu.with_memory_space_constraint(a, pltpu.HBM)


def own_core():
    return lax.rem(lax.axis_index("dom"), 2)


def slot_loop(count, groups, offsets, body):
    m = groups_at_once(groups)
    pair = 2 if m % 2 == 0 else 1

    def chunk(i, carry):
        @pl.when(i * (m * REACH) < count)
        def _():
            for u in range(0, m, pair):
                for o in offsets:
                    body([i * m + u + v for v in range(pair)], o)

        return carry

    lax.fori_loop(0, groups // m, chunk, 0)


def side_by_side(lefts, tiles, contract):
    if len(tiles) == 1:
        left, right = lefts[0], tiles[0]
    else:
        left = jnp.concatenate(lefts, axis=1)
        none = jnp.zeros_like(tiles[0])
        right = jnp.concatenate(
            [jnp.concatenate([tiles[0], none], axis=1), jnp.concatenate([none, tiles[1]], axis=1)], axis=0
        )
    out = lax.dot_general(left, right, (((1,), (contract,)), ((), ())), preferred_element_type=F32)
    return [out[:, i * BLOCK : (i + 1) * BLOCK] for i in range(len(tiles))]


def source(entry):
    return lax.shift_right_logical(entry, 16)


def target(entry, o, blocks):
    return lax.bitwise_and(entry, SRC_UNIT - 1) - o * blocks


def push(xt, tiles, index, count, acc, js, o):
    blocks = xt.shape[0]
    ks = [j * REACH + o for j in js]
    outs = side_by_side([xt[source(index[k])] for k in ks], [tiles[j, o] for j in js], 1)
    for k, out in zip(ks, outs):
        acc[jnp.where(k < count, target(index[k], o, blocks), blocks)] += out


def pull(block, tiles, index, count, acc, js, o):
    blocks = acc.shape[0] - 1
    ks = [j * REACH + o for j in js]
    outs = side_by_side([block(target(index[k], o, blocks)) for k in ks], [tiles[j, o] for j in js], 0)
    for k, out in zip(ks, outs):
        acc[jnp.where(k < count, source(index[k]), blocks)] += out


def forward_swap_kernel(
    count, src_hbm, dst_hbm, x_hbm, tiles_hbm, tiles, xt, swap, index, src, dst, x, acc, small, large
):
    blocks, width, _ = xt.shape
    groups = tiles.shape[0]
    slots = src_hbm.shape[0]
    copies = [
        pltpu.make_async_copy(a, b, small.at[i])
        for i, (a, b) in enumerate(((x_hbm, x), (src_hbm, src), (dst_hbm, dst)))
    ]
    o = 3 - 2 * own_core()
    loads = [
        pltpu.make_async_copy(tiles_hbm.at[:, p], tiles.at[:, p], large.at[i])
        for i, p in enumerate((o, 2, 4 - o, 0))
    ]
    for c in copies + loads:
        c.start()
    acc[...] = jnp.zeros_like(acc)
    row = lax.broadcasted_iota(jnp.int32, (width, x.shape[1]), 0)
    column = lax.broadcasted_iota(jnp.int32, (width, x.shape[1]), 1)
    pick = (column == row + lax.axis_index("feat") * width).astype(BF16)
    for c in copies:
        c.wait()
    for b in range(blocks):
        xt[b] = lax.dot_general(
            pick, x[b * BLOCK : (b + 1) * BLOCK, :], (((1,), (1,)), ((), ())), preferred_element_type=F32
        ).astype(BF16)
    for k in range(slots):
        index[k] = src[k] * SRC_UNIT + dst[k]
    loads[0].wait()
    slot_loop(count[0], groups, (o,), functools.partial(push, xt, tiles, index, count[0], acc))
    swap[...] = acc[:blocks].astype(BF16)
    for c in loads[1:]:
        c.wait()


def forward_send_kernel(count, index, xt, tiles, acc2, direct, acc):
    acc2[...] = jnp.zeros_like(acc2)
    acc[...] = jnp.zeros_like(acc)
    far = 1 + 2 * own_core()

    def body(js, o):
        push(xt, tiles, index, count[0], acc2 if isinstance(o, int) else acc, js, o)

    slot_loop(count[0], tiles.shape[0], (2, far), body)
    direct[...] = acc[: direct.shape[0]].astype(BF16)


def forward_own_kernel(count, index, xt, tiles, acc):
    acc[...] = jnp.zeros_like(acc)
    slot_loop(count[0], tiles.shape[0], (0,), functools.partial(push, xt, tiles, index, count[0], acc))


def sum_kernel(n, first, *refs):
    for out in refs[n:]:
        blocks = out.shape[0]
        total = None
        for r in refs[:n]:
            part = r[...] if r.shape[0] == blocks else r[first : first + blocks]
            total = part.astype(F32) if total is None else total + part.astype(F32)
        out[...] = total.astype(out.dtype)
        first += blocks


def join_kernel(parts, *refs):
    out = refs[-1]
    halves = [refs[i : i + parts] for i in range(0, len(refs) - 1, parts)]
    first = 0
    for half in halves:
        blocks = half[0].shape[0]
        total = half[0][...].astype(F32)
        for r in half[1:]:
            total = total + r[...].astype(F32)
        out[first : first + blocks] = total.astype(out.dtype)
        first += blocks


def middle_kernel(parts, first, bias_ref, w_ref, og_ref, *refs):
    h_refs, (act, ht, grads), g_refs = refs[:parts], refs[parts : parts + 3], refs[parts + 3 :]
    blocks, width, _ = h_refs[0].shape
    f_in = w_ref.shape[0]
    me = lax.axis_index("feat")
    for q in range(parts):
        row = pl.multiple_of(lax.rem(me + q, parts) * width, width)
        for b in range(blocks):
            ht[pl.ds(row, width), b * BLOCK : (b + 1) * BLOCK] = h_refs[q][b]
    ht[f_in:, :] = jnp.ones((ht.shape[0] - f_in, ht.shape[1]), BF16)
    for b in range(blocks):
        rows = slice(b * BLOCK, (b + 1) * BLOCK)
        pre = lax.dot_general(
            ht[:f_in, rows], w_ref[...], (((0,), (0,)), ((), ())), preferred_element_type=F32
        ) + bias_ref[...]
        s = jax.nn.sigmoid(pre)
        act[rows, :] = (pre * s).astype(BF16)
        og = og_ref[(first + b) * BLOCK : (first + b + 1) * BLOCK, :].astype(F32)
        grad = (og * s * (1.0 + pre * (1.0 - s))).astype(BF16)
        grads[rows, :] = grad
        for q in range(parts):
            row = pl.multiple_of(lax.rem(me + q, parts) * width, width)
            g_refs[q][b] = lax.dot_general(
                w_ref[pl.ds(row, width), :], grad, (((1,), (1,)), ((), ())), preferred_element_type=F32
            ).astype(g_refs[q].dtype)


def weight_grad_kernel(n, *refs):
    hts, grads, (mine, other) = refs[:n], refs[n : 2 * n], refs[2 * n :]
    full = sum(jnp.dot(h[...], g[...], preferred_element_type=F32) for h, g in zip(hts, grads))
    full = full.astype(BF16)
    rows = mine.shape[0]
    low, high = full[:rows], full[rows:]
    first = own_core() == 0
    mine[...] = jnp.where(first, low, high)
    other[...] = jnp.where(first, high, low)


def swap_payload_kernel(g, *refs):
    parts, out = refs[:-1], refs[-1]
    blocks, width, _ = g.shape
    for b in range(blocks):
        out[b * width : (b + 1) * width, :] = g[b]
    total = paired_sum([r[...] for r in parts]).astype(BF16)
    rows, hid = total.shape
    if hid < out.shape[1]:
        out[blocks * width :, :] = jnp.zeros((rows, out.shape[1]), BF16)
    out[blocks * width :, :hid] = total


def backward_own_kernel(count, index, tiles, g, *refs):
    acts, (acc, out, sems) = refs[:-3], refs[-3:]
    copies, first = [], 0
    for i, act in enumerate(acts):
        rows = act.shape[0]
        copies.append(pltpu.make_async_copy(act, out.at[pl.ds(first, rows)], sems.at[i]))
        copies[-1].start()
        first += rows
    acc[...] = jnp.zeros_like(acc)
    slot_loop(
        count[0], tiles.shape[0], (0,), functools.partial(pull, lambda d: g[d], tiles, index, count[0], acc)
    )
    for c in copies:
        c.wait()


def backward_near_kernel(count, index, tiles, g2, gd, acc2, accd):
    acc2[...] = jnp.zeros_like(acc2)
    accd[...] = jnp.zeros_like(accd)
    far = 1 + 2 * own_core()

    def body(js, o):
        if isinstance(o, int):
            pull(lambda d: g2[d], tiles, index, count[0], acc2, js, o)
        else:
            pull(lambda d: gd[d], tiles, index, count[0], accd, js, o)

    slot_loop(count[0], tiles.shape[0], (2, far), body)


def backward_last_kernel(count, index, tiles, sent, got, acc0, acc2, accd, out, wg, bias, acc):
    blocks, width = acc.shape[0] - 1, acc.shape[1]
    f_in, hid = wg.shape
    acc[...] = jnp.zeros_like(acc)
    core = own_core()
    far = 3 - 2 * core

    def block(d):
        return got[pl.ds(pl.multiple_of(d * width, width), width), :]

    slot_loop(count[0], tiles.shape[0], (far,), functools.partial(pull, block, tiles, index, count[0], acc))
    for b in range(blocks):
        total = acc[b] + acc0[b] + acc2[b] + accd[b]
        out[:, b * BLOCK : (b + 1) * BLOCK] = total.astype(BF16)
    a, b = (r[blocks * width :, :hid].astype(F32) for r in (sent, got))
    low, high = jnp.where(core == 0, a, b), jnp.where(core == 0, b, a)
    rows = low.shape[0]
    wg[:rows, :] = low
    wg[rows:, :] = high[: f_in - rows]
    bias[...] = high[f_in - rows : f_in - rows + 1]


def paired_sum(parts):
    parts = [p.astype(F32) for p in parts]
    while len(parts) > 1:
        parts = [parts[i] + parts[i + 1] for i in range(0, len(parts), 2)]
    return parts[0]


def paired_sum_kernel(*refs):
    refs[-1][...] = paired_sum([r[...] for r in refs[:-1]]).astype(refs[-1].dtype)


def moved(block, axis, target):
    n = lax.axis_size(axis)
    return lax.ppermute(block, axis, [(i, target(i) % n) for i in range(n)])


def radices(n):
    out = []
    while n > 1:
        r = 4 if n % 4 == 0 else 2
        out.append(r)
        n //= r
    return out


def exchanged(part, axis, stride, r):
    return [part] + [moved(part, axis, lambda i, s=s: i ^ (s * stride)) for s in range(1, r)]


def shards(node_features, weight, bias, tile_values, tile_src, tile_dst, tile_counts, out_grad):
    nodes, f_in = node_features.shape
    hid = weight.shape[1]
    blocks = nodes // BLOCK
    parts = lax.axis_size("feat")
    width = f_in // parts
    capacity = tile_values.shape[0]
    groups = capacity // REACH
    piece = jax.ShapeDtypeStruct((blocks, width, BLOCK), BF16)
    totals = jax.ShapeDtypeStruct((blocks + 1, width, BLOCK), F32)
    acc = pltpu.VMEM(totals.shape, F32)
    tiles = jax.ShapeDtypeStruct((groups, REACH, BLOCK, BLOCK), BF16)
    slots = jax.ShapeDtypeStruct((capacity,), jnp.int32)
    rows = jax.ShapeDtypeStruct((nodes, hid), BF16)
    gradient = jax.ShapeDtypeStruct(((f_in + 32) // 2, hid), BF16)
    flops = 2 * capacity * BLOCK * BLOCK * width // REACH

    def swapped(i):
        return i ^ 1

    tiles, xt, swap, index = call(
        forward_swap_kernel,
        [tiles, piece, piece, slots],
        [SMEM] + [HBM] * 4,
        [VMEM] * 3 + [SMEM],
        [
            pltpu.SMEM((capacity,), jnp.int32),
            pltpu.SMEM((capacity,), jnp.int32),
            pltpu.VMEM(node_features.shape, BF16),
            acc,
            pltpu.SemaphoreType.DMA((3,)),
            pltpu.SemaphoreType.DMA((REACH,)),
        ],
        flops,
    )(tile_counts, *(in_hbm(a) for a in (tile_src, tile_dst, node_features, tile_values.reshape(tiles.shape))))
    index = (tile_counts, index)
    swap = moved(swap, "dom", swapped)
    acc2, direct = call(
        forward_send_kernel, [totals, piece], [SMEM] * 2 + [VMEM] * 2, [VMEM] * 2, [acc], 2 * flops
    )(*index, xt, tiles)
    cut = 2 if blocks % 2 == 0 else 1
    starts = range(0, blocks, blocks // cut)
    half = jax.ShapeDtypeStruct((blocks // cut, width, BLOCK), BF16)
    half_wide = jax.ShapeDtypeStruct(half.shape, F32)
    half_rows = jax.ShapeDtypeStruct((nodes // cut, hid), BF16)
    half_columns = jax.ShapeDtypeStruct((f_in + 32, nodes // cut), BF16)
    chip = call(functools.partial(sum_kernel, 2, 0), [half] * cut, [VMEM] * 2, [VMEM] * cut)(acc2, swap)
    chip = [moved(c, "dom", lambda i: i + 2) for c in chip]
    direct = moved(direct, "dom", lambda i: i + 1 + 2 * (i % 2))
    (acc0,) = call(forward_own_kernel, [totals], [SMEM] * 2 + [VMEM] * 2, [VMEM], (), flops)(*index, xt, tiles)
    h_lists = []
    for first, c in zip(starts, chip):
        (h,) = call(functools.partial(sum_kernel, 3, first), [half], [VMEM] * 3, [VMEM])(acc0, direct, c)
        h_lists.append([h] + [moved(h, "feat", lambda i, q=q: i - q) for q in range(1, parts)])
    acts, hts, grads, g_list = [], [], [], []
    for first, hs in zip(starts, h_lists):
        act, ht, grad, g_own, *g_others = call(
            functools.partial(middle_kernel, parts, first),
            [half_rows, half_columns, half_rows, half_wide] + [half] * (parts - 1),
            [VMEM] * (3 + parts),
            [VMEM] * (3 + parts),
            (),
            4 * nodes * f_in * hid // cut,
        )(bias.reshape(1, hid), weight, out_grad, *hs)
        acts.append(act)
        hts.append(ht)
        grads.append(grad)
        g_list += [g_own] + [moved(g, "feat", lambda i, q=q + 1: i + q) for q, g in enumerate(g_others)]
    wg, wg_other = call(
        functools.partial(weight_grad_kernel, cut),
        [gradient, gradient],
        [VMEM] * (2 * cut),
        [VMEM, VMEM],
        (),
        2 * nodes * f_in * hid,
    )(*hts, *grads)
    r, *more = radices(lax.axis_size("dom"))
    wgs = [wg] + [moved(wg_other if s % 2 else wg, "dom", lambda i, s=s: i ^ s) for s in range(1, r)]
    (g,) = call(functools.partial(join_kernel, parts), [piece], [VMEM] * len(g_list), [VMEM])(*g_list)
    g_chip = moved(g, "dom", lambda i: i - 2)
    g_direct = moved(g, "dom", lambda i: i - 3 + 2 * (i % 2))
    stride = r
    for r in more:
        (wg,) = call(paired_sum_kernel, [gradient], [VMEM] * len(wgs), [VMEM], (), SUM_FLOPS)(*wgs)
        wgs = exchanged(wg, "dom", stride, r)
        stride *= r
    back0, output = call(
        backward_own_kernel,
        [totals, rows],
        [SMEM] * 2 + [VMEM] * (2 + cut),
        [VMEM, HBM],
        [pltpu.SemaphoreType.DMA((cut,))],
        flops,
    )(*index, tiles, g, *acts)
    back0, g_chip, g_direct, *wgs = lax.optimization_barrier((back0, g_chip, g_direct, *wgs))
    payload = jax.ShapeDtypeStruct((blocks * width + gradient.shape[0], BLOCK), BF16)
    (sent,) = call(swap_payload_kernel, [payload], [VMEM] * (1 + len(wgs)), [VMEM])(g_chip, *wgs)
    got = moved(sent, "dom", swapped)
    back2, backd = call(
        backward_near_kernel, [totals, totals], [SMEM] * 2 + [VMEM] * 3, [VMEM] * 2, (), 2 * flops
    )(*index, tiles, g_chip, g_direct)
    input_grad, weight_grad, bias_grad = call(
        backward_last_kernel,
        [
            jax.ShapeDtypeStruct((width, nodes), BF16),
            jax.ShapeDtypeStruct((f_in, hid), F32),
            jax.ShapeDtypeStruct((1, hid), F32),
        ],
        [SMEM] * 2 + [VMEM] * 6,
        [VMEM] * 3,
        [acc],
        flops,
    )(*index, tiles, sent, got, back0, back2, backd)
    return output, weight_grad, bias_grad.reshape(hid), input_grad.T


def solution(mesh):
    return jax.shard_map(
        shards,
        mesh=mesh,
        in_specs=(
            P("dom", None),
            P(None, "feat"),
            P("feat"),
            P("dom", None, None),
            P("dom"),
            P("dom"),
            P("dom"),
            P("dom", "feat"),
        ),
        out_specs=(P("dom", "feat"), P(None, "feat"), P("feat"), P("dom", "feat")),
        check_vma=False,
    )
```

```python
import functools

import jax
import jax.numpy as jnp
from jax import lax
from jax.experimental import pallas as pl
from jax.experimental.pallas import tpu as pltpu
from jax.sharding import PartitionSpec as P

BLOCK = 128
REACH = 4
SUM_FLOPS = 10**9
SRC_UNIT = 2**16
F32 = jnp.float32
BF16 = jnp.bfloat16
VMEM = pl.BlockSpec(memory_space=pltpu.VMEM)
SMEM = pl.BlockSpec(memory_space=pltpu.SMEM)
HBM = pl.BlockSpec(memory_space=pltpu.HBM)


def call(kernel, out_shape, in_specs, out_specs, scratch=(), flops=0):
    return pl.pallas_call(
        kernel,
        out_shape=out_shape,
        in_specs=in_specs,
        out_specs=out_specs,
        scratch_shapes=list(scratch),
        compiler_params=pltpu.CompilerParams(vmem_limit_bytes=24 * 1024 * 1024),
        cost_estimate=pl.CostEstimate(flops=flops, bytes_accessed=2**20, transcendentals=0),
    )


def groups_at_once(groups):
    return next(m for m in (4, 3, 2, 1) if groups % m == 0)


def in_hbm(a):
    return pltpu.with_memory_space_constraint(a, pltpu.HBM)


def own_core():
    return lax.rem(lax.axis_index("dom"), 2)


def slot_loop(count, groups, offsets, body):
    m = groups_at_once(groups)
    pair = 2 if m % 2 == 0 else 1

    def chunk(i, carry):
        @pl.when(i * (m * REACH) < count)
        def _():
            for u in range(0, m, pair):
                for o in offsets:
                    body([i * m + u + v for v in range(pair)], o)

        return carry

    lax.fori_loop(0, groups // m, chunk, 0)


def side_by_side(lefts, tiles, contract):
    if len(tiles) == 1:
        left, right = lefts[0], tiles[0]
    else:
        left = jnp.concatenate(lefts, axis=1)
        none = jnp.zeros_like(tiles[0])
        right = jnp.concatenate(
            [jnp.concatenate([tiles[0], none], axis=1), jnp.concatenate([none, tiles[1]], axis=1)], axis=0
        )
    out = lax.dot_general(left, right, (((1,), (contract,)), ((), ())), preferred_element_type=F32)
    return [out[:, i * BLOCK : (i + 1) * BLOCK] for i in range(len(tiles))]


def source(entry):
    return lax.shift_right_logical(entry, 16)


def target(entry, o, blocks):
    return lax.bitwise_and(entry, SRC_UNIT - 1) - o * blocks


def push(xt, tiles, index, count, acc, js, o):
    blocks = xt.shape[0]
    ks = [j * REACH + o for j in js]
    plane = o if tiles.shape[1] == REACH else 0
    outs = side_by_side([xt[source(index[k])] for k in ks], [tiles[j, plane] for j in js], 1)
    for k, out in zip(ks, outs):
        acc[jnp.where(k < count, target(index[k], o, blocks), blocks)] += out


def pull(block, tiles, index, count, acc, js, o):
    blocks = acc.shape[0] - 1
    ks = [j * REACH + o for j in js]
    outs = side_by_side([block(target(index[k], o, blocks)) for k in ks], [tiles[j, o] for j in js], 0)
    for k, out in zip(ks, outs):
        acc[jnp.where(k < count, source(index[k]), blocks)] += out


def forward_swap_kernel(
    count, src_hbm, dst_hbm, x_hbm, tiles_hbm, xt, swap, index, src, dst, x, tiles, acc, sems
):
    blocks, width, _ = xt.shape
    groups = tiles_hbm.shape[0]
    slots = src_hbm.shape[0]
    o = 3 - 2 * own_core()
    *copies, load = [
        pltpu.make_async_copy(a, b, sems.at[i])
        for i, (a, b) in enumerate(((x_hbm, x), (src_hbm, src), (dst_hbm, dst), (tiles_hbm.at[:, o], tiles.at[:, 0])))
    ]
    for c in (*copies, load):
        c.start()
    acc[...] = jnp.zeros_like(acc)
    row = lax.broadcasted_iota(jnp.int32, (width, x.shape[1]), 0)
    column = lax.broadcasted_iota(jnp.int32, (width, x.shape[1]), 1)
    pick = (column == row + lax.axis_index("feat") * width).astype(BF16)
    for c in copies:
        c.wait()
    for b in range(blocks):
        xt[b] = lax.dot_general(
            pick, x[b * BLOCK : (b + 1) * BLOCK, :], (((1,), (1,)), ((), ())), preferred_element_type=F32
        ).astype(BF16)
    for k in range(slots):
        index[k] = src[k] * SRC_UNIT + dst[k]
    load.wait()
    slot_loop(count[0], groups, (o,), functools.partial(push, xt, tiles, index, count[0], acc))
    swap[...] = acc[:blocks].astype(BF16)


def forward_send_kernel(count, index, xt, tiles, acc2, direct, acc):
    acc2[...] = jnp.zeros_like(acc2)
    acc[...] = jnp.zeros_like(acc)
    far = 1 + 2 * own_core()

    def body(js, o):
        push(xt, tiles, index, count[0], acc2 if isinstance(o, int) else acc, js, o)

    slot_loop(count[0], tiles.shape[0], (2, far), body)
    direct[...] = acc[: direct.shape[0]].astype(BF16)


def forward_own_kernel(count, index, xt, tiles, acc):
    acc[...] = jnp.zeros_like(acc)
    slot_loop(count[0], tiles.shape[0], (0,), functools.partial(push, xt, tiles, index, count[0], acc))


def sum_kernel(n, first, *refs):
    for out in refs[n:]:
        blocks = out.shape[0]
        total = None
        for r in refs[:n]:
            part = r[...] if r.shape[0] == blocks else r[first : first + blocks]
            total = part.astype(F32) if total is None else total + part.astype(F32)
        out[...] = total.astype(out.dtype)
        first += blocks


def join_kernel(parts, *refs):
    out = refs[-1]
    halves = [refs[i : i + parts] for i in range(0, len(refs) - 1, parts)]
    first = 0
    for half in halves:
        blocks = half[0].shape[0]
        total = half[0][...].astype(F32)
        for r in half[1:]:
            total = total + r[...].astype(F32)
        out[first : first + blocks] = total.astype(out.dtype)
        first += blocks


def middle_kernel(parts, first, bias_ref, w_ref, og_ref, *refs):
    h_refs, (act, ht, grads), g_refs = refs[:parts], refs[parts : parts + 3], refs[parts + 3 :]
    blocks, width, _ = h_refs[0].shape
    f_in = w_ref.shape[0]
    me = lax.axis_index("feat")
    for q in range(parts):
        row = pl.multiple_of(lax.rem(me + q, parts) * width, width)
        for b in range(blocks):
            ht[pl.ds(row, width), b * BLOCK : (b + 1) * BLOCK] = h_refs[q][b]
    ht[f_in:, :] = jnp.ones((ht.shape[0] - f_in, ht.shape[1]), BF16)
    for b in range(blocks):
        rows = slice(b * BLOCK, (b + 1) * BLOCK)
        pre = lax.dot_general(
            ht[:f_in, rows], w_ref[...], (((0,), (0,)), ((), ())), preferred_element_type=F32
        ) + bias_ref[...]
        s = jax.nn.sigmoid(pre)
        act[rows, :] = (pre * s).astype(BF16)
        og = og_ref[(first + b) * BLOCK : (first + b + 1) * BLOCK, :].astype(F32)
        grad = (og * s * (1.0 + pre * (1.0 - s))).astype(BF16)
        grads[rows, :] = grad
        for q in range(parts):
            row = pl.multiple_of(lax.rem(me + q, parts) * width, width)
            g_refs[q][b] = lax.dot_general(
                w_ref[pl.ds(row, width), :], grad, (((1,), (1,)), ((), ())), preferred_element_type=F32
            ).astype(g_refs[q].dtype)


def weight_grad_kernel(n, *refs):
    hts, grads, (mine, other) = refs[:n], refs[n : 2 * n], refs[2 * n :]
    full = sum(jnp.dot(h[...], g[...], preferred_element_type=F32) for h, g in zip(hts, grads))
    full = full.astype(BF16)
    rows = mine.shape[0]
    low, high = full[:rows], full[rows:]
    first = own_core() == 0
    mine[...] = jnp.where(first, low, high)
    other[...] = jnp.where(first, high, low)


def swap_payload_kernel(g, *refs):
    parts, out = refs[:-1], refs[-1]
    blocks, width, _ = g.shape
    for b in range(blocks):
        out[b * width : (b + 1) * width, :] = g[b]
    total = paired_sum([r[...] for r in parts]).astype(BF16)
    rows, hid = total.shape
    if hid < out.shape[1]:
        out[blocks * width :, :] = jnp.zeros((rows, out.shape[1]), BF16)
    out[blocks * width :, :hid] = total


def backward_own_kernel(count, index, tiles, g, *refs):
    acts, (acc, out, sems) = refs[:-3], refs[-3:]
    copies, first = [], 0
    for i, act in enumerate(acts):
        rows = act.shape[0]
        copies.append(pltpu.make_async_copy(act, out.at[pl.ds(first, rows)], sems.at[i]))
        copies[-1].start()
        first += rows
    acc[...] = jnp.zeros_like(acc)
    slot_loop(
        count[0], tiles.shape[0], (0,), functools.partial(pull, lambda d: g[d], tiles, index, count[0], acc)
    )
    for c in copies:
        c.wait()


def backward_near_kernel(count, index, tiles, g2, gd, acc2, accd):
    acc2[...] = jnp.zeros_like(acc2)
    accd[...] = jnp.zeros_like(accd)
    far = 1 + 2 * own_core()

    def body(js, o):
        if isinstance(o, int):
            pull(lambda d: g2[d], tiles, index, count[0], acc2, js, o)
        else:
            pull(lambda d: gd[d], tiles, index, count[0], accd, js, o)

    slot_loop(count[0], tiles.shape[0], (2, far), body)


def backward_last_kernel(count, index, tiles, sent, got, acc0, acc2, accd, out, wg, bias, acc):
    blocks, width = acc.shape[0] - 1, acc.shape[1]
    f_in, hid = wg.shape
    acc[...] = jnp.zeros_like(acc)
    core = own_core()
    far = 3 - 2 * core

    def block(d):
        return got[pl.ds(pl.multiple_of(d * width, width), width), :]

    slot_loop(count[0], tiles.shape[0], (far,), functools.partial(pull, block, tiles, index, count[0], acc))
    for b in range(blocks):
        total = acc[b] + acc0[b] + acc2[b] + accd[b]
        out[:, b * BLOCK : (b + 1) * BLOCK] = total.astype(BF16)
    a, b = (r[blocks * width :, :hid].astype(F32) for r in (sent, got))
    low, high = jnp.where(core == 0, a, b), jnp.where(core == 0, b, a)
    rows = low.shape[0]
    wg[:rows, :] = low
    wg[rows:, :] = high[: f_in - rows]
    bias[...] = high[f_in - rows : f_in - rows + 1]


def paired_sum(parts):
    parts = [p.astype(F32) for p in parts]
    while len(parts) > 1:
        parts = [parts[i] + parts[i + 1] for i in range(0, len(parts), 2)]
    return parts[0]


def paired_sum_kernel(*refs):
    refs[-1][...] = paired_sum([r[...] for r in refs[:-1]]).astype(refs[-1].dtype)


def moved(block, axis, target):
    n = lax.axis_size(axis)
    return lax.ppermute(block, axis, [(i, target(i) % n) for i in range(n)])


def radices(n):
    out = []
    while n > 1:
        r = 4 if n % 4 == 0 else 2
        out.append(r)
        n //= r
    return out


def exchanged(part, axis, stride, r):
    return [part] + [moved(part, axis, lambda i, s=s: i ^ (s * stride)) for s in range(1, r)]


def shards(node_features, weight, bias, tile_values, tile_src, tile_dst, tile_counts, out_grad):
    nodes, f_in = node_features.shape
    hid = weight.shape[1]
    blocks = nodes // BLOCK
    parts = lax.axis_size("feat")
    width = f_in // parts
    capacity = tile_values.shape[0]
    groups = capacity // REACH
    piece = jax.ShapeDtypeStruct((blocks, width, BLOCK), BF16)
    totals = jax.ShapeDtypeStruct((blocks + 1, width, BLOCK), F32)
    acc = pltpu.VMEM(totals.shape, F32)
    tiles = tile_values.reshape(groups, REACH, BLOCK, BLOCK)
    slots = jax.ShapeDtypeStruct((capacity,), jnp.int32)
    rows = jax.ShapeDtypeStruct((nodes, hid), BF16)
    gradient = jax.ShapeDtypeStruct(((f_in + 32) // 2, hid), BF16)
    flops = 2 * capacity * BLOCK * BLOCK * width // REACH

    def swapped(i):
        return i ^ 1

    xt, swap, index = call(
        forward_swap_kernel,
        [piece, piece, slots],
        [SMEM] + [HBM] * 4,
        [VMEM] * 2 + [SMEM],
        [
            pltpu.SMEM((capacity,), jnp.int32),
            pltpu.SMEM((capacity,), jnp.int32),
            pltpu.VMEM(node_features.shape, BF16),
            pltpu.VMEM((groups, 1, BLOCK, BLOCK), BF16),
            acc,
            pltpu.SemaphoreType.DMA((4,)),
        ],
        flops,
    )(tile_counts, *(in_hbm(a) for a in (tile_src, tile_dst, node_features, tiles)))
    index = (tile_counts, index)
    swap = moved(swap, "dom", swapped)
    acc2, direct = call(
        forward_send_kernel, [totals, piece], [SMEM] * 2 + [VMEM] * 2, [VMEM] * 2, [acc], 2 * flops
    )(*index, xt, tiles)
    cut = 2 if blocks % 2 == 0 else 1
    starts = range(0, blocks, blocks // cut)
    half = jax.ShapeDtypeStruct((blocks // cut, width, BLOCK), BF16)
    half_wide = jax.ShapeDtypeStruct(half.shape, F32)
    half_rows = jax.ShapeDtypeStruct((nodes // cut, hid), BF16)
    half_columns = jax.ShapeDtypeStruct((f_in + 32, nodes // cut), BF16)
    chip = call(functools.partial(sum_kernel, 2, 0), [half] * cut, [VMEM] * 2, [VMEM] * cut)(acc2, swap)
    direct = moved(direct, "dom", lambda i: i + 1 + 2 * (i % 2))
    (acc0,) = call(forward_own_kernel, [totals], [SMEM] * 2 + [VMEM] * 2, [VMEM], (), flops)(*index, xt, tiles)
    acc0, *later = lax.optimization_barrier((acc0, *chip[1:]))
    chip = [chip[0], *later]
    chip = [moved(c, "dom", lambda i: i + 2) for c in chip]
    h_lists = []
    for first, c in zip(starts, chip):
        (h,) = call(functools.partial(sum_kernel, 3, first), [half], [VMEM] * 3, [VMEM])(acc0, direct, c)
        h_lists.append([h] + [moved(h, "feat", lambda i, q=q: i - q) for q in range(1, parts)])
    acts, hts, grads, g_list = [], [], [], []
    for first, hs in zip(starts, h_lists):
        act, ht, grad, g_own, *g_others = call(
            functools.partial(middle_kernel, parts, first),
            [half_rows, half_columns, half_rows, half_wide] + [half] * (parts - 1),
            [VMEM] * (3 + parts),
            [VMEM] * (3 + parts),
            (),
            4 * nodes * f_in * hid // cut,
        )(bias.reshape(1, hid), weight, out_grad, *hs)
        acts.append(act)
        hts.append(ht)
        grads.append(grad)
        g_list += [g_own] + [moved(g, "feat", lambda i, q=q + 1: i + q) for q, g in enumerate(g_others)]
    wg, wg_other = call(
        functools.partial(weight_grad_kernel, cut),
        [gradient, gradient],
        [VMEM] * (2 * cut),
        [VMEM, VMEM],
        (),
        2 * nodes * f_in * hid,
    )(*hts, *grads)
    r, *more = radices(lax.axis_size("dom"))
    wgs = [wg] + [moved(wg_other if s % 2 else wg, "dom", lambda i, s=s: i ^ s) for s in range(1, r)]
    (g,) = call(functools.partial(join_kernel, parts), [piece], [VMEM] * len(g_list), [VMEM])(*g_list)
    g_chip = moved(g, "dom", lambda i: i - 2)
    g_direct = moved(g, "dom", lambda i: i - 3 + 2 * (i % 2))
    stride = r
    for r in more:
        (wg,) = call(paired_sum_kernel, [gradient], [VMEM] * len(wgs), [VMEM], (), SUM_FLOPS)(*wgs)
        wgs = exchanged(wg, "dom", stride, r)
        stride *= r
    back0, output = call(
        backward_own_kernel,
        [totals, rows],
        [SMEM] * 2 + [VMEM] * (2 + cut),
        [VMEM, HBM],
        [pltpu.SemaphoreType.DMA((cut,))],
        flops,
    )(*index, tiles, g, *acts)
    back0, g_chip, g_direct, *wgs = lax.optimization_barrier((back0, g_chip, g_direct, *wgs))
    payload = jax.ShapeDtypeStruct((blocks * width + gradient.shape[0], BLOCK), BF16)
    (sent,) = call(swap_payload_kernel, [payload], [VMEM] * (1 + len(wgs)), [VMEM])(g_chip, *wgs)
    got = moved(sent, "dom", swapped)
    back2, backd = call(
        backward_near_kernel, [totals, totals], [SMEM] * 2 + [VMEM] * 3, [VMEM] * 2, (), 2 * flops
    )(*index, tiles, g_chip, g_direct)
    input_grad, weight_grad, bias_grad = call(
        backward_last_kernel,
        [
            jax.ShapeDtypeStruct((width, nodes), BF16),
            jax.ShapeDtypeStruct((f_in, hid), F32),
            jax.ShapeDtypeStruct((1, hid), F32),
        ],
        [SMEM] * 2 + [VMEM] * 6,
        [VMEM] * 3,
        [acc],
        flops,
    )(*index, tiles, sent, got, back0, back2, backd)
    return output, weight_grad, bias_grad.reshape(hid), input_grad.T


def solution(mesh):
    return jax.shard_map(
        shards,
        mesh=mesh,
        in_specs=(
            P("dom", None),
            P(None, "feat"),
            P("feat"),
            P("dom", None, None),
            P("dom"),
            P("dom"),
            P("dom"),
            P("dom", "feat"),
        ),
        out_specs=(P("dom", "feat"), P(None, "feat"), P("feat"), P("dom", "feat")),
        check_vma=False,
    )
```

```python
import functools

import jax
import jax.numpy as jnp
from jax import lax
from jax.experimental import pallas as pl
from jax.experimental.pallas import tpu as pltpu
from jax.sharding import PartitionSpec as P

BLOCK = 128
REACH = 4
SUM_FLOPS = 10**9
SRC_UNIT = 2**16
F32 = jnp.float32
BF16 = jnp.bfloat16
VMEM = pl.BlockSpec(memory_space=pltpu.VMEM)
SMEM = pl.BlockSpec(memory_space=pltpu.SMEM)
HBM = pl.BlockSpec(memory_space=pltpu.HBM)


def call(kernel, out_shape, in_specs, out_specs, scratch=(), flops=0):
    return pl.pallas_call(
        kernel,
        out_shape=out_shape,
        in_specs=in_specs,
        out_specs=out_specs,
        scratch_shapes=list(scratch),
        compiler_params=pltpu.CompilerParams(vmem_limit_bytes=24 * 1024 * 1024),
        cost_estimate=pl.CostEstimate(flops=flops, bytes_accessed=2**20, transcendentals=0),
    )


def groups_at_once(groups):
    return next(m for m in (4, 3, 2, 1) if groups % m == 0)


def in_hbm(a):
    return pltpu.with_memory_space_constraint(a, pltpu.HBM)


def own_core():
    return lax.rem(lax.axis_index("dom"), 2)


def slot_loop(count, groups, body):
    m = groups_at_once(groups)
    pair = 2 if m % 2 == 0 else 1

    def chunk(i, carry):
        @pl.when(i * (m * REACH) < count)
        def _():
            for u in range(0, m, pair):
                body([i * m + u + v for v in range(pair)])

        return carry

    lax.fori_loop(0, groups // m, chunk, 0)


def side_by_side(lefts, tiles, contract):
    if len(tiles) == 1:
        left, right = lefts[0], tiles[0]
    else:
        left = jnp.concatenate(lefts, axis=1)
        none = jnp.zeros_like(tiles[0])
        right = jnp.concatenate(
            [jnp.concatenate([tiles[0], none], axis=1), jnp.concatenate([none, tiles[1]], axis=1)], axis=0
        )
    out = lax.dot_general(left, right, (((1,), (contract,)), ((), ())), preferred_element_type=F32)
    return [out[:, i * BLOCK : (i + 1) * BLOCK] for i in range(len(tiles))]


def source(entry):
    return lax.shift_right_logical(entry, 16)


def target(entry, o, blocks):
    return lax.bitwise_and(entry, SRC_UNIT - 1) - o * blocks


def push(xt, tiles, index, count, acc, js, o):
    blocks = xt.shape[0]
    ks = [j * REACH + o for j in js]
    outs = side_by_side([xt[source(index[k])] for k in ks], [tiles[j] for j in js], 1)
    for k, out in zip(ks, outs):
        acc[jnp.where(k < count, target(index[k], o, blocks), blocks)] += out


def pull(block, tiles, index, count, acc, js, o):
    blocks = acc.shape[0] - 1
    ks = [j * REACH + o for j in js]
    outs = side_by_side([block(target(index[k], o, blocks)) for k in ks], [tiles[j] for j in js], 0)
    for k, out in zip(ks, outs):
        acc[jnp.where(k < count, source(index[k]), blocks)] += out


def push_all(xt, tiles, index, count, acc, o):
    slot_loop(count, tiles.shape[0], lambda js: push(xt, tiles, index, count, acc, js, o))


def pull_all(block, tiles, index, count, acc, o):
    slot_loop(count, tiles.shape[0], lambda js: pull(block, tiles, index, count, acc, js, o))


def forward_swap_kernel(
    count, src_hbm, dst_hbm, x_hbm, tiles_hbm, tiles1, tiles2, xt, swap, index, src, dst, x, acc, sems
):
    blocks, width, _ = xt.shape
    o = 3 - 2 * own_core()
    loads = [
        pltpu.make_async_copy(a, b, sems.at[i])
        for i, (a, b) in enumerate(
            (
                (src_hbm, src),
                (dst_hbm, dst),
                (x_hbm, x),
                (tiles_hbm.at[:, o], tiles1),
                (tiles_hbm.at[:, 2], tiles2),
            )
        )
    ]
    for c in loads:
        c.start()
    acc[...] = jnp.zeros_like(acc)
    row = lax.broadcasted_iota(jnp.int32, (width, x.shape[1]), 0)
    column = lax.broadcasted_iota(jnp.int32, (width, x.shape[1]), 1)
    pick = (column == row + lax.axis_index("feat") * width).astype(BF16)
    for c in loads[:3]:
        c.wait()
    for b in range(blocks):
        xt[b] = lax.dot_general(
            pick, x[b * BLOCK : (b + 1) * BLOCK, :], (((1,), (1,)), ((), ())), preferred_element_type=F32
        ).astype(BF16)
    for k in range(src.shape[0]):
        index[k] = src[k] * SRC_UNIT + dst[k]
    loads[3].wait()
    push_all(xt, tiles1, index, count[0], acc, o)
    swap[...] = acc[:blocks].astype(BF16)
    loads[4].wait()


def forward_send_kernel(count, index, xt, tiles2, tiles_hbm, acc2, direct, tiles3, acc, sem):
    o = 1 + 2 * own_core()
    load = pltpu.make_async_copy(tiles_hbm.at[:, o], tiles3, sem)
    load.start()
    acc2[...] = jnp.zeros_like(acc2)
    acc[...] = jnp.zeros_like(acc)
    push_all(xt, tiles2, index, count[0], acc2, 2)
    load.wait()
    push_all(xt, tiles3, index, count[0], acc, o)
    direct[...] = acc[: direct.shape[0]].astype(BF16)


def forward_own_kernel(count, index, xt, tiles_hbm, acc, tiles0, sem):
    load = pltpu.make_async_copy(tiles_hbm.at[:, 0], tiles0, sem)
    load.start()
    acc[...] = jnp.zeros_like(acc)
    load.wait()
    push_all(xt, tiles0, index, count[0], acc, 0)


def sum_kernel(n, first, *refs):
    for out in refs[n:]:
        blocks = out.shape[0]
        total = None
        for r in refs[:n]:
            part = r[...] if r.shape[0] == blocks else r[first : first + blocks]
            total = part.astype(F32) if total is None else total + part.astype(F32)
        out[...] = total.astype(out.dtype)
        first += blocks


def join_kernel(parts, *refs):
    out = refs[-1]
    halves = [refs[i : i + parts] for i in range(0, len(refs) - 1, parts)]
    first = 0
    for half in halves:
        blocks = half[0].shape[0]
        total = half[0][...].astype(F32)
        for r in half[1:]:
            total = total + r[...].astype(F32)
        out[first : first + blocks] = total.astype(out.dtype)
        first += blocks


def middle_kernel(parts, first, bias_ref, w_ref, og_ref, *refs):
    h_refs, (act, ht, grads), g_refs = refs[:parts], refs[parts : parts + 3], refs[parts + 3 :]
    blocks, width, _ = h_refs[0].shape
    f_in = w_ref.shape[0]
    me = lax.axis_index("feat")
    for q in range(parts):
        row = pl.multiple_of(lax.rem(me + q, parts) * width, width)
        for b in range(blocks):
            ht[pl.ds(row, width), b * BLOCK : (b + 1) * BLOCK] = h_refs[q][b]
    ht[f_in:, :] = jnp.ones((ht.shape[0] - f_in, ht.shape[1]), BF16)
    for b in range(blocks):
        rows = slice(b * BLOCK, (b + 1) * BLOCK)
        pre = lax.dot_general(
            ht[:f_in, rows], w_ref[...], (((0,), (0,)), ((), ())), preferred_element_type=F32
        ) + bias_ref[...]
        s = jax.nn.sigmoid(pre)
        act[rows, :] = (pre * s).astype(BF16)
        og = og_ref[(first + b) * BLOCK : (first + b + 1) * BLOCK, :].astype(F32)
        grad = (og * s * (1.0 + pre * (1.0 - s))).astype(BF16)
        grads[rows, :] = grad
        for q in range(parts):
            row = pl.multiple_of(lax.rem(me + q, parts) * width, width)
            g_refs[q][b] = lax.dot_general(
                w_ref[pl.ds(row, width), :], grad, (((1,), (1,)), ((), ())), preferred_element_type=F32
            ).astype(g_refs[q].dtype)


def weight_grad_kernel(n, *refs):
    hts, grads, (mine, other) = refs[:n], refs[n : 2 * n], refs[2 * n :]
    full = sum(jnp.dot(h[...], g[...], preferred_element_type=F32) for h, g in zip(hts, grads))
    full = full.astype(BF16)
    rows = mine.shape[0]
    low, high = full[:rows], full[rows:]
    first = own_core() == 0
    mine[...] = jnp.where(first, low, high)
    other[...] = jnp.where(first, high, low)


def swap_payload_kernel(g, *refs):
    parts, out = refs[:-1], refs[-1]
    blocks, width, _ = g.shape
    for b in range(blocks):
        out[b * width : (b + 1) * width, :] = g[b]
    total = paired_sum([r[...] for r in parts]).astype(BF16)
    rows, hid = total.shape
    if hid < out.shape[1]:
        out[blocks * width :, :] = jnp.zeros((rows, out.shape[1]), BF16)
    out[blocks * width :, :hid] = total


def backward_own_kernel(count, index, tiles, g, *refs):
    acts, (acc, out, sems) = refs[:-3], refs[-3:]
    copies, first = [], 0
    for i, act in enumerate(acts):
        rows = act.shape[0]
        copies.append(pltpu.make_async_copy(act, out.at[pl.ds(first, rows)], sems.at[i]))
        copies[-1].start()
        first += rows
    acc[...] = jnp.zeros_like(acc)
    pull_all(lambda d: g[d], tiles, index, count[0], acc, 0)
    for c in copies:
        c.wait()


def backward_near_kernel(count, index, tiles2, tiles3, g2, g3, acc2, acc3):
    acc2[...] = jnp.zeros_like(acc2)
    acc3[...] = jnp.zeros_like(acc3)
    pull_all(lambda d: g2[d], tiles2, index, count[0], acc2, 2)
    pull_all(lambda d: g3[d], tiles3, index, count[0], acc3, 1 + 2 * own_core())


def backward_last_kernel(count, index, tiles, sent, got, acc0, acc2, accd, out, wg, bias, acc):
    blocks, width = acc.shape[0] - 1, acc.shape[1]
    f_in, hid = wg.shape
    acc[...] = jnp.zeros_like(acc)
    core = own_core()

    def block(d):
        return got[pl.ds(pl.multiple_of(d * width, width), width), :]

    pull_all(block, tiles, index, count[0], acc, 3 - 2 * core)
    for b in range(blocks):
        total = acc[b] + acc0[b] + acc2[b] + accd[b]
        out[:, b * BLOCK : (b + 1) * BLOCK] = total.astype(BF16)
    a, b = (r[blocks * width :, :hid].astype(F32) for r in (sent, got))
    low, high = jnp.where(core == 0, a, b), jnp.where(core == 0, b, a)
    rows = low.shape[0]
    wg[:rows, :] = low
    wg[rows:, :] = high[: f_in - rows]
    bias[...] = high[f_in - rows : f_in - rows + 1]


def paired_sum(parts):
    parts = [p.astype(F32) for p in parts]
    while len(parts) > 1:
        parts = [parts[i] + parts[i + 1] for i in range(0, len(parts), 2)]
    return parts[0]


def paired_sum_kernel(*refs):
    refs[-1][...] = paired_sum([r[...] for r in refs[:-1]]).astype(refs[-1].dtype)


def moved(block, axis, target):
    n = lax.axis_size(axis)
    return lax.ppermute(block, axis, [(i, target(i) % n) for i in range(n)])


def radices(n):
    out = []
    while n > 1:
        r = 4 if n % 4 == 0 else 2
        out.append(r)
        n //= r
    return out


def exchanged(part, axis, stride, r):
    return [part] + [moved(part, axis, lambda i, s=s: i ^ (s * stride)) for s in range(1, r)]


def shards(node_features, weight, bias, tile_values, tile_src, tile_dst, tile_counts, out_grad):
    nodes, f_in = node_features.shape
    hid = weight.shape[1]
    blocks = nodes // BLOCK
    parts = lax.axis_size("feat")
    width = f_in // parts
    capacity = tile_values.shape[0]
    groups = capacity // REACH
    piece = jax.ShapeDtypeStruct((blocks, width, BLOCK), BF16)
    totals = jax.ShapeDtypeStruct((blocks + 1, width, BLOCK), F32)
    acc = pltpu.VMEM(totals.shape, F32)
    tiles = tile_values.reshape(groups, REACH, BLOCK, BLOCK)
    plane = jax.ShapeDtypeStruct((groups, BLOCK, BLOCK), BF16)
    slots = jax.ShapeDtypeStruct((capacity,), jnp.int32)
    rows = jax.ShapeDtypeStruct((nodes, hid), BF16)
    gradient = jax.ShapeDtypeStruct(((f_in + 32) // 2, hid), BF16)
    flops = 2 * capacity * BLOCK * BLOCK * width // REACH

    def swapped(i):
        return i ^ 1

    tiles1, tiles2, xt, swap, index = call(
        forward_swap_kernel,
        [plane, plane, piece, piece, slots],
        [SMEM] + [HBM] * 4,
        [VMEM] * 4 + [SMEM],
        [
            pltpu.SMEM((capacity,), jnp.int32),
            pltpu.SMEM((capacity,), jnp.int32),
            pltpu.VMEM(node_features.shape, BF16),
            acc,
            pltpu.SemaphoreType.DMA((5,)),
        ],
        flops,
    )(tile_counts, *(in_hbm(a) for a in (tile_src, tile_dst, node_features, tiles)))
    index = (tile_counts, index)
    swap = moved(swap, "dom", swapped)
    acc2, direct, tiles3 = call(
        forward_send_kernel,
        [totals, piece, plane],
        [SMEM] * 2 + [VMEM] * 2 + [HBM],
        [VMEM] * 3,
        [acc, pltpu.SemaphoreType.DMA],
        2 * flops,
    )(*index, xt, tiles2, in_hbm(tiles))
    cut = 2 if blocks % 2 == 0 else 1
    starts = range(0, blocks, blocks // cut)
    half = jax.ShapeDtypeStruct((blocks // cut, width, BLOCK), BF16)
    half_wide = jax.ShapeDtypeStruct(half.shape, F32)
    half_rows = jax.ShapeDtypeStruct((nodes // cut, hid), BF16)
    half_columns = jax.ShapeDtypeStruct((f_in + 32, nodes // cut), BF16)
    chip = call(functools.partial(sum_kernel, 2, 0), [half] * cut, [VMEM] * 2, [VMEM] * cut)(acc2, swap)
    chip = [moved(c, "dom", lambda i: i + 2) for c in chip]
    direct = moved(direct, "dom", lambda i: i + 1 + 2 * (i % 2))
    acc0, tiles0 = call(
        forward_own_kernel,
        [totals, plane],
        [SMEM] * 2 + [VMEM, HBM],
        [VMEM] * 2,
        [pltpu.SemaphoreType.DMA],
        flops,
    )(*index, xt, in_hbm(tiles))
    h_lists = []
    for first, c in zip(starts, chip):
        (h,) = call(functools.partial(sum_kernel, 3, first), [half], [VMEM] * 3, [VMEM])(acc0, direct, c)
        h_lists.append([h] + [moved(h, "feat", lambda i, q=q: i - q) for q in range(1, parts)])
    acts, hts, grads, g_list = [], [], [], []
    for first, hs in zip(starts, h_lists):
        act, ht, grad, g_own, *g_others = call(
            functools.partial(middle_kernel, parts, first),
            [half_rows, half_columns, half_rows, half_wide] + [half] * (parts - 1),
            [VMEM] * (3 + parts),
            [VMEM] * (3 + parts),
            (),
            4 * nodes * f_in * hid // cut,
        )(bias.reshape(1, hid), weight, out_grad, *hs)
        acts.append(act)
        hts.append(ht)
        grads.append(grad)
        g_list += [g_own] + [moved(g, "feat", lambda i, q=q + 1: i + q) for q, g in enumerate(g_others)]
    wg, wg_other = call(
        functools.partial(weight_grad_kernel, cut),
        [gradient, gradient],
        [VMEM] * (2 * cut),
        [VMEM, VMEM],
        (),
        2 * nodes * f_in * hid,
    )(*hts, *grads)
    r, *more = radices(lax.axis_size("dom"))
    wgs = [wg] + [moved(wg_other if s % 2 else wg, "dom", lambda i, s=s: i ^ s) for s in range(1, r)]
    (g,) = call(functools.partial(join_kernel, parts), [piece], [VMEM] * len(g_list), [VMEM])(*g_list)
    g_chip = moved(g, "dom", lambda i: i - 2)
    g_direct = moved(g, "dom", lambda i: i - 3 + 2 * (i % 2))
    stride = r
    for r in more:
        (wg,) = call(paired_sum_kernel, [gradient], [VMEM] * len(wgs), [VMEM], (), SUM_FLOPS)(*wgs)
        wgs = exchanged(wg, "dom", stride, r)
        stride *= r
    back0, output = call(
        backward_own_kernel,
        [totals, rows],
        [SMEM] * 2 + [VMEM] * (2 + cut),
        [VMEM, HBM],
        [pltpu.SemaphoreType.DMA((cut,))],
        flops,
    )(*index, tiles0, g, *acts)
    back0, g_chip, g_direct, *wgs = lax.optimization_barrier((back0, g_chip, g_direct, *wgs))
    payload = jax.ShapeDtypeStruct((blocks * width + gradient.shape[0], BLOCK), BF16)
    (sent,) = call(swap_payload_kernel, [payload], [VMEM] * (1 + len(wgs)), [VMEM])(g_chip, *wgs)
    got = moved(sent, "dom", swapped)
    back2, backd = call(
        backward_near_kernel, [totals, totals], [SMEM] * 2 + [VMEM] * 4, [VMEM] * 2, (), 2 * flops
    )(*index, tiles2, tiles3, g_chip, g_direct)
    input_grad, weight_grad, bias_grad = call(
        backward_last_kernel,
        [
            jax.ShapeDtypeStruct((width, nodes), BF16),
            jax.ShapeDtypeStruct((f_in, hid), F32),
            jax.ShapeDtypeStruct((1, hid), F32),
        ],
        [SMEM] * 2 + [VMEM] * 6,
        [VMEM] * 3,
        [acc],
        flops,
    )(*index, tiles1, sent, got, back0, back2, backd)
    return output, weight_grad, bias_grad.reshape(hid), input_grad.T


def solution(mesh):
    return jax.shard_map(
        shards,
        mesh=mesh,
        in_specs=(
            P("dom", None),
            P(None, "feat"),
            P("feat"),
            P("dom", None, None),
            P("dom"),
            P("dom"),
            P("dom"),
            P("dom", "feat"),
        ),
        out_specs=(P("dom", "feat"), P(None, "feat"), P("feat"), P("dom", "feat")),
        check_vma=False,
    )
```

```python
import functools

import jax
import jax.numpy as jnp
from jax import lax
from jax.experimental import pallas as pl
from jax.experimental.pallas import tpu as pltpu
from jax.sharding import PartitionSpec as P

BLOCK = 128
REACH = 4
SUM_FLOPS = 10**9
SRC_UNIT = 2**16
F32 = jnp.float32
BF16 = jnp.bfloat16
VMEM = pl.BlockSpec(memory_space=pltpu.VMEM)
SMEM = pl.BlockSpec(memory_space=pltpu.SMEM)
HBM = pl.BlockSpec(memory_space=pltpu.HBM)


def call(kernel, out_shape, in_specs, out_specs, scratch=(), flops=0):
    return pl.pallas_call(
        kernel,
        out_shape=out_shape,
        in_specs=in_specs,
        out_specs=out_specs,
        scratch_shapes=list(scratch),
        compiler_params=pltpu.CompilerParams(vmem_limit_bytes=24 * 1024 * 1024),
        cost_estimate=pl.CostEstimate(flops=flops, bytes_accessed=2**20, transcendentals=0),
    )


def groups_at_once(groups):
    return next(m for m in (12, 8, 6, 4, 3, 2, 1) if groups % m == 0)


def in_hbm(a):
    return pltpu.with_memory_space_constraint(a, pltpu.HBM)


def own_core():
    return lax.rem(lax.axis_index("dom"), 2)


def slot_loop(count, groups, body):
    m = groups_at_once(groups)
    pair = 2 if m % 2 == 0 else 1

    def chunk(i, carry):
        @pl.when(i * (m * REACH) < count)
        def _():
            for u in range(0, m, pair):
                body([i * m + u + v for v in range(pair)])

        return carry

    lax.fori_loop(0, groups // m, chunk, 0)


def side_by_side(lefts, tiles, contract):
    if len(tiles) == 1:
        left, right = lefts[0], tiles[0]
    else:
        left = jnp.concatenate(lefts, axis=1)
        none = jnp.zeros_like(tiles[0])
        right = jnp.concatenate(
            [jnp.concatenate([tiles[0], none], axis=1), jnp.concatenate([none, tiles[1]], axis=1)], axis=0
        )
    out = lax.dot_general(left, right, (((1,), (contract,)), ((), ())), preferred_element_type=F32)
    return [out[:, i * BLOCK : (i + 1) * BLOCK] for i in range(len(tiles))]


def source(entry):
    return lax.shift_right_logical(entry, 16)


def target(entry, o, blocks):
    return lax.bitwise_and(entry, SRC_UNIT - 1) - o * blocks


def push(xt, tiles, index, count, acc, js, o):
    blocks = xt.shape[0]
    ks = [j * REACH + o for j in js]
    outs = side_by_side([xt[source(index[k])] for k in ks], [tiles[j] for j in js], 1)
    for k, out in zip(ks, outs):
        acc[jnp.where(k < count, target(index[k], o, blocks), blocks)] += out


def pull(block, tiles, index, count, acc, js, o):
    blocks = acc.shape[0] - 1
    ks = [j * REACH + o for j in js]
    outs = side_by_side([block(target(index[k], o, blocks)) for k in ks], [tiles[j] for j in js], 0)
    for k, out in zip(ks, outs):
        acc[jnp.where(k < count, source(index[k]), blocks)] += out


def push_all(xt, index, count, *planes):
    def body(js):
        for tiles, acc, o in planes:
            push(xt, tiles, index, count, acc, js, o)

    slot_loop(count, planes[0][0].shape[0], body)


def pull_all(index, count, *planes):
    def body(js):
        for block, tiles, acc, o in planes:
            pull(block, tiles, index, count, acc, js, o)

    slot_loop(count, planes[0][1].shape[0], body)


def forward_swap_kernel(
    count, src_hbm, dst_hbm, x_hbm, tiles_hbm, tiles1, tiles2, tiles3, xt, swap, index, src, dst, x, acc, sems
):
    blocks, width, _ = xt.shape
    o = 3 - 2 * own_core()
    loads = [
        pltpu.make_async_copy(a, b, sems.at[i])
        for i, (a, b) in enumerate(
            (
                (src_hbm, src),
                (dst_hbm, dst),
                (x_hbm, x),
                (tiles_hbm.at[:, o], tiles1),
                (tiles_hbm.at[:, 2], tiles2),
                (tiles_hbm.at[:, 4 - o], tiles3),
            )
        )
    ]
    for c in loads:
        c.start()
    acc[...] = jnp.zeros_like(acc)
    row = lax.broadcasted_iota(jnp.int32, (width, x.shape[1]), 0)
    column = lax.broadcasted_iota(jnp.int32, (width, x.shape[1]), 1)
    pick = (column == row + lax.axis_index("feat") * width).astype(BF16)
    for c in loads[:2]:
        c.wait()
    for k in range(src.shape[0]):
        index[k] = src[k] * SRC_UNIT + dst[k]
    loads[2].wait()
    for b in range(blocks):
        xt[b] = lax.dot_general(
            pick, x[b * BLOCK : (b + 1) * BLOCK, :], (((1,), (1,)), ((), ())), preferred_element_type=F32
        ).astype(BF16)
    loads[3].wait()
    push_all(xt, index, count[0], (tiles1, acc, o))
    swap[...] = acc[:blocks].astype(BF16)
    for c in loads[4:]:
        c.wait()


def forward_send_kernel(count, index, xt, tiles2, tiles3, acc2, direct, acc):
    acc2[...] = jnp.zeros_like(acc2)
    acc[...] = jnp.zeros_like(acc)
    push_all(xt, index, count[0], (tiles2, acc2, 2), (tiles3, acc, 1 + 2 * own_core()))
    direct[...] = acc[: direct.shape[0]].astype(BF16)


def forward_own_kernel(count, index, xt, tiles_hbm, acc, tiles0, sem):
    load = pltpu.make_async_copy(tiles_hbm.at[:, 0], tiles0, sem)
    load.start()
    acc[...] = jnp.zeros_like(acc)
    load.wait()
    push_all(xt, index, count[0], (tiles0, acc, 0))


def sum_kernel(n, first, *refs):
    for out in refs[n:]:
        blocks = out.shape[0]
        total = None
        for r in refs[:n]:
            part = r[...] if r.shape[0] == blocks else r[first : first + blocks]
            total = part.astype(F32) if total is None else total + part.astype(F32)
        out[...] = total.astype(out.dtype)
        first += blocks


def join_kernel(parts, *refs):
    out = refs[-1]
    halves = [refs[i : i + parts] for i in range(0, len(refs) - 1, parts)]
    first = 0
    for half in halves:
        blocks = half[0].shape[0]
        total = half[0][...].astype(F32)
        for r in half[1:]:
            total = total + r[...].astype(F32)
        out[first : first + blocks] = total.astype(out.dtype)
        first += blocks


def middle_kernel(parts, first, bias_ref, w_ref, og_ref, *refs):
    h_refs, (act, ht, grads), g_refs = refs[:parts], refs[parts : parts + 3], refs[parts + 3 :]
    blocks, width, _ = h_refs[0].shape
    f_in = w_ref.shape[0]
    me = lax.axis_index("feat")
    for q in range(parts):
        row = pl.multiple_of(lax.rem(me + q, parts) * width, width)
        for b in range(blocks):
            ht[pl.ds(row, width), b * BLOCK : (b + 1) * BLOCK] = h_refs[q][b]
    ht[f_in:, :] = jnp.ones((ht.shape[0] - f_in, ht.shape[1]), BF16)
    for b in range(blocks):
        rows = slice(b * BLOCK, (b + 1) * BLOCK)
        pre = lax.dot_general(
            ht[:f_in, rows], w_ref[...], (((0,), (0,)), ((), ())), preferred_element_type=F32
        ) + bias_ref[...]
        s = jax.nn.sigmoid(pre)
        act[rows, :] = (pre * s).astype(BF16)
        og = og_ref[(first + b) * BLOCK : (first + b + 1) * BLOCK, :].astype(F32)
        grad = (og * s * (1.0 + pre * (1.0 - s))).astype(BF16)
        grads[rows, :] = grad
        for q in range(parts):
            row = pl.multiple_of(lax.rem(me + q, parts) * width, width)
            g_refs[q][b] = lax.dot_general(
                w_ref[pl.ds(row, width), :], grad, (((1,), (1,)), ((), ())), preferred_element_type=F32
            ).astype(g_refs[q].dtype)


def weight_grad_kernel(n, *refs):
    hts, grads, (mine, other) = refs[:n], refs[n : 2 * n], refs[2 * n :]
    full = sum(jnp.dot(h[...], g[...], preferred_element_type=F32) for h, g in zip(hts, grads))
    full = full.astype(BF16)
    rows = mine.shape[0]
    low, high = full[:rows], full[rows:]
    first = own_core() == 0
    mine[...] = jnp.where(first, low, high)
    other[...] = jnp.where(first, high, low)


def swap_payload_kernel(g, *refs):
    parts, out = refs[:-1], refs[-1]
    blocks, width, _ = g.shape
    for b in range(blocks):
        out[b * width : (b + 1) * width, :] = g[b]
    total = paired_sum([r[...] for r in parts]).astype(BF16)
    rows, hid = total.shape
    if hid < out.shape[1]:
        out[blocks * width :, :] = jnp.zeros((rows, out.shape[1]), BF16)
    out[blocks * width :, :hid] = total


def backward_own_kernel(count, index, tiles, g, *refs):
    acts, (acc, out, sems) = refs[:-3], refs[-3:]
    copies, first = [], 0
    for i, act in enumerate(acts):
        rows = act.shape[0]
        copies.append(pltpu.make_async_copy(act, out.at[pl.ds(first, rows)], sems.at[i]))
        copies[-1].start()
        first += rows
    acc[...] = jnp.zeros_like(acc)
    pull_all(index, count[0], (lambda d: g[d], tiles, acc, 0))
    for c in copies:
        c.wait()


def backward_near_kernel(count, index, tiles2, tiles3, g2, g3, acc2, acc3):
    acc2[...] = jnp.zeros_like(acc2)
    acc3[...] = jnp.zeros_like(acc3)
    pull_all(
        index,
        count[0],
        (lambda d: g2[d], tiles2, acc2, 2),
        (lambda d: g3[d], tiles3, acc3, 1 + 2 * own_core()),
    )


def backward_last_kernel(count, index, tiles, sent, got, acc0, acc2, accd, out, wg, bias, acc):
    blocks, width = acc.shape[0] - 1, acc.shape[1]
    f_in, hid = wg.shape
    acc[...] = jnp.zeros_like(acc)
    core = own_core()

    def block(d):
        return got[pl.ds(pl.multiple_of(d * width, width), width), :]

    pull_all(index, count[0], (block, tiles, acc, 3 - 2 * core))
    for b in range(blocks):
        total = acc[b] + acc0[b] + acc2[b] + accd[b]
        out[:, b * BLOCK : (b + 1) * BLOCK] = total.astype(BF16)
    a, b = (r[blocks * width :, :hid].astype(F32) for r in (sent, got))
    low, high = jnp.where(core == 0, a, b), jnp.where(core == 0, b, a)
    rows = low.shape[0]
    wg[:rows, :] = low
    wg[rows:, :] = high[: f_in - rows]
    bias[...] = high[f_in - rows : f_in - rows + 1]


def paired_sum(parts):
    parts = [p.astype(F32) for p in parts]
    while len(parts) > 1:
        parts = [parts[i] + parts[i + 1] for i in range(0, len(parts), 2)]
    return parts[0]


def paired_sum_kernel(*refs):
    refs[-1][...] = paired_sum([r[...] for r in refs[:-1]]).astype(refs[-1].dtype)


def moved(block, axis, target):
    n = lax.axis_size(axis)
    return lax.ppermute(block, axis, [(i, target(i) % n) for i in range(n)])


def radices(n):
    out = []
    while n > 1:
        r = 4 if n % 4 == 0 else 2
        out.append(r)
        n //= r
    return out


def exchanged(part, axis, stride, r):
    return [part] + [moved(part, axis, lambda i, s=s: i ^ (s * stride)) for s in range(1, r)]


def shards(node_features, weight, bias, tile_values, tile_src, tile_dst, tile_counts, out_grad):
    nodes, f_in = node_features.shape
    hid = weight.shape[1]
    blocks = nodes // BLOCK
    parts = lax.axis_size("feat")
    width = f_in // parts
    capacity = tile_values.shape[0]
    groups = capacity // REACH
    piece = jax.ShapeDtypeStruct((blocks, width, BLOCK), BF16)
    totals = jax.ShapeDtypeStruct((blocks + 1, width, BLOCK), F32)
    acc = pltpu.VMEM(totals.shape, F32)
    tiles = tile_values.reshape(groups, REACH, BLOCK, BLOCK)
    plane = jax.ShapeDtypeStruct((groups, BLOCK, BLOCK), BF16)
    slots = jax.ShapeDtypeStruct((capacity,), jnp.int32)
    rows = jax.ShapeDtypeStruct((nodes, hid), BF16)
    gradient = jax.ShapeDtypeStruct(((f_in + 32) // 2, hid), BF16)
    flops = 2 * capacity * BLOCK * BLOCK * width // REACH

    def swapped(i):
        return i ^ 1

    tiles1, tiles2, tiles3, xt, swap, index = call(
        forward_swap_kernel,
        [plane, plane, plane, piece, piece, slots],
        [SMEM] + [HBM] * 4,
        [VMEM] * 5 + [SMEM],
        [
            pltpu.SMEM((capacity,), jnp.int32),
            pltpu.SMEM((capacity,), jnp.int32),
            pltpu.VMEM(node_features.shape, BF16),
            acc,
            pltpu.SemaphoreType.DMA((6,)),
        ],
        flops,
    )(tile_counts, *(in_hbm(a) for a in (tile_src, tile_dst, node_features, tiles)))
    index = (tile_counts, index)
    swap = moved(swap, "dom", swapped)
    acc2, direct = call(
        forward_send_kernel, [totals, piece], [SMEM] * 2 + [VMEM] * 3, [VMEM] * 2, [acc], 2 * flops
    )(*index, xt, tiles2, tiles3)
    cut = 2 if blocks % 2 == 0 else 1
    starts = range(0, blocks, blocks // cut)
    half = jax.ShapeDtypeStruct((blocks // cut, width, BLOCK), BF16)
    half_wide = jax.ShapeDtypeStruct(half.shape, F32)
    half_rows = jax.ShapeDtypeStruct((nodes // cut, hid), BF16)
    half_columns = jax.ShapeDtypeStruct((f_in + 32, nodes // cut), BF16)
    chip = call(functools.partial(sum_kernel, 2, 0), [half] * cut, [VMEM] * 2, [VMEM] * cut)(acc2, swap)
    chip = [moved(c, "dom", lambda i: i + 2) for c in chip]
    direct = moved(direct, "dom", lambda i: i + 1 + 2 * (i % 2))
    acc0, tiles0 = call(
        forward_own_kernel,
        [totals, plane],
        [SMEM] * 2 + [VMEM, HBM],
        [VMEM] * 2,
        [pltpu.SemaphoreType.DMA],
        flops,
    )(*index, xt, in_hbm(tiles))
    h_lists = []
    for first, c in zip(starts, chip):
        (h,) = call(functools.partial(sum_kernel, 3, first), [half], [VMEM] * 3, [VMEM])(acc0, direct, c)
        h_lists.append([h] + [moved(h, "feat", lambda i, q=q: i - q) for q in range(1, parts)])
    acts, hts, grads, g_list = [], [], [], []
    for first, hs in zip(starts, h_lists):
        act, ht, grad, g_own, *g_others = call(
            functools.partial(middle_kernel, parts, first),
            [half_rows, half_columns, half_rows, half_wide] + [half] * (parts - 1),
            [VMEM] * (3 + parts),
            [VMEM] * (3 + parts),
            (),
            4 * nodes * f_in * hid // cut,
        )(bias.reshape(1, hid), weight, out_grad, *hs)
        acts.append(act)
        hts.append(ht)
        grads.append(grad)
        g_list += [g_own] + [moved(g, "feat", lambda i, q=q + 1: i + q) for q, g in enumerate(g_others)]
    wg, wg_other = call(
        functools.partial(weight_grad_kernel, cut),
        [gradient, gradient],
        [VMEM] * (2 * cut),
        [VMEM, VMEM],
        (),
        2 * nodes * f_in * hid,
    )(*hts, *grads)
    r, *more = radices(lax.axis_size("dom"))
    wgs = [wg] + [moved(wg_other if s % 2 else wg, "dom", lambda i, s=s: i ^ s) for s in range(1, r)]
    (g,) = call(functools.partial(join_kernel, parts), [piece], [VMEM] * len(g_list), [VMEM])(*g_list)
    g_chip = moved(g, "dom", lambda i: i - 2)
    g_direct = moved(g, "dom", lambda i: i - 3 + 2 * (i % 2))
    stride = r
    for r in more:
        (wg,) = call(paired_sum_kernel, [gradient], [VMEM] * len(wgs), [VMEM], (), SUM_FLOPS)(*wgs)
        wgs = exchanged(wg, "dom", stride, r)
        stride *= r
    back0, output = call(
        backward_own_kernel,
        [totals, rows],
        [SMEM] * 2 + [VMEM] * (2 + cut),
        [VMEM, HBM],
        [pltpu.SemaphoreType.DMA((cut,))],
        flops,
    )(*index, tiles0, g, *acts)
    g_direct, g_chip, back0, *wgs = lax.optimization_barrier((g_direct, g_chip, back0, *wgs))
    payload = jax.ShapeDtypeStruct((blocks * width + gradient.shape[0], BLOCK), BF16)
    (sent,) = call(swap_payload_kernel, [payload], [VMEM] * (1 + len(wgs)), [VMEM])(g_chip, *wgs)
    got = moved(sent, "dom", swapped)
    back2, backd = call(
        backward_near_kernel, [totals, totals], [SMEM] * 2 + [VMEM] * 4, [VMEM] * 2, (), 2 * flops
    )(*index, tiles2, tiles3, g_chip, g_direct)
    input_grad, weight_grad, bias_grad = call(
        backward_last_kernel,
        [
            jax.ShapeDtypeStruct((width, nodes), BF16),
            jax.ShapeDtypeStruct((f_in, hid), F32),
            jax.ShapeDtypeStruct((1, hid), F32),
        ],
        [SMEM] * 2 + [VMEM] * 6,
        [VMEM] * 3,
        [acc],
        flops,
    )(*index, tiles1, sent, got, back0, back2, backd)
    return output, weight_grad, bias_grad.reshape(hid), input_grad.T


def solution(mesh):
    return jax.shard_map(
        shards,
        mesh=mesh,
        in_specs=(
            P("dom", None),
            P(None, "feat"),
            P("feat"),
            P("dom", None, None),
            P("dom"),
            P("dom"),
            P("dom"),
            P("dom", "feat"),
        ),
        out_specs=(P("dom", "feat"), P(None, "feat"), P("feat"), P("dom", "feat")),
        check_vma=False,
    )
```

```python
import functools

import jax
import jax.numpy as jnp
from jax import lax
from jax.experimental import pallas as pl
from jax.experimental.pallas import tpu as pltpu
from jax.sharding import PartitionSpec as P

BLOCK = 128
REACH = 4
SUM_FLOPS = 10**9
SRC_UNIT = 2**16
F32 = jnp.float32
BF16 = jnp.bfloat16
VMEM = pl.BlockSpec(memory_space=pltpu.VMEM)
SMEM = pl.BlockSpec(memory_space=pltpu.SMEM)
HBM = pl.BlockSpec(memory_space=pltpu.HBM)


def call(kernel, out_shape, in_specs, out_specs, scratch=(), flops=0):
    return pl.pallas_call(
        kernel,
        out_shape=out_shape,
        in_specs=in_specs,
        out_specs=out_specs,
        scratch_shapes=list(scratch),
        compiler_params=pltpu.CompilerParams(vmem_limit_bytes=24 * 1024 * 1024),
        cost_estimate=pl.CostEstimate(flops=flops, bytes_accessed=2**20, transcendentals=0),
    )


def groups_at_once(groups):
    return next(m for m in (12, 8, 6, 4, 3, 2, 1) if groups % m == 0)


def in_hbm(a):
    return pltpu.with_memory_space_constraint(a, pltpu.HBM)


def own_core():
    return lax.rem(lax.axis_index("dom"), 2)


def slot_loop(count, groups, body):
    m = groups_at_once(groups)

    def chunk(i, carry):
        @pl.when(i * (m * REACH) < count)
        def _():
            for u in range(m):
                body(i * m + u)

        return carry

    lax.fori_loop(0, groups // m, chunk, 0)


def source(entry):
    return lax.shift_right_logical(entry, 16)


def target(entry, o, blocks):
    return lax.bitwise_and(entry, SRC_UNIT - 1) - o * blocks


def push(xt, tiles, index, count, acc, j, o):
    blocks = xt.shape[0]
    k = j * REACH + o
    entry = index[k]
    out = lax.dot_general(xt[source(entry)], tiles[j], (((1,), (1,)), ((), ())), preferred_element_type=F32)
    acc[jnp.where(k < count, target(entry, o, blocks), blocks)] += out


def pull(block, tiles, index, count, acc, j, o):
    blocks = acc.shape[0] - 1
    k = j * REACH + o
    entry = index[k]
    out = jnp.dot(block(target(entry, o, blocks)), tiles[j], preferred_element_type=F32)
    acc[jnp.where(k < count, source(entry), blocks)] += out


def push_all(xt, index, count, *planes):
    def body(j):
        for tiles, acc, o in planes:
            push(xt, tiles, index, count, acc, j, o)

    slot_loop(count, planes[0][0].shape[0], body)


def pull_all(index, count, *planes):
    def body(j):
        for block, tiles, acc, o in planes:
            pull(block, tiles, index, count, acc, j, o)

    slot_loop(count, planes[0][1].shape[0], body)


def forward_swap_kernel(
    count, src_hbm, dst_hbm, x_hbm, tiles_hbm, tiles1, tiles2, tiles3, xt, swap, index, src, dst, x, acc, sems
):
    blocks, width, _ = xt.shape
    o = 3 - 2 * own_core()
    loads = [
        pltpu.make_async_copy(a, b, sems.at[i])
        for i, (a, b) in enumerate(
            (
                (src_hbm, src),
                (dst_hbm, dst),
                (x_hbm, x),
                (tiles_hbm.at[:, o], tiles1),
                (tiles_hbm.at[:, 2], tiles2),
                (tiles_hbm.at[:, 4 - o], tiles3),
            )
        )
    ]
    for c in loads:
        c.start()
    acc[...] = jnp.zeros_like(acc)
    row = lax.broadcasted_iota(jnp.int32, (width, x.shape[1]), 0)
    column = lax.broadcasted_iota(jnp.int32, (width, x.shape[1]), 1)
    pick = (column == row + lax.axis_index("feat") * width).astype(BF16)
    for c in loads[:2]:
        c.wait()
    for k in range(src.shape[0]):
        index[k] = src[k] * SRC_UNIT + dst[k]
    loads[2].wait()
    for b in range(blocks):
        xt[b] = lax.dot_general(
            pick, x[b * BLOCK : (b + 1) * BLOCK, :], (((1,), (1,)), ((), ())), preferred_element_type=F32
        ).astype(BF16)
    loads[3].wait()
    push_all(xt, index, count[0], (tiles1, acc, o))
    swap[...] = acc[:blocks].astype(BF16)
    for c in loads[4:]:
        c.wait()


def forward_send_kernel(count, index, xt, tiles2, tiles3, tiles_hbm, acc2, direct, tiles0, acc, sem):
    load = pltpu.make_async_copy(tiles_hbm.at[:, 0], tiles0, sem)
    load.start()
    acc2[...] = jnp.zeros_like(acc2)
    acc[...] = jnp.zeros_like(acc)
    push_all(xt, index, count[0], (tiles2, acc2, 2), (tiles3, acc, 1 + 2 * own_core()))
    direct[...] = acc[: direct.shape[0]].astype(BF16)
    load.wait()


def forward_own_kernel(count, index, xt, tiles0, acc):
    acc[...] = jnp.zeros_like(acc)
    push_all(xt, index, count[0], (tiles0, acc, 0))


def sum_kernel(n, first, *refs):
    for out in refs[n:]:
        blocks = out.shape[0]
        total = None
        for r in refs[:n]:
            part = r[...] if r.shape[0] == blocks else r[first : first + blocks]
            total = part.astype(F32) if total is None else total + part.astype(F32)
        out[...] = total.astype(out.dtype)
        first += blocks


def join_kernel(parts, *refs):
    out = refs[-1]
    halves = [refs[i : i + parts] for i in range(0, len(refs) - 1, parts)]
    first = 0
    for half in halves:
        blocks = half[0].shape[0]
        total = half[0][...].astype(F32)
        for r in half[1:]:
            total = total + r[...].astype(F32)
        out[first : first + blocks] = total.astype(out.dtype)
        first += blocks


def middle_kernel(parts, first, bias_ref, w_ref, og_ref, *refs):
    h_refs, (act, ht, grads), g_refs = refs[:parts], refs[parts : parts + 3], refs[parts + 3 :]
    blocks, width, _ = h_refs[0].shape
    f_in = w_ref.shape[0]
    me = lax.axis_index("feat")
    for q in range(parts):
        row = pl.multiple_of(lax.rem(me + q, parts) * width, width)
        for b in range(blocks):
            ht[pl.ds(row, width), b * BLOCK : (b + 1) * BLOCK] = h_refs[q][b]
    ht[f_in:, :] = jnp.ones((ht.shape[0] - f_in, ht.shape[1]), BF16)
    for b in range(blocks):
        rows = slice(b * BLOCK, (b + 1) * BLOCK)
        pre = lax.dot_general(
            ht[:f_in, rows], w_ref[...], (((0,), (0,)), ((), ())), preferred_element_type=F32
        ) + bias_ref[...]
        s = jax.nn.sigmoid(pre)
        act[rows, :] = (pre * s).astype(BF16)
        og = og_ref[(first + b) * BLOCK : (first + b + 1) * BLOCK, :].astype(F32)
        grad = (og * s * (1.0 + pre * (1.0 - s))).astype(BF16)
        grads[rows, :] = grad
        for q in range(parts):
            row = pl.multiple_of(lax.rem(me + q, parts) * width, width)
            g_refs[q][b] = lax.dot_general(
                w_ref[pl.ds(row, width), :], grad, (((1,), (1,)), ((), ())), preferred_element_type=F32
            ).astype(g_refs[q].dtype)


def weight_grad_kernel(n, *refs):
    hts, grads, (mine, other) = refs[:n], refs[n : 2 * n], refs[2 * n :]
    full = sum(jnp.dot(h[...], g[...], preferred_element_type=F32) for h, g in zip(hts, grads))
    full = full.astype(BF16)
    rows = mine.shape[0]
    low, high = full[:rows], full[rows:]
    first = own_core() == 0
    mine[...] = jnp.where(first, low, high)
    other[...] = jnp.where(first, high, low)


def swap_payload_kernel(g, *refs):
    parts, out = refs[:-1], refs[-1]
    blocks, width, _ = g.shape
    for b in range(blocks):
        out[b * width : (b + 1) * width, :] = g[b]
    total = paired_sum([r[...] for r in parts]).astype(BF16)
    rows, hid = total.shape
    if hid < out.shape[1]:
        out[blocks * width :, :] = jnp.zeros((rows, out.shape[1]), BF16)
    out[blocks * width :, :hid] = total


def backward_own_kernel(count, index, tiles, g, *refs):
    acts, (acc, out, sems) = refs[:-3], refs[-3:]
    copies, first = [], 0
    for i, act in enumerate(acts):
        rows = act.shape[0]
        copies.append(pltpu.make_async_copy(act, out.at[pl.ds(first, rows)], sems.at[i]))
        copies[-1].start()
        first += rows
    acc[...] = jnp.zeros_like(acc)
    pull_all(index, count[0], (lambda d: g[d], tiles, acc, 0))
    for c in copies:
        c.wait()


def backward_near_kernel(count, index, tiles2, tiles3, g2, g3, acc2, acc3):
    acc2[...] = jnp.zeros_like(acc2)
    acc3[...] = jnp.zeros_like(acc3)
    pull_all(
        index,
        count[0],
        (lambda d: g2[d], tiles2, acc2, 2),
        (lambda d: g3[d], tiles3, acc3, 1 + 2 * own_core()),
    )


def backward_last_kernel(count, index, tiles1, sent, got, acc0, acc2, acc3, out, wg, bias, acc1):
    blocks, width = acc1.shape[0] - 1, acc1.shape[1]
    f_in, hid = wg.shape
    acc1[...] = jnp.zeros_like(acc1)
    core = own_core()

    def block(d):
        return got[pl.ds(pl.multiple_of(d * width, width), width), :]

    pull_all(index, count[0], (block, tiles1, acc1, 3 - 2 * core))
    for b in range(blocks):
        total = (acc0[b] + acc2[b]) + (acc1[b] + acc3[b])
        out[:, b * BLOCK : (b + 1) * BLOCK] = total.astype(BF16)
    a, b = (r[blocks * width :, :hid].astype(F32) for r in (sent, got))
    low, high = jnp.where(core == 0, a, b), jnp.where(core == 0, b, a)
    rows = low.shape[0]
    wg[:rows, :] = low
    wg[rows:, :] = high[: f_in - rows]
    bias[...] = high[f_in - rows : f_in - rows + 1]


def paired_sum(parts):
    parts = [p.astype(F32) for p in parts]
    while len(parts) > 1:
        parts = [parts[i] + parts[i + 1] for i in range(0, len(parts), 2)]
    return parts[0]


def paired_sum_kernel(*refs):
    refs[-1][...] = paired_sum([r[...] for r in refs[:-1]]).astype(refs[-1].dtype)


def moved(block, axis, target):
    n = lax.axis_size(axis)
    return lax.ppermute(block, axis, [(i, target(i) % n) for i in range(n)])


def radices(n):
    out = []
    while n > 1:
        r = 4 if n % 4 == 0 else 2
        out.append(r)
        n //= r
    return out


def exchanged(part, axis, stride, r):
    return [part] + [moved(part, axis, lambda i, s=s: i ^ (s * stride)) for s in range(1, r)]


def shards(node_features, weight, bias, tile_values, tile_src, tile_dst, tile_counts, out_grad):
    nodes, f_in = node_features.shape
    hid = weight.shape[1]
    blocks = nodes // BLOCK
    parts = lax.axis_size("feat")
    width = f_in // parts
    capacity = tile_values.shape[0]
    groups = capacity // REACH
    piece = jax.ShapeDtypeStruct((blocks, width, BLOCK), BF16)
    totals = jax.ShapeDtypeStruct((blocks + 1, width, BLOCK), F32)
    acc = pltpu.VMEM(totals.shape, F32)
    tiles = tile_values.reshape(groups, REACH, BLOCK, BLOCK)
    plane = jax.ShapeDtypeStruct((groups, BLOCK, BLOCK), BF16)
    slots = jax.ShapeDtypeStruct((capacity,), jnp.int32)
    rows = jax.ShapeDtypeStruct((nodes, hid), BF16)
    gradient = jax.ShapeDtypeStruct(((f_in + 32) // 2, hid), BF16)
    flops = 2 * capacity * BLOCK * BLOCK * width // REACH

    def swapped(i):
        return i ^ 1

    tiles1, tiles2, tiles3, xt, swap, index = call(
        forward_swap_kernel,
        [plane, plane, plane, piece, piece, slots],
        [SMEM] + [HBM] * 4,
        [VMEM] * 5 + [SMEM],
        [
            pltpu.SMEM((capacity,), jnp.int32),
            pltpu.SMEM((capacity,), jnp.int32),
            pltpu.VMEM(node_features.shape, BF16),
            acc,
            pltpu.SemaphoreType.DMA((6,)),
        ],
        flops,
    )(tile_counts, *(in_hbm(a) for a in (tile_src, tile_dst, node_features, tiles)))
    index = (tile_counts, index)
    swap = moved(swap, "dom", swapped)
    acc2, direct, tiles0 = call(
        forward_send_kernel,
        [totals, piece, plane],
        [SMEM] * 2 + [VMEM] * 3 + [HBM],
        [VMEM] * 3,
        [acc, pltpu.SemaphoreType.DMA],
        2 * flops,
    )(*index, xt, tiles2, tiles3, in_hbm(tiles))
    cut = 2 if blocks % 2 == 0 else 1
    starts = range(0, blocks, blocks // cut)
    half = jax.ShapeDtypeStruct((blocks // cut, width, BLOCK), BF16)
    half_wide = jax.ShapeDtypeStruct(half.shape, F32)
    half_rows = jax.ShapeDtypeStruct((nodes // cut, hid), BF16)
    half_columns = jax.ShapeDtypeStruct((f_in + 32, nodes // cut), BF16)
    chip = call(functools.partial(sum_kernel, 2, 0), [half] * cut, [VMEM] * 2, [VMEM] * cut)(acc2, swap)
    chip = [moved(c, "dom", lambda i: i + 2) for c in chip]
    direct = moved(direct, "dom", lambda i: i + 1 + 2 * (i % 2))
    (acc0,) = call(forward_own_kernel, [totals], [SMEM] * 2 + [VMEM] * 2, [VMEM], (), flops)(*index, xt, tiles0)
    h_lists = []
    for first, c in zip(starts, chip):
        (h,) = call(functools.partial(sum_kernel, 3, first), [half], [VMEM] * 3, [VMEM])(acc0, direct, c)
        h_lists.append([h] + [moved(h, "feat", lambda i, q=q: i - q) for q in range(1, parts)])
    acts, hts, grads, g_list = [], [], [], []
    for first, hs in zip(starts, h_lists):
        act, ht, grad, g_own, *g_others = call(
            functools.partial(middle_kernel, parts, first),
            [half_rows, half_columns, half_rows, half_wide] + [half] * (parts - 1),
            [VMEM] * (3 + parts),
            [VMEM] * (3 + parts),
            (),
            4 * nodes * f_in * hid // cut,
        )(bias.reshape(1, hid), weight, out_grad, *hs)
        acts.append(act)
        hts.append(ht)
        grads.append(grad)
        g_list += [g_own] + [moved(g, "feat", lambda i, q=q + 1: i + q) for q, g in enumerate(g_others)]
    wg, wg_other = call(
        functools.partial(weight_grad_kernel, cut),
        [gradient, gradient],
        [VMEM] * (2 * cut),
        [VMEM, VMEM],
        (),
        2 * nodes * f_in * hid,
    )(*hts, *grads)
    r, *more = radices(lax.axis_size("dom"))
    wgs = [wg] + [moved(wg_other if s % 2 else wg, "dom", lambda i, s=s: i ^ s) for s in range(1, r)]
    (g,) = call(functools.partial(join_kernel, parts), [piece], [VMEM] * len(g_list), [VMEM])(*g_list)
    g_chip = moved(g, "dom", lambda i: i - 2)
    g_direct = moved(g, "dom", lambda i: i - 3 + 2 * (i % 2))
    stride = r
    for r in more:
        (wg,) = call(paired_sum_kernel, [gradient], [VMEM] * len(wgs), [VMEM], (), SUM_FLOPS)(*wgs)
        wgs = exchanged(wg, "dom", stride, r)
        stride *= r
    back0, output = call(
        backward_own_kernel,
        [totals, rows],
        [SMEM] * 2 + [VMEM] * (2 + cut),
        [VMEM, HBM],
        [pltpu.SemaphoreType.DMA((cut,))],
        flops,
    )(*index, tiles0, g, *acts)
    g_direct, g_chip, back0, *wgs = lax.optimization_barrier((g_direct, g_chip, back0, *wgs))
    payload = jax.ShapeDtypeStruct((blocks * width + gradient.shape[0], BLOCK), BF16)
    (sent,) = call(swap_payload_kernel, [payload], [VMEM] * (1 + len(wgs)), [VMEM])(g_chip, *wgs)
    got = moved(sent, "dom", swapped)
    back2, back3 = call(
        backward_near_kernel, [totals, totals], [SMEM] * 2 + [VMEM] * 4, [VMEM] * 2, (), 2 * flops
    )(*index, tiles2, tiles3, g_chip, g_direct)
    input_grad, weight_grad, bias_grad = call(
        backward_last_kernel,
        [
            jax.ShapeDtypeStruct((width, nodes), BF16),
            jax.ShapeDtypeStruct((f_in, hid), F32),
            jax.ShapeDtypeStruct((1, hid), F32),
        ],
        [SMEM] * 2 + [VMEM] * 6,
        [VMEM] * 3,
        [acc],
        flops,
    )(*index, tiles1, sent, got, back0, back2, back3)
    return output, weight_grad, bias_grad.reshape(hid), input_grad.T


def solution(mesh):
    return jax.shard_map(
        shards,
        mesh=mesh,
        in_specs=(
            P("dom", None),
            P(None, "feat"),
            P("feat"),
            P("dom", None, None),
            P("dom"),
            P("dom"),
            P("dom"),
            P("dom", "feat"),
        ),
        out_specs=(P("dom", "feat"), P(None, "feat"), P("feat"), P("dom", "feat")),
        check_vma=False,
    )
```

```python
import functools

import jax
import jax.numpy as jnp
from jax import lax
from jax.experimental import pallas as pl
from jax.experimental.pallas import tpu as pltpu
from jax.sharding import PartitionSpec as P

BLOCK = 128
REACH = 4
PLANE = 4
SUM_FLOPS = 10**9
SRC_UNIT = 2**16
PIECES = 4
F32 = jnp.float32
BF16 = jnp.bfloat16
VMEM = pl.BlockSpec(memory_space=pltpu.VMEM)
SMEM = pl.BlockSpec(memory_space=pltpu.SMEM)
HBM = pl.BlockSpec(memory_space=pltpu.HBM)


def call(kernel, out_shape, in_specs, out_specs, scratch=(), flops=0):
    return pl.pallas_call(
        kernel,
        out_shape=out_shape,
        in_specs=in_specs,
        out_specs=out_specs,
        scratch_shapes=list(scratch),
        compiler_params=pltpu.CompilerParams(vmem_limit_bytes=24 * 1024 * 1024),
        cost_estimate=pl.CostEstimate(flops=flops, bytes_accessed=2**20, transcendentals=0),
    )


def groups_at_once(groups):
    return next(m for m in (12, 8, 6, 4, 3, 2, 1) if groups % m == 0)


def in_hbm(a):
    return pltpu.with_memory_space_constraint(a, pltpu.HBM)


def own_core():
    return lax.rem(lax.axis_index("dom"), 2)


def slot_loop(count, groups, body):
    m = groups_at_once(groups)

    def chunk(i, carry):
        @pl.when(i * (m * REACH) < count)
        def _():
            for u in range(m):
                body(i * m + u)

        return carry

    lax.fori_loop(0, groups // m, chunk, 0)


def source(entry):
    return lax.shift_right_logical(entry, 16)


def target(entry, o, blocks):
    return lax.bitwise_and(entry, SRC_UNIT - 1) - o * blocks


def push(xt, tiles, index, count, acc, j, o):
    blocks = xt.shape[0]
    k = j * REACH + o
    entry = index[k]
    out = lax.dot_general(xt[source(entry)], tiles[j], (((1,), (1,)), ((), ())), preferred_element_type=F32)
    acc[jnp.where(k < count, target(entry, o, blocks), blocks)] += out


def pull(block, tiles, index, count, acc, j, o):
    blocks = acc.shape[0] - 1
    k = j * REACH + o
    entry = index[k]
    out = jnp.dot(block(target(entry, o, blocks)), tiles[j], preferred_element_type=F32)
    acc[jnp.where(k < count, source(entry), blocks)] += out


class Copy:
    def __init__(self, source, destination, sems, first, pieces):
        rows = destination.shape[0] // pieces
        cuts = [pl.ds(i * rows, rows) for i in range(pieces)]
        self.pieces = [
            pltpu.make_async_copy(source.at[cut], destination.at[cut], sems.at[first + i])
            for i, cut in enumerate(cuts)
        ]

    def start(self):
        for p in self.pieces:
            p.start()

    def wait(self):
        for p in self.pieces:
            p.wait()


def push_all(xt, index, count, *planes):
    def body(j):
        for tiles, acc, o in planes:
            push(xt, tiles, index, count, acc, j, o)

    slot_loop(count, planes[0][0].shape[0], body)


def pull_all(index, count, *planes):
    def body(j):
        for block, tiles, acc, o in planes:
            pull(block, tiles, index, count, acc, j, o)

    slot_loop(count, planes[0][1].shape[0], body)


def forward_swap_kernel(
    count, src_hbm, dst_hbm, x_hbm, tiles_hbm, tiles1, tiles2, tiles3, xt, swap, index, src, dst, x, acc, sems
):
    blocks, width, _ = xt.shape
    o = 3 - 2 * own_core()
    loads = [
        Copy(a, b, sems, i * PIECES, PIECES if i > 1 else 1)
        for i, (a, b) in enumerate(
            (
                (src_hbm, src),
                (dst_hbm, dst),
                (x_hbm, x),
                (tiles_hbm.at[:, o], tiles1),
                (tiles_hbm.at[:, 2], tiles2),
                (tiles_hbm.at[:, 4 - o], tiles3),
            )
        )
    ]
    for c in loads:
        c.start()
    acc[...] = jnp.zeros_like(acc)
    row = lax.broadcasted_iota(jnp.int32, (width, x.shape[1]), 0)
    column = lax.broadcasted_iota(jnp.int32, (width, x.shape[1]), 1)
    pick = (column == row + lax.axis_index("feat") * width).astype(BF16)
    for c in loads[:2]:
        c.wait()
    for k in range(src.shape[0]):
        index[k] = src[k] * SRC_UNIT + dst[k]
    loads[2].wait()
    for b in range(blocks):
        xt[b] = lax.dot_general(
            pick, x[b * BLOCK : (b + 1) * BLOCK, :], (((1,), (1,)), ((), ())), preferred_element_type=F32
        ).astype(BF16)
    loads[3].wait()
    push_all(xt, index, count[0], (tiles1, acc, o))
    swap[...] = acc[:blocks].astype(BF16)
    for c in loads[4:]:
        c.wait()


def forward_send_kernel(count, index, xt, tiles2, tiles3, tiles_hbm, acc2, direct, tiles0, acc, sems):
    load = Copy(tiles_hbm.at[:, 0], tiles0, sems, 0, PIECES)
    load.start()
    acc2[...] = jnp.zeros_like(acc2)
    acc[...] = jnp.zeros_like(acc)
    push_all(xt, index, count[0], (tiles2, acc2, 2), (tiles3, acc, 1 + 2 * own_core()))
    direct[...] = acc[: direct.shape[0]].astype(BF16)
    load.wait()


def forward_own_kernel(count, index, xt, tiles0, acc):
    acc[...] = jnp.zeros_like(acc)
    push_all(xt, index, count[0], (tiles0, acc, 0))


def sum_kernel(n, first, *refs):
    for out in refs[n:]:
        blocks = out.shape[0]
        total = None
        for r in refs[:n]:
            part = r[...] if r.shape[0] == blocks else r[first : first + blocks]
            total = part.astype(F32) if total is None else total + part.astype(F32)
        out[...] = total.astype(out.dtype)
        first += blocks


def join_kernel(parts, *refs):
    out = refs[-1]
    halves = [refs[i : i + parts] for i in range(0, len(refs) - 1, parts)]
    first = 0
    for half in halves:
        blocks = half[0].shape[0]
        total = half[0][...].astype(F32)
        for r in half[1:]:
            total = total + r[...].astype(F32)
        out[first : first + blocks] = total.astype(out.dtype)
        first += blocks


def middle_kernel(parts, first, bias_ref, w_ref, og_ref, *refs):
    h_refs, (act, ht, grads), g_refs = refs[:parts], refs[parts : parts + 3], refs[parts + 3 :]
    blocks, width, _ = h_refs[0].shape
    f_in = w_ref.shape[0]
    me = lax.axis_index("feat")
    for q in range(parts):
        row = pl.multiple_of(lax.rem(me + q, parts) * width, width)
        for b in range(blocks):
            ht[pl.ds(row, width), b * BLOCK : (b + 1) * BLOCK] = h_refs[q][b]
    ht[f_in:, :] = jnp.ones((ht.shape[0] - f_in, ht.shape[1]), BF16)
    for b in range(blocks):
        rows = slice(b * BLOCK, (b + 1) * BLOCK)
        pre = lax.dot_general(
            ht[:f_in, rows], w_ref[...], (((0,), (0,)), ((), ())), preferred_element_type=F32
        ) + bias_ref[...]
        s = jax.nn.sigmoid(pre)
        act[rows, :] = (pre * s).astype(BF16)
        og = og_ref[(first + b) * BLOCK : (first + b + 1) * BLOCK, :].astype(F32)
        grad = (og * s * (1.0 + pre * (1.0 - s))).astype(BF16)
        grads[rows, :] = grad
        for q in range(parts):
            row = pl.multiple_of(lax.rem(me + q, parts) * width, width)
            g_refs[q][b] = lax.dot_general(
                w_ref[pl.ds(row, width), :], grad, (((1,), (1,)), ((), ())), preferred_element_type=F32
            ).astype(g_refs[q].dtype)


def weight_grad_kernel(n, *refs):
    hts, grads, out = refs[:n], refs[n : 2 * n], refs[2 * n]
    full = sum(jnp.dot(h[...], g[...], preferred_element_type=F32) for h, g in zip(hts, grads))
    out[...] = full.astype(BF16)


def halves_kernel(*refs):
    parts, (mine, other) = refs[:-2], refs[-2:]
    full = paired_sum([r[...] for r in parts]).astype(BF16)
    rows = mine.shape[0]
    low, high = full[:rows], full[rows:]
    first = own_core() == 0
    mine[...] = jnp.where(first, low, high)
    other[...] = jnp.where(first, high, low)


def swap_payload_kernel(g, *refs):
    parts, out = refs[:-1], refs[-1]
    blocks, width, _ = g.shape
    for b in range(blocks):
        out[b * width : (b + 1) * width, :] = g[b]
    total = paired_sum([r[...] for r in parts]).astype(BF16)
    rows, hid = total.shape
    if hid < out.shape[1]:
        out[blocks * width :, :] = jnp.zeros((rows, out.shape[1]), BF16)
    out[blocks * width :, :hid] = total


def backward_own_kernel(count, index, tiles, g, *refs):
    acts, (acc, out, sems) = refs[:-3], refs[-3:]
    copies, first = [], 0
    for i, act in enumerate(acts):
        rows = act.shape[0]
        copies.append(pltpu.make_async_copy(act, out.at[pl.ds(first, rows)], sems.at[i]))
        copies[-1].start()
        first += rows
    acc[...] = jnp.zeros_like(acc)
    pull_all(index, count[0], (lambda d: g[d], tiles, acc, 0))
    for c in copies:
        c.wait()


def backward_near_kernel(count, index, tiles2, tiles3, g2, g3, acc2, acc3):
    acc2[...] = jnp.zeros_like(acc2)
    acc3[...] = jnp.zeros_like(acc3)
    pull_all(
        index,
        count[0],
        (lambda d: g2[d], tiles2, acc2, 2),
        (lambda d: g3[d], tiles3, acc3, 1 + 2 * own_core()),
    )


def backward_last_kernel(count, index, tiles1, sent, got, acc0, acc2, acc3, out, wg, bias, acc1):
    blocks, width = acc1.shape[0] - 1, acc1.shape[1]
    f_in, hid = wg.shape
    acc1[...] = jnp.zeros_like(acc1)
    core = own_core()

    def block(d):
        return got[pl.ds(pl.multiple_of(d * width, width), width), :]

    pull_all(index, count[0], (block, tiles1, acc1, 3 - 2 * core))
    for b in range(blocks):
        total = (acc0[b] + acc2[b]) + (acc1[b] + acc3[b])
        out[:, b * BLOCK : (b + 1) * BLOCK] = total.astype(BF16)
    a, b = (r[blocks * width :, :hid].astype(F32) for r in (sent, got))
    low, high = jnp.where(core == 0, a, b), jnp.where(core == 0, b, a)
    rows = low.shape[0]
    wg[:rows, :] = low
    wg[rows:, :] = high[: f_in - rows]
    bias[...] = high[f_in - rows : f_in - rows + 1]


def paired_sum(parts):
    parts = [p.astype(F32) for p in parts]
    while len(parts) > 1:
        parts = [parts[i] + parts[i + 1] for i in range(0, len(parts), 2)]
    return parts[0]


def paired_sum_kernel(*refs):
    refs[-1][...] = paired_sum([r[...] for r in refs[:-1]]).astype(refs[-1].dtype)


def moved(block, axis, target):
    n = lax.axis_size(axis)
    return lax.ppermute(block, axis, [(i, target(i) % n) for i in range(n)])


def radices(n):
    out = []
    while n > 1:
        r = 4 if n % 4 == 0 else 2
        out.append(r)
        n //= r
    return out


def exchanged(part, axis, stride, r):
    return [part] + [moved(part, axis, lambda i, s=s: i ^ (s * stride)) for s in range(1, r)]


def shards(node_features, weight, bias, tile_values, tile_src, tile_dst, tile_counts, out_grad):
    nodes, f_in = node_features.shape
    hid = weight.shape[1]
    blocks = nodes // BLOCK
    parts = lax.axis_size("feat")
    width = f_in // parts
    capacity = tile_values.shape[0]
    groups = capacity // REACH
    piece = jax.ShapeDtypeStruct((blocks, width, BLOCK), BF16)
    totals = jax.ShapeDtypeStruct((blocks + 1, width, BLOCK), F32)
    acc = pltpu.VMEM(totals.shape, F32)
    tiles = tile_values.reshape(groups, REACH, BLOCK, BLOCK)
    plane = jax.ShapeDtypeStruct((groups, BLOCK, BLOCK), BF16)
    slots = jax.ShapeDtypeStruct((capacity,), jnp.int32)
    rows = jax.ShapeDtypeStruct((nodes, hid), BF16)
    gradient = jax.ShapeDtypeStruct((f_in + 32, hid), BF16)
    half_gradient = jax.ShapeDtypeStruct(((f_in + 32) // 2, hid), BF16)
    flops = 2 * capacity * BLOCK * BLOCK * width // REACH

    def swapped(i):
        return i ^ 1

    tiles1, tiles2, tiles3, xt, swap, index = call(
        forward_swap_kernel,
        [plane, plane, plane, piece, piece, slots],
        [SMEM] + [HBM] * 4,
        [VMEM] * 5 + [SMEM],
        [
            pltpu.SMEM((capacity,), jnp.int32),
            pltpu.SMEM((capacity,), jnp.int32),
            pltpu.VMEM(node_features.shape, BF16),
            acc,
            pltpu.SemaphoreType.DMA((6 * PIECES,)),
        ],
        flops,
    )(tile_counts, *(in_hbm(a) for a in (tile_src, tile_dst, node_features, tiles)))
    index = (tile_counts, index)
    swap = moved(swap, "dom", swapped)
    acc2, direct, tiles0 = call(
        forward_send_kernel,
        [totals, piece, plane],
        [SMEM] * 2 + [VMEM] * 3 + [HBM],
        [VMEM] * 3,
        [acc, pltpu.SemaphoreType.DMA((PIECES,))],
        2 * flops,
    )(*index, xt, tiles2, tiles3, in_hbm(tiles))
    cut = 2 if blocks % 2 == 0 else 1
    starts = range(0, blocks, blocks // cut)
    half = jax.ShapeDtypeStruct((blocks // cut, width, BLOCK), BF16)
    half_wide = jax.ShapeDtypeStruct(half.shape, F32)
    half_rows = jax.ShapeDtypeStruct((nodes // cut, hid), BF16)
    half_columns = jax.ShapeDtypeStruct((f_in + 32, nodes // cut), BF16)
    chip = call(functools.partial(sum_kernel, 2, 0), [half] * cut, [VMEM] * 2, [VMEM] * cut)(acc2, swap)
    chip = [moved(c, "dom", lambda i: i + 2) for c in chip]
    direct = moved(direct, "dom", lambda i: i + 1 + 2 * (i % 2))
    (acc0,) = call(forward_own_kernel, [totals], [SMEM] * 2 + [VMEM] * 2, [VMEM], (), flops)(*index, xt, tiles0)
    h_lists = []
    for first, c in zip(starts, chip):
        (h,) = call(functools.partial(sum_kernel, 3, first), [half], [VMEM] * 3, [VMEM])(acc0, direct, c)
        h_lists.append([h] + [moved(h, "feat", lambda i, q=q: i - q) for q in range(1, parts)])
    acts, hts, grads, g_list = [], [], [], []
    for first, hs in zip(starts, h_lists):
        act, ht, grad, g_own, *g_others = call(
            functools.partial(middle_kernel, parts, first),
            [half_rows, half_columns, half_rows, half_wide] + [half] * (parts - 1),
            [VMEM] * (3 + parts),
            [VMEM] * (3 + parts),
            (),
            4 * nodes * f_in * hid // cut,
        )(bias.reshape(1, hid), weight, out_grad, *hs)
        acts.append(act)
        hts.append(ht)
        grads.append(grad)
        g_list += [g_own] + [moved(g, "feat", lambda i, q=q + 1: i + q) for q, g in enumerate(g_others)]
    (wg,) = call(
        functools.partial(weight_grad_kernel, cut),
        [gradient],
        [VMEM] * (2 * cut),
        [VMEM],
        (),
        2 * nodes * f_in * hid,
    )(*hts, *grads)
    far, stride = lax.axis_size("dom") // PLANE, PLANE
    for r in radices(far):
        if stride > PLANE:
            (wg,) = call(paired_sum_kernel, [gradient], [VMEM] * len(wgs), [VMEM], (), SUM_FLOPS)(*wgs)
        wgs = exchanged(wg, "dom", stride, r)
        stride *= r
    (g,) = call(functools.partial(join_kernel, parts), [piece], [VMEM] * len(g_list), [VMEM])(*g_list)
    g_chip = moved(g, "dom", lambda i: i - 2)
    g_direct = moved(g, "dom", lambda i: i - 3 + 2 * (i % 2))
    mine, other = call(
        halves_kernel, [half_gradient] * 2, [VMEM] * len(wgs), [VMEM] * 2, (), SUM_FLOPS
    )(*wgs)
    wgs = [mine] + [moved(other if s % 2 else mine, "dom", lambda i, s=s: i ^ s) for s in range(1, PLANE)]
    back0, output = call(
        backward_own_kernel,
        [totals, rows],
        [SMEM] * 2 + [VMEM] * (2 + cut),
        [VMEM, HBM],
        [pltpu.SemaphoreType.DMA((cut,))],
        flops,
    )(*index, tiles0, g, *acts)
    g_direct, g_chip, back0, *wgs = lax.optimization_barrier((g_direct, g_chip, back0, *wgs))
    payload = jax.ShapeDtypeStruct((blocks * width + half_gradient.shape[0], BLOCK), BF16)
    (sent,) = call(swap_payload_kernel, [payload], [VMEM] * (1 + len(wgs)), [VMEM])(g_chip, *wgs)
    got = moved(sent, "dom", swapped)
    back2, back3 = call(
        backward_near_kernel, [totals, totals], [SMEM] * 2 + [VMEM] * 4, [VMEM] * 2, (), 2 * flops
    )(*index, tiles2, tiles3, g_chip, g_direct)
    input_grad, weight_grad, bias_grad = call(
        backward_last_kernel,
        [
            jax.ShapeDtypeStruct((width, nodes), BF16),
            jax.ShapeDtypeStruct((f_in, hid), F32),
            jax.ShapeDtypeStruct((1, hid), F32),
        ],
        [SMEM] * 2 + [VMEM] * 6,
        [VMEM] * 3,
        [acc],
        flops,
    )(*index, tiles1, sent, got, back0, back2, back3)
    return output, weight_grad, bias_grad.reshape(hid), input_grad.T


def solution(mesh):
    return jax.shard_map(
        shards,
        mesh=mesh,
        in_specs=(
            P("dom", None),
            P(None, "feat"),
            P("feat"),
            P("dom", None, None),
            P("dom"),
            P("dom"),
            P("dom"),
            P("dom", "feat"),
        ),
        out_specs=(P("dom", "feat"), P(None, "feat"), P("feat"), P("dom", "feat")),
        check_vma=False,
    )
```

```python
import functools

import jax
import jax.numpy as jnp
from jax import lax
from jax.experimental import pallas as pl
from jax.experimental.pallas import tpu as pltpu
from jax.sharding import PartitionSpec as P

BLOCK = 128
REACH = 4
SUM_FLOPS = 10**9
SRC_UNIT = 2**16
F32 = jnp.float32
BF16 = jnp.bfloat16
VMEM = pl.BlockSpec(memory_space=pltpu.VMEM)
SMEM = pl.BlockSpec(memory_space=pltpu.SMEM)
HBM = pl.BlockSpec(memory_space=pltpu.HBM)


def call(kernel, out_shape, in_specs, out_specs, scratch=(), flops=0):
    return pl.pallas_call(
        kernel,
        out_shape=out_shape,
        in_specs=in_specs,
        out_specs=out_specs,
        scratch_shapes=list(scratch),
        compiler_params=pltpu.CompilerParams(vmem_limit_bytes=24 * 1024 * 1024),
        cost_estimate=pl.CostEstimate(flops=flops, bytes_accessed=2**20, transcendentals=0),
    )


def groups_at_once(groups):
    return next(m for m in (12, 8, 6, 4, 3, 2, 1) if groups % m == 0)


def in_hbm(a):
    return pltpu.with_memory_space_constraint(a, pltpu.HBM)


def own_core():
    return lax.rem(lax.axis_index("dom"), 2)


def slot_loop(count, groups, body):
    m = groups_at_once(groups)

    def chunk(i, carry):
        @pl.when(i * (m * REACH) < count)
        def _():
            for u in range(m):
                body(i * m + u)

        return carry

    lax.fori_loop(0, groups // m, chunk, 0)


def source(entry):
    return lax.shift_right_logical(entry, 16)


def target(entry, o, blocks):
    return lax.bitwise_and(entry, SRC_UNIT - 1) - o * blocks


def push(xt, tiles, index, count, acc, j, o):
    blocks = xt.shape[0]
    k = j * REACH + o
    entry = index[k]
    out = lax.dot_general(xt[source(entry)], tiles[j], (((1,), (1,)), ((), ())), preferred_element_type=F32)
    acc[jnp.where(k < count, target(entry, o, blocks), blocks)] += out


def pull(block, tiles, index, count, acc, j, o):
    blocks = acc.shape[0] - 1
    k = j * REACH + o
    entry = index[k]
    out = jnp.dot(block(target(entry, o, blocks)), tiles[j], preferred_element_type=F32)
    acc[jnp.where(k < count, source(entry), blocks)] += out


def push_all(xt, index, count, *planes):
    def body(j):
        for tiles, acc, o in planes:
            push(xt, tiles, index, count, acc, j, o)

    slot_loop(count, planes[0][0].shape[0], body)


def pull_all(index, count, *planes):
    def body(j):
        for block, tiles, acc, o in planes:
            pull(block, tiles, index, count, acc, j, o)

    slot_loop(count, planes[0][1].shape[0], body)


def forward_swap_kernel(
    count, src_hbm, dst_hbm, x_hbm, tiles_hbm, tiles1, tiles2, tiles3, xt, swap, index, src, dst, x, acc, sems
):
    blocks, width, _ = xt.shape
    o = 3 - 2 * own_core()
    loads = [
        pltpu.make_async_copy(a, b, sems.at[i])
        for i, (a, b) in enumerate(
            (
                (src_hbm, src),
                (dst_hbm, dst),
                (x_hbm, x),
                (tiles_hbm.at[:, o], tiles1),
                (tiles_hbm.at[:, 2], tiles2),
                (tiles_hbm.at[:, 4 - o], tiles3),
            )
        )
    ]
    for c in loads:
        c.start()
    acc[...] = jnp.zeros_like(acc)
    row = lax.broadcasted_iota(jnp.int32, (width, x.shape[1]), 0)
    column = lax.broadcasted_iota(jnp.int32, (width, x.shape[1]), 1)
    pick = (column == row + lax.axis_index("feat") * width).astype(BF16)
    for c in loads[:2]:
        c.wait()
    for k in range(src.shape[0]):
        index[k] = src[k] * SRC_UNIT + dst[k]
    loads[2].wait()
    for b in range(blocks):
        xt[b] = lax.dot_general(
            pick, x[b * BLOCK : (b + 1) * BLOCK, :], (((1,), (1,)), ((), ())), preferred_element_type=F32
        ).astype(BF16)
    loads[3].wait()
    push_all(xt, index, count[0], (tiles1, acc, o))
    swap[...] = acc[:blocks].astype(BF16)
    for c in loads[4:]:
        c.wait()


def forward_send_kernel(count, index, xt, tiles2, tiles3, acc2, *refs):
    direct, acc = refs[:-1], refs[-1]
    acc2[...] = jnp.zeros_like(acc2)
    acc[...] = jnp.zeros_like(acc)
    push_all(xt, index, count[0], (tiles2, acc2, 2), (tiles3, acc, 1 + 2 * own_core()))
    first = 0
    for d in direct:
        d[...] = acc[first : first + d.shape[0]].astype(BF16)
        first += d.shape[0]


def forward_own_kernel(count, index, xt, tiles_hbm, acc, tiles0, sem):
    load = pltpu.make_async_copy(tiles_hbm.at[:, 0], tiles0, sem)
    load.start()
    acc[...] = jnp.zeros_like(acc)
    load.wait()
    push_all(xt, index, count[0], (tiles0, acc, 0))


def sum_kernel(n, first, *refs):
    for out in refs[n:]:
        blocks = out.shape[0]
        total = None
        for r in refs[:n]:
            part = r[...] if r.shape[0] == blocks else r[first : first + blocks]
            total = part.astype(F32) if total is None else total + part.astype(F32)
        out[...] = total.astype(out.dtype)
        first += blocks


def join_kernel(parts, *refs):
    out = refs[-1]
    halves = [refs[i : i + parts] for i in range(0, len(refs) - 1, parts)]
    first = 0
    for half in halves:
        blocks = half[0].shape[0]
        total = half[0][...].astype(F32)
        for r in half[1:]:
            total = total + r[...].astype(F32)
        out[first : first + blocks] = total.astype(out.dtype)
        first += blocks


def middle_kernel(parts, first, bias_ref, w_ref, og_ref, *refs):
    h_refs, (act, ht, grads), g_refs = refs[:parts], refs[parts : parts + 3], refs[parts + 3 :]
    blocks, width, _ = h_refs[0].shape
    f_in = w_ref.shape[0]
    me = lax.axis_index("feat")
    for q in range(parts):
        row = pl.multiple_of(lax.rem(me + q, parts) * width, width)
        for b in range(blocks):
            ht[pl.ds(row, width), b * BLOCK : (b + 1) * BLOCK] = h_refs[q][b]
    ht[f_in:, :] = jnp.ones((ht.shape[0] - f_in, ht.shape[1]), BF16)
    for b in range(blocks):
        rows = slice(b * BLOCK, (b + 1) * BLOCK)
        pre = lax.dot_general(
            ht[:f_in, rows], w_ref[...], (((0,), (0,)), ((), ())), preferred_element_type=F32
        ) + bias_ref[...]
        s = jax.nn.sigmoid(pre)
        act[rows, :] = (pre * s).astype(BF16)
        og = og_ref[(first + b) * BLOCK : (first + b + 1) * BLOCK, :].astype(F32)
        grad = (og * s * (1.0 + pre * (1.0 - s))).astype(BF16)
        grads[rows, :] = grad
        for q in range(parts):
            row = pl.multiple_of(lax.rem(me + q, parts) * width, width)
            g_refs[q][b] = lax.dot_general(
                w_ref[pl.ds(row, width), :], grad, (((1,), (1,)), ((), ())), preferred_element_type=F32
            ).astype(g_refs[q].dtype)


def weight_grad_kernel(n, *refs):
    hts, grads, (mine, other) = refs[:n], refs[n : 2 * n], refs[2 * n :]
    full = sum(jnp.dot(h[...], g[...], preferred_element_type=F32) for h, g in zip(hts, grads))
    full = full.astype(BF16)
    rows = mine.shape[0]
    low, high = full[:rows], full[rows:]
    first = own_core() == 0
    mine[...] = jnp.where(first, low, high)
    other[...] = jnp.where(first, high, low)


def swap_payload_kernel(g, *refs):
    parts, out = refs[:-1], refs[-1]
    blocks, width, _ = g.shape
    for b in range(blocks):
        out[b * width : (b + 1) * width, :] = g[b]
    total = paired_sum([r[...] for r in parts]).astype(BF16)
    rows, hid = total.shape
    if hid < out.shape[1]:
        out[blocks * width :, :] = jnp.zeros((rows, out.shape[1]), BF16)
    out[blocks * width :, :hid] = total


def backward_own_kernel(count, index, tiles, g, *refs):
    acts, (acc, out, sems) = refs[:-3], refs[-3:]
    copies, first = [], 0
    for i, act in enumerate(acts):
        rows = act.shape[0]
        copies.append(pltpu.make_async_copy(act, out.at[pl.ds(first, rows)], sems.at[i]))
        copies[-1].start()
        first += rows
    acc[...] = jnp.zeros_like(acc)
    pull_all(index, count[0], (lambda d: g[d], tiles, acc, 0))
    for c in copies:
        c.wait()


def backward_near_kernel(count, index, tiles2, tiles3, g2, g3, acc2, acc3):
    acc2[...] = jnp.zeros_like(acc2)
    acc3[...] = jnp.zeros_like(acc3)
    pull_all(
        index,
        count[0],
        (lambda d: g2[d], tiles2, acc2, 2),
        (lambda d: g3[d], tiles3, acc3, 1 + 2 * own_core()),
    )


def backward_last_kernel(count, index, tiles1, sent, got, acc0, acc2, acc3, out, wg, bias, acc1):
    blocks, width = acc1.shape[0] - 1, acc1.shape[1]
    f_in, hid = wg.shape
    acc1[...] = jnp.zeros_like(acc1)
    core = own_core()

    def block(d):
        return got[pl.ds(pl.multiple_of(d * width, width), width), :]

    pull_all(index, count[0], (block, tiles1, acc1, 3 - 2 * core))
    for b in range(blocks):
        total = (acc0[b] + acc2[b]) + (acc1[b] + acc3[b])
        out[:, b * BLOCK : (b + 1) * BLOCK] = total.astype(BF16)
    a, b = (r[blocks * width :, :hid].astype(F32) for r in (sent, got))
    low, high = jnp.where(core == 0, a, b), jnp.where(core == 0, b, a)
    rows = low.shape[0]
    wg[:rows, :] = low
    wg[rows:, :] = high[: f_in - rows]
    bias[...] = high[f_in - rows : f_in - rows + 1]


def paired_sum(parts):
    parts = [p.astype(F32) for p in parts]
    while len(parts) > 1:
        parts = [parts[i] + parts[i + 1] for i in range(0, len(parts), 2)]
    return parts[0]


def paired_sum_kernel(*refs):
    refs[-1][...] = paired_sum([r[...] for r in refs[:-1]]).astype(refs[-1].dtype)


def moved(block, axis, target):
    n = lax.axis_size(axis)
    return lax.ppermute(block, axis, [(i, target(i) % n) for i in range(n)])


def radices(n):
    out = []
    while n > 1:
        r = 4 if n % 4 == 0 else 2
        out.append(r)
        n //= r
    return out


def exchanged(part, axis, stride, r):
    return [part] + [moved(part, axis, lambda i, s=s: i ^ (s * stride)) for s in range(1, r)]


def shards(node_features, weight, bias, tile_values, tile_src, tile_dst, tile_counts, out_grad):
    nodes, f_in = node_features.shape
    hid = weight.shape[1]
    blocks = nodes // BLOCK
    parts = lax.axis_size("feat")
    width = f_in // parts
    capacity = tile_values.shape[0]
    groups = capacity // REACH
    piece = jax.ShapeDtypeStruct((blocks, width, BLOCK), BF16)
    totals = jax.ShapeDtypeStruct((blocks + 1, width, BLOCK), F32)
    acc = pltpu.VMEM(totals.shape, F32)
    tiles = tile_values.reshape(groups, REACH, BLOCK, BLOCK)
    plane = jax.ShapeDtypeStruct((groups, BLOCK, BLOCK), BF16)
    slots = jax.ShapeDtypeStruct((capacity,), jnp.int32)
    rows = jax.ShapeDtypeStruct((nodes, hid), BF16)
    gradient = jax.ShapeDtypeStruct(((f_in + 32) // 2, hid), BF16)
    flops = 2 * capacity * BLOCK * BLOCK * width // REACH

    def swapped(i):
        return i ^ 1

    tiles1, tiles2, tiles3, xt, swap, index = call(
        forward_swap_kernel,
        [plane, plane, plane, piece, piece, slots],
        [SMEM] + [HBM] * 4,
        [VMEM] * 5 + [SMEM],
        [
            pltpu.SMEM((capacity,), jnp.int32),
            pltpu.SMEM((capacity,), jnp.int32),
            pltpu.VMEM(node_features.shape, BF16),
            acc,
            pltpu.SemaphoreType.DMA((6,)),
        ],
        flops,
    )(tile_counts, *(in_hbm(a) for a in (tile_src, tile_dst, node_features, tiles)))
    index = (tile_counts, index)
    swap = moved(swap, "dom", swapped)
    cut = 2 if blocks % 2 == 0 else 1
    starts = range(0, blocks, blocks // cut)
    half = jax.ShapeDtypeStruct((blocks // cut, width, BLOCK), BF16)
    half_wide = jax.ShapeDtypeStruct(half.shape, F32)
    half_rows = jax.ShapeDtypeStruct((nodes // cut, hid), BF16)
    half_columns = jax.ShapeDtypeStruct((f_in + 32, nodes // cut), BF16)
    acc2, *direct = call(
        forward_send_kernel,
        [totals] + [half] * cut,
        [SMEM] * 2 + [VMEM] * 3,
        [VMEM] * (1 + cut),
        [acc],
        2 * flops,
    )(*index, xt, tiles2, tiles3)
    chip = call(functools.partial(sum_kernel, 2, 0), [half] * cut, [VMEM] * 2, [VMEM] * cut)(acc2, swap)
    chip = [moved(c, "dom", lambda i: i + 2) for c in chip]
    acc0, tiles0 = call(
        forward_own_kernel,
        [totals, plane],
        [SMEM] * 2 + [VMEM, HBM],
        [VMEM] * 2,
        [pltpu.SemaphoreType.DMA],
        flops,
    )(*index, xt, in_hbm(tiles))
    acc0, direct[0] = lax.optimization_barrier((acc0, direct[0]))
    direct = [moved(d, "dom", lambda i: i + 1 + 2 * (i % 2)) for d in direct]
    h_lists = []
    for first, c, d in zip(starts, chip, direct):
        (h,) = call(functools.partial(sum_kernel, 3, first), [half], [VMEM] * 3, [VMEM])(acc0, d, c)
        h_lists.append([h] + [moved(h, "feat", lambda i, q=q: i - q) for q in range(1, parts)])
    acts, hts, grads, g_list = [], [], [], []
    for first, hs in zip(starts, h_lists):
        act, ht, grad, g_own, *g_others = call(
            functools.partial(middle_kernel, parts, first),
            [half_rows, half_columns, half_rows, half_wide] + [half] * (parts - 1),
            [VMEM] * (3 + parts),
            [VMEM] * (3 + parts),
            (),
            4 * nodes * f_in * hid // cut,
        )(bias.reshape(1, hid), weight, out_grad, *hs)
        acts.append(act)
        hts.append(ht)
        grads.append(grad)
        g_list += [g_own] + [moved(g, "feat", lambda i, q=q + 1: i + q) for q, g in enumerate(g_others)]
    wg, wg_other = call(
        functools.partial(weight_grad_kernel, cut),
        [gradient, gradient],
        [VMEM] * (2 * cut),
        [VMEM, VMEM],
        (),
        2 * nodes * f_in * hid,
    )(*hts, *grads)
    r, *more = radices(lax.axis_size("dom"))
    wgs = [wg] + [moved(wg_other if s % 2 else wg, "dom", lambda i, s=s: i ^ s) for s in range(1, r)]
    (g,) = call(functools.partial(join_kernel, parts), [piece], [VMEM] * len(g_list), [VMEM])(*g_list)
    g_chip = moved(g, "dom", lambda i: i - 2)
    g_direct = moved(g, "dom", lambda i: i - 3 + 2 * (i % 2))
    stride = r
    for r in more:
        (wg,) = call(paired_sum_kernel, [gradient], [VMEM] * len(wgs), [VMEM], (), SUM_FLOPS)(*wgs)
        wgs = exchanged(wg, "dom", stride, r)
        stride *= r
    back0, output = call(
        backward_own_kernel,
        [totals, rows],
        [SMEM] * 2 + [VMEM] * (2 + cut),
        [VMEM, HBM],
        [pltpu.SemaphoreType.DMA((cut,))],
        flops,
    )(*index, tiles0, g, *acts)
    g_direct, g_chip, back0, *wgs = lax.optimization_barrier((g_direct, g_chip, back0, *wgs))
    payload = jax.ShapeDtypeStruct((blocks * width + gradient.shape[0], BLOCK), BF16)
    (sent,) = call(swap_payload_kernel, [payload], [VMEM] * (1 + len(wgs)), [VMEM])(g_chip, *wgs)
    got = moved(sent, "dom", swapped)
    back2, back3 = call(
        backward_near_kernel, [totals, totals], [SMEM] * 2 + [VMEM] * 4, [VMEM] * 2, (), 2 * flops
    )(*index, tiles2, tiles3, g_chip, g_direct)
    input_grad, weight_grad, bias_grad = call(
        backward_last_kernel,
        [
            jax.ShapeDtypeStruct((width, nodes), BF16),
            jax.ShapeDtypeStruct((f_in, hid), F32),
            jax.ShapeDtypeStruct((1, hid), F32),
        ],
        [SMEM] * 2 + [VMEM] * 6,
        [VMEM] * 3,
        [acc],
        flops,
    )(*index, tiles1, sent, got, back0, back2, back3)
    return output, weight_grad, bias_grad.reshape(hid), input_grad.T


def solution(mesh):
    return jax.shard_map(
        shards,
        mesh=mesh,
        in_specs=(
            P("dom", None),
            P(None, "feat"),
            P("feat"),
            P("dom", None, None),
            P("dom"),
            P("dom"),
            P("dom"),
            P("dom", "feat"),
        ),
        out_specs=(P("dom", "feat"), P(None, "feat"), P("feat"), P("dom", "feat")),
        check_vma=False,
    )
```

```python
import functools

import jax
import jax.numpy as jnp
from jax import lax
from jax.experimental import pallas as pl
from jax.experimental.pallas import tpu as pltpu
from jax.sharding import PartitionSpec as P

BLOCK = 128
REACH = 4
SUM_FLOPS = 10**9
SRC_UNIT = 2**16
F32 = jnp.float32
BF16 = jnp.bfloat16
VMEM = pl.BlockSpec(memory_space=pltpu.VMEM)
SMEM = pl.BlockSpec(memory_space=pltpu.SMEM)
HBM = pl.BlockSpec(memory_space=pltpu.HBM)


def call(kernel, out_shape, in_specs, out_specs, scratch=(), flops=0):
    return pl.pallas_call(
        kernel,
        out_shape=out_shape,
        in_specs=in_specs,
        out_specs=out_specs,
        scratch_shapes=list(scratch),
        compiler_params=pltpu.CompilerParams(vmem_limit_bytes=24 * 1024 * 1024),
        cost_estimate=pl.CostEstimate(flops=flops, bytes_accessed=2**20, transcendentals=0),
    )


def groups_at_once(groups):
    return next(m for m in (12, 8, 6, 4, 3, 2, 1) if groups % m == 0)


def in_hbm(a):
    return pltpu.with_memory_space_constraint(a, pltpu.HBM)


def own_core():
    return lax.rem(lax.axis_index("dom"), 2)


def slot_loop(count, groups, body):
    m = groups_at_once(groups)

    def chunk(i, carry):
        @pl.when(i * (m * REACH) < count)
        def _():
            for u in range(m):
                body(i * m + u)

        return carry

    lax.fori_loop(0, groups // m, chunk, 0)


def source(entry):
    return lax.shift_right_logical(entry, 16)


def target(entry, o, blocks):
    return lax.bitwise_and(entry, SRC_UNIT - 1) - o * blocks


def push(xt, tiles, index, count, acc, j, o):
    blocks = xt.shape[0]
    k = j * REACH + o
    entry = index[k]
    out = lax.dot_general(xt[source(entry)], tiles[j], (((1,), (1,)), ((), ())), preferred_element_type=F32)
    acc[jnp.where(k < count, target(entry, o, blocks), blocks)] += out


def pull(block, tiles, index, count, acc, j, o):
    blocks = acc.shape[0] - 1
    k = j * REACH + o
    entry = index[k]
    out = jnp.dot(block(target(entry, o, blocks)), tiles[j], preferred_element_type=F32)
    acc[jnp.where(k < count, source(entry), blocks)] += out


def push_all(xt, index, count, *planes):
    def body(j):
        for tiles, acc, o in planes:
            push(xt, tiles, index, count, acc, j, o)

    slot_loop(count, planes[0][0].shape[0], body)


def pull_all(index, count, *planes):
    def body(j):
        for block, tiles, acc, o in planes:
            pull(block, tiles, index, count, acc, j, o)

    slot_loop(count, planes[0][1].shape[0], body)


def forward_swap_kernel(
    count, src_hbm, dst_hbm, x_hbm, tiles_hbm, tiles1, tiles2, tiles3, xt, swap, index, src, dst, x, acc, sems
):
    blocks, width, _ = xt.shape
    o = 3 - 2 * own_core()
    loads = [
        pltpu.make_async_copy(a, b, sems.at[i])
        for i, (a, b) in enumerate(
            (
                (src_hbm, src),
                (dst_hbm, dst),
                (x_hbm, x),
                (tiles_hbm.at[:, o], tiles1),
                (tiles_hbm.at[:, 2], tiles2),
                (tiles_hbm.at[:, 4 - o], tiles3),
            )
        )
    ]
    for c in loads:
        c.start()
    acc[...] = jnp.zeros_like(acc)
    row = lax.broadcasted_iota(jnp.int32, (width, x.shape[1]), 0)
    column = lax.broadcasted_iota(jnp.int32, (width, x.shape[1]), 1)
    pick = (column == row + lax.axis_index("feat") * width).astype(BF16)
    for c in loads[:2]:
        c.wait()
    for k in range(src.shape[0]):
        index[k] = src[k] * SRC_UNIT + dst[k]
    loads[2].wait()
    for b in range(blocks):
        xt[b] = lax.dot_general(
            pick, x[b * BLOCK : (b + 1) * BLOCK, :], (((1,), (1,)), ((), ())), preferred_element_type=F32
        ).astype(BF16)
    loads[3].wait()
    push_all(xt, index, count[0], (tiles1, acc, o))
    swap[...] = acc[:blocks].astype(BF16)
    for c in loads[4:]:
        c.wait()


def forward_send_kernel(count, index, xt, tiles2, tiles3, acc2, direct, acc):
    acc2[...] = jnp.zeros_like(acc2)
    acc[...] = jnp.zeros_like(acc)
    push_all(xt, index, count[0], (tiles2, acc2, 2), (tiles3, acc, 1 + 2 * own_core()))
    direct[...] = acc[: direct.shape[0]].astype(BF16)


def unit(n):
    shape = (n, n)
    return (lax.broadcasted_iota(jnp.int32, shape, 0) == lax.broadcasted_iota(jnp.int32, shape, 1)).astype(BF16)


def turned(block):
    n = block.shape[1]
    return lax.dot_general(
        unit(n), block, (((1,), (1,)), ((), ())), preferred_element_type=F32
    ).astype(BF16)


def forward_own_kernel(
    count, index, xt, bias_ref, w_ref, og_hbm, tiles_hbm, acc, tiles0, bias_t, w_t, og_t, og_ref, sems
):
    load_og = pltpu.make_async_copy(og_hbm, og_ref, sems.at[0])
    load_og.start()
    load = pltpu.make_async_copy(tiles_hbm.at[:, 0], tiles0, sems.at[1])
    load.start()
    acc[...] = jnp.zeros_like(acc)
    bias_t[...] = jnp.broadcast_to(bias_ref[...], (BLOCK, bias_ref.shape[1])).T
    w_t[...] = turned(w_ref[...])
    load_og.wait()
    for first in range(0, og_ref.shape[0], BLOCK):
        og_t[:, first : first + BLOCK] = turned(og_ref[first : first + BLOCK, :])
    load.wait()
    push_all(xt, index, count[0], (tiles0, acc, 0))


def sum_kernel(n, first, *refs):
    for out in refs[n:]:
        blocks = out.shape[0]
        total = None
        for r in refs[:n]:
            part = r[...] if r.shape[0] == blocks else r[first : first + blocks]
            total = part.astype(F32) if total is None else total + part.astype(F32)
        out[...] = total.astype(out.dtype)
        first += blocks


def join_kernel(parts, *refs):
    out = refs[-1]
    halves = [refs[i : i + parts] for i in range(0, len(refs) - 1, parts)]
    first = 0
    for half in halves:
        blocks = half[0].shape[0]
        total = half[0][...].astype(F32)
        for r in half[1:]:
            total = total + r[...].astype(F32)
        out[first : first + blocks] = total.astype(out.dtype)
        first += blocks


def middle_kernel(parts, first, bias_ref, w_ref, w_t_ref, og_ref, *refs):
    h_refs, (act, ht, grads), g_refs = refs[:parts], refs[parts : parts + 3], refs[parts + 3 :]
    blocks, width, _ = h_refs[0].shape
    f_in = w_ref.shape[0]
    me = lax.axis_index("feat")
    rows = [pl.multiple_of(lax.rem(me + q, parts) * width, width) for q in range(parts)]
    for q in range(parts):
        for b in range(blocks):
            ht[pl.ds(rows[q], width), b * BLOCK : (b + 1) * BLOCK] = h_refs[q][b]
    ht[f_in:, :] = jnp.ones((ht.shape[0] - f_in, ht.shape[1]), BF16)
    for b in range(blocks):
        cols = slice(b * BLOCK, (b + 1) * BLOCK)
        pre = jnp.dot(w_t_ref[...], ht[:f_in, cols], preferred_element_type=F32) + bias_ref[...]
        s = jax.nn.sigmoid(pre)
        act[:, cols] = (pre * s).astype(BF16)
        og = og_ref[:, (first + b) * BLOCK : (first + b + 1) * BLOCK].astype(F32)
        grad = (og * s * (1.0 + pre * (1.0 - s))).astype(BF16)
        grads[:, cols] = grad
        for q in range(parts):
            g_refs[q][b] = jnp.dot(
                w_ref[pl.ds(rows[q], width), :], grad, preferred_element_type=F32
            ).astype(g_refs[q].dtype)


def weight_grad_kernel(n, *refs):
    hts, grads, (mine, other) = refs[:n], refs[n : 2 * n], refs[2 * n :]
    full = sum(
        lax.dot_general(h[...], g[...], (((1,), (1,)), ((), ())), preferred_element_type=F32)
        for h, g in zip(hts, grads)
    )
    full = full.astype(BF16)
    rows = mine.shape[0]
    low, high = full[:rows], full[rows:]
    first = own_core() == 0
    mine[...] = jnp.where(first, low, high)
    other[...] = jnp.where(first, high, low)


def swap_payload_kernel(g, *refs):
    parts, out = refs[:-1], refs[-1]
    blocks, width, _ = g.shape
    for b in range(blocks):
        out[b * width : (b + 1) * width, :] = g[b]
    total = paired_sum([r[...] for r in parts]).astype(BF16)
    rows, hid = total.shape
    if hid < out.shape[1]:
        out[blocks * width :, :] = jnp.zeros((rows, out.shape[1]), BF16)
    out[blocks * width :, :hid] = total


def backward_own_kernel(count, index, tiles, g, *refs):
    acts, (acc, out, rows, sems) = refs[:-4], refs[-4:]
    copies, first = [], 0
    for i, act in enumerate(acts):
        for col in range(0, act.shape[1], BLOCK):
            rows[first + col : first + col + BLOCK, :] = turned(act[:, col : col + BLOCK])
        part = pl.ds(first, act.shape[1])
        copies.append(pltpu.make_async_copy(rows.at[part], out.at[part], sems.at[i]))
        copies[-1].start()
        first += act.shape[1]
    acc[...] = jnp.zeros_like(acc)
    pull_all(index, count[0], (lambda d: g[d], tiles, acc, 0))
    for c in copies:
        c.wait()


def backward_near_kernel(count, index, tiles2, tiles3, g2, g3, acc2, acc3):
    acc2[...] = jnp.zeros_like(acc2)
    acc3[...] = jnp.zeros_like(acc3)
    pull_all(
        index,
        count[0],
        (lambda d: g2[d], tiles2, acc2, 2),
        (lambda d: g3[d], tiles3, acc3, 1 + 2 * own_core()),
    )


def backward_last_kernel(count, index, tiles1, sent, got, acc0, acc2, acc3, out, wg, bias, acc1):
    blocks, width = acc1.shape[0] - 1, acc1.shape[1]
    f_in, hid = wg.shape
    acc1[...] = jnp.zeros_like(acc1)
    core = own_core()

    def block(d):
        return got[pl.ds(pl.multiple_of(d * width, width), width), :]

    pull_all(index, count[0], (block, tiles1, acc1, 3 - 2 * core))
    for b in range(blocks):
        total = (acc0[b] + acc2[b]) + (acc1[b] + acc3[b])
        out[:, b * BLOCK : (b + 1) * BLOCK] = total.astype(BF16)
    a, b = (r[blocks * width :, :hid].astype(F32) for r in (sent, got))
    low, high = jnp.where(core == 0, a, b), jnp.where(core == 0, b, a)
    rows = low.shape[0]
    wg[:rows, :] = low
    wg[rows:, :] = high[: f_in - rows]
    bias[...] = high[f_in - rows : f_in - rows + 1]


def paired_sum(parts):
    parts = [p.astype(F32) for p in parts]
    while len(parts) > 1:
        parts = [parts[i] + parts[i + 1] for i in range(0, len(parts), 2)]
    return parts[0]


def paired_sum_kernel(*refs):
    refs[-1][...] = paired_sum([r[...] for r in refs[:-1]]).astype(refs[-1].dtype)


def moved(block, axis, target):
    n = lax.axis_size(axis)
    return lax.ppermute(block, axis, [(i, target(i) % n) for i in range(n)])


def radices(n):
    out = []
    while n > 1:
        r = 4 if n % 4 == 0 else 2
        out.append(r)
        n //= r
    return out


def exchanged(part, axis, stride, r):
    return [part] + [moved(part, axis, lambda i, s=s: i ^ (s * stride)) for s in range(1, r)]


def shards(node_features, weight, bias, tile_values, tile_src, tile_dst, tile_counts, out_grad):
    nodes, f_in = node_features.shape
    hid = weight.shape[1]
    blocks = nodes // BLOCK
    parts = lax.axis_size("feat")
    width = f_in // parts
    capacity = tile_values.shape[0]
    groups = capacity // REACH
    piece = jax.ShapeDtypeStruct((blocks, width, BLOCK), BF16)
    totals = jax.ShapeDtypeStruct((blocks + 1, width, BLOCK), F32)
    acc = pltpu.VMEM(totals.shape, F32)
    tiles = tile_values.reshape(groups, REACH, BLOCK, BLOCK)
    plane = jax.ShapeDtypeStruct((groups, BLOCK, BLOCK), BF16)
    slots = jax.ShapeDtypeStruct((capacity,), jnp.int32)
    rows = jax.ShapeDtypeStruct((nodes, hid), BF16)
    gradient = jax.ShapeDtypeStruct(((f_in + 32) // 2, hid), BF16)
    flops = 2 * capacity * BLOCK * BLOCK * width // REACH

    def swapped(i):
        return i ^ 1

    tiles1, tiles2, tiles3, xt, swap, index = call(
        forward_swap_kernel,
        [plane, plane, plane, piece, piece, slots],
        [SMEM] + [HBM] * 4,
        [VMEM] * 5 + [SMEM],
        [
            pltpu.SMEM((capacity,), jnp.int32),
            pltpu.SMEM((capacity,), jnp.int32),
            pltpu.VMEM(node_features.shape, BF16),
            acc,
            pltpu.SemaphoreType.DMA((6,)),
        ],
        flops,
    )(tile_counts, *(in_hbm(a) for a in (tile_src, tile_dst, node_features, tiles)))
    index = (tile_counts, index)
    swap = moved(swap, "dom", swapped)
    acc2, direct = call(
        forward_send_kernel, [totals, piece], [SMEM] * 2 + [VMEM] * 3, [VMEM] * 2, [acc], 2 * flops
    )(*index, xt, tiles2, tiles3)
    cut = 2 if blocks % 2 == 0 else 1
    starts = range(0, blocks, blocks // cut)
    half = jax.ShapeDtypeStruct((blocks // cut, width, BLOCK), BF16)
    half_wide = jax.ShapeDtypeStruct(half.shape, F32)
    half_rows = jax.ShapeDtypeStruct((hid, nodes // cut), BF16)
    half_columns = jax.ShapeDtypeStruct((f_in + 32, nodes // cut), BF16)
    chip = call(functools.partial(sum_kernel, 2, 0), [half] * cut, [VMEM] * 2, [VMEM] * cut)(acc2, swap)
    chip = [moved(c, "dom", lambda i: i + 2) for c in chip]
    direct = moved(direct, "dom", lambda i: i + 1 + 2 * (i % 2))
    acc0, tiles0, bias_t, w_t, og_t = call(
        forward_own_kernel,
        [
            totals,
            plane,
            jax.ShapeDtypeStruct((hid, BLOCK), F32),
            jax.ShapeDtypeStruct((hid, f_in), BF16),
            jax.ShapeDtypeStruct((hid, nodes), BF16),
        ],
        [SMEM] * 2 + [VMEM] * 3 + [HBM] * 2,
        [VMEM] * 5,
        [pltpu.VMEM(out_grad.shape, BF16), pltpu.SemaphoreType.DMA((2,))],
        flops,
    )(*index, xt, bias.reshape(1, hid), weight, in_hbm(out_grad), in_hbm(tiles))
    h_lists = []
    for first, c in zip(starts, chip):
        (h,) = call(functools.partial(sum_kernel, 3, first), [half], [VMEM] * 3, [VMEM])(acc0, direct, c)
        h_lists.append([h] + [moved(h, "feat", lambda i, q=q: i - q) for q in range(1, parts)])
    acts, hts, grads, g_list = [], [], [], []
    for first, hs in zip(starts, h_lists):
        act, ht, grad, g_own, *g_others = call(
            functools.partial(middle_kernel, parts, first),
            [half_rows, half_columns, half_rows, half_wide] + [half] * (parts - 1),
            [VMEM] * (4 + parts),
            [VMEM] * (3 + parts),
            (),
            4 * nodes * f_in * hid // cut,
        )(bias_t, weight, w_t, og_t, *hs)
        acts.append(act)
        hts.append(ht)
        grads.append(grad)
        g_list += [g_own] + [moved(g, "feat", lambda i, q=q + 1: i + q) for q, g in enumerate(g_others)]
    wg, wg_other = call(
        functools.partial(weight_grad_kernel, cut),
        [gradient, gradient],
        [VMEM] * (2 * cut),
        [VMEM, VMEM],
        (),
        2 * nodes * f_in * hid,
    )(*hts, *grads)
    r, *more = radices(lax.axis_size("dom"))
    wgs = [wg] + [moved(wg_other if s % 2 else wg, "dom", lambda i, s=s: i ^ s) for s in range(1, r)]
    (g,) = call(functools.partial(join_kernel, parts), [piece], [VMEM] * len(g_list), [VMEM])(*g_list)
    g_chip = moved(g, "dom", lambda i: i - 2)
    g_direct = moved(g, "dom", lambda i: i - 3 + 2 * (i % 2))
    stride = r
    for r in more:
        (wg,) = call(paired_sum_kernel, [gradient], [VMEM] * len(wgs), [VMEM], (), SUM_FLOPS)(*wgs)
        wgs = exchanged(wg, "dom", stride, r)
        stride *= r
    back0, output = call(
        backward_own_kernel,
        [totals, rows],
        [SMEM] * 2 + [VMEM] * (2 + cut),
        [VMEM, HBM],
        [pltpu.VMEM(rows.shape, BF16), pltpu.SemaphoreType.DMA((cut,))],
        flops,
    )(*index, tiles0, g, *acts)
    g_direct, g_chip, back0, *wgs = lax.optimization_barrier((g_direct, g_chip, back0, *wgs))
    payload = jax.ShapeDtypeStruct((blocks * width + gradient.shape[0], BLOCK), BF16)
    (sent,) = call(swap_payload_kernel, [payload], [VMEM] * (1 + len(wgs)), [VMEM])(g_chip, *wgs)
    got = moved(sent, "dom", swapped)
    back2, back3 = call(
        backward_near_kernel, [totals, totals], [SMEM] * 2 + [VMEM] * 4, [VMEM] * 2, (), 2 * flops
    )(*index, tiles2, tiles3, g_chip, g_direct)
    input_grad, weight_grad, bias_grad = call(
        backward_last_kernel,
        [
            jax.ShapeDtypeStruct((width, nodes), BF16),
            jax.ShapeDtypeStruct((f_in, hid), F32),
            jax.ShapeDtypeStruct((1, hid), F32),
        ],
        [SMEM] * 2 + [VMEM] * 6,
        [VMEM] * 3,
        [acc],
        flops,
    )(*index, tiles1, sent, got, back0, back2, back3)
    return output, weight_grad, bias_grad.reshape(hid), input_grad.T


def solution(mesh):
    return jax.shard_map(
        shards,
        mesh=mesh,
        in_specs=(
            P("dom", None),
            P(None, "feat"),
            P("feat"),
            P("dom", None, None),
            P("dom"),
            P("dom"),
            P("dom"),
            P("dom", "feat"),
        ),
        out_specs=(P("dom", "feat"), P(None, "feat"), P("feat"), P("dom", "feat")),
        check_vma=False,
    )
```

```python
import functools

import jax
import jax.numpy as jnp
from jax import lax
from jax.experimental import pallas as pl
from jax.experimental.pallas import tpu as pltpu
from jax.sharding import PartitionSpec as P

BLOCK = 128
REACH = 4
SUM_FLOPS = 10**9
SRC_UNIT = 2**16
F32 = jnp.float32
BF16 = jnp.bfloat16
VMEM = pl.BlockSpec(memory_space=pltpu.VMEM)
SMEM = pl.BlockSpec(memory_space=pltpu.SMEM)
HBM = pl.BlockSpec(memory_space=pltpu.HBM)


def call(kernel, out_shape, in_specs, out_specs, scratch=(), flops=0):
    return pl.pallas_call(
        kernel,
        out_shape=out_shape,
        in_specs=in_specs,
        out_specs=out_specs,
        scratch_shapes=list(scratch),
        compiler_params=pltpu.CompilerParams(vmem_limit_bytes=24 * 1024 * 1024),
        cost_estimate=pl.CostEstimate(flops=flops, bytes_accessed=2**20, transcendentals=0),
    )


def groups_at_once(groups):
    return next(m for m in (12, 8, 6, 4, 3, 2, 1) if groups % m == 0)


def in_hbm(a):
    return pltpu.with_memory_space_constraint(a, pltpu.HBM)


def own_core():
    return lax.rem(lax.axis_index("dom"), 2)


def slot_loop(count, groups, body):
    m = groups_at_once(groups)

    def chunk(i, carry):
        @pl.when(i * (m * REACH) < count)
        def _():
            for u in range(m):
                body(i * m + u)

        return carry

    lax.fori_loop(0, groups // m, chunk, 0)


def source(entry):
    return lax.shift_right_logical(entry, 16)


def target(entry, o, blocks):
    return lax.bitwise_and(entry, SRC_UNIT - 1) - o * blocks


def push(xt, tiles, index, count, acc, j, o):
    blocks = xt.shape[0]
    k = j * REACH + o
    entry = index[k]
    out = lax.dot_general(xt[source(entry)], tiles[j], (((1,), (1,)), ((), ())), preferred_element_type=F32)
    acc[jnp.where(k < count, target(entry, o, blocks), blocks)] += out


def pull(block, tiles, index, count, acc, j, o):
    blocks = acc.shape[0] - 1
    k = j * REACH + o
    entry = index[k]
    out = jnp.dot(block(target(entry, o, blocks)), tiles[j], preferred_element_type=F32)
    acc[jnp.where(k < count, source(entry), blocks)] += out


def push_all(xt, index, count, *planes):
    def body(j):
        for tiles, acc, o in planes:
            push(xt, tiles, index, count, acc, j, o)

    slot_loop(count, planes[0][0].shape[0], body)


def pull_all(index, count, *planes):
    def body(j):
        for block, tiles, acc, o in planes:
            pull(block, tiles, index, count, acc, j, o)

    slot_loop(count, planes[0][1].shape[0], body)


def unit(n):
    shape = (n, n)
    return (lax.broadcasted_iota(jnp.int32, shape, 0) == lax.broadcasted_iota(jnp.int32, shape, 1)).astype(BF16)


def turned(block):
    n = block.shape[1]
    return lax.dot_general(
        unit(n), block, (((1,), (1,)), ((), ())), preferred_element_type=F32
    ).astype(BF16)


def forward_swap_kernel(
    count, src_hbm, dst_hbm, x_hbm, tiles_hbm, tiles1, tiles2, tiles3, xt, swap, index, src, dst, x, acc, sems
):
    blocks = xt.shape[0]
    o = 3 - 2 * own_core()
    loads = [
        pltpu.make_async_copy(a, b, sems.at[i])
        for i, (a, b) in enumerate(
            (
                (src_hbm, src),
                (dst_hbm, dst),
                (x_hbm, x),
                (tiles_hbm.at[:, o], tiles1),
                (tiles_hbm.at[:, 2], tiles2),
                (tiles_hbm.at[:, 4 - o], tiles3),
            )
        )
    ]
    for c in loads:
        c.start()
    acc[...] = jnp.zeros_like(acc)
    for c in loads[:2]:
        c.wait()
    for k in range(src.shape[0]):
        index[k] = src[k] * SRC_UNIT + dst[k]
    loads[2].wait()
    for b in range(blocks):
        xt[b] = turned(x[b * BLOCK : (b + 1) * BLOCK, :])
    loads[3].wait()
    push_all(xt, index, count[0], (tiles1, acc, o))
    swap[...] = acc[:blocks].astype(BF16)
    for c in loads[4:]:
        c.wait()


def forward_send_kernel(count, index, xt, tiles2, tiles3, acc2, direct, acc):
    acc2[...] = jnp.zeros_like(acc2)
    acc[...] = jnp.zeros_like(acc)
    push_all(xt, index, count[0], (tiles2, acc2, 2), (tiles3, acc, 1 + 2 * own_core()))
    direct[...] = acc[: direct.shape[0]].astype(BF16)


def forward_own_kernel(
    count, index, xt, bias_ref, w_ref, og_hbm, tiles_hbm, acc, tiles0, bias_t, w_t, og_t, og_ref, sems
):
    load_og = pltpu.make_async_copy(og_hbm, og_ref, sems.at[0])
    load_og.start()
    load = pltpu.make_async_copy(tiles_hbm.at[:, 0], tiles0, sems.at[1])
    load.start()
    acc[...] = jnp.zeros_like(acc)
    bias_t[...] = jnp.broadcast_to(bias_ref[...], (BLOCK, bias_ref.shape[1])).T
    w_t[...] = turned(w_ref[...])
    load_og.wait()
    for first in range(0, og_ref.shape[0], BLOCK):
        og_t[:, first : first + BLOCK] = turned(og_ref[first : first + BLOCK, :])
    load.wait()
    push_all(xt, index, count[0], (tiles0, acc, 0))


def sum_kernel(n, first, *refs):
    for out in refs[n:]:
        blocks = out.shape[0]
        total = None
        for r in refs[:n]:
            part = r[...] if r.shape[0] == blocks else r[first : first + blocks]
            total = part.astype(F32) if total is None else total + part.astype(F32)
        out[...] = total.astype(out.dtype)
        first += blocks


def join_kernel(parts, *refs):
    out = refs[-1]
    halves = [refs[i : i + parts] for i in range(0, len(refs) - 1, parts)]
    first = 0
    for half in halves:
        blocks = half[0].shape[0]
        total = half[0][...].astype(F32)
        for r in half[1:]:
            total = total + r[...].astype(F32)
        out[first : first + blocks] = total.astype(out.dtype)
        first += blocks


def middle_kernel(parts, first, bias_ref, w_ref, w_t_ref, og_ref, h_ref, act, ht, grads, *g_refs):
    blocks, f_in, _ = h_ref.shape
    width = f_in // parts
    me = lax.axis_index("feat")
    rows = [pl.multiple_of(lax.rem(me + q, parts) * width, width) for q in range(parts)]
    for b in range(blocks):
        ht[:f_in, b * BLOCK : (b + 1) * BLOCK] = h_ref[b]
    ht[f_in:, :] = jnp.ones((ht.shape[0] - f_in, ht.shape[1]), BF16)
    for b in range(blocks):
        cols = slice(b * BLOCK, (b + 1) * BLOCK)
        pre = jnp.dot(w_t_ref[...], h_ref[b], preferred_element_type=F32) + bias_ref[...]
        s = jax.nn.sigmoid(pre)
        act[:, cols] = (pre * s).astype(BF16)
        og = og_ref[:, (first + b) * BLOCK : (first + b + 1) * BLOCK].astype(F32)
        grad = (og * s * (1.0 + pre * (1.0 - s))).astype(BF16)
        grads[:, cols] = grad
        for q in range(parts):
            g_refs[q][b] = jnp.dot(
                w_ref[pl.ds(rows[q], width), :], grad, preferred_element_type=F32
            ).astype(g_refs[q].dtype)


def weight_grad_kernel(n, *refs):
    hts, grads, (mine, other) = refs[:n], refs[n : 2 * n], refs[2 * n :]
    full = sum(
        lax.dot_general(h[...], g[...], (((1,), (1,)), ((), ())), preferred_element_type=F32)
        for h, g in zip(hts, grads)
    )
    full = full.astype(BF16)
    rows = mine.shape[0]
    low, high = full[:rows], full[rows:]
    first = own_core() == 0
    mine[...] = jnp.where(first, low, high)
    other[...] = jnp.where(first, high, low)


def swap_payload_kernel(g, *refs):
    parts, out = refs[:-1], refs[-1]
    blocks, width, _ = g.shape
    for b in range(blocks):
        out[b * width : (b + 1) * width, :] = g[b]
    total = paired_sum([r[...] for r in parts]).astype(BF16)
    rows, hid = total.shape
    if hid < out.shape[1]:
        out[blocks * width :, :] = jnp.zeros((rows, out.shape[1]), BF16)
    out[blocks * width :, :hid] = total


def backward_own_kernel(count, index, tiles, g, *refs):
    acts, (acc, out, rows, sems) = refs[:-4], refs[-4:]
    copies, first = [], 0
    for i, act in enumerate(acts):
        for col in range(0, act.shape[1], BLOCK):
            rows[first + col : first + col + BLOCK, :] = turned(act[:, col : col + BLOCK])
        part = pl.ds(first, act.shape[1])
        copies.append(pltpu.make_async_copy(rows.at[part], out.at[part], sems.at[i]))
        copies[-1].start()
        first += act.shape[1]
    acc[...] = jnp.zeros_like(acc)
    pull_all(index, count[0], (lambda d: g[d], tiles, acc, 0))
    for c in copies:
        c.wait()


def backward_near_kernel(count, index, tiles2, tiles3, g2, g3, acc2, acc3):
    acc2[...] = jnp.zeros_like(acc2)
    acc3[...] = jnp.zeros_like(acc3)
    pull_all(
        index,
        count[0],
        (lambda d: g2[d], tiles2, acc2, 2),
        (lambda d: g3[d], tiles3, acc3, 1 + 2 * own_core()),
    )


def backward_last_kernel(count, index, tiles1, sent, got, acc0, acc2, acc3, out, wg, bias, acc1):
    blocks, width = acc1.shape[0] - 1, acc1.shape[1]
    f_in, hid = wg.shape
    acc1[...] = jnp.zeros_like(acc1)
    core = own_core()

    def block(d):
        return got[pl.ds(pl.multiple_of(d * width, width), width), :]

    pull_all(index, count[0], (block, tiles1, acc1, 3 - 2 * core))
    for b in range(blocks):
        total = (acc0[b] + acc2[b]) + (acc1[b] + acc3[b])
        out[:, b * BLOCK : (b + 1) * BLOCK] = total.astype(BF16)
    a, b = (r[blocks * width :, :hid].astype(F32) for r in (sent, got))
    low, high = jnp.where(core == 0, a, b), jnp.where(core == 0, b, a)
    rows = low.shape[0]
    wg[:rows, :] = low
    wg[rows:, :] = high[: f_in - rows]
    bias[...] = high[f_in - rows : f_in - rows + 1]


def paired_sum(parts):
    parts = [p.astype(F32) for p in parts]
    while len(parts) > 1:
        parts = [parts[i] + parts[i + 1] for i in range(0, len(parts), 2)]
    return parts[0]


def paired_sum_kernel(*refs):
    refs[-1][...] = paired_sum([r[...] for r in refs[:-1]]).astype(refs[-1].dtype)


def moved(block, axis, target):
    n = lax.axis_size(axis)
    return lax.ppermute(block, axis, [(i, target(i) % n) for i in range(n)])


def radices(n):
    out = []
    while n > 1:
        r = 4 if n % 4 == 0 else 2
        out.append(r)
        n //= r
    return out


def exchanged(part, axis, stride, r):
    return [part] + [moved(part, axis, lambda i, s=s: i ^ (s * stride)) for s in range(1, r)]


def shards(node_features, weight, bias, tile_values, tile_src, tile_dst, tile_counts, out_grad):
    nodes, f_in = node_features.shape
    hid = weight.shape[1]
    blocks = nodes // BLOCK
    parts = lax.axis_size("feat")
    width = f_in // parts
    capacity = tile_values.shape[0]
    groups = capacity // REACH
    piece = jax.ShapeDtypeStruct((blocks, width, BLOCK), BF16)
    totals = jax.ShapeDtypeStruct((blocks + 1, width, BLOCK), F32)
    piece_x = jax.ShapeDtypeStruct((blocks, f_in, BLOCK), BF16)
    totals_x = jax.ShapeDtypeStruct((blocks + 1, f_in, BLOCK), F32)
    acc_x = pltpu.VMEM(totals_x.shape, F32)
    acc = pltpu.VMEM(totals.shape, F32)
    tiles = tile_values.reshape(groups, REACH, BLOCK, BLOCK)
    plane = jax.ShapeDtypeStruct((groups, BLOCK, BLOCK), BF16)
    slots = jax.ShapeDtypeStruct((capacity,), jnp.int32)
    rows = jax.ShapeDtypeStruct((nodes, hid), BF16)
    gradient = jax.ShapeDtypeStruct(((f_in + 32) // 2, hid), BF16)
    flops = 2 * capacity * BLOCK * BLOCK * width // REACH

    def swapped(i):
        return i ^ 1

    tiles1, tiles2, tiles3, xt, swap, index = call(
        forward_swap_kernel,
        [plane, plane, plane, piece_x, piece_x, slots],
        [SMEM] + [HBM] * 4,
        [VMEM] * 5 + [SMEM],
        [
            pltpu.SMEM((capacity,), jnp.int32),
            pltpu.SMEM((capacity,), jnp.int32),
            pltpu.VMEM(node_features.shape, BF16),
            acc_x,
            pltpu.SemaphoreType.DMA((6,)),
        ],
        flops,
    )(tile_counts, *(in_hbm(a) for a in (tile_src, tile_dst, node_features, tiles)))
    index = (tile_counts, index)
    swap = moved(swap, "dom", swapped)
    acc2, direct = call(
        forward_send_kernel, [totals_x, piece_x], [SMEM] * 2 + [VMEM] * 3, [VMEM] * 2, [acc_x], 2 * flops
    )(*index, xt, tiles2, tiles3)
    cut = 2 if blocks % 2 == 0 else 1
    starts = range(0, blocks, blocks // cut)
    half = jax.ShapeDtypeStruct((blocks // cut, width, BLOCK), BF16)
    half_x = jax.ShapeDtypeStruct((blocks // cut, f_in, BLOCK), BF16)
    half_wide = jax.ShapeDtypeStruct(half.shape, F32)
    half_rows = jax.ShapeDtypeStruct((hid, nodes // cut), BF16)
    half_columns = jax.ShapeDtypeStruct((f_in + 32, nodes // cut), BF16)
    chip = call(functools.partial(sum_kernel, 2, 0), [half_x] * cut, [VMEM] * 2, [VMEM] * cut)(acc2, swap)
    chip = [moved(c, "dom", lambda i: i + 2) for c in chip]
    direct = moved(direct, "dom", lambda i: i + 1 + 2 * (i % 2))
    acc0, tiles0, bias_t, w_t, og_t = call(
        forward_own_kernel,
        [
            totals_x,
            plane,
            jax.ShapeDtypeStruct((hid, BLOCK), F32),
            jax.ShapeDtypeStruct((hid, f_in), BF16),
            jax.ShapeDtypeStruct((hid, nodes), BF16),
        ],
        [SMEM] * 2 + [VMEM] * 3 + [HBM] * 2,
        [VMEM] * 5,
        [pltpu.VMEM(out_grad.shape, BF16), pltpu.SemaphoreType.DMA((2,))],
        flops,
    )(*index, xt, bias.reshape(1, hid), weight, in_hbm(out_grad), in_hbm(tiles))
    h_list = []
    for first, c in zip(starts, chip):
        (h,) = call(functools.partial(sum_kernel, 3, first), [half_x], [VMEM] * 3, [VMEM])(acc0, direct, c)
        h_list.append(h)
    acts, hts, grads, g_list = [], [], [], []
    for first, h in zip(starts, h_list):
        act, ht, grad, g_own, *g_others = call(
            functools.partial(middle_kernel, parts, first),
            [half_rows, half_columns, half_rows, half_wide] + [half] * (parts - 1),
            [VMEM] * 5,
            [VMEM] * (3 + parts),
            (),
            4 * nodes * f_in * hid // cut,
        )(bias_t, weight, w_t, og_t, h)
        acts.append(act)
        hts.append(ht)
        grads.append(grad)
        g_list += [g_own] + [moved(g, "feat", lambda i, q=q + 1: i + q) for q, g in enumerate(g_others)]
    wg, wg_other = call(
        functools.partial(weight_grad_kernel, cut),
        [gradient, gradient],
        [VMEM] * (2 * cut),
        [VMEM, VMEM],
        (),
        2 * nodes * f_in * hid,
    )(*hts, *grads)
    r, *more = radices(lax.axis_size("dom"))
    wgs = [wg] + [moved(wg_other if s % 2 else wg, "dom", lambda i, s=s: i ^ s) for s in range(1, r)]
    (g,) = call(functools.partial(join_kernel, parts), [piece], [VMEM] * len(g_list), [VMEM])(*g_list)
    g_chip = moved(g, "dom", lambda i: i - 2)
    g_direct = moved(g, "dom", lambda i: i - 3 + 2 * (i % 2))
    stride = r
    for r in more:
        (wg,) = call(paired_sum_kernel, [gradient], [VMEM] * len(wgs), [VMEM], (), SUM_FLOPS)(*wgs)
        wgs = exchanged(wg, "dom", stride, r)
        stride *= r
    back0, output = call(
        backward_own_kernel,
        [totals, rows],
        [SMEM] * 2 + [VMEM] * (2 + cut),
        [VMEM, HBM],
        [pltpu.VMEM(rows.shape, BF16), pltpu.SemaphoreType.DMA((cut,))],
        flops,
    )(*index, tiles0, g, *acts)
    g_direct, g_chip, back0, *wgs = lax.optimization_barrier((g_direct, g_chip, back0, *wgs))
    payload = jax.ShapeDtypeStruct((blocks * width + gradient.shape[0], BLOCK), BF16)
    (sent,) = call(swap_payload_kernel, [payload], [VMEM] * (1 + len(wgs)), [VMEM])(g_chip, *wgs)
    got = moved(sent, "dom", swapped)
    back2, back3 = call(
        backward_near_kernel, [totals, totals], [SMEM] * 2 + [VMEM] * 4, [VMEM] * 2, (), 2 * flops
    )(*index, tiles2, tiles3, g_chip, g_direct)
    input_grad, weight_grad, bias_grad = call(
        backward_last_kernel,
        [
            jax.ShapeDtypeStruct((width, nodes), BF16),
            jax.ShapeDtypeStruct((f_in, hid), F32),
            jax.ShapeDtypeStruct((1, hid), F32),
        ],
        [SMEM] * 2 + [VMEM] * 6,
        [VMEM] * 3,
        [acc],
        flops,
    )(*index, tiles1, sent, got, back0, back2, back3)
    return output, weight_grad, bias_grad.reshape(hid), input_grad.T


def solution(mesh):
    return jax.shard_map(
        shards,
        mesh=mesh,
        in_specs=(
            P("dom", None),
            P(None, "feat"),
            P("feat"),
            P("dom", None, None),
            P("dom"),
            P("dom"),
            P("dom"),
            P("dom", "feat"),
        ),
        out_specs=(P("dom", "feat"), P(None, "feat"), P("feat"), P("dom", "feat")),
        check_vma=False,
    )
```

```python
import functools

import jax
import jax.numpy as jnp
from jax import lax
from jax.experimental import pallas as pl
from jax.experimental.pallas import tpu as pltpu
from jax.sharding import PartitionSpec as P

BLOCK = 128
REACH = 4
SUM_FLOPS = 10**9
SRC_UNIT = 2**16
F32 = jnp.float32
BF16 = jnp.bfloat16
VMEM = pl.BlockSpec(memory_space=pltpu.VMEM)
SMEM = pl.BlockSpec(memory_space=pltpu.SMEM)
HBM = pl.BlockSpec(memory_space=pltpu.HBM)


def call(kernel, out_shape, in_specs, out_specs, scratch=(), flops=0):
    return pl.pallas_call(
        kernel,
        out_shape=out_shape,
        in_specs=in_specs,
        out_specs=out_specs,
        scratch_shapes=list(scratch),
        compiler_params=pltpu.CompilerParams(vmem_limit_bytes=24 * 1024 * 1024),
        cost_estimate=pl.CostEstimate(flops=flops, bytes_accessed=2**20, transcendentals=0),
    )


def groups_at_once(groups):
    return next(m for m in (12, 8, 6, 4, 3, 2, 1) if groups % m == 0)


def in_hbm(a):
    return pltpu.with_memory_space_constraint(a, pltpu.HBM)


def own_core():
    return lax.rem(lax.axis_index("dom"), 2)


def slot_loop(count, groups, body):
    m = groups_at_once(groups)

    def chunk(i, carry):
        @pl.when(i * (m * REACH) < count)
        def _():
            for u in range(m):
                body(i * m + u)

        return carry

    lax.fori_loop(0, groups // m, chunk, 0)


def source(entry):
    return lax.shift_right_logical(entry, 16)


def target(entry, o, blocks):
    return lax.bitwise_and(entry, SRC_UNIT - 1) - o * blocks


def push(xt, tiles, index, count, acc, j, o):
    blocks = xt.shape[0]
    k = j * REACH + o
    entry = index[k]
    out = lax.dot_general(xt[source(entry)], tiles[j], (((1,), (1,)), ((), ())), preferred_element_type=F32)
    acc[jnp.where(k < count, target(entry, o, blocks), blocks)] += out


def pull(block, tiles, index, count, acc, j, o):
    blocks = acc.shape[0] - 1
    k = j * REACH + o
    entry = index[k]
    out = jnp.dot(block(target(entry, o, blocks)), tiles[j], preferred_element_type=F32)
    acc[jnp.where(k < count, source(entry), blocks)] += out


def push_all(xt, index, count, *planes):
    def body(j):
        for tiles, acc, o in planes:
            push(xt, tiles, index, count, acc, j, o)

    slot_loop(count, planes[0][0].shape[0], body)


def pull_all(index, count, *planes):
    def body(j):
        for block, tiles, acc, o in planes:
            pull(block, tiles, index, count, acc, j, o)

    slot_loop(count, planes[0][1].shape[0], body)


def unit(n):
    shape = (n, n)
    return (lax.broadcasted_iota(jnp.int32, shape, 0) == lax.broadcasted_iota(jnp.int32, shape, 1)).astype(BF16)


def turned(block):
    n = block.shape[1]
    return lax.dot_general(
        unit(n), block, (((1,), (1,)), ((), ())), preferred_element_type=F32
    ).astype(BF16)


def forward_swap_kernel(
    count, src_hbm, dst_hbm, x_hbm, tiles_hbm, tiles1, tiles2, tiles3, xt, swap, index, src, dst, x, acc, sems
):
    blocks = xt.shape[0]
    o = 3 - 2 * own_core()
    loads = [
        pltpu.make_async_copy(a, b, sems.at[i])
        for i, (a, b) in enumerate(
            (
                (src_hbm, src),
                (dst_hbm, dst),
                (x_hbm, x),
                (tiles_hbm.at[:, o], tiles1),
                (tiles_hbm.at[:, 2], tiles2),
                (tiles_hbm.at[:, 4 - o], tiles3),
            )
        )
    ]
    for c in loads:
        c.start()
    acc[...] = jnp.zeros_like(acc)
    for c in loads[:2]:
        c.wait()
    for k in range(src.shape[0]):
        index[k] = src[k] * SRC_UNIT + dst[k]
    loads[2].wait()
    for b in range(blocks):
        xt[b] = turned(x[b * BLOCK : (b + 1) * BLOCK, :])
    loads[3].wait()
    push_all(xt, index, count[0], (tiles1, acc, o))
    swap[...] = acc[:blocks].astype(BF16)
    for c in loads[4:]:
        c.wait()


def forward_send_kernel(count, index, xt, tiles2, tiles3, acc2, *refs):
    direct, acc = refs[:-1], refs[-1]
    acc2[...] = jnp.zeros_like(acc2)
    acc[...] = jnp.zeros_like(acc)
    push_all(xt, index, count[0], (tiles2, acc2, 2), (tiles3, acc, 1 + 2 * own_core()))
    first = 0
    for d in direct:
        d[...] = acc[first : first + d.shape[0]].astype(BF16)
        first += d.shape[0]


def forward_own_kernel(
    count, index, xt, bias_ref, w_ref, og_hbm, tiles_hbm, acc, tiles0, bias_t, w_t, og_t, og_ref, sems
):
    load_og = pltpu.make_async_copy(og_hbm, og_ref, sems.at[0])
    load_og.start()
    load = pltpu.make_async_copy(tiles_hbm.at[:, 0], tiles0, sems.at[1])
    load.start()
    acc[...] = jnp.zeros_like(acc)
    bias_t[...] = jnp.broadcast_to(bias_ref[...], (BLOCK, bias_ref.shape[1])).T
    w_t[...] = turned(w_ref[...])
    load_og.wait()
    for first in range(0, og_ref.shape[0], BLOCK):
        og_t[:, first : first + BLOCK] = turned(og_ref[first : first + BLOCK, :])
    load.wait()
    push_all(xt, index, count[0], (tiles0, acc, 0))


def sum_kernel(n, first, *refs):
    for out in refs[n:]:
        blocks = out.shape[0]
        total = None
        for r in refs[:n]:
            part = r[...] if r.shape[0] == blocks else r[first : first + blocks]
            total = part.astype(F32) if total is None else total + part.astype(F32)
        out[...] = total.astype(out.dtype)
        first += blocks


def join_kernel(parts, *refs):
    out = refs[-1]
    halves = [refs[i : i + parts] for i in range(0, len(refs) - 1, parts)]
    first = 0
    for half in halves:
        blocks = half[0].shape[0]
        total = half[0][...].astype(F32)
        for r in half[1:]:
            total = total + r[...].astype(F32)
        out[first : first + blocks] = total.astype(out.dtype)
        first += blocks


def middle_kernel(parts, first, bias_ref, w_ref, w_t_ref, og_ref, h_ref, act, ht, grads, *g_refs):
    blocks, f_in, _ = h_ref.shape
    width = f_in // parts
    me = lax.axis_index("feat")
    rows = [pl.multiple_of(lax.rem(me + q, parts) * width, width) for q in range(parts)]
    for b in range(blocks):
        ht[:f_in, b * BLOCK : (b + 1) * BLOCK] = h_ref[b]
    ht[f_in:, :] = jnp.ones((ht.shape[0] - f_in, ht.shape[1]), BF16)
    for b in range(blocks):
        cols = slice(b * BLOCK, (b + 1) * BLOCK)
        pre = jnp.dot(w_t_ref[...], h_ref[b], preferred_element_type=F32) + bias_ref[...]
        s = jax.nn.sigmoid(pre)
        act[:, cols] = (pre * s).astype(BF16)
        og = og_ref[:, (first + b) * BLOCK : (first + b + 1) * BLOCK].astype(F32)
        grad = (og * s * (1.0 + pre * (1.0 - s))).astype(BF16)
        grads[:, cols] = grad
        for q in range(parts):
            g_refs[q][b] = jnp.dot(
                w_ref[pl.ds(rows[q], width), :], grad, preferred_element_type=F32
            ).astype(g_refs[q].dtype)


def weight_grad_kernel(n, *refs):
    hts, grads, (mine, other) = refs[:n], refs[n : 2 * n], refs[2 * n :]
    full = sum(
        lax.dot_general(h[...], g[...], (((1,), (1,)), ((), ())), preferred_element_type=F32)
        for h, g in zip(hts, grads)
    )
    full = full.astype(BF16)
    rows = mine.shape[0]
    low, high = full[:rows], full[rows:]
    first = own_core() == 0
    mine[...] = jnp.where(first, low, high)
    other[...] = jnp.where(first, high, low)


def swap_payload_kernel(g, *refs):
    parts, out = refs[:-1], refs[-1]
    blocks, width, _ = g.shape
    for b in range(blocks):
        out[b * width : (b + 1) * width, :] = g[b]
    total = paired_sum([r[...] for r in parts]).astype(BF16)
    rows, hid = total.shape
    if hid < out.shape[1]:
        out[blocks * width :, :] = jnp.zeros((rows, out.shape[1]), BF16)
    out[blocks * width :, :hid] = total


def backward_own_kernel(count, index, tiles, g, *refs):
    acts, (acc, out, rows, sems) = refs[:-4], refs[-4:]
    copies, first = [], 0
    for i, act in enumerate(acts):
        for col in range(0, act.shape[1], BLOCK):
            rows[first + col : first + col + BLOCK, :] = turned(act[:, col : col + BLOCK])
        part = pl.ds(first, act.shape[1])
        copies.append(pltpu.make_async_copy(rows.at[part], out.at[part], sems.at[i]))
        copies[-1].start()
        first += act.shape[1]
    acc[...] = jnp.zeros_like(acc)
    pull_all(index, count[0], (lambda d: g[d], tiles, acc, 0))
    for c in copies:
        c.wait()


def backward_near_kernel(count, index, tiles2, tiles3, g2, g3, acc2, acc3):
    acc2[...] = jnp.zeros_like(acc2)
    acc3[...] = jnp.zeros_like(acc3)
    pull_all(
        index,
        count[0],
        (lambda d: g2[d], tiles2, acc2, 2),
        (lambda d: g3[d], tiles3, acc3, 1 + 2 * own_core()),
    )


def backward_last_kernel(count, index, tiles1, sent, got, acc0, acc2, acc3, out, wg, bias, acc1):
    blocks, width = acc1.shape[0] - 1, acc1.shape[1]
    f_in, hid = wg.shape
    acc1[...] = jnp.zeros_like(acc1)
    core = own_core()

    def block(d):
        return got[pl.ds(pl.multiple_of(d * width, width), width), :]

    pull_all(index, count[0], (block, tiles1, acc1, 3 - 2 * core))
    for b in range(blocks):
        total = (acc0[b] + acc2[b]) + (acc1[b] + acc3[b])
        out[:, b * BLOCK : (b + 1) * BLOCK] = total.astype(BF16)
    a, b = (r[blocks * width :, :hid].astype(F32) for r in (sent, got))
    low, high = jnp.where(core == 0, a, b), jnp.where(core == 0, b, a)
    rows = low.shape[0]
    wg[:rows, :] = low
    wg[rows:, :] = high[: f_in - rows]
    bias[...] = high[f_in - rows : f_in - rows + 1]


def paired_sum(parts):
    parts = [p.astype(F32) for p in parts]
    while len(parts) > 1:
        parts = [parts[i] + parts[i + 1] for i in range(0, len(parts), 2)]
    return parts[0]


def paired_sum_kernel(*refs):
    refs[-1][...] = paired_sum([r[...] for r in refs[:-1]]).astype(refs[-1].dtype)


def moved(block, axis, target):
    n = lax.axis_size(axis)
    return lax.ppermute(block, axis, [(i, target(i) % n) for i in range(n)])


def radices(n):
    out = []
    while n > 1:
        r = 4 if n % 4 == 0 else 2
        out.append(r)
        n //= r
    return out


def exchanged(part, axis, stride, r):
    return [part] + [moved(part, axis, lambda i, s=s: i ^ (s * stride)) for s in range(1, r)]


def shards(node_features, weight, bias, tile_values, tile_src, tile_dst, tile_counts, out_grad):
    nodes, f_in = node_features.shape
    hid = weight.shape[1]
    blocks = nodes // BLOCK
    parts = lax.axis_size("feat")
    width = f_in // parts
    capacity = tile_values.shape[0]
    groups = capacity // REACH
    piece = jax.ShapeDtypeStruct((blocks, width, BLOCK), BF16)
    totals = jax.ShapeDtypeStruct((blocks + 1, width, BLOCK), F32)
    piece_x = jax.ShapeDtypeStruct((blocks, f_in, BLOCK), BF16)
    totals_x = jax.ShapeDtypeStruct((blocks + 1, f_in, BLOCK), F32)
    acc_x = pltpu.VMEM(totals_x.shape, F32)
    acc = pltpu.VMEM(totals.shape, F32)
    tiles = tile_values.reshape(groups, REACH, BLOCK, BLOCK)
    plane = jax.ShapeDtypeStruct((groups, BLOCK, BLOCK), BF16)
    slots = jax.ShapeDtypeStruct((capacity,), jnp.int32)
    rows = jax.ShapeDtypeStruct((nodes, hid), BF16)
    gradient = jax.ShapeDtypeStruct(((f_in + 32) // 2, hid), BF16)
    flops = 2 * capacity * BLOCK * BLOCK * width // REACH

    def swapped(i):
        return i ^ 1

    tiles1, tiles2, tiles3, xt, swap, index = call(
        forward_swap_kernel,
        [plane, plane, plane, piece_x, piece_x, slots],
        [SMEM] + [HBM] * 4,
        [VMEM] * 5 + [SMEM],
        [
            pltpu.SMEM((capacity,), jnp.int32),
            pltpu.SMEM((capacity,), jnp.int32),
            pltpu.VMEM(node_features.shape, BF16),
            acc_x,
            pltpu.SemaphoreType.DMA((6,)),
        ],
        flops,
    )(tile_counts, *(in_hbm(a) for a in (tile_src, tile_dst, node_features, tiles)))
    index = (tile_counts, index)
    swap = moved(swap, "dom", swapped)
    cut = 2 if blocks % 2 == 0 else 1
    starts = range(0, blocks, blocks // cut)
    half = jax.ShapeDtypeStruct((blocks // cut, width, BLOCK), BF16)
    half_x = jax.ShapeDtypeStruct((blocks // cut, f_in, BLOCK), BF16)
    half_wide = jax.ShapeDtypeStruct(half.shape, F32)
    half_rows = jax.ShapeDtypeStruct((hid, nodes // cut), BF16)
    half_columns = jax.ShapeDtypeStruct((f_in + 32, nodes // cut), BF16)
    acc2, *direct = call(
        forward_send_kernel,
        [totals_x] + [half_x] * cut,
        [SMEM] * 2 + [VMEM] * 3,
        [VMEM] * (1 + cut),
        [acc_x],
        2 * flops,
    )(*index, xt, tiles2, tiles3)
    chip = call(functools.partial(sum_kernel, 2, 0), [half_x] * cut, [VMEM] * 2, [VMEM] * cut)(acc2, swap)
    chip = lax.optimization_barrier((*chip, *direct[1:]))
    direct, chip = [direct[0], *chip[cut:]], chip[:cut]
    chip = [moved(c, "dom", lambda i: i + 2) for c in chip]
    acc0, tiles0, bias_t, w_t, og_t = call(
        forward_own_kernel,
        [
            totals_x,
            plane,
            jax.ShapeDtypeStruct((hid, BLOCK), F32),
            jax.ShapeDtypeStruct((hid, f_in), BF16),
            jax.ShapeDtypeStruct((hid, nodes), BF16),
        ],
        [SMEM] * 2 + [VMEM] * 3 + [HBM] * 2,
        [VMEM] * 5,
        [pltpu.VMEM(out_grad.shape, BF16), pltpu.SemaphoreType.DMA((2,))],
        flops,
    )(*index, xt, bias.reshape(1, hid), weight, in_hbm(out_grad), in_hbm(tiles))
    direct = [moved(d, "dom", lambda i: i + 1 + 2 * (i % 2)) for d in direct]
    h_list = []
    for first, c, d in zip(starts, chip, direct):
        (h,) = call(functools.partial(sum_kernel, 3, first), [half_x], [VMEM] * 3, [VMEM])(acc0, d, c)
        h_list.append(h)
    acts, hts, grads, g_list = [], [], [], []
    for first, h in zip(starts, h_list):
        act, ht, grad, g_own, *g_others = call(
            functools.partial(middle_kernel, parts, first),
            [half_rows, half_columns, half_rows, half_wide] + [half] * (parts - 1),
            [VMEM] * 5,
            [VMEM] * (3 + parts),
            (),
            4 * nodes * f_in * hid // cut,
        )(bias_t, weight, w_t, og_t, h)
        acts.append(act)
        hts.append(ht)
        grads.append(grad)
        g_list += [g_own] + [moved(g, "feat", lambda i, q=q + 1: i + q) for q, g in enumerate(g_others)]
    wg, wg_other = call(
        functools.partial(weight_grad_kernel, cut),
        [gradient, gradient],
        [VMEM] * (2 * cut),
        [VMEM, VMEM],
        (),
        2 * nodes * f_in * hid,
    )(*hts, *grads)
    r, *more = radices(lax.axis_size("dom"))
    wgs = [wg] + [moved(wg_other if s % 2 else wg, "dom", lambda i, s=s: i ^ s) for s in range(1, r)]
    (g,) = call(functools.partial(join_kernel, parts), [piece], [VMEM] * len(g_list), [VMEM])(*g_list)
    g_chip = moved(g, "dom", lambda i: i - 2)
    g_direct = moved(g, "dom", lambda i: i - 3 + 2 * (i % 2))
    stride = r
    for r in more:
        (wg,) = call(paired_sum_kernel, [gradient], [VMEM] * len(wgs), [VMEM], (), SUM_FLOPS)(*wgs)
        wgs = exchanged(wg, "dom", stride, r)
        stride *= r
    back0, output = call(
        backward_own_kernel,
        [totals, rows],
        [SMEM] * 2 + [VMEM] * (2 + cut),
        [VMEM, HBM],
        [pltpu.VMEM(rows.shape, BF16), pltpu.SemaphoreType.DMA((cut,))],
        flops,
    )(*index, tiles0, g, *acts)
    g_direct, g_chip, back0, *wgs = lax.optimization_barrier((g_direct, g_chip, back0, *wgs))
    payload = jax.ShapeDtypeStruct((blocks * width + gradient.shape[0], BLOCK), BF16)
    (sent,) = call(swap_payload_kernel, [payload], [VMEM] * (1 + len(wgs)), [VMEM])(g_chip, *wgs)
    got = moved(sent, "dom", swapped)
    back2, back3 = call(
        backward_near_kernel, [totals, totals], [SMEM] * 2 + [VMEM] * 4, [VMEM] * 2, (), 2 * flops
    )(*index, tiles2, tiles3, g_chip, g_direct)
    input_grad, weight_grad, bias_grad = call(
        backward_last_kernel,
        [
            jax.ShapeDtypeStruct((width, nodes), BF16),
            jax.ShapeDtypeStruct((f_in, hid), F32),
            jax.ShapeDtypeStruct((1, hid), F32),
        ],
        [SMEM] * 2 + [VMEM] * 6,
        [VMEM] * 3,
        [acc],
        flops,
    )(*index, tiles1, sent, got, back0, back2, back3)
    return output, weight_grad, bias_grad.reshape(hid), input_grad.T


def solution(mesh):
    return jax.shard_map(
        shards,
        mesh=mesh,
        in_specs=(
            P("dom", None),
            P(None, "feat"),
            P("feat"),
            P("dom", None, None),
            P("dom"),
            P("dom"),
            P("dom"),
            P("dom", "feat"),
        ),
        out_specs=(P("dom", "feat"), P(None, "feat"), P("feat"), P("dom", "feat")),
        check_vma=False,
    )
```

```python
import functools

import jax
import jax.numpy as jnp
from jax import lax
from jax.experimental import pallas as pl
from jax.experimental.pallas import tpu as pltpu
from jax.sharding import PartitionSpec as P

BLOCK = 128
REACH = 4
SUM_FLOPS = 10**9
SRC_UNIT = 2**16
F32 = jnp.float32
BF16 = jnp.bfloat16
VMEM = pl.BlockSpec(memory_space=pltpu.VMEM)
SMEM = pl.BlockSpec(memory_space=pltpu.SMEM)
HBM = pl.BlockSpec(memory_space=pltpu.HBM)


def call(kernel, out_shape, in_specs, out_specs, scratch=(), flops=0, aliases=None):
    return pl.pallas_call(
        kernel,
        out_shape=out_shape,
        in_specs=in_specs,
        out_specs=out_specs,
        scratch_shapes=list(scratch),
        input_output_aliases=aliases or {},
        compiler_params=pltpu.CompilerParams(vmem_limit_bytes=24 * 1024 * 1024),
        cost_estimate=pl.CostEstimate(flops=flops, bytes_accessed=2**20, transcendentals=0),
    )


def groups_at_once(groups):
    return next(m for m in (12, 8, 6, 4, 3, 2, 1) if groups % m == 0)


def in_hbm(a):
    return pltpu.with_memory_space_constraint(a, pltpu.HBM)


def own_core():
    return lax.rem(lax.axis_index("dom"), 2)


def slot_loop(count, groups, body):
    m = groups_at_once(groups)

    def chunk(i, carry):
        @pl.when(i * (m * REACH) < count)
        def _():
            for u in range(m):
                body(i * m + u)

        return carry

    lax.fori_loop(0, groups // m, chunk, 0)


def source(entry):
    return lax.shift_right_logical(entry, 16)


def target(entry, o, blocks):
    return lax.bitwise_and(entry, SRC_UNIT - 1) - o * blocks


def push(xt, tiles, index, count, acc, j, o):
    blocks = xt.shape[0]
    k = j * REACH + o
    entry = index[k]
    out = lax.dot_general(xt[source(entry)], tiles[j], (((1,), (1,)), ((), ())), preferred_element_type=F32)
    acc[jnp.where(k < count, target(entry, o, blocks), blocks)] += out


def pull(block, tiles, index, count, acc, j, o):
    blocks = acc.shape[0] - 1
    k = j * REACH + o
    entry = index[k]
    out = jnp.dot(block(target(entry, o, blocks)), tiles[j], preferred_element_type=F32)
    acc[jnp.where(k < count, source(entry), blocks)] += out


def push_all(xt, index, count, *planes):
    def body(j):
        for tiles, acc, o in planes:
            push(xt, tiles, index, count, acc, j, o)

    slot_loop(count, planes[0][0].shape[0], body)


def pull_all(index, count, *planes):
    def body(j):
        for block, tiles, acc, o in planes:
            pull(block, tiles, index, count, acc, j, o)

    slot_loop(count, planes[0][1].shape[0], body)


def unit(n):
    shape = (n, n)
    return (lax.broadcasted_iota(jnp.int32, shape, 0) == lax.broadcasted_iota(jnp.int32, shape, 1)).astype(BF16)


def turned(block):
    n = block.shape[1]
    return lax.dot_general(
        unit(n), block, (((1,), (1,)), ((), ())), preferred_element_type=F32
    ).astype(BF16)


def forward_swap_kernel(
    count, src_hbm, dst_hbm, x_hbm, tiles_hbm, tiles1, tiles2, tiles3, xt, swap, index, src, dst, x, acc, sems
):
    blocks = xt.shape[0]
    o = 3 - 2 * own_core()
    loads = [
        pltpu.make_async_copy(a, b, sems.at[i])
        for i, (a, b) in enumerate(
            (
                (src_hbm, src),
                (dst_hbm, dst),
                (x_hbm, x),
                (tiles_hbm.at[:, o], tiles1),
                (tiles_hbm.at[:, 2], tiles2),
                (tiles_hbm.at[:, 4 - o], tiles3),
            )
        )
    ]
    for c in loads:
        c.start()
    acc[...] = jnp.zeros_like(acc)
    for c in loads[:2]:
        c.wait()
    for k in range(src.shape[0]):
        index[k] = src[k] * SRC_UNIT + dst[k]
    loads[2].wait()
    for b in range(blocks):
        xt[b] = turned(x[b * BLOCK : (b + 1) * BLOCK, :])
    loads[3].wait()
    push_all(xt, index, count[0], (tiles1, acc, o))
    swap[...] = acc[:blocks].astype(BF16)
    for c in loads[4:]:
        c.wait()


def forward_send_kernel(count, index, xt, tiles2, tiles3, acc2, *refs):
    direct, acc = refs[:-1], refs[-1]
    acc2[...] = jnp.zeros_like(acc2)
    acc[...] = jnp.zeros_like(acc)
    push_all(xt, index, count[0], (tiles2, acc2, 2), (tiles3, acc, 1 + 2 * own_core()))
    first = 0
    for d in direct:
        d[...] = acc[first : first + d.shape[0]].astype(BF16)
        first += d.shape[0]


def forward_own_kernel(
    count, index, xt, bias_ref, w_ref, og_hbm, tiles_hbm, acc, tiles0, bias_t, w_t, og_t, og_ref, sems
):
    load_og = pltpu.make_async_copy(og_hbm, og_ref, sems.at[0])
    load_og.start()
    load = pltpu.make_async_copy(tiles_hbm.at[:, 0], tiles0, sems.at[1])
    load.start()
    acc[...] = jnp.zeros_like(acc)
    bias_t[...] = jnp.broadcast_to(bias_ref[...], (BLOCK, bias_ref.shape[1])).T
    w_t[...] = turned(w_ref[...])
    load_og.wait()
    for first in range(0, og_ref.shape[0], BLOCK):
        og_t[:, first : first + BLOCK] = turned(og_ref[first : first + BLOCK, :])
    load.wait()
    push_all(xt, index, count[0], (tiles0, acc, 0))


def sum_kernel(n, first, *refs):
    for out in refs[n:]:
        blocks = out.shape[0]
        total = None
        for r in refs[:n]:
            part = r[...] if r.shape[0] == blocks else r[first : first + blocks]
            total = part.astype(F32) if total is None else total + part.astype(F32)
        out[...] = total.astype(out.dtype)
        first += blocks


def join_kernel(parts, *refs):
    out = refs[-1]
    halves = [refs[i : i + parts] for i in range(0, len(refs) - 1, parts)]
    first = 0
    for half in halves:
        blocks = half[0].shape[0]
        total = half[0][...].astype(F32)
        for r in half[1:]:
            total = total + r[...].astype(F32)
        out[first : first + blocks] = total.astype(out.dtype)
        first += blocks


def middle_kernel(parts, first, bias_ref, w_ref, w_t_ref, og_ref, h_ref, act, ht, grads, *g_refs):
    blocks, f_in, _ = h_ref.shape
    width = f_in // parts
    me = lax.axis_index("feat")
    rows = [pl.multiple_of(lax.rem(me + q, parts) * width, width) for q in range(parts)]
    for b in range(blocks):
        ht[:f_in, b * BLOCK : (b + 1) * BLOCK] = h_ref[b]
    ht[f_in:, :] = jnp.ones((ht.shape[0] - f_in, ht.shape[1]), BF16)
    for b in range(blocks):
        cols = slice(b * BLOCK, (b + 1) * BLOCK)
        pre = jnp.dot(w_t_ref[...], h_ref[b], preferred_element_type=F32) + bias_ref[...]
        s = jax.nn.sigmoid(pre)
        act[:, cols] = (pre * s).astype(BF16)
        og = og_ref[:, (first + b) * BLOCK : (first + b + 1) * BLOCK].astype(F32)
        grad = (og * s * (1.0 + pre * (1.0 - s))).astype(BF16)
        grads[:, cols] = grad
        for q in range(parts):
            g_refs[q][b] = jnp.dot(
                w_ref[pl.ds(rows[q], width), :], grad, preferred_element_type=F32
            ).astype(g_refs[q].dtype)


def weight_grad_kernel(n, *refs):
    hts, grads, (mine, other) = refs[:n], refs[n : 2 * n], refs[2 * n :]
    full = sum(
        lax.dot_general(h[...], g[...], (((1,), (1,)), ((), ())), preferred_element_type=F32)
        for h, g in zip(hts, grads)
    )
    full = full.astype(BF16)
    rows = mine.shape[0]
    low, high = full[:rows], full[rows:]
    first = own_core() == 0
    mine[...] = jnp.where(first, low, high)
    other[...] = jnp.where(first, high, low)


def swap_payload_kernel(g, *refs):
    parts, out = refs[:-1], refs[-1]
    blocks, width, _ = g.shape
    for b in range(blocks):
        out[b * width : (b + 1) * width, :] = g[b]
    total = paired_sum([r[...] for r in parts]).astype(BF16)
    rows, hid = total.shape
    if hid < out.shape[1]:
        out[blocks * width :, :] = jnp.zeros((rows, out.shape[1]), BF16)
    out[blocks * width :, :hid] = total


def turned_rows(act, rows, out, first, sem):
    for col in range(0, act.shape[1], BLOCK):
        rows[col : col + BLOCK, :] = turned(act[:, col : col + BLOCK])
    copy = pltpu.make_async_copy(rows, out.at[pl.ds(first, act.shape[1])], sem)
    copy.start()
    return copy


def activation_kernel(first, act, out, rows, sem):
    turned_rows(act, rows, out, first, sem).wait()


def backward_own_kernel(count, index, tiles, g, act, out_before, acc, out, rows, sem):
    copy = turned_rows(act, rows, out, 0, sem)
    acc[...] = jnp.zeros_like(acc)
    pull_all(index, count[0], (lambda d: g[d], tiles, acc, 0))
    copy.wait()


def backward_near_kernel(count, index, tiles2, tiles3, g2, g3, acc2, acc3):
    acc2[...] = jnp.zeros_like(acc2)
    acc3[...] = jnp.zeros_like(acc3)
    pull_all(
        index,
        count[0],
        (lambda d: g2[d], tiles2, acc2, 2),
        (lambda d: g3[d], tiles3, acc3, 1 + 2 * own_core()),
    )


def backward_last_kernel(count, index, tiles1, sent, got, acc0, acc2, acc3, out, wg, bias, acc1):
    blocks, width = acc1.shape[0] - 1, acc1.shape[1]
    f_in, hid = wg.shape
    acc1[...] = jnp.zeros_like(acc1)
    core = own_core()

    def block(d):
        return got[pl.ds(pl.multiple_of(d * width, width), width), :]

    pull_all(index, count[0], (block, tiles1, acc1, 3 - 2 * core))
    for b in range(blocks):
        total = (acc0[b] + acc2[b]) + (acc1[b] + acc3[b])
        out[:, b * BLOCK : (b + 1) * BLOCK] = total.astype(BF16)
    a, b = (r[blocks * width :, :hid].astype(F32) for r in (sent, got))
    low, high = jnp.where(core == 0, a, b), jnp.where(core == 0, b, a)
    rows = low.shape[0]
    wg[:rows, :] = low
    wg[rows:, :] = high[: f_in - rows]
    bias[...] = high[f_in - rows : f_in - rows + 1]


def paired_sum(parts):
    parts = [p.astype(F32) for p in parts]
    while len(parts) > 1:
        parts = [parts[i] + parts[i + 1] for i in range(0, len(parts), 2)]
    return parts[0]


def paired_sum_kernel(*refs):
    refs[-1][...] = paired_sum([r[...] for r in refs[:-1]]).astype(refs[-1].dtype)


def moved(block, axis, target):
    n = lax.axis_size(axis)
    return lax.ppermute(block, axis, [(i, target(i) % n) for i in range(n)])


def radices(n):
    out = []
    while n > 1:
        r = 4 if n % 4 == 0 else 2
        out.append(r)
        n //= r
    return out


def exchanged(part, axis, stride, r):
    return [part] + [moved(part, axis, lambda i, s=s: i ^ (s * stride)) for s in range(1, r)]


def shards(node_features, weight, bias, tile_values, tile_src, tile_dst, tile_counts, out_grad):
    nodes, f_in = node_features.shape
    hid = weight.shape[1]
    blocks = nodes // BLOCK
    parts = lax.axis_size("feat")
    width = f_in // parts
    capacity = tile_values.shape[0]
    groups = capacity // REACH
    piece = jax.ShapeDtypeStruct((blocks, width, BLOCK), BF16)
    totals = jax.ShapeDtypeStruct((blocks + 1, width, BLOCK), F32)
    piece_x = jax.ShapeDtypeStruct((blocks, f_in, BLOCK), BF16)
    totals_x = jax.ShapeDtypeStruct((blocks + 1, f_in, BLOCK), F32)
    acc_x = pltpu.VMEM(totals_x.shape, F32)
    acc = pltpu.VMEM(totals.shape, F32)
    tiles = tile_values.reshape(groups, REACH, BLOCK, BLOCK)
    plane = jax.ShapeDtypeStruct((groups, BLOCK, BLOCK), BF16)
    slots = jax.ShapeDtypeStruct((capacity,), jnp.int32)
    rows = jax.ShapeDtypeStruct((nodes, hid), BF16)
    gradient = jax.ShapeDtypeStruct(((f_in + 32) // 2, hid), BF16)
    flops = 2 * capacity * BLOCK * BLOCK * width // REACH

    def swapped(i):
        return i ^ 1

    tiles1, tiles2, tiles3, xt, swap, index = call(
        forward_swap_kernel,
        [plane, plane, plane, piece_x, piece_x, slots],
        [SMEM] + [HBM] * 4,
        [VMEM] * 5 + [SMEM],
        [
            pltpu.SMEM((capacity,), jnp.int32),
            pltpu.SMEM((capacity,), jnp.int32),
            pltpu.VMEM(node_features.shape, BF16),
            acc_x,
            pltpu.SemaphoreType.DMA((6,)),
        ],
        flops,
    )(tile_counts, *(in_hbm(a) for a in (tile_src, tile_dst, node_features, tiles)))
    index = (tile_counts, index)
    swap = moved(swap, "dom", swapped)
    cut = 2
    sizes = (blocks * 3 // 8, blocks - blocks * 3 // 8)
    starts = (0, sizes[0])
    half = [jax.ShapeDtypeStruct((n, width, BLOCK), BF16) for n in sizes]
    half_x = [jax.ShapeDtypeStruct((n, f_in, BLOCK), BF16) for n in sizes]
    half_wide = [jax.ShapeDtypeStruct((n, width, BLOCK), F32) for n in sizes]
    half_rows = [jax.ShapeDtypeStruct((hid, n * BLOCK), BF16) for n in sizes]
    half_columns = [jax.ShapeDtypeStruct((f_in + 32, n * BLOCK), BF16) for n in sizes]
    acc2, *direct = call(
        forward_send_kernel,
        [totals_x] + half_x,
        [SMEM] * 2 + [VMEM] * 3,
        [VMEM] * (1 + cut),
        [acc_x],
        2 * flops,
    )(*index, xt, tiles2, tiles3)
    chip = call(functools.partial(sum_kernel, 2, 0), half_x, [VMEM] * 2, [VMEM] * cut)(acc2, swap)
    chip = lax.optimization_barrier((*chip, *direct[1:]))
    direct, chip = [direct[0], *chip[cut:]], chip[:cut]
    chip = [moved(c, "dom", lambda i: i + 2) for c in chip]
    acc0, tiles0, bias_t, w_t, og_t = call(
        forward_own_kernel,
        [
            totals_x,
            plane,
            jax.ShapeDtypeStruct((hid, BLOCK), F32),
            jax.ShapeDtypeStruct((hid, f_in), BF16),
            jax.ShapeDtypeStruct((hid, nodes), BF16),
        ],
        [SMEM] * 2 + [VMEM] * 3 + [HBM] * 2,
        [VMEM] * 5,
        [pltpu.VMEM(out_grad.shape, BF16), pltpu.SemaphoreType.DMA((2,))],
        flops,
    )(*index, xt, bias.reshape(1, hid), weight, in_hbm(out_grad), in_hbm(tiles))
    direct = [moved(d, "dom", lambda i: i + 1 + 2 * (i % 2)) for d in direct]
    halves = [None, None]
    for i in (1, 0):
        (h,) = call(functools.partial(sum_kernel, 3, starts[i]), [half_x[i]], [VMEM] * 3, [VMEM])(
            acc0, direct[i], chip[i]
        )
        halves[i] = call(
            functools.partial(middle_kernel, parts, starts[i]),
            [half_rows[i], half_columns[i], half_rows[i], half_wide[i]] + [half[i]] * (parts - 1),
            [VMEM] * 5,
            [VMEM] * (3 + parts),
            (),
            4 * sizes[i] * BLOCK * f_in * hid,
        )(bias_t, weight, w_t, og_t, h)
        if i == 1:
            (output,) = call(
                functools.partial(activation_kernel, starts[1] * BLOCK),
                [rows],
                [VMEM],
                [HBM],
                [pltpu.VMEM((sizes[1] * BLOCK, hid), BF16), pltpu.SemaphoreType.DMA],
            )(halves[1][0])
            acc0, output = lax.optimization_barrier((acc0, output))
    acts, hts, grads, *_ = zip(*halves)
    g_list = []
    for _, _, _, g_own, *g_others in halves:
        g_list += [g_own] + [moved(g, "feat", lambda i, q=q + 1: i + q) for q, g in enumerate(g_others)]
    wg, wg_other = call(
        functools.partial(weight_grad_kernel, cut),
        [gradient, gradient],
        [VMEM] * (2 * cut),
        [VMEM, VMEM],
        (),
        2 * nodes * f_in * hid,
    )(*hts, *grads)
    r, *more = radices(lax.axis_size("dom"))
    wgs = [wg] + [moved(wg_other if s % 2 else wg, "dom", lambda i, s=s: i ^ s) for s in range(1, r)]
    (g,) = call(functools.partial(join_kernel, parts), [piece], [VMEM] * len(g_list), [VMEM])(*g_list)
    g_chip = moved(g, "dom", lambda i: i - 2)
    g_direct = moved(g, "dom", lambda i: i - 3 + 2 * (i % 2))
    stride = r
    for r in more:
        (wg,) = call(paired_sum_kernel, [gradient], [VMEM] * len(wgs), [VMEM], (), SUM_FLOPS)(*wgs)
        wgs = exchanged(wg, "dom", stride, r)
        stride *= r
    back0, output = call(
        backward_own_kernel,
        [totals, rows],
        [SMEM] * 2 + [VMEM] * 3 + [HBM],
        [VMEM, HBM],
        [pltpu.VMEM((sizes[0] * BLOCK, hid), BF16), pltpu.SemaphoreType.DMA],
        flops,
        {5: 1},
    )(*index, tiles0, g, acts[0], output)
    g_direct, g_chip, back0, *wgs = lax.optimization_barrier((g_direct, g_chip, back0, *wgs))
    payload = jax.ShapeDtypeStruct((blocks * width + gradient.shape[0], BLOCK), BF16)
    (sent,) = call(swap_payload_kernel, [payload], [VMEM] * (1 + len(wgs)), [VMEM])(g_chip, *wgs)
    got = moved(sent, "dom", swapped)
    back2, back3 = call(
        backward_near_kernel, [totals, totals], [SMEM] * 2 + [VMEM] * 4, [VMEM] * 2, (), 2 * flops
    )(*index, tiles2, tiles3, g_chip, g_direct)
    input_grad, weight_grad, bias_grad = call(
        backward_last_kernel,
        [
            jax.ShapeDtypeStruct((width, nodes), BF16),
            jax.ShapeDtypeStruct((f_in, hid), F32),
            jax.ShapeDtypeStruct((1, hid), F32),
        ],
        [SMEM] * 2 + [VMEM] * 6,
        [VMEM] * 3,
        [acc],
        flops,
    )(*index, tiles1, sent, got, back0, back2, back3)
    return output, weight_grad, bias_grad.reshape(hid), input_grad.T


def solution(mesh):
    return jax.shard_map(
        shards,
        mesh=mesh,
        in_specs=(
            P("dom", None),
            P(None, "feat"),
            P("feat"),
            P("dom", None, None),
            P("dom"),
            P("dom"),
            P("dom"),
            P("dom", "feat"),
        ),
        out_specs=(P("dom", "feat"), P(None, "feat"), P("feat"), P("dom", "feat")),
        check_vma=False,
    )
```

```python
import functools

import jax
import jax.numpy as jnp
from jax import lax
from jax.experimental import pallas as pl
from jax.experimental.pallas import tpu as pltpu
from jax.sharding import PartitionSpec as P

BLOCK = 128
REACH = 4
SUM_FLOPS = 10**9
SRC_UNIT = 2**16
F32 = jnp.float32
BF16 = jnp.bfloat16
VMEM = pl.BlockSpec(memory_space=pltpu.VMEM)
SMEM = pl.BlockSpec(memory_space=pltpu.SMEM)
HBM = pl.BlockSpec(memory_space=pltpu.HBM)


def call(kernel, out_shape, in_specs, out_specs, scratch=(), flops=0):
    return pl.pallas_call(
        kernel,
        out_shape=out_shape,
        in_specs=in_specs,
        out_specs=out_specs,
        scratch_shapes=list(scratch),
        compiler_params=pltpu.CompilerParams(vmem_limit_bytes=24 * 1024 * 1024),
        cost_estimate=pl.CostEstimate(flops=flops, bytes_accessed=2**20, transcendentals=0),
    )


def groups_at_once(groups):
    return next(m for m in (12, 8, 6, 4, 3, 2, 1) if groups % m == 0)


def in_hbm(a):
    return pltpu.with_memory_space_constraint(a, pltpu.HBM)


def own_core():
    return lax.rem(lax.axis_index("dom"), 2)


def slot_loop(count, groups, body):
    m = groups_at_once(groups)

    def chunk(i, carry):
        @pl.when(i * (m * REACH) < count)
        def _():
            for u in range(m):
                body(i * m + u)

        return carry

    lax.fori_loop(0, groups // m, chunk, 0)


def source(entry):
    return lax.shift_right_logical(entry, 16)


def target(entry, o, blocks):
    return lax.bitwise_and(entry, SRC_UNIT - 1) - o * blocks


def push(xt, tiles, index, count, acc, j, o):
    blocks = xt.shape[0]
    k = j * REACH + o
    entry = index[k]
    out = lax.dot_general(xt[source(entry)], tiles[j], (((1,), (1,)), ((), ())), preferred_element_type=F32)
    acc[jnp.where(k < count, target(entry, o, blocks), blocks)] += out


def pull(block, tiles, index, count, acc, j, o):
    blocks = acc.shape[0] - 1
    k = j * REACH + o
    entry = index[k]
    out = jnp.dot(block(target(entry, o, blocks)), tiles[j], preferred_element_type=F32)
    acc[jnp.where(k < count, source(entry), blocks)] += out


def push_all(xt, index, count, *planes):
    def body(j):
        for tiles, acc, o in planes:
            push(xt, tiles, index, count, acc, j, o)

    slot_loop(count, planes[0][0].shape[0], body)


def pull_all(index, count, *planes):
    def body(j):
        for block, tiles, acc, o in planes:
            pull(block, tiles, index, count, acc, j, o)

    slot_loop(count, planes[0][1].shape[0], body)


def unit(n):
    shape = (n, n)
    return (lax.broadcasted_iota(jnp.int32, shape, 0) == lax.broadcasted_iota(jnp.int32, shape, 1)).astype(BF16)


def turned(block):
    n = block.shape[1]
    return lax.dot_general(
        unit(n), block, (((1,), (1,)), ((), ())), preferred_element_type=F32
    ).astype(BF16)


def forward_swap_kernel(
    count, src_hbm, dst_hbm, x_hbm, tiles_hbm, tiles1, tiles2, tiles3, xt, swap, index, src, dst, x, acc, sems
):
    blocks = xt.shape[0]
    o = 3 - 2 * own_core()
    loads = [
        pltpu.make_async_copy(a, b, sems.at[i])
        for i, (a, b) in enumerate(
            (
                (src_hbm, src),
                (dst_hbm, dst),
                (x_hbm, x),
                (tiles_hbm.at[:, o], tiles1),
                (tiles_hbm.at[:, 2], tiles2),
                (tiles_hbm.at[:, 4 - o], tiles3),
            )
        )
    ]
    for c in loads:
        c.start()
    acc[...] = jnp.zeros_like(acc)
    for c in loads[:2]:
        c.wait()
    for k in range(src.shape[0]):
        index[k] = src[k] * SRC_UNIT + dst[k]
    loads[2].wait()
    for b in range(blocks):
        xt[b] = turned(x[b * BLOCK : (b + 1) * BLOCK, :])
    loads[3].wait()
    push_all(xt, index, count[0], (tiles1, acc, o))
    swap[...] = acc[:blocks].astype(BF16)
    for c in loads[4:]:
        c.wait()


def forward_send_kernel(count, index, xt, tiles2, tiles3, acc2, *refs):
    direct, acc = refs[:-1], refs[-1]
    acc2[...] = jnp.zeros_like(acc2)
    acc[...] = jnp.zeros_like(acc)
    push_all(xt, index, count[0], (tiles2, acc2, 2), (tiles3, acc, 1 + 2 * own_core()))
    first = 0
    for d in direct:
        d[...] = acc[first : first + d.shape[0]].astype(BF16)
        first += d.shape[0]


def forward_own_kernel(
    count, index, xt, bias_ref, w_ref, og_hbm, tiles_hbm, acc, tiles0, bias_t, w_t, og_t, og_ref, sems
):
    load_og = pltpu.make_async_copy(og_hbm, og_ref, sems.at[0])
    load_og.start()
    load = pltpu.make_async_copy(tiles_hbm.at[:, 0], tiles0, sems.at[1])
    load.start()
    acc[...] = jnp.zeros_like(acc)
    bias_t[...] = jnp.broadcast_to(bias_ref[...], (BLOCK, bias_ref.shape[1])).T
    w_t[...] = turned(w_ref[...])
    load_og.wait()
    for first in range(0, og_ref.shape[0], BLOCK):
        og_t[:, first : first + BLOCK] = turned(og_ref[first : first + BLOCK, :])
    load.wait()
    push_all(xt, index, count[0], (tiles0, acc, 0))


def sum_kernel(n, first, *refs):
    for out in refs[n:]:
        blocks = out.shape[0]
        total = None
        for r in refs[:n]:
            part = r[...] if r.shape[0] == blocks else r[first : first + blocks]
            total = part.astype(F32) if total is None else total + part.astype(F32)
        out[...] = total.astype(out.dtype)
        first += blocks


def join_kernel(parts, *refs):
    out = refs[-1]
    halves = [refs[i : i + parts] for i in range(0, len(refs) - 1, parts)]
    first = 0
    for half in halves:
        blocks = half[0].shape[0]
        total = half[0][...].astype(F32)
        for r in half[1:]:
            total = total + r[...].astype(F32)
        out[first : first + blocks] = total.astype(out.dtype)
        first += blocks


def middle_kernel(parts, first, bias_ref, w_ref, w_t_ref, og_ref, h_ref, act, ht, grads, *g_refs):
    blocks, f_in, _ = h_ref.shape
    width = f_in // parts
    me = lax.axis_index("feat")
    rows = [pl.multiple_of(lax.rem(me + q, parts) * width, width) for q in range(parts)]
    for b in range(blocks):
        ht[:f_in, b * BLOCK : (b + 1) * BLOCK] = h_ref[b]
    ht[f_in:, :] = jnp.ones((ht.shape[0] - f_in, ht.shape[1]), BF16)
    for b in range(blocks):
        cols = slice(b * BLOCK, (b + 1) * BLOCK)
        pre = jnp.dot(w_t_ref[...], h_ref[b], preferred_element_type=F32) + bias_ref[...]
        s = jax.nn.sigmoid(pre)
        act[:, cols] = (pre * s).astype(BF16)
        og = og_ref[:, (first + b) * BLOCK : (first + b + 1) * BLOCK].astype(F32)
        grad = (og * s * (1.0 + pre * (1.0 - s))).astype(BF16)
        grads[:, cols] = grad
        for q in range(parts):
            g_refs[q][b] = jnp.dot(
                w_ref[pl.ds(rows[q], width), :], grad, preferred_element_type=F32
            ).astype(g_refs[q].dtype)


def weight_grad_kernel(n, *refs):
    hts, grads, (mine, other) = refs[:n], refs[n : 2 * n], refs[2 * n :]
    full = sum(
        lax.dot_general(h[...], g[...], (((1,), (1,)), ((), ())), preferred_element_type=F32)
        for h, g in zip(hts, grads)
    )
    full = full.astype(BF16)
    rows = mine.shape[0]
    low, high = full[:rows], full[rows:]
    first = own_core() == 0
    mine[...] = jnp.where(first, low, high)
    other[...] = jnp.where(first, high, low)


def swap_payload_kernel(g, *refs):
    parts, out = refs[:-1], refs[-1]
    blocks, width, _ = g.shape
    for b in range(blocks):
        out[b * width : (b + 1) * width, :] = g[b]
    total = paired_sum([r[...] for r in parts]).astype(BF16)
    rows, hid = total.shape
    if hid < out.shape[1]:
        out[blocks * width :, :] = jnp.zeros((rows, out.shape[1]), BF16)
    out[blocks * width :, :hid] = total


def backward_own_kernel(count, index, tiles, g, *refs):
    acts, (acc, out, rows, sems) = refs[:-4], refs[-4:]
    copies, first = [], 0
    for i, act in enumerate(acts):
        for col in range(0, act.shape[1], BLOCK):
            rows[first + col : first + col + BLOCK, :] = turned(act[:, col : col + BLOCK])
        part = pl.ds(first, act.shape[1])
        copies.append(pltpu.make_async_copy(rows.at[part], out.at[part], sems.at[i]))
        copies[-1].start()
        first += act.shape[1]
    acc[...] = jnp.zeros_like(acc)
    pull_all(index, count[0], (lambda d: g[d], tiles, acc, 0))
    for c in copies:
        c.wait()


def backward_near_kernel(count, index, tiles2, tiles3, g2, g3, acc2, acc3):
    acc2[...] = jnp.zeros_like(acc2)
    acc3[...] = jnp.zeros_like(acc3)
    pull_all(
        index,
        count[0],
        (lambda d: g2[d], tiles2, acc2, 2),
        (lambda d: g3[d], tiles3, acc3, 1 + 2 * own_core()),
    )


def backward_last_kernel(count, index, tiles1, sent, got, acc0, acc2, acc3, out, wg, bias, acc1):
    blocks, width = acc1.shape[0] - 1, acc1.shape[1]
    f_in, hid = wg.shape
    acc1[...] = jnp.zeros_like(acc1)
    core = own_core()

    def block(d):
        return got[pl.ds(pl.multiple_of(d * width, width), width), :]

    pull_all(index, count[0], (block, tiles1, acc1, 3 - 2 * core))
    for b in range(blocks):
        total = (acc0[b] + acc2[b]) + (acc1[b] + acc3[b])
        out[:, b * BLOCK : (b + 1) * BLOCK] = total.astype(BF16)
    a, b = (r[blocks * width :, :hid].astype(F32) for r in (sent, got))
    low, high = jnp.where(core == 0, a, b), jnp.where(core == 0, b, a)
    rows = low.shape[0]
    wg[:rows, :] = low
    wg[rows:, :] = high[: f_in - rows]
    bias[...] = high[f_in - rows : f_in - rows + 1]


def paired_sum(parts):
    parts = [p.astype(F32) for p in parts]
    while len(parts) > 1:
        parts = [parts[i] + parts[i + 1] for i in range(0, len(parts), 2)]
    return parts[0]


def paired_sum_kernel(*refs):
    refs[-1][...] = paired_sum([r[...] for r in refs[:-1]]).astype(refs[-1].dtype)


def moved(block, axis, target):
    n = lax.axis_size(axis)
    return lax.ppermute(block, axis, [(i, target(i) % n) for i in range(n)])


def radices(n):
    out = []
    while n > 1:
        r = 4 if n % 4 == 0 else 2
        out.append(r)
        n //= r
    return out


def exchanged(part, axis, stride, r):
    return [part] + [moved(part, axis, lambda i, s=s: i ^ (s * stride)) for s in range(1, r)]


def shards(node_features, weight, bias, tile_values, tile_src, tile_dst, tile_counts, out_grad):
    nodes, f_in = node_features.shape
    hid = weight.shape[1]
    blocks = nodes // BLOCK
    parts = lax.axis_size("feat")
    width = f_in // parts
    capacity = tile_values.shape[0]
    groups = capacity // REACH
    piece = jax.ShapeDtypeStruct((blocks, width, BLOCK), BF16)
    totals = jax.ShapeDtypeStruct((blocks + 1, width, BLOCK), F32)
    piece_x = jax.ShapeDtypeStruct((blocks, f_in, BLOCK), BF16)
    totals_x = jax.ShapeDtypeStruct((blocks + 1, f_in, BLOCK), F32)
    acc_x = pltpu.VMEM(totals_x.shape, F32)
    acc = pltpu.VMEM(totals.shape, F32)
    tiles = tile_values.reshape(groups, REACH, BLOCK, BLOCK)
    plane = jax.ShapeDtypeStruct((groups, BLOCK, BLOCK), BF16)
    slots = jax.ShapeDtypeStruct((capacity,), jnp.int32)
    rows = jax.ShapeDtypeStruct((nodes, hid), BF16)
    gradient = jax.ShapeDtypeStruct(((f_in + 32) // 2, hid), BF16)
    flops = 2 * capacity * BLOCK * BLOCK * width // REACH

    def swapped(i):
        return i ^ 1

    tiles1, tiles2, tiles3, xt, swap, index = call(
        forward_swap_kernel,
        [plane, plane, plane, piece_x, piece_x, slots],
        [SMEM] + [HBM] * 4,
        [VMEM] * 5 + [SMEM],
        [
            pltpu.SMEM((capacity,), jnp.int32),
            pltpu.SMEM((capacity,), jnp.int32),
            pltpu.VMEM(node_features.shape, BF16),
            acc_x,
            pltpu.SemaphoreType.DMA((6,)),
        ],
        flops,
    )(tile_counts, *(in_hbm(a) for a in (tile_src, tile_dst, node_features, tiles)))
    index = (tile_counts, index)
    swap = moved(swap, "dom", swapped)
    cut = 2 if blocks % 2 == 0 else 1
    starts = range(0, blocks, blocks // cut)
    half = jax.ShapeDtypeStruct((blocks // cut, width, BLOCK), BF16)
    half_x = jax.ShapeDtypeStruct((blocks // cut, f_in, BLOCK), BF16)
    half_wide = jax.ShapeDtypeStruct(half.shape, F32)
    half_rows = jax.ShapeDtypeStruct((hid, nodes // cut), BF16)
    half_columns = jax.ShapeDtypeStruct((f_in + 32, nodes // cut), BF16)
    acc2, *direct = call(
        forward_send_kernel,
        [totals_x] + [half_x] * cut,
        [SMEM] * 2 + [VMEM] * 3,
        [VMEM] * (1 + cut),
        [acc_x],
        2 * flops,
    )(*index, xt, tiles2, tiles3)
    chip = call(functools.partial(sum_kernel, 2, 0), [half_x] * cut, [VMEM] * 2, [VMEM] * cut)(acc2, swap)
    chip = lax.optimization_barrier((*chip, *direct))
    direct, chip = chip[cut:], chip[:cut]
    chip = [moved(c, "dom", lambda i: i + 2) for c in chip]
    acc0, tiles0, bias_t, w_t, og_t = call(
        forward_own_kernel,
        [
            totals_x,
            plane,
            jax.ShapeDtypeStruct((hid, BLOCK), F32),
            jax.ShapeDtypeStruct((hid, f_in), BF16),
            jax.ShapeDtypeStruct((hid, nodes), BF16),
        ],
        [SMEM] * 2 + [VMEM] * 3 + [HBM] * 2,
        [VMEM] * 5,
        [pltpu.VMEM(out_grad.shape, BF16), pltpu.SemaphoreType.DMA((2,))],
        flops,
    )(*index, xt, bias.reshape(1, hid), weight, in_hbm(out_grad), in_hbm(tiles))
    direct = [moved(d, "dom", lambda i: i + 1 + 2 * (i % 2)) for d in direct]
    h_list = []
    for first, c, d in zip(starts, chip, direct):
        (h,) = call(functools.partial(sum_kernel, 3, first), [half_x], [VMEM] * 3, [VMEM])(acc0, c, d)
        h_list.append(h)
    acts, hts, grads, g_list = [], [], [], []
    for first, h in zip(starts, h_list):
        act, ht, grad, g_own, *g_others = call(
            functools.partial(middle_kernel, parts, first),
            [half_rows, half_columns, half_rows, half_wide] + [half] * (parts - 1),
            [VMEM] * 5,
            [VMEM] * (3 + parts),
            (),
            4 * nodes * f_in * hid // cut,
        )(bias_t, weight, w_t, og_t, h)
        acts.append(act)
        hts.append(ht)
        grads.append(grad)
        g_list += [g_own] + [moved(g, "feat", lambda i, q=q + 1: i + q) for q, g in enumerate(g_others)]
    wg, wg_other = call(
        functools.partial(weight_grad_kernel, cut),
        [gradient, gradient],
        [VMEM] * (2 * cut),
        [VMEM, VMEM],
        (),
        2 * nodes * f_in * hid,
    )(*hts, *grads)
    r, *more = radices(lax.axis_size("dom"))
    wgs = [wg] + [moved(wg_other if s % 2 else wg, "dom", lambda i, s=s: i ^ s) for s in range(1, r)]
    (g,) = call(functools.partial(join_kernel, parts), [piece], [VMEM] * len(g_list), [VMEM])(*g_list)
    g_chip = moved(g, "dom", lambda i: i - 2)
    g_direct = moved(g, "dom", lambda i: i - 3 + 2 * (i % 2))
    stride = r
    for r in more:
        (wg,) = call(paired_sum_kernel, [gradient], [VMEM] * len(wgs), [VMEM], (), SUM_FLOPS)(*wgs)
        wgs = exchanged(wg, "dom", stride, r)
        stride *= r
    back0, output = call(
        backward_own_kernel,
        [totals, rows],
        [SMEM] * 2 + [VMEM] * (2 + cut),
        [VMEM, HBM],
        [pltpu.VMEM(rows.shape, BF16), pltpu.SemaphoreType.DMA((cut,))],
        flops,
    )(*index, tiles0, g, *acts)
    g_direct, g_chip, back0, *wgs = lax.optimization_barrier((g_direct, g_chip, back0, *wgs))
    payload = jax.ShapeDtypeStruct((blocks * width + gradient.shape[0], BLOCK), BF16)
    (sent,) = call(swap_payload_kernel, [payload], [VMEM] * (1 + len(wgs)), [VMEM])(g_chip, *wgs)
    got = moved(sent, "dom", swapped)
    back2, back3 = call(
        backward_near_kernel, [totals, totals], [SMEM] * 2 + [VMEM] * 4, [VMEM] * 2, (), 2 * flops
    )(*index, tiles2, tiles3, g_chip, g_direct)
    input_grad, weight_grad, bias_grad = call(
        backward_last_kernel,
        [
            jax.ShapeDtypeStruct((width, nodes), BF16),
            jax.ShapeDtypeStruct((f_in, hid), F32),
            jax.ShapeDtypeStruct((1, hid), F32),
        ],
        [SMEM] * 2 + [VMEM] * 6,
        [VMEM] * 3,
        [acc],
        flops,
    )(*index, tiles1, sent, got, back0, back2, back3)
    return output, weight_grad, bias_grad.reshape(hid), input_grad.T


def solution(mesh):
    return jax.shard_map(
        shards,
        mesh=mesh,
        in_specs=(
            P("dom", None),
            P(None, "feat"),
            P("feat"),
            P("dom", None, None),
            P("dom"),
            P("dom"),
            P("dom"),
            P("dom", "feat"),
        ),
        out_specs=(P("dom", "feat"), P(None, "feat"), P("feat"), P("dom", "feat")),
        check_vma=False,
    )
```

```python
import functools

import jax
import jax.numpy as jnp
from jax import lax
from jax.experimental import pallas as pl
from jax.experimental.pallas import tpu as pltpu
from jax.sharding import PartitionSpec as P

BLOCK = 128
REACH = 4
SUM_FLOPS = 10**9
SRC_UNIT = 2**16
F32 = jnp.float32
BF16 = jnp.bfloat16
VMEM = pl.BlockSpec(memory_space=pltpu.VMEM)
SMEM = pl.BlockSpec(memory_space=pltpu.SMEM)
HBM = pl.BlockSpec(memory_space=pltpu.HBM)


def call(kernel, out_shape, in_specs, out_specs, scratch=(), flops=0):
    return pl.pallas_call(
        kernel,
        out_shape=out_shape,
        in_specs=in_specs,
        out_specs=out_specs,
        scratch_shapes=list(scratch),
        compiler_params=pltpu.CompilerParams(vmem_limit_bytes=24 * 1024 * 1024),
        cost_estimate=pl.CostEstimate(flops=flops, bytes_accessed=2**20, transcendentals=0),
    )


def groups_at_once(groups):
    return next(m for m in (12, 8, 6, 4, 3, 2, 1) if groups % m == 0)


def in_hbm(a):
    return pltpu.with_memory_space_constraint(a, pltpu.HBM)


def own_core():
    return lax.rem(lax.axis_index("dom"), 2)


def slot_loop(count, groups, body):
    m = groups_at_once(groups)

    def chunk(i, carry):
        @pl.when(i * (m * REACH) < count)
        def _():
            for u in range(m):
                body(i * m + u)

        return carry

    lax.fori_loop(0, groups // m, chunk, 0)


def source(entry):
    return lax.shift_right_logical(entry, 16)


def target(entry, o, blocks):
    return lax.bitwise_and(entry, SRC_UNIT - 1) - o * blocks


def push(xt, tiles, index, count, acc, j, o):
    blocks = xt.shape[0]
    k = j * REACH + o
    entry = index[k]
    out = lax.dot_general(xt[source(entry)], tiles[j], (((1,), (1,)), ((), ())), preferred_element_type=F32)
    acc[jnp.where(k < count, target(entry, o, blocks), blocks)] += out


def pull(block, tiles, index, count, acc, j, o):
    blocks = acc.shape[0] - 1
    k = j * REACH + o
    entry = index[k]
    out = jnp.dot(block(target(entry, o, blocks)), tiles[j], preferred_element_type=F32)
    acc[jnp.where(k < count, source(entry), blocks)] += out


def push_all(xt, index, count, *planes):
    def body(j):
        for tiles, acc, o in planes:
            push(xt, tiles, index, count, acc, j, o)

    slot_loop(count, planes[0][0].shape[0], body)


def pull_all(index, count, *planes):
    def body(j):
        for block, tiles, acc, o in planes:
            pull(block, tiles, index, count, acc, j, o)

    slot_loop(count, planes[0][1].shape[0], body)


def unit(n):
    shape = (n, n)
    return (lax.broadcasted_iota(jnp.int32, shape, 0) == lax.broadcasted_iota(jnp.int32, shape, 1)).astype(BF16)


def turned(block):
    n = block.shape[1]
    return lax.dot_general(
        unit(n), block, (((1,), (1,)), ((), ())), preferred_element_type=F32
    ).astype(BF16)


def forward_swap_kernel(
    count, src_hbm, dst_hbm, x_hbm, tiles_hbm, tiles1, tiles2, tiles3, xt, swap, index, src, dst, x, acc, sems
):
    blocks = xt.shape[0]
    o = 3 - 2 * own_core()
    loads = [
        pltpu.make_async_copy(a, b, sems.at[i])
        for i, (a, b) in enumerate(
            (
                (src_hbm, src),
                (dst_hbm, dst),
                (x_hbm, x),
                (tiles_hbm.at[:, o], tiles1),
                (tiles_hbm.at[:, 2], tiles2),
                (tiles_hbm.at[:, 4 - o], tiles3),
            )
        )
    ]
    for c in loads:
        c.start()
    acc[...] = jnp.zeros_like(acc)
    for c in loads[:2]:
        c.wait()
    for k in range(src.shape[0]):
        index[k] = src[k] * SRC_UNIT + dst[k]
    loads[2].wait()
    for b in range(blocks):
        xt[b] = turned(x[b * BLOCK : (b + 1) * BLOCK, :])
    loads[3].wait()
    push_all(xt, index, count[0], (tiles1, acc, o))
    swap[...] = acc[:blocks].astype(BF16)
    for c in loads[4:]:
        c.wait()


def forward_send_kernel(count, index, xt, tiles2, tiles3, acc2, *refs):
    direct, acc = refs[:-1], refs[-1]
    acc2[...] = jnp.zeros_like(acc2)
    acc[...] = jnp.zeros_like(acc)
    push_all(xt, index, count[0], (tiles2, acc2, 2), (tiles3, acc, 1 + 2 * own_core()))
    first = 0
    for d in direct:
        d[...] = acc[first : first + d.shape[0]].astype(BF16)
        first += d.shape[0]


def forward_own_kernel(
    count, index, xt, bias_ref, w_ref, og_hbm, tiles_hbm, acc, tiles0, bias_t, w_t, og_t, og_ref, sems
):
    load_og = pltpu.make_async_copy(og_hbm, og_ref, sems.at[0])
    load_og.start()
    load = pltpu.make_async_copy(tiles_hbm.at[:, 0], tiles0, sems.at[1])
    load.start()
    acc[...] = jnp.zeros_like(acc)
    bias_t[...] = jnp.broadcast_to(bias_ref[...], (BLOCK, bias_ref.shape[1])).T
    w_t[...] = turned(w_ref[...])
    load_og.wait()
    for first in range(0, og_ref.shape[0], BLOCK):
        og_t[:, first : first + BLOCK] = turned(og_ref[first : first + BLOCK, :])
    load.wait()
    push_all(xt, index, count[0], (tiles0, acc, 0))


def sum_kernel(n, first, *refs):
    for out in refs[n:]:
        blocks = out.shape[0]
        total = None
        for r in refs[:n]:
            part = r[...] if r.shape[0] == blocks else r[first : first + blocks]
            total = part.astype(F32) if total is None else total + part.astype(F32)
        out[...] = total.astype(out.dtype)
        first += blocks


def join_kernel(parts, *refs):
    out = refs[-1]
    halves = [refs[i : i + parts] for i in range(0, len(refs) - 1, parts)]
    first = 0
    for half in halves:
        blocks = half[0].shape[0]
        total = half[0][...].astype(F32)
        for r in half[1:]:
            total = total + r[...].astype(F32)
        out[first : first + blocks] = total.astype(out.dtype)
        first += blocks


def middle_kernel(parts, first, bias_ref, w_ref, w_t_ref, og_ref, h_ref, act, ht, grads, *g_refs):
    blocks, f_in, _ = h_ref.shape
    width = f_in // parts
    me = lax.axis_index("feat")
    rows = [pl.multiple_of(lax.rem(me + q, parts) * width, width) for q in range(parts)]
    for b in range(blocks):
        ht[:f_in, b * BLOCK : (b + 1) * BLOCK] = h_ref[b]
    ht[f_in:, :] = jnp.ones((ht.shape[0] - f_in, ht.shape[1]), BF16)
    for b in range(blocks):
        cols = slice(b * BLOCK, (b + 1) * BLOCK)
        pre = jnp.dot(w_t_ref[...], h_ref[b], preferred_element_type=F32) + bias_ref[...]
        s = jax.nn.sigmoid(pre)
        act[:, cols] = (pre * s).astype(BF16)
        og = og_ref[:, (first + b) * BLOCK : (first + b + 1) * BLOCK].astype(F32)
        grad = (og * s * (1.0 + pre * (1.0 - s))).astype(BF16)
        grads[:, cols] = grad
        for q in range(parts):
            g_refs[q][b] = jnp.dot(
                w_ref[pl.ds(rows[q], width), :], grad, preferred_element_type=F32
            ).astype(g_refs[q].dtype)


def weight_grad_kernel(n, *refs):
    hts, grads, (mine, other) = refs[:n], refs[n : 2 * n], refs[2 * n :]
    full = sum(
        lax.dot_general(h[...], g[...], (((1,), (1,)), ((), ())), preferred_element_type=F32)
        for h, g in zip(hts, grads)
    )
    full = full.astype(BF16)
    rows = mine.shape[0]
    low, high = full[:rows], full[rows:]
    first = own_core() == 0
    mine[...] = jnp.where(first, low, high)
    other[...] = jnp.where(first, high, low)


def swap_payload_kernel(g, *refs):
    parts, out = refs[:-1], refs[-1]
    blocks, width, _ = g.shape
    for b in range(blocks):
        out[b * width : (b + 1) * width, :] = g[b]
    total = paired_sum([r[...] for r in parts]).astype(BF16)
    rows, hid = total.shape
    if hid < out.shape[1]:
        out[blocks * width :, :] = jnp.zeros((rows, out.shape[1]), BF16)
    out[blocks * width :, :hid] = total


def backward_own_kernel(count, index, tiles, g, *refs):
    acts, (acc, out, rows, sems) = refs[:-4], refs[-4:]
    copies, first = [], 0
    for i, act in enumerate(acts):
        for col in range(0, act.shape[1], BLOCK):
            rows[first + col : first + col + BLOCK, :] = turned(act[:, col : col + BLOCK])
        part = pl.ds(first, act.shape[1])
        copies.append(pltpu.make_async_copy(rows.at[part], out.at[part], sems.at[i]))
        copies[-1].start()
        first += act.shape[1]
    acc[...] = jnp.zeros_like(acc)
    pull_all(index, count[0], (lambda d: g[d], tiles, acc, 0))
    for c in copies:
        c.wait()


def backward_near_kernel(count, index, tiles2, tiles3, g2, g3, acc2, acc3):
    acc2[...] = jnp.zeros_like(acc2)
    acc3[...] = jnp.zeros_like(acc3)
    pull_all(
        index,
        count[0],
        (lambda d: g2[d], tiles2, acc2, 2),
        (lambda d: g3[d], tiles3, acc3, 1 + 2 * own_core()),
    )


def backward_last_kernel(count, index, tiles1, sent, got, acc0, acc2, acc3, out, wg, bias, acc1):
    blocks, width = acc1.shape[0] - 1, acc1.shape[1]
    f_in, hid = wg.shape
    acc1[...] = jnp.zeros_like(acc1)
    core = own_core()

    def block(d):
        return got[pl.ds(pl.multiple_of(d * width, width), width), :]

    pull_all(index, count[0], (block, tiles1, acc1, 3 - 2 * core))
    for b in range(blocks):
        total = (acc0[b] + acc2[b]) + (acc1[b] + acc3[b])
        out[:, b * BLOCK : (b + 1) * BLOCK] = total.astype(BF16)
    a, b = (r[blocks * width :, :hid].astype(F32) for r in (sent, got))
    low, high = jnp.where(core == 0, a, b), jnp.where(core == 0, b, a)
    rows = low.shape[0]
    wg[:rows, :] = low
    wg[rows:, :] = high[: f_in - rows]
    bias[...] = high[f_in - rows : f_in - rows + 1]


def paired_sum(parts):
    parts = [p.astype(F32) for p in parts]
    while len(parts) > 1:
        parts = [parts[i] + parts[i + 1] for i in range(0, len(parts), 2)]
    return parts[0]


def paired_sum_kernel(*refs):
    refs[-1][...] = paired_sum([r[...] for r in refs[:-1]]).astype(refs[-1].dtype)


def moved(block, axis, target):
    n = lax.axis_size(axis)
    return lax.ppermute(block, axis, [(i, target(i) % n) for i in range(n)])


def radices(n):
    out = []
    while n > 1:
        r = 4 if n % 4 == 0 else 2
        out.append(r)
        n //= r
    return out


def exchanged(part, axis, stride, r):
    return [part] + [moved(part, axis, lambda i, s=s: i ^ (s * stride)) for s in range(1, r)]


def shards(node_features, weight, bias, tile_values, tile_src, tile_dst, tile_counts, out_grad):
    nodes, f_in = node_features.shape
    hid = weight.shape[1]
    blocks = nodes // BLOCK
    parts = lax.axis_size("feat")
    width = f_in // parts
    capacity = tile_values.shape[0]
    groups = capacity // REACH
    piece = jax.ShapeDtypeStruct((blocks, width, BLOCK), BF16)
    totals = jax.ShapeDtypeStruct((blocks + 1, width, BLOCK), F32)
    piece_x = jax.ShapeDtypeStruct((blocks, f_in, BLOCK), BF16)
    totals_x = jax.ShapeDtypeStruct((blocks + 1, f_in, BLOCK), F32)
    acc_x = pltpu.VMEM(totals_x.shape, F32)
    acc = pltpu.VMEM(totals.shape, F32)
    tiles = tile_values.reshape(groups, REACH, BLOCK, BLOCK)
    plane = jax.ShapeDtypeStruct((groups, BLOCK, BLOCK), BF16)
    slots = jax.ShapeDtypeStruct((capacity,), jnp.int32)
    rows = jax.ShapeDtypeStruct((nodes, hid), BF16)
    gradient = jax.ShapeDtypeStruct(((f_in + 32) // 2, hid), BF16)
    flops = 2 * capacity * BLOCK * BLOCK * width // REACH

    def swapped(i):
        return i ^ 1

    tiles1, tiles2, tiles3, xt, swap, index = call(
        forward_swap_kernel,
        [plane, plane, plane, piece_x, piece_x, slots],
        [SMEM] + [HBM] * 4,
        [VMEM] * 5 + [SMEM],
        [
            pltpu.SMEM((capacity,), jnp.int32),
            pltpu.SMEM((capacity,), jnp.int32),
            pltpu.VMEM(node_features.shape, BF16),
            acc_x,
            pltpu.SemaphoreType.DMA((6,)),
        ],
        flops,
    )(tile_counts, *(in_hbm(a) for a in (tile_src, tile_dst, node_features, tiles)))
    index = (tile_counts, index)
    swap = moved(swap, "dom", swapped)
    cut = 2 if blocks % 2 == 0 else 1
    starts = range(0, blocks, blocks // cut)
    half = jax.ShapeDtypeStruct((blocks // cut, width, BLOCK), BF16)
    half_x = jax.ShapeDtypeStruct((blocks // cut, f_in, BLOCK), BF16)
    half_wide = jax.ShapeDtypeStruct(half.shape, F32)
    half_rows = jax.ShapeDtypeStruct((hid, nodes // cut), BF16)
    half_columns = jax.ShapeDtypeStruct((f_in + 32, nodes // cut), BF16)
    acc2, *direct = call(
        forward_send_kernel,
        [totals_x] + [half_x] * cut,
        [SMEM] * 2 + [VMEM] * 3,
        [VMEM] * (1 + cut),
        [acc_x],
        2 * flops,
    )(*index, xt, tiles2, tiles3)
    chip = call(functools.partial(sum_kernel, 2, 0), [half_x] * cut, [VMEM] * 2, [VMEM] * cut)(acc2, swap)
    chip = lax.optimization_barrier((*chip, *direct[1:]))
    direct, chip = [direct[0], *chip[cut:]], chip[:cut]
    chip = [moved(c, "dom", lambda i: i + 2) for c in chip]
    acc0, tiles0, bias_t, w_t, og_t = call(
        forward_own_kernel,
        [
            totals_x,
            plane,
            jax.ShapeDtypeStruct((hid, BLOCK), F32),
            jax.ShapeDtypeStruct((hid, f_in), BF16),
            jax.ShapeDtypeStruct((hid, nodes), BF16),
        ],
        [SMEM] * 2 + [VMEM] * 3 + [HBM] * 2,
        [VMEM] * 5,
        [pltpu.VMEM(out_grad.shape, BF16), pltpu.SemaphoreType.DMA((2,))],
        flops,
    )(*index, xt, bias.reshape(1, hid), weight, in_hbm(out_grad), in_hbm(tiles))
    direct = [moved(d, "dom", lambda i: i + 1 + 2 * (i % 2)) for d in direct]
    h_list = []
    for first, c, d in zip(starts, chip, direct):
        (h,) = call(functools.partial(sum_kernel, 3, first), [half_x], [VMEM] * 3, [VMEM])(acc0, c, d)
        h_list.append(h)
    acts, hts, grads, g_list = [], [], [], []
    for first, h in zip(starts, h_list):
        act, ht, grad, g_own, *g_others = call(
            functools.partial(middle_kernel, parts, first),
            [half_rows, half_columns, half_rows, half_wide] + [half] * (parts - 1),
            [VMEM] * 5,
            [VMEM] * (3 + parts),
            (),
            4 * nodes * f_in * hid // cut,
        )(bias_t, weight, w_t, og_t, h)
        acts.append(act)
        hts.append(ht)
        grads.append(grad)
        g_list += [g_own] + [moved(g, "feat", lambda i, q=q + 1: i + q) for q, g in enumerate(g_others)]
    wg, wg_other = call(
        functools.partial(weight_grad_kernel, cut),
        [gradient, gradient],
        [VMEM] * (2 * cut),
        [VMEM, VMEM],
        (),
        2 * nodes * f_in * hid,
    )(*hts, *grads)
    r, *more = radices(lax.axis_size("dom"))
    wgs = [wg] + [moved(wg_other if s % 2 else wg, "dom", lambda i, s=s: i ^ s) for s in range(1, r)]
    (g,) = call(functools.partial(join_kernel, parts), [piece], [VMEM] * len(g_list), [VMEM])(*g_list)
    g_chip = moved(g, "dom", lambda i: i - 2)
    g_direct = moved(g, "dom", lambda i: i - 3 + 2 * (i % 2))
    stride = r
    for r in more:
        (wg,) = call(paired_sum_kernel, [gradient], [VMEM] * len(wgs), [VMEM], (), SUM_FLOPS)(*wgs)
        wgs = exchanged(wg, "dom", stride, r)
        stride *= r
    back0, output = call(
        backward_own_kernel,
        [totals, rows],
        [SMEM] * 2 + [VMEM] * (2 + cut),
        [VMEM, HBM],
        [pltpu.VMEM(rows.shape, BF16), pltpu.SemaphoreType.DMA((cut,))],
        flops,
    )(*index, tiles0, g, *acts)
    g_direct, g_chip, back0, *wgs = lax.optimization_barrier((g_direct, g_chip, back0, *wgs))
    payload = jax.ShapeDtypeStruct((blocks * width + gradient.shape[0], BLOCK), BF16)
    (sent,) = call(swap_payload_kernel, [payload], [VMEM] * (1 + len(wgs)), [VMEM])(g_chip, *wgs)
    got = moved(sent, "dom", swapped)
    back2, back3 = call(
        backward_near_kernel, [totals, totals], [SMEM] * 2 + [VMEM] * 4, [VMEM] * 2, (), 2 * flops
    )(*index, tiles2, tiles3, g_chip, g_direct)
    input_grad, weight_grad, bias_grad = call(
        backward_last_kernel,
        [
            jax.ShapeDtypeStruct((width, nodes), BF16),
            jax.ShapeDtypeStruct((f_in, hid), F32),
            jax.ShapeDtypeStruct((1, hid), F32),
        ],
        [SMEM] * 2 + [VMEM] * 6,
        [VMEM] * 3,
        [acc],
        flops,
    )(*index, tiles1, sent, got, back0, back2, back3)
    return output, weight_grad, bias_grad.reshape(hid), input_grad.T


def solution(mesh):
    return jax.shard_map(
        shards,
        mesh=mesh,
        in_specs=(
            P("dom", None),
            P(None, "feat"),
            P("feat"),
            P("dom", None, None),
            P("dom"),
            P("dom"),
            P("dom"),
            P("dom", "feat"),
        ),
        out_specs=(P("dom", "feat"), P(None, "feat"), P("feat"), P("dom", "feat")),
        check_vma=False,
    )
```

```python
import functools

import jax
import jax.numpy as jnp
from jax import lax
from jax.experimental import pallas as pl
from jax.experimental.pallas import tpu as pltpu
from jax.sharding import PartitionSpec as P

BLOCK = 128
REACH = 4
SUM_FLOPS = 10**9
SRC_UNIT = 2**16
F32 = jnp.float32
BF16 = jnp.bfloat16
VMEM = pl.BlockSpec(memory_space=pltpu.VMEM)
SMEM = pl.BlockSpec(memory_space=pltpu.SMEM)
HBM = pl.BlockSpec(memory_space=pltpu.HBM)


def call(kernel, out_shape, in_specs, out_specs, scratch=(), flops=0):
    return pl.pallas_call(
        kernel,
        out_shape=out_shape,
        in_specs=in_specs,
        out_specs=out_specs,
        scratch_shapes=list(scratch),
        compiler_params=pltpu.CompilerParams(vmem_limit_bytes=24 * 1024 * 1024),
        cost_estimate=pl.CostEstimate(flops=flops, bytes_accessed=2**20, transcendentals=0),
    )


def groups_at_once(groups):
    return next(m for m in (12, 8, 6, 4, 3, 2, 1) if groups % m == 0)


def in_hbm(a):
    return pltpu.with_memory_space_constraint(a, pltpu.HBM)


def own_core():
    return lax.rem(lax.axis_index("dom"), 2)


def slot_loop(count, groups, body):
    m = groups_at_once(groups)

    def chunk(i, carry):
        @pl.when(i * (m * REACH) < count)
        def _():
            for u in range(m):
                body(i * m + u)

        return carry

    lax.fori_loop(0, groups // m, chunk, 0)


def source(entry):
    return lax.shift_right_logical(entry, 16)


def target(entry, o, blocks):
    return lax.bitwise_and(entry, SRC_UNIT - 1) - o * blocks


def push(xt, tiles, index, count, acc, j, o):
    blocks = xt.shape[0]
    k = j * REACH + o
    entry = index[k]
    out = lax.dot_general(xt[source(entry)], tiles[j], (((1,), (1,)), ((), ())), preferred_element_type=F32)
    acc[jnp.where(k < count, target(entry, o, blocks), blocks)] += out


def pull(block, tiles, index, count, acc, j, o):
    blocks = acc.shape[0] - 1
    k = j * REACH + o
    entry = index[k]
    out = jnp.dot(block(target(entry, o, blocks)), tiles[j], preferred_element_type=F32)
    acc[jnp.where(k < count, source(entry), blocks)] += out


def push_all(xt, index, count, *planes):
    def body(j):
        for tiles, acc, o in planes:
            push(xt, tiles, index, count, acc, j, o)

    slot_loop(count, planes[0][0].shape[0], body)


def pull_all(index, count, *planes):
    def body(j):
        for block, tiles, acc, o in planes:
            pull(block, tiles, index, count, acc, j, o)

    slot_loop(count, planes[0][1].shape[0], body)


def unit(n):
    shape = (n, n)
    return (lax.broadcasted_iota(jnp.int32, shape, 0) == lax.broadcasted_iota(jnp.int32, shape, 1)).astype(BF16)


def turned(block):
    n = block.shape[1]
    return lax.dot_general(
        unit(n), block, (((1,), (1,)), ((), ())), preferred_element_type=F32
    ).astype(BF16)


def forward_swap_kernel(
    count, src_hbm, dst_hbm, x_hbm, tiles_hbm, tiles1, tiles2, tiles3, xt, swap, index, src, dst, x, acc, sems
):
    blocks = xt.shape[0]
    o = 3 - 2 * own_core()
    loads = [
        pltpu.make_async_copy(a, b, sems.at[i])
        for i, (a, b) in enumerate(
            (
                (src_hbm, src),
                (dst_hbm, dst),
                (x_hbm, x),
                (tiles_hbm.at[:, o], tiles1),
                (tiles_hbm.at[:, 2], tiles2),
                (tiles_hbm.at[:, 4 - o], tiles3),
            )
        )
    ]
    for c in loads:
        c.start()
    acc[...] = jnp.zeros_like(acc)
    for c in loads[:2]:
        c.wait()
    for k in range(src.shape[0]):
        index[k] = src[k] * SRC_UNIT + dst[k]
    loads[2].wait()
    for b in range(blocks):
        xt[b] = turned(x[b * BLOCK : (b + 1) * BLOCK, :])
    loads[3].wait()
    push_all(xt, index, count[0], (tiles1, acc, o))
    swap[...] = acc[:blocks].astype(BF16)
    for c in loads[4:]:
        c.wait()


def forward_send_kernel(count, index, xt, tiles2, tiles3, acc2, *refs):
    direct, acc = refs[:-1], refs[-1]
    acc2[...] = jnp.zeros_like(acc2)
    acc[...] = jnp.zeros_like(acc)
    push_all(xt, index, count[0], (tiles2, acc2, 2), (tiles3, acc, 1 + 2 * own_core()))
    first = 0
    for d in direct:
        d[...] = acc[first : first + d.shape[0]].astype(BF16)
        first += d.shape[0]


def forward_own_kernel(
    count, index, xt, bias_ref, w_ref, og_hbm, tiles_hbm, acc, tiles0, bias_t, w_t, og_t, og_ref, sems
):
    load_og = pltpu.make_async_copy(og_hbm, og_ref, sems.at[0])
    load_og.start()
    load = pltpu.make_async_copy(tiles_hbm.at[:, 0], tiles0, sems.at[1])
    load.start()
    acc[...] = jnp.zeros_like(acc)
    bias_t[...] = jnp.broadcast_to(bias_ref[...], (BLOCK, bias_ref.shape[1])).T
    w_t[...] = turned(w_ref[...])
    load_og.wait()
    for first in range(0, og_ref.shape[0], BLOCK):
        og_t[:, first : first + BLOCK] = turned(og_ref[first : first + BLOCK, :])
    load.wait()
    push_all(xt, index, count[0], (tiles0, acc, 0))


def sum_kernel(n, first, *refs):
    for out in refs[n:]:
        blocks = out.shape[0]
        total = None
        for r in refs[:n]:
            part = r[...] if r.shape[0] == blocks else r[first : first + blocks]
            total = part.astype(F32) if total is None else total + part.astype(F32)
        out[...] = total.astype(out.dtype)
        first += blocks


def join_kernel(parts, *refs):
    out = refs[-1]
    halves = [refs[i : i + parts] for i in range(0, len(refs) - 1, parts)]
    first = 0
    for half in halves:
        blocks = half[0].shape[0]
        total = half[0][...].astype(F32)
        for r in half[1:]:
            total = total + r[...].astype(F32)
        out[first : first + blocks] = total.astype(out.dtype)
        first += blocks


def middle_kernel(parts, first, bias_ref, w_ref, w_t_ref, og_ref, h_ref, act, ht, grads, *g_refs):
    blocks, f_in, _ = h_ref.shape
    width = f_in // parts
    me = lax.axis_index("feat")
    rows = [pl.multiple_of(lax.rem(me + q, parts) * width, width) for q in range(parts)]
    for b in range(blocks):
        ht[:f_in, b * BLOCK : (b + 1) * BLOCK] = h_ref[b]
    ht[f_in:, :] = jnp.ones((ht.shape[0] - f_in, ht.shape[1]), BF16)
    for b in range(blocks):
        cols = slice(b * BLOCK, (b + 1) * BLOCK)
        pre = jnp.dot(w_t_ref[...], h_ref[b], preferred_element_type=F32) + bias_ref[...]
        s = jax.nn.sigmoid(pre)
        act[:, cols] = (pre * s).astype(BF16)
        og = og_ref[:, (first + b) * BLOCK : (first + b + 1) * BLOCK].astype(F32)
        grad = (og * s * (1.0 + pre * (1.0 - s))).astype(BF16)
        grads[:, cols] = grad
        for q in range(parts):
            g_refs[q][b] = jnp.dot(
                w_ref[pl.ds(rows[q], width), :], grad, preferred_element_type=F32
            ).astype(g_refs[q].dtype)


def weight_grad_kernel(n, *refs):
    hts, grads, (mine, other) = refs[:n], refs[n : 2 * n], refs[2 * n :]
    full = sum(
        lax.dot_general(h[...], g[...], (((1,), (1,)), ((), ())), preferred_element_type=F32)
        for h, g in zip(hts, grads)
    )
    full = full.astype(BF16)
    rows = mine.shape[0]
    low, high = full[:rows], full[rows:]
    first = own_core() == 0
    mine[...] = jnp.where(first, low, high)
    other[...] = jnp.where(first, high, low)


def swap_payload_kernel(g, *refs):
    parts, out = refs[:-1], refs[-1]
    blocks, width, _ = g.shape
    for b in range(blocks):
        out[b * width : (b + 1) * width, :] = g[b]
    total = paired_sum([r[...] for r in parts]).astype(BF16)
    rows, hid = total.shape
    if hid < out.shape[1]:
        out[blocks * width :, :] = jnp.zeros((rows, out.shape[1]), BF16)
    out[blocks * width :, :hid] = total


def backward_own_kernel(count, index, tiles, g, *refs):
    acts, (acc, out, rows, sems) = refs[:-4], refs[-4:]
    copies, first = [], 0
    for i, act in enumerate(acts):
        for col in range(0, act.shape[1], BLOCK):
            rows[first + col : first + col + BLOCK, :] = turned(act[:, col : col + BLOCK])
        part = pl.ds(first, act.shape[1])
        copies.append(pltpu.make_async_copy(rows.at[part], out.at[part], sems.at[i]))
        copies[-1].start()
        first += act.shape[1]
    acc[...] = jnp.zeros_like(acc)
    pull_all(index, count[0], (lambda d: g[d], tiles, acc, 0))
    for c in copies:
        c.wait()


def backward_near_kernel(count, index, tiles2, tiles3, g2, g3, acc2, acc3):
    acc2[...] = jnp.zeros_like(acc2)
    acc3[...] = jnp.zeros_like(acc3)
    pull_all(
        index,
        count[0],
        (lambda d: g2[d], tiles2, acc2, 2),
        (lambda d: g3[d], tiles3, acc3, 1 + 2 * own_core()),
    )


def backward_last_kernel(count, index, tiles1, sent, got, acc0, acc2, acc3, out, wg, bias, acc1):
    blocks, width = acc1.shape[0] - 1, acc1.shape[1]
    f_in, hid = wg.shape
    acc1[...] = jnp.zeros_like(acc1)
    core = own_core()

    def block(d):
        return got[pl.ds(pl.multiple_of(d * width, width), width), :]

    pull_all(index, count[0], (block, tiles1, acc1, 3 - 2 * core))
    for b in range(blocks):
        total = (acc0[b] + acc2[b]) + (acc1[b] + acc3[b])
        out[:, b * BLOCK : (b + 1) * BLOCK] = total.astype(BF16)
    a, b = (r[blocks * width :, :hid].astype(F32) for r in (sent, got))
    low, high = jnp.where(core == 0, a, b), jnp.where(core == 0, b, a)
    rows = low.shape[0]
    wg[:rows, :] = low
    wg[rows:, :] = high[: f_in - rows]
    bias[...] = high[f_in - rows : f_in - rows + 1]


def paired_sum(parts):
    parts = [p.astype(F32) for p in parts]
    while len(parts) > 1:
        parts = [parts[i] + parts[i + 1] for i in range(0, len(parts), 2)]
    return parts[0]


def paired_sum_kernel(*refs):
    refs[-1][...] = paired_sum([r[...] for r in refs[:-1]]).astype(refs[-1].dtype)


def moved(block, axis, target):
    n = lax.axis_size(axis)
    return lax.ppermute(block, axis, [(i, target(i) % n) for i in range(n)])


def radices(n):
    out = []
    while n > 1:
        r = 4 if n % 4 == 0 else 2
        out.append(r)
        n //= r
    return out


def exchanged(part, axis, stride, r):
    return [part] + [moved(part, axis, lambda i, s=s: i ^ (s * stride)) for s in range(1, r)]


def shards(node_features, weight, bias, tile_values, tile_src, tile_dst, tile_counts, out_grad):
    nodes, f_in = node_features.shape
    hid = weight.shape[1]
    blocks = nodes // BLOCK
    parts = lax.axis_size("feat")
    width = f_in // parts
    capacity = tile_values.shape[0]
    groups = capacity // REACH
    piece = jax.ShapeDtypeStruct((blocks, width, BLOCK), BF16)
    totals = jax.ShapeDtypeStruct((blocks + 1, width, BLOCK), F32)
    piece_x = jax.ShapeDtypeStruct((blocks, f_in, BLOCK), BF16)
    totals_x = jax.ShapeDtypeStruct((blocks + 1, f_in, BLOCK), F32)
    acc_x = pltpu.VMEM(totals_x.shape, F32)
    acc = pltpu.VMEM(totals.shape, F32)
    tiles = tile_values.reshape(groups, REACH, BLOCK, BLOCK)
    plane = jax.ShapeDtypeStruct((groups, BLOCK, BLOCK), BF16)
    slots = jax.ShapeDtypeStruct((capacity,), jnp.int32)
    rows = jax.ShapeDtypeStruct((nodes, hid), BF16)
    gradient = jax.ShapeDtypeStruct(((f_in + 32) // 2, hid), BF16)
    flops = 2 * capacity * BLOCK * BLOCK * width // REACH

    def swapped(i):
        return i ^ 1

    tiles1, tiles2, tiles3, xt, swap, index = call(
        forward_swap_kernel,
        [plane, plane, plane, piece_x, piece_x, slots],
        [SMEM] + [HBM] * 4,
        [VMEM] * 5 + [SMEM],
        [
            pltpu.SMEM((capacity,), jnp.int32),
            pltpu.SMEM((capacity,), jnp.int32),
            pltpu.VMEM(node_features.shape, BF16),
            acc_x,
            pltpu.SemaphoreType.DMA((6,)),
        ],
        flops,
    )(tile_counts, *(in_hbm(a) for a in (tile_src, tile_dst, node_features, tiles)))
    index = (tile_counts, index)
    swap = moved(swap, "dom", swapped)
    cut = 2 if blocks % 2 == 0 else 1
    starts = range(0, blocks, blocks // cut)
    half = jax.ShapeDtypeStruct((blocks // cut, width, BLOCK), BF16)
    half_x = jax.ShapeDtypeStruct((blocks // cut, f_in, BLOCK), BF16)
    half_wide = jax.ShapeDtypeStruct(half.shape, F32)
    half_rows = jax.ShapeDtypeStruct((hid, nodes // cut), BF16)
    half_columns = jax.ShapeDtypeStruct((f_in + 32, nodes // cut), BF16)
    acc2, *direct = call(
        forward_send_kernel,
        [totals_x] + [half_x] * cut,
        [SMEM] * 2 + [VMEM] * 3,
        [VMEM] * (1 + cut),
        [acc_x],
        2 * flops,
    )(*index, xt, tiles2, tiles3)
    chip = call(functools.partial(sum_kernel, 2, 0), [half_x] * cut, [VMEM] * 2, [VMEM] * cut)(acc2, swap)
    chip = lax.optimization_barrier((*chip, *direct[1:]))
    direct, chip = [direct[0], *chip[cut:]], chip[:cut]
    chip = [moved(c, "dom", lambda i: i + 2) for c in chip]
    acc0, tiles0, bias_t, w_t, og_t = call(
        forward_own_kernel,
        [
            totals_x,
            plane,
            jax.ShapeDtypeStruct((hid, BLOCK), F32),
            jax.ShapeDtypeStruct((hid, f_in), BF16),
            jax.ShapeDtypeStruct((hid, nodes), BF16),
        ],
        [SMEM] * 2 + [VMEM] * 3 + [HBM] * 2,
        [VMEM] * 5,
        [pltpu.VMEM(out_grad.shape, BF16), pltpu.SemaphoreType.DMA((2,))],
        flops,
    )(*index, xt, bias.reshape(1, hid), weight, in_hbm(out_grad), in_hbm(tiles))
    direct = [moved(d, "dom", lambda i: i + 1 + 2 * (i % 2)) for d in direct]
    h_list = []
    for first, c, d in zip(starts, chip, direct):
        (h,) = call(functools.partial(sum_kernel, 3, first), [half_x], [VMEM] * 3, [VMEM])(acc0, c, d)
        h_list.append(h)
    acts, hts, grads, g_list = [], [], [], []
    for first, h in zip(starts, h_list):
        act, ht, grad, g_own, *g_others = call(
            functools.partial(middle_kernel, parts, first),
            [half_rows, half_columns, half_rows, half_wide] + [half] * (parts - 1),
            [VMEM] * 5,
            [VMEM] * (3 + parts),
            (),
            4 * nodes * f_in * hid // cut,
        )(bias_t, weight, w_t, og_t, h)
        acts.append(act)
        hts.append(ht)
        grads.append(grad)
        g_list += [g_own] + [moved(g, "feat", lambda i, q=q + 1: i + q) for q, g in enumerate(g_others)]
    wg, wg_other = call(
        functools.partial(weight_grad_kernel, cut),
        [gradient, gradient],
        [VMEM] * (2 * cut),
        [VMEM, VMEM],
        (),
        2 * nodes * f_in * hid,
    )(*hts, *grads)
    r, *more = radices(lax.axis_size("dom"))
    wgs = [wg] + [moved(wg_other if s % 2 else wg, "dom", lambda i, s=s: i ^ s) for s in range(1, r)]
    (g,) = call(functools.partial(join_kernel, parts), [piece], [VMEM] * len(g_list), [VMEM])(*g_list)
    g_chip = moved(g, "dom", lambda i: i - 2)
    g_direct = moved(g, "dom", lambda i: i - 3 + 2 * (i % 2))
    stride = r
    for r in more:
        (wg,) = call(paired_sum_kernel, [gradient], [VMEM] * len(wgs), [VMEM], (), SUM_FLOPS)(*wgs)
        wgs = exchanged(wg, "dom", stride, r)
        stride *= r
    back0, output = call(
        backward_own_kernel,
        [totals, rows],
        [SMEM] * 2 + [VMEM] * (2 + cut),
        [VMEM, HBM],
        [pltpu.VMEM(rows.shape, BF16), pltpu.SemaphoreType.DMA((cut,))],
        flops,
    )(*index, tiles0, g, *acts)
    wgs.reverse()
    g_direct, g_chip, back0, *wgs = lax.optimization_barrier((g_direct, g_chip, back0, *wgs))
    payload = jax.ShapeDtypeStruct((blocks * width + gradient.shape[0], BLOCK), BF16)
    (sent,) = call(swap_payload_kernel, [payload], [VMEM] * (1 + len(wgs)), [VMEM])(g_chip, *wgs)
    got = moved(sent, "dom", swapped)
    back2, back3 = call(
        backward_near_kernel, [totals, totals], [SMEM] * 2 + [VMEM] * 4, [VMEM] * 2, (), 2 * flops
    )(*index, tiles2, tiles3, g_chip, g_direct)
    input_grad, weight_grad, bias_grad = call(
        backward_last_kernel,
        [
            jax.ShapeDtypeStruct((width, nodes), BF16),
            jax.ShapeDtypeStruct((f_in, hid), F32),
            jax.ShapeDtypeStruct((1, hid), F32),
        ],
        [SMEM] * 2 + [VMEM] * 6,
        [VMEM] * 3,
        [acc],
        flops,
    )(*index, tiles1, sent, got, back0, back2, back3)
    return output, weight_grad, bias_grad.reshape(hid), input_grad.T


def solution(mesh):
    return jax.shard_map(
        shards,
        mesh=mesh,
        in_specs=(
            P("dom", None),
            P(None, "feat"),
            P("feat"),
            P("dom", None, None),
            P("dom"),
            P("dom"),
            P("dom"),
            P("dom", "feat"),
        ),
        out_specs=(P("dom", "feat"), P(None, "feat"), P("feat"), P("dom", "feat")),
        check_vma=False,
    )
```

```python
import functools

import jax
import jax.numpy as jnp
from jax import lax
from jax.experimental import pallas as pl
from jax.experimental.pallas import tpu as pltpu
from jax.sharding import PartitionSpec as P

BLOCK = 128
REACH = 4
SUM_FLOPS = 10**9
SRC_UNIT = 2**16
F32 = jnp.float32
BF16 = jnp.bfloat16
VMEM = pl.BlockSpec(memory_space=pltpu.VMEM)
SMEM = pl.BlockSpec(memory_space=pltpu.SMEM)
HBM = pl.BlockSpec(memory_space=pltpu.HBM)


def call(kernel, out_shape, in_specs, out_specs, scratch=(), flops=0):
    return pl.pallas_call(
        kernel,
        out_shape=out_shape,
        in_specs=in_specs,
        out_specs=out_specs,
        scratch_shapes=list(scratch),
        compiler_params=pltpu.CompilerParams(vmem_limit_bytes=24 * 1024 * 1024),
        cost_estimate=pl.CostEstimate(flops=flops, bytes_accessed=2**20, transcendentals=0),
    )


def groups_at_once(groups):
    return next(m for m in (12, 8, 6, 4, 3, 2, 1) if groups % m == 0)


def in_hbm(a):
    return pltpu.with_memory_space_constraint(a, pltpu.HBM)


def own_core():
    return lax.rem(lax.axis_index("dom"), 2)


def slot_loop(count, groups, body):
    m = groups_at_once(groups)

    def chunk(i, carry):
        @pl.when(i * (m * REACH) < count)
        def _():
            for u in range(m):
                body(i * m + u)

        return carry

    lax.fori_loop(0, groups // m, chunk, 0)


def source(entry):
    return lax.shift_right_logical(entry, 16)


def target(entry, o, blocks):
    return lax.bitwise_and(entry, SRC_UNIT - 1) - o * blocks


def push(xt, tiles, index, count, acc, j, o):
    blocks = xt.shape[0]
    k = j * REACH + o
    entry = index[k]
    out = lax.dot_general(xt[source(entry)], tiles[j], (((1,), (1,)), ((), ())), preferred_element_type=F32)
    acc[jnp.where(k < count, target(entry, o, blocks), blocks)] += out


def pull(block, tiles, index, count, acc, j, o):
    blocks = acc.shape[0] - 1
    k = j * REACH + o
    entry = index[k]
    out = jnp.dot(block(target(entry, o, blocks)), tiles[j], preferred_element_type=F32)
    acc[jnp.where(k < count, source(entry), blocks)] += out


def push_all(xt, index, count, *planes):
    def body(j):
        for tiles, acc, o in planes:
            push(xt, tiles, index, count, acc, j, o)

    slot_loop(count, planes[0][0].shape[0], body)


def pull_all(index, count, *planes):
    def body(j):
        for block, tiles, acc, o in planes:
            pull(block, tiles, index, count, acc, j, o)

    slot_loop(count, planes[0][1].shape[0], body)


def unit(n):
    shape = (n, n)
    return (lax.broadcasted_iota(jnp.int32, shape, 0) == lax.broadcasted_iota(jnp.int32, shape, 1)).astype(BF16)


def turned(block):
    n = block.shape[1]
    return lax.dot_general(
        unit(n), block, (((1,), (1,)), ((), ())), preferred_element_type=F32
    ).astype(BF16)


def forward_swap_kernel(
    count, src_hbm, dst_hbm, x_hbm, tiles_hbm, tiles1, tiles2, tiles3, xt, swap, index, src, dst, x, acc, sems
):
    blocks = xt.shape[0]
    o = 3 - 2 * own_core()
    loads = [
        pltpu.make_async_copy(a, b, sems.at[i])
        for i, (a, b) in enumerate(
            (
                (src_hbm, src),
                (dst_hbm, dst),
                (x_hbm, x),
                (tiles_hbm.at[:, o], tiles1),
                (tiles_hbm.at[:, 2], tiles2),
                (tiles_hbm.at[:, 4 - o], tiles3),
            )
        )
    ]
    for c in loads:
        c.start()
    acc[...] = jnp.zeros_like(acc)
    for c in loads[:2]:
        c.wait()
    for k in range(src.shape[0]):
        index[k] = src[k] * SRC_UNIT + dst[k]
    loads[2].wait()
    for b in range(blocks):
        xt[b] = turned(x[b * BLOCK : (b + 1) * BLOCK, :])
    loads[3].wait()
    push_all(xt, index, count[0], (tiles1, acc, o))
    swap[...] = acc[:blocks].astype(BF16)
    for c in loads[4:]:
        c.wait()


def forward_send_kernel(count, index, xt, tiles2, tiles3, acc2, *refs):
    direct, acc = refs[:-1], refs[-1]
    acc2[...] = jnp.zeros_like(acc2)
    acc[...] = jnp.zeros_like(acc)
    push_all(xt, index, count[0], (tiles2, acc2, 2), (tiles3, acc, 1 + 2 * own_core()))
    first = 0
    for d in direct:
        d[...] = acc[first : first + d.shape[0]].astype(BF16)
        first += d.shape[0]


def forward_own_kernel(
    count, index, xt, bias_ref, w_ref, og_hbm, tiles_hbm, acc, tiles0, bias_t, w_t, og_t, og_ref, sems
):
    load_og = pltpu.make_async_copy(og_hbm, og_ref, sems.at[0])
    load_og.start()
    load = pltpu.make_async_copy(tiles_hbm.at[:, 0], tiles0, sems.at[1])
    load.start()
    acc[...] = jnp.zeros_like(acc)
    bias_t[...] = jnp.broadcast_to(bias_ref[...], (BLOCK, bias_ref.shape[1])).T
    w_t[...] = turned(w_ref[...])
    load_og.wait()
    for first in range(0, og_ref.shape[0], BLOCK):
        og_t[:, first : first + BLOCK] = turned(og_ref[first : first + BLOCK, :])
    load.wait()
    push_all(xt, index, count[0], (tiles0, acc, 0))


def sum_kernel(n, first, *refs):
    for out in refs[n:]:
        blocks = out.shape[0]
        total = None
        for r in refs[:n]:
            part = r[...] if r.shape[0] == blocks else r[first : first + blocks]
            total = part.astype(F32) if total is None else total + part.astype(F32)
        out[...] = total.astype(out.dtype)
        first += blocks


def join_kernel(parts, *refs):
    out = refs[-1]
    halves = [refs[i : i + parts] for i in range(0, len(refs) - 1, parts)]
    first = 0
    for half in halves:
        blocks = half[0].shape[0]
        total = half[0][...].astype(F32)
        for r in half[1:]:
            total = total + r[...].astype(F32)
        out[first : first + blocks] = total.astype(out.dtype)
        first += blocks


def middle_kernel(parts, first, bias_ref, w_ref, w_t_ref, og_ref, h_ref, act, ht, grads, *g_refs):
    blocks, f_in, _ = h_ref.shape
    width = f_in // parts
    me = lax.axis_index("feat")
    rows = [pl.multiple_of(lax.rem(me + q, parts) * width, width) for q in range(parts)]
    for b in range(blocks):
        ht[:f_in, b * BLOCK : (b + 1) * BLOCK] = h_ref[b]
    ht[f_in:, :] = jnp.ones((ht.shape[0] - f_in, ht.shape[1]), BF16)
    for b in range(blocks):
        cols = slice(b * BLOCK, (b + 1) * BLOCK)
        pre = jnp.dot(w_t_ref[...], h_ref[b], preferred_element_type=F32) + bias_ref[...]
        s = jax.nn.sigmoid(pre)
        act[:, cols] = (pre * s).astype(BF16)
        og = og_ref[:, (first + b) * BLOCK : (first + b + 1) * BLOCK].astype(F32)
        grad = (og * s * (1.0 + pre * (1.0 - s))).astype(BF16)
        grads[:, cols] = grad
        for q in range(parts):
            g_refs[q][b] = jnp.dot(
                w_ref[pl.ds(rows[q], width), :], grad, preferred_element_type=F32
            ).astype(g_refs[q].dtype)


def weight_grad_kernel(n, *refs):
    hts, grads, (mine, other) = refs[:n], refs[n : 2 * n], refs[2 * n :]
    full = sum(
        lax.dot_general(h[...], g[...], (((1,), (1,)), ((), ())), preferred_element_type=F32)
        for h, g in zip(hts, grads)
    )
    full = full.astype(BF16)
    rows = mine.shape[0]
    low, high = full[:rows], full[rows:]
    first = own_core() == 0
    mine[...] = jnp.where(first, low, high)
    other[...] = jnp.where(first, high, low)


def swap_payload_kernel(g, *refs):
    parts, out = refs[:-1], refs[-1]
    blocks, width, _ = g.shape
    for b in range(blocks):
        out[b * width : (b + 1) * width, :] = g[b]
    total = paired_sum([r[...] for r in parts]).astype(BF16)
    rows, hid = total.shape
    if hid < out.shape[1]:
        out[blocks * width :, :] = jnp.zeros((rows, out.shape[1]), BF16)
    out[blocks * width :, :hid] = total


def backward_own_kernel(count, index, tiles, g, *refs):
    acts, (acc, out, rows, sems) = refs[:-4], refs[-4:]
    copies, first = [], 0
    for i, act in enumerate(acts):
        for col in range(0, act.shape[1], BLOCK):
            rows[first + col : first + col + BLOCK, :] = turned(act[:, col : col + BLOCK])
        part = pl.ds(first, act.shape[1])
        copies.append(pltpu.make_async_copy(rows.at[part], out.at[part], sems.at[i]))
        copies[-1].start()
        first += act.shape[1]
    acc[...] = jnp.zeros_like(acc)
    pull_all(index, count[0], (lambda d: g[d], tiles, acc, 0))
    for c in copies:
        c.wait()


def backward_near_kernel(count, index, tiles2, tiles3, g2, g3, acc2, acc3):
    acc2[...] = jnp.zeros_like(acc2)
    acc3[...] = jnp.zeros_like(acc3)
    pull_all(
        index,
        count[0],
        (lambda d: g2[d], tiles2, acc2, 2),
        (lambda d: g3[d], tiles3, acc3, 1 + 2 * own_core()),
    )


def backward_last_kernel(count, index, tiles1, sent, got, acc0, acc2, acc3, out, wg, bias, acc1):
    blocks, width = acc1.shape[0] - 1, acc1.shape[1]
    f_in, hid = wg.shape
    acc1[...] = jnp.zeros_like(acc1)
    core = own_core()

    def block(d):
        return got[pl.ds(pl.multiple_of(d * width, width), width), :]

    pull_all(index, count[0], (block, tiles1, acc1, 3 - 2 * core))
    for b in range(blocks):
        total = (acc0[b] + acc2[b]) + (acc1[b] + acc3[b])
        out[:, b * BLOCK : (b + 1) * BLOCK] = total.astype(BF16)
    a, b = (r[blocks * width :, :hid].astype(F32) for r in (sent, got))
    low, high = jnp.where(core == 0, a, b), jnp.where(core == 0, b, a)
    rows = low.shape[0]
    wg[:rows, :] = low
    wg[rows:, :] = high[: f_in - rows]
    bias[...] = high[f_in - rows : f_in - rows + 1]


def paired_sum(parts):
    parts = [p.astype(F32) for p in parts]
    while len(parts) > 1:
        parts = [parts[i] + parts[i + 1] for i in range(0, len(parts), 2)]
    return parts[0]


def paired_sum_kernel(*refs):
    refs[-1][...] = paired_sum([r[...] for r in refs[:-1]]).astype(refs[-1].dtype)


def moved(block, axis, target):
    n = lax.axis_size(axis)
    return lax.ppermute(block, axis, [(i, target(i) % n) for i in range(n)])


def radices(n):
    out = []
    while n > 1:
        r = 4 if n % 4 == 0 else 2
        out.append(r)
        n //= r
    return out


def exchanged(part, axis, stride, r):
    return [part] + [moved(part, axis, lambda i, s=s: i ^ (s * stride)) for s in range(1, r)]


def shards(node_features, weight, bias, tile_values, tile_src, tile_dst, tile_counts, out_grad):
    nodes, f_in = node_features.shape
    hid = weight.shape[1]
    blocks = nodes // BLOCK
    parts = lax.axis_size("feat")
    width = f_in // parts
    capacity = tile_values.shape[0]
    groups = capacity // REACH
    piece = jax.ShapeDtypeStruct((blocks, width, BLOCK), BF16)
    totals = jax.ShapeDtypeStruct((blocks + 1, width, BLOCK), F32)
    piece_x = jax.ShapeDtypeStruct((blocks, f_in, BLOCK), BF16)
    totals_x = jax.ShapeDtypeStruct((blocks + 1, f_in, BLOCK), F32)
    acc_x = pltpu.VMEM(totals_x.shape, F32)
    acc = pltpu.VMEM(totals.shape, F32)
    tiles = tile_values.reshape(groups, REACH, BLOCK, BLOCK)
    plane = jax.ShapeDtypeStruct((groups, BLOCK, BLOCK), BF16)
    slots = jax.ShapeDtypeStruct((capacity,), jnp.int32)
    rows = jax.ShapeDtypeStruct((nodes, hid), BF16)
    gradient = jax.ShapeDtypeStruct(((f_in + 32) // 2, hid), BF16)
    flops = 2 * capacity * BLOCK * BLOCK * width // REACH

    def swapped(i):
        return i ^ 1

    tiles1, tiles2, tiles3, xt, swap, index = call(
        forward_swap_kernel,
        [plane, plane, plane, piece_x, piece_x, slots],
        [SMEM] + [HBM] * 4,
        [VMEM] * 5 + [SMEM],
        [
            pltpu.SMEM((capacity,), jnp.int32),
            pltpu.SMEM((capacity,), jnp.int32),
            pltpu.VMEM(node_features.shape, BF16),
            acc_x,
            pltpu.SemaphoreType.DMA((6,)),
        ],
        flops,
    )(tile_counts, *(in_hbm(a) for a in (tile_src, tile_dst, node_features, tiles)))
    index = (tile_counts, index)
    swap = moved(swap, "dom", swapped)
    cut = 2 if blocks % 2 == 0 else 1
    starts = range(0, blocks, blocks // cut)
    half = jax.ShapeDtypeStruct((blocks // cut, width, BLOCK), BF16)
    half_x = jax.ShapeDtypeStruct((blocks // cut, f_in, BLOCK), BF16)
    half_wide = jax.ShapeDtypeStruct(half.shape, F32)
    half_rows = jax.ShapeDtypeStruct((hid, nodes // cut), BF16)
    half_columns = jax.ShapeDtypeStruct((f_in + 32, nodes // cut), BF16)
    acc2, *direct = call(
        forward_send_kernel,
        [totals_x] + [half_x] * cut,
        [SMEM] * 2 + [VMEM] * 3,
        [VMEM] * (1 + cut),
        [acc_x],
        2 * flops,
    )(*index, xt, tiles2, tiles3)
    chip = call(functools.partial(sum_kernel, 2, 0), [half_x] * cut, [VMEM] * 2, [VMEM] * cut)(acc2, swap)
    chip = lax.optimization_barrier((*chip, *direct))
    direct, chip = chip[cut:], chip[:cut]
    chip = [moved(c, "dom", lambda i: i + 2) for c in chip]
    acc0, tiles0, bias_t, w_t, og_t = call(
        forward_own_kernel,
        [
            totals_x,
            plane,
            jax.ShapeDtypeStruct((hid, BLOCK), F32),
            jax.ShapeDtypeStruct((hid, f_in), BF16),
            jax.ShapeDtypeStruct((hid, nodes), BF16),
        ],
        [SMEM] * 2 + [VMEM] * 3 + [HBM] * 2,
        [VMEM] * 5,
        [pltpu.VMEM(out_grad.shape, BF16), pltpu.SemaphoreType.DMA((2,))],
        flops,
    )(*index, xt, bias.reshape(1, hid), weight, in_hbm(out_grad), in_hbm(tiles))
    direct = [moved(d, "dom", lambda i: i + 1 + 2 * (i % 2)) for d in direct]
    h_list = []
    for first, c, d in zip(starts, chip, direct):
        (h,) = call(functools.partial(sum_kernel, 3, first), [half_x], [VMEM] * 3, [VMEM])(
            acc0, *((c, d) if first == 0 else (d, c))
        )
        h_list.append(h)
    acts, hts, grads, g_list = [], [], [], []
    for first, h in zip(starts, h_list):
        act, ht, grad, g_own, *g_others = call(
            functools.partial(middle_kernel, parts, first),
            [half_rows, half_columns, half_rows, half_wide] + [half] * (parts - 1),
            [VMEM] * 5,
            [VMEM] * (3 + parts),
            (),
            4 * nodes * f_in * hid // cut,
        )(bias_t, weight, w_t, og_t, h)
        acts.append(act)
        hts.append(ht)
        grads.append(grad)
        g_list += [g_own] + [moved(g, "feat", lambda i, q=q + 1: i + q) for q, g in enumerate(g_others)]
    wg, wg_other = call(
        functools.partial(weight_grad_kernel, cut),
        [gradient, gradient],
        [VMEM] * (2 * cut),
        [VMEM, VMEM],
        (),
        2 * nodes * f_in * hid,
    )(*hts, *grads)
    r, *more = radices(lax.axis_size("dom"))
    wgs = [wg] + [moved(wg_other if s % 2 else wg, "dom", lambda i, s=s: i ^ s) for s in range(1, r)]
    (g,) = call(functools.partial(join_kernel, parts), [piece], [VMEM] * len(g_list), [VMEM])(*g_list)
    g_chip = moved(g, "dom", lambda i: i - 2)
    g_direct = moved(g, "dom", lambda i: i - 3 + 2 * (i % 2))
    stride = r
    for r in more:
        (wg,) = call(paired_sum_kernel, [gradient], [VMEM] * len(wgs), [VMEM], (), SUM_FLOPS)(*wgs)
        wgs = exchanged(wg, "dom", stride, r)
        stride *= r
    back0, output = call(
        backward_own_kernel,
        [totals, rows],
        [SMEM] * 2 + [VMEM] * (2 + cut),
        [VMEM, HBM],
        [pltpu.VMEM(rows.shape, BF16), pltpu.SemaphoreType.DMA((cut,))],
        flops,
    )(*index, tiles0, g, *acts)
    g_direct, g_chip, back0, *wgs = lax.optimization_barrier((g_direct, g_chip, back0, *wgs))
    payload = jax.ShapeDtypeStruct((blocks * width + gradient.shape[0], BLOCK), BF16)
    (sent,) = call(swap_payload_kernel, [payload], [VMEM] * (1 + len(wgs)), [VMEM])(g_chip, *wgs)
    got = moved(sent, "dom", swapped)
    back2, back3 = call(
        backward_near_kernel, [totals, totals], [SMEM] * 2 + [VMEM] * 4, [VMEM] * 2, (), 2 * flops
    )(*index, tiles2, tiles3, g_chip, g_direct)
    input_grad, weight_grad, bias_grad = call(
        backward_last_kernel,
        [
            jax.ShapeDtypeStruct((width, nodes), BF16),
            jax.ShapeDtypeStruct((f_in, hid), F32),
            jax.ShapeDtypeStruct((1, hid), F32),
        ],
        [SMEM] * 2 + [VMEM] * 6,
        [VMEM] * 3,
        [acc],
        flops,
    )(*index, tiles1, sent, got, back0, back2, back3)
    return output, weight_grad, bias_grad.reshape(hid), input_grad.T


def solution(mesh):
    return jax.shard_map(
        shards,
        mesh=mesh,
        in_specs=(
            P("dom", None),
            P(None, "feat"),
            P("feat"),
            P("dom", None, None),
            P("dom"),
            P("dom"),
            P("dom"),
            P("dom", "feat"),
        ),
        out_specs=(P("dom", "feat"), P(None, "feat"), P("feat"), P("dom", "feat")),
        check_vma=False,
    )
```

```python
import functools

import jax
import jax.numpy as jnp
from jax import lax
from jax.experimental import pallas as pl
from jax.experimental.pallas import tpu as pltpu
from jax.sharding import PartitionSpec as P

BLOCK = 128
REACH = 4
SUM_FLOPS = 10**9
SRC_UNIT = 2**16
F32 = jnp.float32
BF16 = jnp.bfloat16
VMEM = pl.BlockSpec(memory_space=pltpu.VMEM)
SMEM = pl.BlockSpec(memory_space=pltpu.SMEM)
HBM = pl.BlockSpec(memory_space=pltpu.HBM)


def call(kernel, out_shape, in_specs, out_specs, scratch=(), flops=0):
    return pl.pallas_call(
        kernel,
        out_shape=out_shape,
        in_specs=in_specs,
        out_specs=out_specs,
        scratch_shapes=list(scratch),
        compiler_params=pltpu.CompilerParams(vmem_limit_bytes=24 * 1024 * 1024),
        cost_estimate=pl.CostEstimate(flops=flops, bytes_accessed=2**20, transcendentals=0),
    )


def groups_at_once(groups):
    return next(m for m in (12, 8, 6, 4, 3, 2, 1) if groups % m == 0)


def in_hbm(a):
    return pltpu.with_memory_space_constraint(a, pltpu.HBM)


def own_core():
    return lax.rem(lax.axis_index("dom"), 2)


def slot_loop(count, groups, body):
    m = groups_at_once(groups)

    def chunk(i, carry):
        @pl.when(i * (m * REACH) < count)
        def _():
            for u in range(m):
                body(i * m + u)

        return carry

    lax.fori_loop(0, groups // m, chunk, 0)


def source(entry):
    return lax.shift_right_logical(entry, 16)


def target(entry, o, blocks):
    return lax.bitwise_and(entry, SRC_UNIT - 1) - o * blocks


def push(xt, tiles, index, count, acc, j, o):
    blocks = xt.shape[0]
    k = j * REACH + o
    entry = index[k]
    out = lax.dot_general(xt[source(entry)], tiles[j], (((1,), (1,)), ((), ())), preferred_element_type=F32)
    acc[jnp.where(k < count, target(entry, o, blocks), blocks)] += out


def pull(block, tiles, index, count, acc, j, o):
    blocks = acc.shape[0] - 1
    k = j * REACH + o
    entry = index[k]
    out = jnp.dot(block(target(entry, o, blocks)), tiles[j], preferred_element_type=F32)
    acc[jnp.where(k < count, source(entry), blocks)] += out


def push_all(xt, index, count, *planes):
    def body(j):
        for tiles, acc, o in planes:
            push(xt, tiles, index, count, acc, j, o)

    slot_loop(count, planes[0][0].shape[0], body)


def pull_all(index, count, *planes):
    def body(j):
        for block, tiles, acc, o in planes:
            pull(block, tiles, index, count, acc, j, o)

    slot_loop(count, planes[0][1].shape[0], body)


def unit(n):
    shape = (n, n)
    return (lax.broadcasted_iota(jnp.int32, shape, 0) == lax.broadcasted_iota(jnp.int32, shape, 1)).astype(BF16)


def turned(block):
    n = block.shape[1]
    return lax.dot_general(
        unit(n), block, (((1,), (1,)), ((), ())), preferred_element_type=F32
    ).astype(BF16)


def forward_swap_kernel(
    count, src_hbm, dst_hbm, x_hbm, tiles_hbm, tiles1, tiles2, tiles3, xt, swap, index, src, dst, x, acc, sems
):
    blocks = xt.shape[0]
    o = 3 - 2 * own_core()
    loads = [
        pltpu.make_async_copy(a, b, sems.at[i])
        for i, (a, b) in enumerate(
            (
                (src_hbm, src),
                (dst_hbm, dst),
                (x_hbm, x),
                (tiles_hbm.at[:, o], tiles1),
                (tiles_hbm.at[:, 2], tiles2),
                (tiles_hbm.at[:, 4 - o], tiles3),
            )
        )
    ]
    for c in loads:
        c.start()
    acc[...] = jnp.zeros_like(acc)
    for c in loads[:2]:
        c.wait()
    for k in range(src.shape[0]):
        index[k] = src[k] * SRC_UNIT + dst[k]
    loads[2].wait()
    for b in range(blocks):
        xt[b] = turned(x[b * BLOCK : (b + 1) * BLOCK, :])
    loads[3].wait()
    push_all(xt, index, count[0], (tiles1, acc, o))
    swap[...] = acc[:blocks].astype(BF16)
    for c in loads[4:]:
        c.wait()


def forward_send_kernel(count, index, xt, tiles2, tiles3, acc2, *refs):
    direct, acc = refs[:-1], refs[-1]
    acc2[...] = jnp.zeros_like(acc2)
    acc[...] = jnp.zeros_like(acc)
    push_all(xt, index, count[0], (tiles2, acc2, 2), (tiles3, acc, 1 + 2 * own_core()))
    first = 0
    for d in direct:
        d[...] = acc[first : first + d.shape[0]].astype(BF16)
        first += d.shape[0]


def forward_own_kernel(
    count, index, xt, bias_ref, w_ref, og_hbm, tiles_hbm, acc, tiles0, bias_t, w_t, og_t, og_ref, sems
):
    load_og = pltpu.make_async_copy(og_hbm, og_ref, sems.at[0])
    load_og.start()
    load = pltpu.make_async_copy(tiles_hbm.at[:, 0], tiles0, sems.at[1])
    load.start()
    acc[...] = jnp.zeros_like(acc)
    bias_t[...] = jnp.broadcast_to(bias_ref[...], (BLOCK, bias_ref.shape[1])).T
    w_t[...] = turned(w_ref[...])
    load_og.wait()
    for first in range(0, og_ref.shape[0], BLOCK):
        og_t[:, first : first + BLOCK] = turned(og_ref[first : first + BLOCK, :])
    load.wait()
    push_all(xt, index, count[0], (tiles0, acc, 0))


def sum_kernel(n, first, *refs):
    for out in refs[n:]:
        blocks = out.shape[0]
        total = None
        for r in refs[:n]:
            part = r[...] if r.shape[0] == blocks else r[first : first + blocks]
            total = part.astype(F32) if total is None else total + part.astype(F32)
        out[...] = total.astype(out.dtype)
        first += blocks


def join_kernel(parts, *refs):
    out = refs[-1]
    halves = [refs[i : i + parts] for i in range(0, len(refs) - 1, parts)]
    first = 0
    for half in halves:
        blocks = half[0].shape[0]
        total = half[0][...].astype(F32)
        for r in half[1:]:
            total = total + r[...].astype(F32)
        out[first : first + blocks] = total.astype(out.dtype)
        first += blocks


def middle_kernel(parts, first, bias_ref, w_ref, w_t_ref, og_ref, h_ref, act, ht, grads, *g_refs):
    blocks, f_in, _ = h_ref.shape
    width = f_in // parts
    me = lax.axis_index("feat")
    rows = [pl.multiple_of(lax.rem(me + q, parts) * width, width) for q in range(parts)]
    for b in range(blocks):
        ht[:f_in, b * BLOCK : (b + 1) * BLOCK] = h_ref[b]
    ht[f_in:, :] = jnp.ones((ht.shape[0] - f_in, ht.shape[1]), BF16)
    for b in range(blocks):
        cols = slice(b * BLOCK, (b + 1) * BLOCK)
        pre = jnp.dot(w_t_ref[...], h_ref[b], preferred_element_type=F32) + bias_ref[...]
        s = 0.5 * jnp.tanh(0.5 * pre) + 0.5
        act[:, cols] = (pre * s).astype(BF16)
        og = og_ref[:, (first + b) * BLOCK : (first + b + 1) * BLOCK].astype(F32)
        grad = (og * s * (1.0 + pre * (1.0 - s))).astype(BF16)
        grads[:, cols] = grad
        for q in range(parts):
            g_refs[q][b] = jnp.dot(
                w_ref[pl.ds(rows[q], width), :], grad, preferred_element_type=F32
            ).astype(g_refs[q].dtype)


def weight_grad_kernel(n, *refs):
    hts, grads, (mine, other) = refs[:n], refs[n : 2 * n], refs[2 * n :]
    full = sum(
        lax.dot_general(h[...], g[...], (((1,), (1,)), ((), ())), preferred_element_type=F32)
        for h, g in zip(hts, grads)
    )
    full = full.astype(BF16)
    rows = mine.shape[0]
    low, high = full[:rows], full[rows:]
    first = own_core() == 0
    mine[...] = jnp.where(first, low, high)
    other[...] = jnp.where(first, high, low)


def swap_payload_kernel(g, *refs):
    parts, out = refs[:-1], refs[-1]
    blocks, width, _ = g.shape
    for b in range(blocks):
        out[b * width : (b + 1) * width, :] = g[b]
    total = paired_sum([r[...] for r in parts]).astype(BF16)
    rows, hid = total.shape
    if hid < out.shape[1]:
        out[blocks * width :, :] = jnp.zeros((rows, out.shape[1]), BF16)
    out[blocks * width :, :hid] = total


def backward_own_kernel(count, index, tiles, g, *refs):
    acts, (acc, out, rows, sems) = refs[:-4], refs[-4:]
    copies, first = [], 0
    for i, act in enumerate(acts):
        for col in range(0, act.shape[1], BLOCK):
            rows[first + col : first + col + BLOCK, :] = turned(act[:, col : col + BLOCK])
        part = pl.ds(first, act.shape[1])
        copies.append(pltpu.make_async_copy(rows.at[part], out.at[part], sems.at[i]))
        copies[-1].start()
        first += act.shape[1]
    acc[...] = jnp.zeros_like(acc)
    pull_all(index, count[0], (lambda d: g[d], tiles, acc, 0))
    for c in copies:
        c.wait()


def backward_near_kernel(count, index, tiles2, tiles3, g2, g3, acc2, acc3):
    acc2[...] = jnp.zeros_like(acc2)
    acc3[...] = jnp.zeros_like(acc3)
    pull_all(
        index,
        count[0],
        (lambda d: g2[d], tiles2, acc2, 2),
        (lambda d: g3[d], tiles3, acc3, 1 + 2 * own_core()),
    )


def backward_last_kernel(count, index, tiles1, sent, got, acc0, acc2, acc3, out, wg, bias, acc1):
    blocks, width = acc1.shape[0] - 1, acc1.shape[1]
    f_in, hid = wg.shape
    acc1[...] = jnp.zeros_like(acc1)
    core = own_core()

    def block(d):
        return got[pl.ds(pl.multiple_of(d * width, width), width), :]

    pull_all(index, count[0], (block, tiles1, acc1, 3 - 2 * core))
    for b in range(blocks):
        total = (acc0[b] + acc2[b]) + (acc1[b] + acc3[b])
        out[:, b * BLOCK : (b + 1) * BLOCK] = total.astype(BF16)
    a, b = (r[blocks * width :, :hid].astype(F32) for r in (sent, got))
    low, high = jnp.where(core == 0, a, b), jnp.where(core == 0, b, a)
    rows = low.shape[0]
    wg[:rows, :] = low
    wg[rows:, :] = high[: f_in - rows]
    bias[...] = high[f_in - rows : f_in - rows + 1]


def paired_sum(parts):
    parts = [p.astype(F32) for p in parts]
    while len(parts) > 1:
        parts = [parts[i] + parts[i + 1] for i in range(0, len(parts), 2)]
    return parts[0]


def paired_sum_kernel(*refs):
    refs[-1][...] = paired_sum([r[...] for r in refs[:-1]]).astype(refs[-1].dtype)


def moved(block, axis, target):
    n = lax.axis_size(axis)
    return lax.ppermute(block, axis, [(i, target(i) % n) for i in range(n)])


def radices(n):
    out = []
    while n > 1:
        r = 4 if n % 4 == 0 else 2
        out.append(r)
        n //= r
    return out


def exchanged(part, axis, stride, r):
    return [part] + [moved(part, axis, lambda i, s=s: i ^ (s * stride)) for s in range(1, r)]


def shards(node_features, weight, bias, tile_values, tile_src, tile_dst, tile_counts, out_grad):
    nodes, f_in = node_features.shape
    hid = weight.shape[1]
    blocks = nodes // BLOCK
    parts = lax.axis_size("feat")
    width = f_in // parts
    capacity = tile_values.shape[0]
    groups = capacity // REACH
    piece = jax.ShapeDtypeStruct((blocks, width, BLOCK), BF16)
    totals = jax.ShapeDtypeStruct((blocks + 1, width, BLOCK), F32)
    piece_x = jax.ShapeDtypeStruct((blocks, f_in, BLOCK), BF16)
    totals_x = jax.ShapeDtypeStruct((blocks + 1, f_in, BLOCK), F32)
    acc_x = pltpu.VMEM(totals_x.shape, F32)
    acc = pltpu.VMEM(totals.shape, F32)
    tiles = tile_values.reshape(groups, REACH, BLOCK, BLOCK)
    plane = jax.ShapeDtypeStruct((groups, BLOCK, BLOCK), BF16)
    slots = jax.ShapeDtypeStruct((capacity,), jnp.int32)
    rows = jax.ShapeDtypeStruct((nodes, hid), BF16)
    gradient = jax.ShapeDtypeStruct(((f_in + 32) // 2, hid), BF16)
    flops = 2 * capacity * BLOCK * BLOCK * width // REACH

    def swapped(i):
        return i ^ 1

    tiles1, tiles2, tiles3, xt, swap, index = call(
        forward_swap_kernel,
        [plane, plane, plane, piece_x, piece_x, slots],
        [SMEM] + [HBM] * 4,
        [VMEM] * 5 + [SMEM],
        [
            pltpu.SMEM((capacity,), jnp.int32),
            pltpu.SMEM((capacity,), jnp.int32),
            pltpu.VMEM(node_features.shape, BF16),
            acc_x,
            pltpu.SemaphoreType.DMA((6,)),
        ],
        flops,
    )(tile_counts, *(in_hbm(a) for a in (tile_src, tile_dst, node_features, tiles)))
    index = (tile_counts, index)
    swap = moved(swap, "dom", swapped)
    cut = 2 if blocks % 2 == 0 else 1
    starts = range(0, blocks, blocks // cut)
    half = jax.ShapeDtypeStruct((blocks // cut, width, BLOCK), BF16)
    half_x = jax.ShapeDtypeStruct((blocks // cut, f_in, BLOCK), BF16)
    half_wide = jax.ShapeDtypeStruct(half.shape, F32)
    half_rows = jax.ShapeDtypeStruct((hid, nodes // cut), BF16)
    half_columns = jax.ShapeDtypeStruct((f_in + 32, nodes // cut), BF16)
    acc2, *direct = call(
        forward_send_kernel,
        [totals_x] + [half_x] * cut,
        [SMEM] * 2 + [VMEM] * 3,
        [VMEM] * (1 + cut),
        [acc_x],
        2 * flops,
    )(*index, xt, tiles2, tiles3)
    chip = call(functools.partial(sum_kernel, 2, 0), [half_x] * cut, [VMEM] * 2, [VMEM] * cut)(acc2, swap)
    chip = lax.optimization_barrier((*chip, *direct[1:]))
    direct, chip = [direct[0], *chip[cut:]], chip[:cut]
    chip = [moved(c, "dom", lambda i: i + 2) for c in chip]
    acc0, tiles0, bias_t, w_t, og_t = call(
        forward_own_kernel,
        [
            totals_x,
            plane,
            jax.ShapeDtypeStruct((hid, BLOCK), F32),
            jax.ShapeDtypeStruct((hid, f_in), BF16),
            jax.ShapeDtypeStruct((hid, nodes), BF16),
        ],
        [SMEM] * 2 + [VMEM] * 3 + [HBM] * 2,
        [VMEM] * 5,
        [pltpu.VMEM(out_grad.shape, BF16), pltpu.SemaphoreType.DMA((2,))],
        flops,
    )(*index, xt, bias.reshape(1, hid), weight, in_hbm(out_grad), in_hbm(tiles))
    direct = [moved(d, "dom", lambda i: i + 1 + 2 * (i % 2)) for d in direct]
    h_list = []
    for first, c, d in zip(starts, chip, direct):
        (h,) = call(functools.partial(sum_kernel, 3, first), [half_x], [VMEM] * 3, [VMEM])(acc0, d, c)
        h_list.append(h)
    acts, hts, grads, g_list = [], [], [], []
    for first, h in zip(starts, h_list):
        act, ht, grad, g_own, *g_others = call(
            functools.partial(middle_kernel, parts, first),
            [half_rows, half_columns, half_rows, half_wide] + [half] * (parts - 1),
            [VMEM] * 5,
            [VMEM] * (3 + parts),
            (),
            4 * nodes * f_in * hid // cut,
        )(bias_t, weight, w_t, og_t, h)
        acts.append(act)
        hts.append(ht)
        grads.append(grad)
        g_list += [g_own] + [moved(g, "feat", lambda i, q=q + 1: i + q) for q, g in enumerate(g_others)]
    wg, wg_other = call(
        functools.partial(weight_grad_kernel, cut),
        [gradient, gradient],
        [VMEM] * (2 * cut),
        [VMEM, VMEM],
        (),
        2 * nodes * f_in * hid,
    )(*hts, *grads)
    r, *more = radices(lax.axis_size("dom"))
    wgs = [wg] + [moved(wg_other if s % 2 else wg, "dom", lambda i, s=s: i ^ s) for s in range(1, r)]
    (g,) = call(functools.partial(join_kernel, parts), [piece], [VMEM] * len(g_list), [VMEM])(*g_list)
    g_chip = moved(g, "dom", lambda i: i - 2)
    g_direct = moved(g, "dom", lambda i: i - 3 + 2 * (i % 2))
    stride = r
    for r in more:
        (wg,) = call(paired_sum_kernel, [gradient], [VMEM] * len(wgs), [VMEM], (), SUM_FLOPS)(*wgs)
        wgs = exchanged(wg, "dom", stride, r)
        stride *= r
    back0, output = call(
        backward_own_kernel,
        [totals, rows],
        [SMEM] * 2 + [VMEM] * (2 + cut),
        [VMEM, HBM],
        [pltpu.VMEM(rows.shape, BF16), pltpu.SemaphoreType.DMA((cut,))],
        flops,
    )(*index, tiles0, g, *acts)
    g_direct, g_chip, back0, *wgs = lax.optimization_barrier((g_direct, g_chip, back0, *wgs))
    payload = jax.ShapeDtypeStruct((blocks * width + gradient.shape[0], BLOCK), BF16)
    (sent,) = call(swap_payload_kernel, [payload], [VMEM] * (1 + len(wgs)), [VMEM])(g_chip, *wgs)
    got = moved(sent, "dom", swapped)
    back2, back3 = call(
        backward_near_kernel, [totals, totals], [SMEM] * 2 + [VMEM] * 4, [VMEM] * 2, (), 2 * flops
    )(*index, tiles2, tiles3, g_chip, g_direct)
    input_grad, weight_grad, bias_grad = call(
        backward_last_kernel,
        [
            jax.ShapeDtypeStruct((width, nodes), BF16),
            jax.ShapeDtypeStruct((f_in, hid), F32),
            jax.ShapeDtypeStruct((1, hid), F32),
        ],
        [SMEM] * 2 + [VMEM] * 6,
        [VMEM] * 3,
        [acc],
        flops,
    )(*index, tiles1, sent, got, back0, back2, back3)
    return output, weight_grad, bias_grad.reshape(hid), input_grad.T


def solution(mesh):
    return jax.shard_map(
        shards,
        mesh=mesh,
        in_specs=(
            P("dom", None),
            P(None, "feat"),
            P("feat"),
            P("dom", None, None),
            P("dom"),
            P("dom"),
            P("dom"),
            P("dom", "feat"),
        ),
        out_specs=(P("dom", "feat"), P(None, "feat"), P("feat"), P("dom", "feat")),
        check_vma=False,
    )
```
